32 devices in a mesh: member: 4 (over z), tile: 8 (over y, x, core).
Axes of the slice: x: 2, y: 2, z: 4, core: 2. Of those that a mesh axis runs over, the one named last changes fastest.
Arguments:
- teacher_logits: bfloat16 [16, 1024, 4096], P('member', 'tile'), may hold values from -8 to 260
- coverage: int32 [1024], P('tile'), may hold values from 0 to 7, as said below
- features: bfloat16 [4, 256, 64, 256], P('member', 'tile'), may hold values from -6 to 6
- labels: int32 [4, 256, 64], P('member', 'tile'), may hold values from 0 to 63
- first_weight: bfloat16 [3, 3, 256, 256], replicated, may hold values from -0.125 to 0.125
- second_weight: bfloat16 [3, 3, 256, 256], replicated, may hold values from -0.125 to 0.125
- head_weight: bfloat16 [256, 64], replicated, may hold values from -0.375 to 0.375
Outputs:
- first_kernel_grad: float32 [3, 3, 256, 256], replicated
- second_kernel_grad: float32 [3, 3, 256, 256], replicated
- head_kernel_grad: float32 [256, 64], replicated
- loss_value: float32 [], replicated
The draws below stay inside these ranges and needn't reach their ends.
Inputs may be any that keep to these rules, and one draw needn't show every extreme that they name: Slot k of column t goes to column coverage[t * 128 + k]; for every slot each column receives it from exactly one column. Within each block of 32 consecutive slots a column sends at most 8 tiles to any one column and exactly 8 to one; over all 128 slots at most 32 to any one column, reached.
All inputs are finite; a program needn't handle non-finite values.
Results may differ from the reference program's by a relative error of at most 0.013.
The reference program's roundings to bfloat16 on the way (of `hidden_one`, `hidden_two`, `logit_grad`, `grad_two` and `grad_one`) count: a program that leaves them out, or rounds other values in their place, can miss the bound.
Values may be sent and summed in bfloat16 or wider, within the bound.
No kernel may reach another device: no remote copies, remote signals or barrier semaphores. Data moves between devices by JAX's collectives and lax.ppermute only.
A program may use at most 128 MiB of HBM per device.

```python
import math
import jax
import jax.numpy as jnp
from jax import lax

C = 256
K = 64
TE = 8
W = 64
RD = 32
MEMBERS = 16
SD = 32
TD = 128
TILES = 1024
CAPB = 8
ROWS = 256
N_MEMBER = 4
N_TILE = 8


def draw_teacher_logits(key, part):
    array_shape = (MEMBERS, TILES, TE * TE, K)
    values = jnp.clip(2.0 * jax.random.normal(key, array_shape, jnp.float32), -8.0, 8.0)
    return values.reshape(MEMBERS, TILES, TE * TE * K).astype(jnp.bfloat16)


def draw_coverage(key, part):
    source_column = jax.random.randint(jax.random.fold_in(key, 11), (), 0, N_TILE).astype(jnp.int32)
    target_column = jax.random.randint(jax.random.fold_in(key, 12), (), 0, N_TILE).astype(jnp.int32)
    columns = jnp.arange(N_TILE, dtype=jnp.int32)
    blocks = []
    for group_index in range(N_MEMBER):
        ordering = jax.random.permutation(jax.random.fold_in(key, 300 + group_index), N_TILE).astype(jnp.int32)
        mapping = jnp.zeros((N_TILE,), jnp.int32).at[ordering].set(columns)
        forced = (ordering[target_column] - source_column) % N_TILE
        others = (forced + 1 + jnp.arange(N_TILE - 1, dtype=jnp.int32)) % N_TILE
        offset_pool = jnp.repeat(others, CAPB)
        shuffled = jax.random.permutation(jax.random.fold_in(key, 100 + group_index), offset_pool)[:SD - CAPB]
        chosen = jnp.concatenate([jnp.full((CAPB,), forced, jnp.int32), shuffled.astype(jnp.int32)])
        offsets = jax.random.permutation(jax.random.fold_in(key, 200 + group_index), chosen)
        shifted = (columns[:, None] + offsets[None, :]) % N_TILE
        blocks.append(mapping[shifted])
    return jnp.concatenate(blocks, axis=1).reshape(TILES).astype(jnp.int32)


def plant(result, stream_key, smallest, largest):
    longest = result.shape.index(max(result.shape))
    spots = []
    for shift in (0, 1):
        where = [jax.random.randint(jax.random.fold_in(stream_key, axis), (), 0, length) for axis, length in enumerate(result.shape)]
        where[longest] = (where[longest] + shift) % result.shape[longest]
        spots.append(tuple(where))
    return result.at[spots[0]].set(smallest).at[spots[1]].set(largest)


def block_levels(own_key, extent, pieces, least, high):
    factor_of, own = 1.0, jax.random.fold_in(own_key, 6)
    for position, blocks in pieces:
        draws = jnp.exp(jax.random.uniform(jax.random.fold_in(own, position), (blocks,), jnp.float32, least / len(pieces), high / len(pieces)))
        factor_of = factor_of * jnp.repeat(draws, extent[position] // blocks).reshape([-1 if axis == position else 1 for axis in range(len(extent))])
    return factor_of


def bell_draw(key, shape, deviation, bound, pieces=(), kind=jnp.bfloat16):
    result = jax.random.normal(key, shape, jnp.float32) * deviation
    if len(pieces) > 0:
        result = block_levels(key, shape, pieces, -0.22, 0.18) * result
    return jnp.clip(result, min=-bound, max=bound).astype(kind)


def setup_inputs(seed: int = 0) -> dict:
    splits = jax.random.split(jax.random.key(seed), 8)
    teacher_logits = draw_teacher_logits(jax.random.fold_in(splits[7], 71), 0)
    coverage = draw_coverage(jax.random.fold_in(splits[7], 71), 0)
    features = bell_draw(splits[2], (N_MEMBER, ROWS, W, C), 1.0, 6.0, ((0, 4), (1, 8)))
    labels = plant(jax.random.randint(splits[3], (N_MEMBER, ROWS, W), 0, K), jax.random.fold_in(splits[3], 1), 0, K - 1).astype(jnp.int32)
    first_weight = bell_draw(splits[4], (3, 3, C, C), (9 * C) ** -0.5, 0.125)
    second_weight = bell_draw(splits[5], (3, 3, C, C), (9 * C) ** -0.5, 0.125)
    head_weight = bell_draw(splits[6], (C, K), C ** -0.5, 0.375)
    return {"teacher_logits": teacher_logits, "coverage": coverage, "features": features, "labels": labels, "first_weight": first_weight, "second_weight": second_weight, "head_weight": head_weight}


def conv_taps(padded, kernel, dilation, row_count, col_count):
    channels = padded.shape[-1]
    summed = jnp.zeros((row_count * col_count, kernel.shape[-1]), jnp.float32)
    for row_tap in range(3):
        for col_tap in range(3):
            window = padded[row_tap * dilation:row_tap * dilation + row_count, col_tap * dilation:col_tap * dilation + col_count]
            summed = summed + jnp.dot(window.reshape(-1, channels), kernel[row_tap, col_tap], preferred_element_type=jnp.float32)
    return summed

def kernel_grad(padded, grads, dilation, row_count, col_count):
    channels = padded.shape[-1]
    flat_grads = grads.reshape(row_count * col_count, -1)
    outer = []
    for row_tap in range(3):
        inner = []
        for col_tap in range(3):
            window = padded[row_tap * dilation:row_tap * dilation + row_count, col_tap * dilation:col_tap * dilation + col_count]
            inner.append(jnp.dot(window.reshape(-1, channels).T, flat_grads, preferred_element_type=jnp.float32))
        outer.append(jnp.stack(inner))
    return jnp.stack(outer)

def input_grad(padded_grads, kernel, dilation, row_count, col_count):
    channels = padded_grads.shape[-1]
    summed = jnp.zeros((row_count * col_count, kernel.shape[2]), jnp.float32)
    for row_tap in range(3):
        for col_tap in range(3):
            row_from = (2 - row_tap) * dilation
            col_from = (2 - col_tap) * dilation
            window = padded_grads[row_from:row_from + row_count, col_from:col_from + col_count]
            summed = summed + jnp.dot(window.reshape(-1, channels), kernel[row_tap, col_tap].T, preferred_element_type=jnp.float32)
    return summed

def head_terms(hidden_two, head_weight, teacher_mean, spread_sum, label_rows, scale):
    classes = head_weight.shape[1]
    logits = jnp.dot(hidden_two, head_weight, preferred_element_type=jnp.float32)
    log_student = jax.nn.log_softmax(logits, axis=-1)
    student_probs = jnp.exp(log_student)
    cell_weight = 1.0 / (0.1 + spread_sum)
    onehot = (label_rows[:, None] == jnp.arange(classes, dtype=jnp.int32)[None, :]).astype(jnp.float32)
    entropy_part = lax.optimization_barrier(jnp.sum(jax.scipy.special.xlogy(teacher_mean, teacher_mean), axis=-1))
    pixel_loss = cell_weight * (entropy_part - lax.optimization_barrier(jnp.sum(teacher_mean * log_student, axis=-1))) - lax.optimization_barrier(jnp.sum(onehot * log_student, axis=-1))
    logit_grad = ((cell_weight[:, None] * (student_probs - teacher_mean) + student_probs - onehot) * scale).astype(jnp.bfloat16)
    head_grad = jnp.dot(hidden_two.T, logit_grad, preferred_element_type=jnp.float32)
    return (jnp.sum(pixel_loss), logit_grad, head_grad)

def reference(teacher_logits, coverage, features, labels, first_weight, second_weight, head_weight):
    pixel_count = TE * TE

    def one_column(column):
        block_logits = lax.dynamic_slice_in_dim(teacher_logits, column * TD, TD, 1)
        probabilities = jax.nn.softmax(block_logits.astype(jnp.float32).reshape(MEMBERS, TD, pixel_count, K), axis=-1)
        return (lax.optimization_barrier(jnp.sum(probabilities, 0)), lax.optimization_barrier(jnp.sum(probabilities * probabilities, axis=(0, 3))))
    first_sum, second_sum = lax.map(one_column, jnp.arange(N_TILE, dtype=jnp.int32))
    teacher_mean = first_sum / MEMBERS
    spread_sum = second_sum / MEMBERS - lax.optimization_barrier(jnp.sum(teacher_mean * teacher_mean, axis=-1))
    slot_index = jnp.arange(TD, dtype=jnp.int32)
    destination = ((slot_index // SD)[None, :] * (N_TILE * SD) + coverage.reshape(N_TILE, TD) * SD + (slot_index % SD)[None, :]).reshape(-1)
    mean_tiles = jnp.zeros((N_MEMBER * N_TILE * SD, pixel_count, K), jnp.float32).at[destination].set(teacher_mean.reshape(-1, pixel_count, K))
    spread_tiles = jnp.zeros((N_MEMBER * N_TILE * SD, pixel_count), jnp.float32).at[destination].set(spread_sum.reshape(-1, pixel_count))
    mean_map = mean_tiles.reshape(N_MEMBER, N_TILE, RD // TE, W // TE, TE, TE, K).transpose(0, 1, 2, 4, 3, 5, 6).reshape(N_MEMBER, N_TILE * RD, W, K)
    spread_map = spread_tiles.reshape(N_MEMBER, N_TILE, RD // TE, W // TE, TE, TE).transpose(0, 1, 2, 4, 3, 5).reshape(N_MEMBER, N_TILE * RD, W)
    scale = 1.0 / math.sqrt(N_MEMBER * N_TILE * RD * W)
    row_total = N_TILE * RD

    def strip(inputs):
        strip_features, strip_labels, strip_mean, strip_spread = inputs
        padded = jnp.pad(strip_features, ((1, 1), (1, 1), (0, 0)))
        pre_one = conv_taps(padded, first_weight, 1, row_total, W)
        hidden_one = jnp.where(pre_one > 0, pre_one, 0.0).astype(jnp.bfloat16).reshape(row_total, W, C)
        padded_one = jnp.pad(hidden_one, ((2, 2), (2, 2), (0, 0)))
        pre_two = conv_taps(padded_one, second_weight, 2, row_total, W)
        hidden_two = jnp.where(pre_two > 0, pre_two, 0.0).astype(jnp.bfloat16)
        loss_sum, logit_grad, head_grad = head_terms(hidden_two, head_weight, strip_mean.reshape(-1, K), strip_spread.reshape(-1), strip_labels.reshape(-1), scale)
        hidden_grad = jnp.dot(logit_grad, head_weight.T, preferred_element_type=jnp.float32)
        grad_two = jnp.where(pre_two > 0, hidden_grad, 0.0).astype(jnp.bfloat16).reshape(row_total, W, C)
        second_grad = kernel_grad(padded_one, grad_two, 2, row_total, W)
        back_one = input_grad(jnp.pad(grad_two, ((2, 2), (2, 2), (0, 0))), second_weight, 2, row_total, W)
        grad_one = jnp.where(pre_one > 0, back_one, 0.0).astype(jnp.bfloat16).reshape(row_total, W, C)
        first_grad = kernel_grad(padded, grad_one, 1, row_total, W)
        return (first_grad, second_grad, head_grad, loss_sum)
    first_all, second_all, head_all, loss_all = lax.map(strip, (features, labels, mean_map, spread_map))
    return (lax.optimization_barrier(jnp.sum(first_all, 0)), lax.optimization_barrier(jnp.sum(second_all, 0)), lax.optimization_barrier(jnp.sum(head_all, 0)), jnp.sum(loss_all) / (N_MEMBER * N_TILE * RD * W))
```

```python
import math

import jax
import jax.numpy as jnp
from jax import lax
from jax.sharding import PartitionSpec as P


def with_halo(array, sides, width):
    for axis, dim in sides:
        count, length = (lax.axis_size(axis), array.shape[dim])
        up = [(i, (i + 1) % count) for i in range(count - 1)]
        down = [(j, i) for i, j in up]
        last = lax.slice_in_dim(array, length - width, length, axis=dim)
        initial = lax.slice_in_dim(array, 0, width, axis=dim)
        before = lax.ppermute(last, axis, up)
        after = lax.ppermute(initial, axis, down)
        array = jnp.concatenate([before, array, after], axis=dim)
    return array


def conv_taps(padded, kernel, dilation, row_count, col_count):
    channels = padded.shape[-1]
    summed = jnp.zeros((row_count * col_count, kernel.shape[-1]), jnp.float32)
    for row_tap in range(3):
        for col_tap in range(3):
            window = padded[
                row_tap * dilation : row_tap * dilation + row_count,
                col_tap * dilation : col_tap * dilation + col_count,
            ]
            summed = summed + jnp.dot(
                window.reshape(-1, channels),
                kernel[row_tap, col_tap],
                preferred_element_type=jnp.float32,
            )
    return summed


def kernel_grad(padded, grads, dilation, row_count, col_count):
    channels = padded.shape[-1]
    flat_grads = grads.reshape(row_count * col_count, -1)
    outer = []
    for row_tap in range(3):
        inner = []
        for col_tap in range(3):
            window = padded[
                row_tap * dilation : row_tap * dilation + row_count,
                col_tap * dilation : col_tap * dilation + col_count,
            ]
            inner.append(
                jnp.dot(
                    window.reshape(-1, channels).T, flat_grads, preferred_element_type=jnp.float32
                )
            )
        outer.append(jnp.stack(inner))
    return jnp.stack(outer)


def input_grad(padded_grads, kernel, dilation, row_count, col_count):
    channels = padded_grads.shape[-1]
    summed = jnp.zeros((row_count * col_count, kernel.shape[2]), jnp.float32)
    for row_tap in range(3):
        for col_tap in range(3):
            row_from = (2 - row_tap) * dilation
            col_from = (2 - col_tap) * dilation
            window = padded_grads[row_from : row_from + row_count, col_from : col_from + col_count]
            summed = summed + jnp.dot(
                window.reshape(-1, channels),
                kernel[row_tap, col_tap].T,
                preferred_element_type=jnp.float32,
            )
    return summed


def head_terms(hidden_two, head_weight, teacher_mean, spread_sum, label_rows, scale):
    classes = head_weight.shape[1]
    logits = jnp.dot(hidden_two, head_weight, preferred_element_type=jnp.float32)
    log_student = jax.nn.log_softmax(logits, axis=-1)
    student_probs = jnp.exp(log_student)
    cell_weight = 1.0 / (0.1 + spread_sum)
    onehot = (label_rows[:, None] == jnp.arange(classes, dtype=jnp.int32)[None, :]).astype(
        jnp.float32
    )
    entropy_part = jnp.sum(jax.scipy.special.xlogy(teacher_mean, teacher_mean), axis=-1)
    pixel_loss = cell_weight * (
        entropy_part - jnp.sum(teacher_mean * log_student, axis=-1)
    ) - jnp.sum(onehot * log_student, axis=-1)
    logit_grad = (
        (cell_weight[:, None] * (student_probs - teacher_mean) + student_probs - onehot) * scale
    ).astype(jnp.bfloat16)
    head_grad = jnp.dot(hidden_two.T, logit_grad, preferred_element_type=jnp.float32)
    return (jnp.sum(pixel_loss), logit_grad, head_grad)


def slot_matrix(destination, columns, capacity):
    item_count = destination.shape[0]
    onehot = (destination[:, None] == jnp.arange(columns, dtype=jnp.int32)[None, :]).astype(jnp.int32)
    before = jnp.cumsum(onehot, axis=0) - onehot
    slot = destination * capacity + jnp.sum(before * onehot, axis=1)
    return slot[None, :] == jnp.arange(columns * capacity, dtype=jnp.int32)[:, None]


def split_two(value):
    high = value.astype(jnp.bfloat16)
    return (high, (value - high.astype(jnp.float32)).astype(jnp.bfloat16))


def exchange(array, axis):
    return lax.all_to_all(array, axis, split_axis=0, concat_axis=0, tiled=True)


def gradient_total(blocks, groups, chips):
    rows, width = blocks.shape[1:]
    core = lax.axis_index("core")
    halves = blocks.reshape(groups, chips, 2, rows, width)
    keep = lax.dynamic_index_in_dim(halves, core, 2, keepdims=False)
    give = lax.dynamic_index_in_dim(halves, 1 - core, 2, keepdims=False)
    got = lax.ppermute(give.astype(jnp.bfloat16), "core", [(0, 1), (1, 0)])
    mine = (keep + got.astype(jnp.float32)).astype(jnp.bfloat16)
    mine = exchange(mine.transpose(1, 0, 2, 3), "chip")
    mine = jnp.sum(mine.astype(jnp.float32), axis=0).astype(jnp.bfloat16)
    mine = exchange(mine, "member")
    mine = jnp.sum(mine.astype(jnp.float32), axis=0).astype(jnp.bfloat16)
    mine = exchange(jnp.broadcast_to(mine[None], (groups, rows, width)), "member")
    mine = exchange(jnp.broadcast_to(mine[None], (chips, groups, rows, width)), "chip")
    other = lax.ppermute(mine, "core", [(0, 1), (1, 0)])
    zero = jnp.where(core == 0, mine, other)
    one = jnp.where(core == 0, other, mine)
    return jnp.stack([zero, one], axis=2).transpose(1, 0, 2, 3, 4).astype(jnp.float32).reshape(groups * chips * 2, rows, width)


def body(teacher_logits, coverage, features, labels, first_weight, second_weight, head_weight):
    channels, classes = head_weight.shape
    members_here, tiles_here, flat_width = teacher_logits.shape
    pixel_count = flat_width // classes
    tile_edge = math.isqrt(pixel_count)
    groups = lax.axis_size("member")
    chips = lax.axis_size("chip")
    columns = chips * 2
    block_tiles = tiles_here // groups
    member_total = members_here * groups
    cap_block = max(2, 2 * block_tiles // columns)
    probabilities = jax.nn.softmax(
        teacher_logits.astype(jnp.float32).reshape(members_here, tiles_here, pixel_count, classes),
        axis=-1,
    )
    first_sum = jnp.sum(probabilities, 0)
    second_sum = jnp.sum(probabilities * probabilities, axis=(0, 3))
    within = second_sum - jnp.sum(first_sum * first_sum, axis=-1) / members_here
    payload = jnp.concatenate(
        [first_sum.reshape(tiles_here, flat_width).astype(jnp.bfloat16), *split_two(within)], axis=1
    )
    got = exchange(payload.reshape(groups, block_tiles, -1), "member").astype(jnp.float32)
    sums = got[:, :, :flat_width]
    total_within = jnp.sum(got[:, :, flat_width : flat_width + pixel_count] + got[:, :, flat_width + pixel_count :], axis=0)
    mean = jnp.sum(sums, axis=0) / member_total
    gap = sums / members_here - mean[None]
    between = jnp.sum((gap * gap).reshape(groups, block_tiles, pixel_count, classes), axis=(0, 3)) / groups
    spread = total_within / member_total + between
    row = jnp.concatenate([mean.astype(jnp.bfloat16), *split_two(spread)], axis=1)
    destination = lax.dynamic_index_in_dim(coverage.reshape(groups, block_tiles), lax.axis_index("member"), 0, keepdims=False)
    place = slot_matrix(destination, columns, cap_block)
    sent = jnp.dot(place.astype(jnp.bfloat16), row, preferred_element_type=jnp.float32).astype(jnp.bfloat16)
    tile_of = jnp.sum(jnp.where(place, jnp.arange(1, block_tiles + 1, dtype=jnp.int32)[None, :], 0), axis=1) - 1
    tile_got = exchange(tile_of.reshape(columns, cap_block), ("chip", "core")).reshape(-1)
    got_rows = exchange(sent.reshape(columns, cap_block, -1), ("chip", "core")).reshape(columns * cap_block, -1)
    take = tile_got[None, :] == jnp.arange(block_tiles, dtype=jnp.int32)[:, None]
    own = jnp.dot(take.astype(jnp.bfloat16), got_rows, preferred_element_type=jnp.float32)
    teacher_mean = own[:, :flat_width]
    spread_sum = own[:, flat_width : flat_width + pixel_count] + own[:, flat_width + pixel_count :]
    local_features = features[0]
    row_count, col_count = (local_features.shape[0], local_features.shape[1])
    tile_rows = row_count // tile_edge
    tile_cols = col_count // tile_edge
    mean_map = (
        teacher_mean.reshape(tile_rows, tile_cols, tile_edge, tile_edge, classes)
        .transpose(0, 2, 1, 3, 4)
        .reshape(row_count * col_count, classes)
    )
    spread_map = (
        spread_sum.reshape(tile_rows, tile_cols, tile_edge, tile_edge)
        .transpose(0, 2, 1, 3)
        .reshape(row_count * col_count)
    )
    cell_total = groups * columns * row_count * col_count
    scale = 1.0 / math.sqrt(cell_total)
    extended = with_halo(local_features, ((("chip", "core"), 0),), 3)
    padded = jnp.pad(extended, ((0, 0), (1, 1), (0, 0)))
    pre_one = conv_taps(padded, first_weight, 1, row_count + 4, col_count).reshape(
        row_count + 4, col_count, channels
    )
    global_rows = (
        lax.axis_index(("chip", "core")) * row_count - 2 + jnp.arange(row_count + 4, dtype=jnp.int32)
    )
    inside = (global_rows >= 0) & (global_rows < columns * row_count)
    hidden_one = jnp.where(inside[:, None, None] & (pre_one > 0), pre_one, 0.0).astype(jnp.bfloat16)
    padded_one = jnp.pad(hidden_one, ((0, 0), (2, 2), (0, 0)))
    pre_two = conv_taps(padded_one, second_weight, 2, row_count, col_count)
    hidden_two = jnp.where(pre_two > 0, pre_two, 0.0).astype(jnp.bfloat16)
    loss_sum, logit_grad, head_grad = head_terms(
        hidden_two, head_weight, mean_map, spread_map, labels[0].reshape(-1), scale
    )
    hidden_grad = jnp.dot(logit_grad, head_weight.T, preferred_element_type=jnp.float32)
    grad_two = (
        jnp.where(pre_two > 0, hidden_grad, 0.0)
        .astype(jnp.bfloat16)
        .reshape(row_count, col_count, channels)
    )
    second_grad = kernel_grad(padded_one, grad_two, 2, row_count, col_count)
    grad_rows = with_halo(grad_two, ((("chip", "core"), 0),), 2)
    back_one = input_grad(
        jnp.pad(grad_rows, ((0, 0), (2, 2), (0, 0))), second_weight, 2, row_count, col_count
    )
    local_pre = pre_one[2 : row_count + 2].reshape(row_count * col_count, channels)
    grad_one = (
        jnp.where(local_pre > 0, back_one, 0.0)
        .astype(jnp.bfloat16)
        .reshape(row_count, col_count, channels)
    )
    first_grad = kernel_grad(padded[2 : row_count + 4], grad_one, 1, row_count, col_count)
    devices = groups * columns
    loss_high, loss_low = split_two(loss_sum)
    loss_rows = jnp.zeros((devices, 1, channels), jnp.float32)
    loss_rows = loss_rows.at[:, :, 0].set(loss_high.astype(jnp.float32)).at[:, :, 1].set(loss_low.astype(jnp.float32))
    head_rows = head_grad.reshape(-1, channels)
    head_count = -(-head_rows.shape[0] // devices)
    head_rows = jnp.pad(head_rows, ((0, head_count * devices - head_rows.shape[0]), (0, 0))).reshape(devices, head_count, channels)
    parts = jnp.concatenate(
        [
            first_grad.reshape(devices, -1, channels),
            second_grad.reshape(devices, -1, channels),
            head_rows,
            loss_rows,
        ],
        axis=1,
    )
    size = 9 * channels // devices
    totals = gradient_total(parts, groups, chips)
    first_total = totals[:, :size].reshape(first_grad.shape)
    second_total = totals[:, size : 2 * size].reshape(second_grad.shape)
    head_total = totals[:, 2 * size : -1].reshape(-1)[: head_grad.size].reshape(head_grad.shape)
    loss_total = totals[0, -1, 0] + totals[0, -1, 1]
    return (first_total, second_total, head_total, loss_total / cell_total)


def solution(mesh):
    groups, columns = mesh.shape["member"], mesh.shape["tile"]
    split = jax.sharding.Mesh(
        mesh.devices.reshape(groups, columns // 2, 2), ("member", "chip", "core")
    )
    tile = ("chip", "core")
    return jax.shard_map(
        body,
        mesh=split,
        in_specs=(
            P("member", tile, None),
            P(tile),
            P("member", tile, None, None),
            P("member", tile, None),
            P(),
            P(),
            P(),
        ),
        out_specs=(P(), P(), P(), P()),
        check_vma=False,
    )
```

```python
import functools
import math

import jax
import jax.numpy as jnp
from jax import lax
from jax.experimental import pallas as pl
from jax.experimental.pallas import tpu as pltpu
from jax.sharding import PartitionSpec as P

BF16 = jnp.bfloat16
F32 = jnp.float32
LANES = 128
MXU = 256


def whole(count):
    return [pl.BlockSpec(memory_space=pltpu.VMEM)] * count


def iota(shape, axis):
    return lax.broadcasted_iota(jnp.int32, shape, axis)


def dot(left, right):
    return jnp.dot(left, right, preferred_element_type=F32)


def split_lanes(value):
    high = value.astype(BF16).astype(F32)
    return jnp.where(iota(value.shape, 1) < 64, high, value - high).astype(BF16)


def join_lanes(value):
    return value + pltpu.roll(value, 64, 1)


def class_sums(value, classes):
    pick = (iota((MXU, LANES), 0) // classes == iota((MXU, LANES), 1) % (MXU // classes)).astype(BF16)
    high = value.astype(BF16)
    low = (value - high.astype(F32)).astype(BF16)
    return dot(high, pick) + dot(low, pick)


def teacher_kernel(classes, x_ref, out_ref, acc_ref):
    step = pl.program_id(0)
    members, tiles, width = x_ref.shape
    same = (iota((width, width), 0) // classes == iota((width, width), 1) // classes).astype(BF16)
    x = x_ref[...].astype(F32).reshape(members * tiles, width)
    root = jnp.exp(x * 0.25)
    root = root * pl.reciprocal(dot(root.astype(BF16), same), approx=True)
    square = root * root
    power = square * square
    probs = (power / dot(power.astype(BF16), same)).reshape(members, tiles, width)
    first = jnp.sum(probs, axis=0)
    within = jnp.sum(probs * probs, axis=0) - first * first * (1.0 / members)
    out_ref[:, pl.ds(pl.multiple_of(step * width, width), width)] = first.astype(BF16)
    sums = class_sums(within, classes)
    per = width // classes
    hit = iota(sums.shape, 1) % 64 // per == step

    @pl.when(step == 0)
    def _():
        acc_ref[...] = jnp.zeros_like(acc_ref)

    acc_ref[...] = jnp.where(hit, sums, acc_ref[...])

    @pl.when(step == pl.num_programs(0) - 1)
    def _():
        out_ref[:, pl.num_programs(0) * width :] = split_lanes(acc_ref[...])


def teacher_moments(logits, classes):
    members, tiles, width = logits.shape
    return pl.pallas_call(
        functools.partial(teacher_kernel, classes),
        grid=(width // MXU,),
        in_specs=[pl.BlockSpec((members, tiles, MXU), lambda i: (0, 0, i))],
        out_specs=pl.BlockSpec((tiles, width + LANES), lambda i: (0, 0)),
        out_shape=jax.ShapeDtypeStruct((tiles, width + LANES), BF16),
        scratch_shapes=[pltpu.VMEM((tiles, LANES), F32)],
        compiler_params=pltpu.CompilerParams(vmem_limit_bytes=24 << 20),
        cost_estimate=pl.CostEstimate(flops=3_000_000_000, bytes_accessed=5_300_000, transcendentals=6_000_000),
        name="teacher_moments",
    )(logits)


def combine_kernel(classes, members, columns, capacity, where_ref, got_ref, cover_ref, out_ref):
    groups, tiles, extended = got_ref.shape
    width = extended - LANES
    means, gaps = [], []
    for start in range(0, width, MXU):
        sums = [got_ref[g, :, start : start + MXU].astype(F32) for g in range(groups)]
        total = sums[0]
        for one in sums[1:]:
            total = total + one
        mean = total * (1.0 / (members * groups))
        means.append(mean.astype(BF16))
        gap = jnp.zeros_like(mean)
        for one in sums:
            off = one * (1.0 / members) - mean
            gap = gap + off * off
        gaps.append(gap)
    between = class_sums(jnp.concatenate(gaps, axis=0), classes)
    lane = iota((tiles, LANES), 1)
    spread = jnp.zeros((tiles, LANES), F32)
    per = MXU // classes
    for i in range(width // MXU):
        spread = jnp.where(lane % 64 // per == i, between[i * tiles : (i + 1) * tiles], spread)
    inner = got_ref[0, :, width:].astype(F32)
    for g in range(1, groups):
        inner = inner + got_ref[g, :, width:].astype(F32)
    spread = spread * (1.0 / groups) + join_lanes(inner) * (1.0 / (members * groups))
    index = (iota((tiles, LANES), 0) + 1).astype(F32).astype(BF16)
    rows = jnp.concatenate([*means, split_lanes(spread), index], axis=1)
    target = cover_ref[where_ref[0]]
    onehot = (iota((columns, tiles), 0) == target).astype(F32)
    earlier = (iota((tiles, tiles), 0) < iota((tiles, tiles), 1)).astype(BF16)
    before = dot(onehot.astype(BF16), earlier)
    rank = jnp.sum(before * onehot, axis=0, keepdims=True).astype(jnp.int32)
    place = (iota((columns * capacity, tiles), 0) == target * capacity + rank).astype(BF16)
    out_ref[...] = dot(place, rows).astype(BF16)


def combine(got, cover, where, classes, members, columns, capacity):
    extended = got.shape[2]
    return pl.pallas_call(
        functools.partial(combine_kernel, classes, members, columns, capacity),
        in_specs=[pl.BlockSpec(memory_space=pltpu.SMEM), *whole(2)],
        out_specs=pl.BlockSpec(memory_space=pltpu.VMEM),
        out_shape=jax.ShapeDtypeStruct((columns * capacity, extended + LANES), BF16),
        compiler_params=pltpu.CompilerParams(vmem_limit_bytes=24 << 20),
        cost_estimate=pl.CostEstimate(flops=100_000_000, bytes_accessed=1_700_000, transcendentals=0),
        name="combine",
    )(where, got, cover)


def put_shifted(ref, start, value, shift, width):
    rows, channels = value.shape
    col = iota(value.shape, 0) % width
    left = jnp.where(col >= shift, pltpu.roll(value, shift, 0), 0.0)
    right = jnp.where(col < width - shift, pltpu.roll(value, rows - shift, 0), 0.0)
    ref[pl.ds(start, rows), :channels] = left.astype(BF16)
    ref[pl.ds(start, rows), channels : 2 * channels] = value.astype(BF16)
    ref[pl.ds(start, rows), 2 * channels :] = right.astype(BF16)


def three_dots(ref, start, step, rows, weight_ref):
    total = None
    for tap in range(3):
        part = dot(ref[pl.ds(start + tap * step, rows), :], weight_ref[tap])
        total = part if total is None else total + part
    return total


def student_kernel(
    width, edge_ref, before_ref, x_ref, after_ref, first_ref, second_ref, head_ref, label_ref,
    xt_ref, ht_ref, one_ref, two_ref, twot_ref, wt_ref, log_ref, base_ref, label_sum_ref,
    xcat, hcat, logit_ref,
):
    cells, channels = x_ref.shape
    halo = before_ref.shape[0]
    block = 4 * width

    @pl.loop(0, halo // width)
    def _(i):
        start = pl.multiple_of(i * width, width)
        put_shifted(xcat, start, before_ref[pl.ds(start, width)].astype(F32), 1, width)
        low = pl.multiple_of(halo + cells + start, width)
        put_shifted(xcat, low, after_ref[pl.ds(start, width)].astype(F32), 1, width)

    @pl.loop(0, cells // block)
    def _(i):
        start = pl.multiple_of(i * block, block)
        low = pl.multiple_of(halo + start, width)
        put_shifted(xcat, low, x_ref[pl.ds(start, block)].astype(F32), 1, width)

    lines = cells // width

    @pl.loop(0, (cells + block) // block)
    def _(i):
        start = pl.multiple_of(i * block, block)
        value = three_dots(xcat, start, width, block, first_ref)
        line = i * 4 + iota(value.shape, 0) // width
        low = jnp.where(edge_ref[0] == 1, 2, 0)
        high = jnp.where(edge_ref[1] == 1, lines + 2, lines + 4)
        value = jnp.where((line >= low) & (line < high) & (value > 0), value, 0.0)
        put_shifted(hcat, start, value, 2, width)

    @pl.loop(0, cells // block)
    def _(i):
        start = pl.multiple_of(i * block, block)
        value = three_dots(hcat, start, 2 * width, block, second_ref)
        value = jnp.where(value > 0, value, 0.0)
        two = value.astype(BF16)
        two_ref[pl.ds(start, block), :] = two
        one_ref[pl.ds(start, block), :] = hcat[pl.ds(start + 2 * width, block), channels : 2 * channels]
        twot_ref[:, pl.ds(start, block)] = value.T.astype(BF16)
        logit_ref[pl.ds(start, block), :] = dot(two, head_ref[...])

    @pl.loop(0, xt_ref.shape[1] // LANES)
    def _(i):
        start = pl.multiple_of(i * LANES, LANES)
        for tap in range(3):
            part = slice(tap * channels, (tap + 1) * channels)
            xt_ref[part, pl.ds(start, LANES)] = xcat[pl.ds(start + halo - width, LANES), part].astype(F32).T.astype(BF16)

    @pl.loop(0, ht_ref.shape[1] // LANES)
    def _(i):
        start = pl.multiple_of(i * LANES, LANES)
        for tap in range(3):
            part = slice(tap * channels, (tap + 1) * channels)
            ht_ref[part, pl.ds(start, LANES)] = hcat[pl.ds(start, LANES), part].astype(F32).T.astype(BF16)

    @pl.loop(0, 3)
    def _(i):
        for tap in range(3):
            part = slice(tap * channels, (tap + 1) * channels)
            mirror = slice((2 - tap) * channels, (3 - tap) * channels)
            wt_ref[i, part, :] = second_ref[i, mirror, :].astype(F32).T.astype(BF16)

    tiles, pixels = label_ref.shape
    edge = math.isqrt(pixels)
    across = width // edge
    lane = iota((tiles, LANES), 1)
    even = lane < 64
    label_sum = jnp.zeros((tiles, LANES), F32)
    for pair in range(pixels // 2):
        row, col = 2 * pair // edge, 2 * pair % edge
        parts = []
        for down in range(tiles // across):
            start = (down * edge + row) * width + col
            left = logit_ref[pl.ds(start, across, stride=edge), :]
            right = logit_ref[pl.ds(start + 1, across, stride=edge), :]
            parts.append(jnp.where(iota(left.shape, 1) < 64, left, right))
        value = jnp.concatenate(parts, axis=0)
        top = jnp.where(
            even,
            jnp.max(jnp.where(even, value, -jnp.inf), axis=1, keepdims=True),
            jnp.max(jnp.where(even, -jnp.inf, value), axis=1, keepdims=True),
        )
        value = value - top
        power = jnp.exp(value)
        total = jnp.where(
            even,
            jnp.sum(jnp.where(even, power, 0.0), axis=1, keepdims=True),
            jnp.sum(jnp.where(even, 0.0, power), axis=1, keepdims=True),
        )
        value = value - jnp.log(total)
        label = jnp.where(even, label_ref[:, 2 * pair : 2 * pair + 1], label_ref[:, 2 * pair + 1 : 2 * pair + 2])
        hit = label == lane % 64
        label_sum = label_sum + jnp.where(hit, value, 0.0)
        log_ref[pair * tiles : (pair + 1) * tiles, :] = value
        base_ref[pair * tiles : (pair + 1) * tiles, :] = jnp.exp(value) - hit.astype(F32)
    label_sum_ref[...] = label_sum


def student_forward(edges, before, x, after, first, second, head, labels, width):
    cells, channels = x.shape
    halo = before.shape[0]
    tiles, pixels = labels.shape
    shape = jax.ShapeDtypeStruct
    return pl.pallas_call(
        functools.partial(student_kernel, width),
        in_specs=[pl.BlockSpec(memory_space=pltpu.SMEM), *whole(7)],
        out_specs=whole(9),
        out_shape=[
            shape((3 * channels, cells + 2 * width), BF16),
            shape((3 * channels, cells + 4 * width), BF16),
            shape((cells, channels), BF16),
            shape((cells, channels), BF16),
            shape((channels, cells), BF16),
            shape((3, 3 * channels, channels), BF16),
            shape((cells // 2, LANES), F32),
            shape((cells // 2, LANES), F32),
            shape((tiles, LANES), F32),
        ],
        scratch_shapes=[
            pltpu.VMEM((cells + 2 * halo, 3 * channels), BF16),
            pltpu.VMEM((cells + 4 * width, 3 * channels), BF16),
            pltpu.VMEM((cells, LANES), F32),
        ],
        compiler_params=pltpu.CompilerParams(vmem_limit_bytes=40 << 20),
        cost_estimate=pl.CostEstimate(flops=6_000_000_000, bytes_accessed=18_000_000, transcendentals=500_000),
        name="student_forward",
    )(edges, before, x, after, first, second, head, labels)


def head_kernel(
    scale, width, got_ref, log_ref, base_ref, label_sum_ref, two_ref, twot_ref, headt_ref,
    grad_ref, top_ref, bottom_ref, head_grad_ref, natural,
):
    slots, extended = got_ref.shape
    tiles = label_sum_ref.shape[0]
    flat = extended - 2 * LANES
    pixels = flat // 64
    edge = math.isqrt(pixels)
    across = width // edge
    index = got_ref[:, flat + LANES :].astype(F32)
    take = (index == (iota((slots, LANES), 1) + 1).astype(F32)).astype(F32).T[:tiles].astype(BF16)
    spread = join_lanes(dot(take, got_ref[:, flat : flat + LANES]))
    weight = 1.0 / (0.1 + spread)
    even = iota((tiles, LANES), 1) < 64
    loss = -label_sum_ref[...]
    for pair in range(pixels // 2):
        rows = slice(pair * tiles, (pair + 1) * tiles)
        if pair % 2 == 0:
            both = dot(take, got_ref[:, pair * LANES : (pair + 2) * LANES])
        mean = both[:, pair % 2 * LANES : (pair % 2 + 1) * LANES]
        cell = jnp.where(even, weight[:, 2 * pair : 2 * pair + 1], weight[:, 2 * pair + 1 : 2 * pair + 2])
        value = log_ref[rows, :]
        held = mean > 0
        loss = loss + cell * jnp.where(held, mean * (jnp.log(jnp.where(held, mean, 1.0)) - value), 0.0)
        grad = (cell * (jnp.exp(value) - mean) + base_ref[rows, :]) * scale
        turned = pltpu.roll(grad, 64, 1)
        row, col = 2 * pair // edge, 2 * pair % edge
        for down in range(tiles // across):
            start = (down * edge + row) * width + col
            natural[pl.ds(start, across, stride=edge), :] = grad[down * across : (down + 1) * across]
            natural[pl.ds(start + 1, across, stride=edge), :] = turned[down * across : (down + 1) * across]
    cells, channels = two_ref.shape
    logit_grad = natural[...].astype(BF16)
    head_grad_ref[:channels, :] = dot(twot_ref[...], logit_grad)
    head_grad_ref[channels:, :] = loss
    block = 4 * width
    for start in range(0, cells, block):
        rows = slice(start, start + block)
        grad = dot(logit_grad[rows], headt_ref[...])
        grad_ref[rows, :] = jnp.where(two_ref[rows, :].astype(F32) > 0, grad, 0.0).astype(BF16)
    top_ref[...] = grad_ref[: 2 * width, :]
    bottom_ref[...] = grad_ref[cells - 2 * width :, :]


def head_step(got, log, base, label_sum, two, twot, headt, scale, width):
    cells, channels = two.shape
    shape = jax.ShapeDtypeStruct
    return pl.pallas_call(
        functools.partial(head_kernel, scale, width),
        in_specs=whole(7),
        out_specs=whole(4),
        out_shape=[
            shape((cells, channels), BF16),
            shape((2 * width, channels), BF16),
            shape((2 * width, channels), BF16),
            shape((channels + label_sum.shape[0], LANES), F32),
        ],
        scratch_shapes=[pltpu.VMEM((cells, LANES), F32)],
        compiler_params=pltpu.CompilerParams(vmem_limit_bytes=32 << 20),
        cost_estimate=pl.CostEstimate(flops=400_000_000, bytes_accessed=5_000_000, transcendentals=500_000),
        name="head_step",
    )(got, log, base, label_sum, two, twot, headt)


def second_kernel(width, core_ref, ht_ref, grad_ref, head_grad_ref, keep_ref, give_ref, whole_ref):
    cells, channels = grad_ref.shape
    half = keep_ref.shape[0]
    for tap in range(3):
        part = dot(ht_ref[:, 2 * width * tap : 2 * width * tap + cells], grad_ref[...])
        whole_ref[tap * 3 * channels : (tap + 1) * 3 * channels, :] = part.astype(BF16)
    rows = 9 * channels
    lane = iota((channels // 2, LANES), 1)
    loss = jnp.sum(head_grad_ref[channels:, :])
    high = loss.astype(BF16).astype(F32)
    extra = jnp.where(lane == 64, high, jnp.where(lane == 65, loss - high, 0.0))
    for side in range(2):
        value = jnp.where(lane < 64, head_grad_ref[side * channels // 2 : (side + 1) * channels // 2, :], extra)
        whole_ref[rows : rows + channels // 2, side * LANES : (side + 1) * LANES] = value.astype(BF16)
    whole_ref[rows + channels // 2 :, :] = jnp.zeros((channels // 2, channels), BF16)
    core = core_ref[0]
    keep_ref[...] = whole_ref[pl.ds(pl.multiple_of(core * half, 16), half), :]
    give_ref[...] = whole_ref[pl.ds(pl.multiple_of((1 - core) * half, 16), half), :]


def second_step(core, ht, grad, head_grad, width):
    channels = grad.shape[1]
    rows = 10 * channels
    half = jax.ShapeDtypeStruct((rows // 2, channels), BF16)
    return pl.pallas_call(
        functools.partial(second_kernel, width),
        in_specs=[pl.BlockSpec(memory_space=pltpu.SMEM), *whole(3)],
        out_specs=whole(2),
        out_shape=[half, half],
        scratch_shapes=[pltpu.VMEM((rows, channels), BF16)],
        compiler_params=pltpu.CompilerParams(vmem_limit_bytes=32 << 20),
        cost_estimate=pl.CostEstimate(flops=2_500_000_000, bytes_accessed=7_000_000, transcendentals=0),
        name="second_step",
    )(core, ht, grad, head_grad)


def first_kernel(
    width, core_ref, before_ref, grad_ref, after_ref, wt_ref, one_ref, xt_ref, keep_ref, give_ref, gcat, padded, whole_ref
):
    cells, channels = grad_ref.shape
    halo = before_ref.shape[0]
    block = 4 * width
    put_shifted(gcat, 0, before_ref[...].astype(F32), 2, width)
    put_shifted(gcat, halo + cells, after_ref[...].astype(F32), 2, width)
    for start in range(0, cells, block):
        put_shifted(gcat, halo + start, grad_ref[start : start + block, :].astype(F32), 2, width)
    padded[: 2 * width, :] = jnp.zeros((2 * width, channels), BF16)
    padded[2 * width + cells :, :] = jnp.zeros((2 * width, channels), BF16)
    for start in range(0, cells, block):
        value = None
        for tap in range(3):
            low = start + (2 - tap) * 2 * width
            part = dot(gcat[low : low + block, :], wt_ref[tap])
            value = part if value is None else value + part
        held = one_ref[start : start + block, :].astype(F32) > 0
        padded[2 * width + start : 2 * width + start + block, :] = jnp.where(held, value, 0.0).astype(BF16)
    span = cells + 2 * width
    for tap in range(3):
        part = dot(xt_ref[...], padded[(2 - tap) * width : (2 - tap) * width + span, :])
        whole_ref[tap * 3 * channels : (tap + 1) * 3 * channels, :] = part.astype(BF16)
    half = keep_ref.shape[0]
    core = core_ref[0]
    keep_ref[...] = whole_ref[pl.ds(pl.multiple_of(core * half, 16), half), :]
    give_ref[...] = whole_ref[pl.ds(pl.multiple_of((1 - core) * half, 16), half), :]


def first_step(core, before, grad, after, wt, one, xt, width):
    cells, channels = grad.shape
    halo = before.shape[0]
    rows = 9 * channels
    half = jax.ShapeDtypeStruct((rows // 2, channels), BF16)
    return pl.pallas_call(
        functools.partial(first_kernel, width),
        in_specs=[pl.BlockSpec(memory_space=pltpu.SMEM), *whole(6)],
        out_specs=whole(2),
        out_shape=[half, half],
        scratch_shapes=[
            pltpu.VMEM((cells + 2 * halo, 3 * channels), BF16),
            pltpu.VMEM((cells + 4 * width, channels), BF16),
            pltpu.VMEM((rows, channels), BF16),
        ],
        compiler_params=pltpu.CompilerParams(vmem_limit_bytes=32 << 20),
        cost_estimate=pl.CostEstimate(flops=5_000_000_000, bytes_accessed=10_000_000, transcendentals=0),
        name="first_step",
    )(core, before, grad, after, wt, one, xt)


def exchange(array, axis):
    return lax.all_to_all(array, axis, split_axis=0, concat_axis=0, tiled=True)


def neighbours(first, last, axis):
    count = lax.axis_size(axis)
    up = [(i, i + 1) for i in range(count - 1)]
    down = [(i + 1, i) for i in range(count - 1)]
    return (lax.ppermute(last, axis, up), lax.ppermute(first, axis, down))


def gradient_total(keep, give, groups, chips):
    half, width = keep.shape
    core = lax.axis_index("core")
    got = lax.ppermute(give, "core", [(0, 1), (1, 0)])
    mine = (keep.astype(F32) + got.astype(F32)).astype(BF16)
    mine = exchange(mine.reshape(chips, half // chips, width), "chip")
    mine = jnp.sum(mine.astype(F32), axis=0).astype(BF16)
    mine = exchange(mine.reshape(groups, half // (chips * groups), width), "member")
    mine = jnp.sum(mine.astype(F32), axis=0).astype(BF16)
    mine = exchange(jnp.broadcast_to(mine[None], (groups, *mine.shape)), "member").reshape(half // chips, width)
    mine = exchange(jnp.broadcast_to(mine[None], (chips, *mine.shape)), "chip").reshape(half, width)
    other = lax.ppermute(mine, "core", [(0, 1), (1, 0)])
    zero = jnp.where(core == 0, mine, other)
    one = jnp.where(core == 0, other, mine)
    return jnp.concatenate([zero, one], axis=0).astype(F32)


def body(teacher_logits, coverage, features, labels, first_weight, second_weight, head_weight):
    channels, classes = head_weight.shape
    members, tiles_here, flat_width = teacher_logits.shape
    pixels = flat_width // classes
    edge = math.isqrt(pixels)
    groups = lax.axis_size("member")
    chips = lax.axis_size("chip")
    columns = chips * 2
    tile_axes = ("chip", "core")
    block_tiles = tiles_here // groups
    capacity = max(2, 2 * block_tiles // columns)
    local = features[0]
    lines, width = local.shape[:2]
    cells = lines * width
    cell_total = groups * columns * cells
    column = lax.axis_index(tile_axes)
    core = lax.axis_index("core").astype(jnp.int32).reshape(1)
    member = lax.axis_index("member").astype(jnp.int32).reshape(1)
    edges = jnp.stack([column == 0, column == columns - 1]).astype(jnp.int32)

    flat = local.reshape(cells, channels)
    before, after = neighbours(flat[: 3 * width], flat[cells - 3 * width :], tile_axes)
    payload = teacher_moments(teacher_logits, classes)
    got = exchange(payload.reshape(groups, block_tiles, -1), "member")
    label_rows = (
        labels[0].reshape(lines // edge, edge, width // edge, edge).transpose(0, 2, 1, 3).reshape(block_tiles, pixels)
    )
    xt, ht, one, two, twot, wt, log, base, label_sum = student_forward(
        edges,
        before,
        flat,
        after,
        first_weight.reshape(3, 3 * channels, channels),
        second_weight.reshape(3, 3 * channels, channels),
        jnp.concatenate([head_weight, head_weight], axis=1),
        label_rows,
        width,
    )
    sent = combine(got, coverage.reshape(groups, 1, block_tiles), member, classes, members, columns, capacity)
    received = exchange(sent.reshape(columns, capacity, -1), tile_axes).reshape(columns * capacity, -1)
    headt = jnp.pad(head_weight.T, ((0, LANES - classes), (0, 0)))
    grad_two, top, bottom, head_grad = head_step(
        received, log, base, label_sum, two, twot, headt, 1.0 / math.sqrt(cell_total), width
    )
    grad_before, grad_after = neighbours(top, bottom, tile_axes)
    second_total = gradient_total(*second_step(core, ht, grad_two, head_grad, width), groups, chips)
    first_total = gradient_total(*first_step(core, grad_before, grad_two, grad_after, wt, one, xt, width), groups, chips)
    rows = 9 * channels
    extra = second_total[rows : rows + channels // 2]
    head_total = jnp.concatenate([extra[:, :classes], extra[:, LANES : LANES + classes]], axis=0)
    loss_total = (extra[0, 64] + extra[0, 65]) / cell_total
    kernel_shape = (3, 3, channels, channels)
    return (first_total.reshape(kernel_shape), second_total[:rows].reshape(kernel_shape), head_total, loss_total)


def solution(mesh):
    groups, columns = mesh.shape["member"], mesh.shape["tile"]
    split = jax.sharding.Mesh(mesh.devices.reshape(groups, columns // 2, 2), ("member", "chip", "core"))
    tile = ("chip", "core")
    return jax.shard_map(
        body,
        mesh=split,
        in_specs=(
            P("member", tile, None),
            P(tile),
            P("member", tile, None, None),
            P("member", tile, None),
            P(),
            P(),
            P(),
        ),
        out_specs=(P(), P(), P(), P()),
        check_vma=False,
    )
```

```python
import functools
import math

import jax
import jax.numpy as jnp
from jax import lax
from jax.experimental import pallas as pl
from jax.experimental.pallas import tpu as pltpu
from jax.sharding import PartitionSpec as P

BF16 = jnp.bfloat16
F32 = jnp.float32
LANES = 128
MXU = 256


def whole(count):
    return [pl.BlockSpec(memory_space=pltpu.VMEM)] * count


def iota(shape, axis):
    return lax.broadcasted_iota(jnp.int32, shape, axis)


def dot(left, right):
    return jnp.dot(left, right, preferred_element_type=F32)


def split_lanes(value):
    high = value.astype(BF16).astype(F32)
    return jnp.where(iota(value.shape, 1) < 64, high, value - high).astype(BF16)


def join_lanes(value):
    return value + pltpu.roll(value, 64, 1)


def class_sums(value, classes):
    pick = (iota((MXU, LANES), 0) // classes == iota((MXU, LANES), 1) % (MXU // classes)).astype(BF16)
    high = value.astype(BF16)
    low = (value - high.astype(F32)).astype(BF16)
    return dot(high, pick) + dot(low, pick)


def teacher_kernel(classes, x_ref, out_ref, acc_ref):
    step = pl.program_id(0)
    members, tiles, width = x_ref.shape
    per = MXU // classes
    same = (iota((MXU, MXU), 0) // classes == iota((MXU, MXU), 1) // classes).astype(BF16)

    @pl.when(step == 0)
    def _():
        acc_ref[...] = jnp.zeros_like(acc_ref)

    for part in range(width // MXU):
        place = step * (width // MXU) + part
        x = x_ref[:, :, part * MXU : (part + 1) * MXU].astype(F32).reshape(members * tiles, MXU)
        root = jnp.exp(x * 0.25)
        root = root * pl.reciprocal(dot(root.astype(BF16), same), approx=True)
        square = root * root
        power = square * square
        total = dot(power.astype(BF16), same)
        inverse = pl.reciprocal(total, approx=True)
        inverse = inverse * (2.0 - total * inverse)
        probs = (power * inverse).reshape(members, tiles, MXU)
        first = jnp.sum(probs, axis=0)
        within = jnp.sum(probs * probs, axis=0) - first * first * (1.0 / members)
        out_ref[:, pl.ds(pl.multiple_of(place * MXU, MXU), MXU)] = first.astype(BF16)
        sums = class_sums(within, classes)
        hit = iota(sums.shape, 1) % 64 // per == place
        acc_ref[...] = jnp.where(hit, sums, acc_ref[...])

    @pl.when(step == pl.num_programs(0) - 1)
    def _():
        out_ref[:, pl.num_programs(0) * width :] = split_lanes(acc_ref[...])


def teacher_moments(logits, classes):
    members, tiles, width = logits.shape
    block = width // 4
    return pl.pallas_call(
        functools.partial(teacher_kernel, classes),
        grid=(width // block,),
        in_specs=[pl.BlockSpec((members, tiles, block), lambda i: (0, 0, i))],
        out_specs=pl.BlockSpec((tiles, width + LANES), lambda i: (0, 0)),
        out_shape=jax.ShapeDtypeStruct((tiles, width + LANES), BF16),
        scratch_shapes=[pltpu.VMEM((tiles, LANES), F32)],
        compiler_params=pltpu.CompilerParams(vmem_limit_bytes=58 << 20),
        cost_estimate=pl.CostEstimate(flops=3_000_000_000, bytes_accessed=5_300_000, transcendentals=6_000_000),
        name="teacher_moments",
    )(logits)


def combine_kernel(classes, members, columns, capacity, where_ref, got_ref, cover_ref, after_ref, out_ref):
    groups, tiles, extended = got_ref.shape
    width = extended - LANES
    means, gaps = [], []
    for start in range(0, width, MXU):
        sums = [got_ref[g, :, start : start + MXU].astype(F32) for g in range(groups)]
        total = sums[0]
        for one in sums[1:]:
            total = total + one
        mean = total * (1.0 / (members * groups))
        means.append(mean.astype(BF16))
        gap = jnp.zeros_like(mean)
        for one in sums:
            off = one * (1.0 / members) - mean
            gap = gap + off * off
        gaps.append(gap)
    between = class_sums(jnp.concatenate(gaps, axis=0), classes)
    lane = iota((tiles, LANES), 1)
    spread = jnp.zeros((tiles, LANES), F32)
    per = MXU // classes
    for i in range(width // MXU):
        spread = jnp.where(lane % 64 // per == i, between[i * tiles : (i + 1) * tiles], spread)
    inner = got_ref[0, :, width:].astype(F32)
    for g in range(1, groups):
        inner = inner + got_ref[g, :, width:].astype(F32)
    spread = spread * (1.0 / groups) + join_lanes(inner) * (1.0 / (members * groups))
    index = (iota((tiles, LANES), 0) + 1).astype(F32).astype(BF16)
    rows = jnp.concatenate([*means, split_lanes(spread), index], axis=1)
    target = cover_ref[where_ref[0]]
    onehot = (iota((columns, tiles), 0) == target).astype(F32)
    earlier = (iota((tiles, tiles), 0) < iota((tiles, tiles), 1)).astype(BF16)
    before = dot(onehot.astype(BF16), earlier)
    rank = jnp.sum(before * onehot, axis=0, keepdims=True).astype(jnp.int32)
    place = (iota((columns * capacity, tiles), 0) == target * capacity + rank).astype(BF16)
    out_ref[...] = dot(place, rows).astype(BF16)


def combine(got, cover, where, after, classes, members, columns, capacity):
    extended = got.shape[2]
    return pl.pallas_call(
        functools.partial(combine_kernel, classes, members, columns, capacity),
        in_specs=[pl.BlockSpec(memory_space=pltpu.SMEM), *whole(2), pl.BlockSpec(memory_space=pl.ANY)],
        out_specs=pl.BlockSpec(memory_space=pltpu.VMEM),
        out_shape=jax.ShapeDtypeStruct((columns * capacity, extended + LANES), BF16),
        compiler_params=pltpu.CompilerParams(vmem_limit_bytes=12 << 20),
        cost_estimate=pl.CostEstimate(flops=100_000_000, bytes_accessed=1_700_000, transcendentals=0),
        name="combine",
    )(where, got, cover, after)


def put_shifted(ref, start, value, shift, width):
    rows, channels = value.shape
    col = iota(value.shape, 0) % width
    left = jnp.where(col >= shift, pltpu.roll(value, shift, 0), 0.0)
    right = jnp.where(col < width - shift, pltpu.roll(value, rows - shift, 0), 0.0)
    ref[pl.ds(start, rows), :channels] = left.astype(BF16)
    ref[pl.ds(start, rows), channels : 2 * channels] = value.astype(BF16)
    ref[pl.ds(start, rows), 2 * channels :] = right.astype(BF16)


def three_dots(ref, start, step, rows, weight_ref):
    total = None
    for tap in range(3):
        part = dot(ref[pl.ds(start + tap * step, rows), :], weight_ref[tap])
        total = part if total is None else total + part
    return total


def student_kernel(
    width, edge_ref, before_ref, x_ref, after_ref, first_ref, second_ref, head_ref, label_ref, payload_ref,
    one_ref, two_ref, log_ref, base_ref, label_sum_ref, xcat, hcat, logit_ref,
):
    cells, channels = x_ref.shape
    halo = before_ref.shape[0]
    block = 4 * width

    @pl.loop(0, halo // width)
    def _(i):
        start = pl.multiple_of(i * width, width)
        put_shifted(xcat, start, before_ref[pl.ds(start, width)].astype(F32), 1, width)
        low = pl.multiple_of(halo + cells + start, width)
        put_shifted(xcat, low, after_ref[pl.ds(start, width)].astype(F32), 1, width)

    @pl.loop(0, cells // block)
    def _(i):
        start = pl.multiple_of(i * block, block)
        low = pl.multiple_of(halo + start, width)
        put_shifted(xcat, low, x_ref[pl.ds(start, block)].astype(F32), 1, width)

    lines = cells // width

    @pl.loop(0, (cells + block) // block)
    def _(i):
        start = pl.multiple_of(i * block, block)
        value = three_dots(xcat, start, width, block, first_ref)
        line = i * 4 + iota(value.shape, 0) // width
        low = jnp.where(edge_ref[0] == 1, 2, 0)
        high = jnp.where(edge_ref[1] == 1, lines + 2, lines + 4)
        value = jnp.where((line >= low) & (line < high) & (value > 0), value, 0.0)
        put_shifted(hcat, start, value, 2, width)
        one_ref[pl.ds(start, block), :] = value.astype(BF16)

    @pl.loop(0, cells // block)
    def _(i):
        start = pl.multiple_of(i * block, block)
        value = three_dots(hcat, start, 2 * width, block, second_ref)
        value = jnp.where(value > 0, value, 0.0)
        two = value.astype(BF16)
        two_ref[pl.ds(start, block), :] = two
        logit_ref[pl.ds(start, block), :] = dot(two, head_ref[...])

    tiles, pixels = label_ref.shape
    edge = math.isqrt(pixels)
    across = width // edge
    lane = iota((tiles, LANES), 1)
    even = lane < 64
    label_sum = jnp.zeros((tiles, LANES), F32)
    for pair in range(pixels // 2):
        row, col = 2 * pair // edge, 2 * pair % edge
        parts = []
        for down in range(tiles // across):
            start = (down * edge + row) * width + col
            left = logit_ref[pl.ds(start, across, stride=edge), :]
            right = logit_ref[pl.ds(start + 1, across, stride=edge), :]
            parts.append(jnp.where(iota(left.shape, 1) < 64, left, right))
        value = jnp.concatenate(parts, axis=0)
        top = jnp.where(
            even,
            jnp.max(jnp.where(even, value, -jnp.inf), axis=1, keepdims=True),
            jnp.max(jnp.where(even, -jnp.inf, value), axis=1, keepdims=True),
        )
        value = value - top
        power = jnp.exp(value)
        total = jnp.where(
            even,
            jnp.sum(jnp.where(even, power, 0.0), axis=1, keepdims=True),
            jnp.sum(jnp.where(even, 0.0, power), axis=1, keepdims=True),
        )
        value = value - jnp.log(total)
        label = jnp.where(even, label_ref[:, 2 * pair : 2 * pair + 1], label_ref[:, 2 * pair + 1 : 2 * pair + 2])
        hit = label == lane % 64
        label_sum = label_sum + jnp.where(hit, value, 0.0)
        log_ref[pair * tiles : (pair + 1) * tiles, :] = value
        base_ref[pair * tiles : (pair + 1) * tiles, :] = jnp.exp(value) - hit.astype(F32)
    label_sum_ref[...] = label_sum


def student_forward(edges, before, x, after, first, second, head, labels, payload, width):
    cells, channels = x.shape
    halo = before.shape[0]
    tiles, pixels = labels.shape
    shape = jax.ShapeDtypeStruct
    return pl.pallas_call(
        functools.partial(student_kernel, width),
        in_specs=[pl.BlockSpec(memory_space=pltpu.SMEM), *whole(7), pl.BlockSpec(memory_space=pl.ANY)],
        out_specs=whole(5),
        out_shape=[
            shape((cells + 4 * width, channels), BF16),
            shape((cells, channels), BF16),
            shape((cells // 2, LANES), F32),
            shape((cells // 2, LANES), F32),
            shape((tiles, LANES), F32),
        ],
        scratch_shapes=[
            pltpu.VMEM((cells + 2 * halo, 3 * channels), BF16),
            pltpu.VMEM((cells + 4 * width, 3 * channels), BF16),
            pltpu.VMEM((cells, LANES), F32),
        ],
        compiler_params=pltpu.CompilerParams(vmem_limit_bytes=28 << 20),
        cost_estimate=pl.CostEstimate(flops=6_000_000_000, bytes_accessed=18_000_000, transcendentals=500_000),
        name="student_forward",
    )(edges, before, x, after, first, second, head, labels, payload)


def put_turned(ref, start, value, shift, width):
    rows, channels = value.shape
    col = iota(value.shape, 0) % width
    left = jnp.where(col >= shift, pltpu.roll(value, shift, 0), 0.0)
    right = jnp.where(col < width - shift, pltpu.roll(value, rows - shift, 0), 0.0)
    for tap, one in enumerate((left, value, right)):
        ref[tap * channels : (tap + 1) * channels, pl.ds(start, rows)] = one.T.astype(BF16)


def turn_kernel(
    width, before_ref, x_ref, after_ref, one_ref, two_ref, second_ref, sent_ref, xt_ref, ht_ref, twot_ref, wt_ref
):
    cells, channels = x_ref.shape
    halo = before_ref.shape[0]
    pair = 2 * width
    first = jnp.concatenate([before_ref[halo - width :], x_ref[:width]], axis=0).astype(F32)
    put_turned(xt_ref, 0, first, 1, width)
    last = jnp.concatenate([x_ref[cells - width :], after_ref[:width]], axis=0).astype(F32)
    put_turned(xt_ref, cells, last, 1, width)

    @pl.loop(1, cells // pair)
    def _(i):
        start = pl.multiple_of(i * pair, pair)
        put_turned(xt_ref, start, x_ref[pl.ds(pl.multiple_of(start - width, width), pair)].astype(F32), 1, width)

    @pl.loop(0, one_ref.shape[0] // pair)
    def _(i):
        start = pl.multiple_of(i * pair, pair)
        put_turned(ht_ref, start, one_ref[pl.ds(start, pair)].astype(F32), 2, width)

    @pl.loop(0, cells // MXU)
    def _(i):
        start = pl.multiple_of(i * MXU, MXU)
        twot_ref[:, pl.ds(start, MXU)] = two_ref[pl.ds(start, MXU)].astype(F32).T.astype(BF16)

    @pl.loop(0, 3)
    def _(i):
        for tap in range(3):
            part = slice(tap * channels, (tap + 1) * channels)
            mirror = slice((2 - tap) * channels, (3 - tap) * channels)
            wt_ref[i, part, :] = second_ref[i, mirror, :].astype(F32).T.astype(BF16)


def turn(before, x, after, one, two, second, sent, width):
    cells, channels = x.shape
    shape = jax.ShapeDtypeStruct
    return pl.pallas_call(
        functools.partial(turn_kernel, width),
        in_specs=[*whole(6), pl.BlockSpec(memory_space=pl.ANY)],
        out_specs=whole(4),
        out_shape=[
            shape((3 * channels, cells + 2 * width), BF16),
            shape((3 * channels, cells + 4 * width), BF16),
            shape((channels, cells), BF16),
            shape((3, 3 * channels, channels), BF16),
        ],
        compiler_params=pltpu.CompilerParams(vmem_limit_bytes=20 << 20),
        cost_estimate=pl.CostEstimate(flops=3_000_000_000, bytes_accessed=14_000_000, transcendentals=0),
        name="turn",
    )(before, x, after, one, two, second, sent)


def head_kernel(
    scale, width, got_ref, log_ref, base_ref, label_sum_ref, two_ref, twot_ref, headt_ref,
    grad_ref, top_ref, bottom_ref, head_grad_ref, natural,
):
    slots, extended = got_ref.shape
    tiles = label_sum_ref.shape[0]
    flat = extended - 2 * LANES
    pixels = flat // 64
    edge = math.isqrt(pixels)
    across = width // edge
    index = got_ref[:, flat + LANES :].astype(F32)
    take = (index == (iota((slots, LANES), 1) + 1).astype(F32)).astype(F32).T[:tiles].astype(BF16)
    spread = join_lanes(dot(take, got_ref[:, flat : flat + LANES]))
    weight = 1.0 / (0.1 + spread)
    even = iota((tiles, LANES), 1) < 64
    loss = -label_sum_ref[...]
    for pair in range(pixels // 2):
        rows = slice(pair * tiles, (pair + 1) * tiles)
        if pair % 2 == 0:
            both = dot(take, got_ref[:, pair * LANES : (pair + 2) * LANES])
        mean = both[:, pair % 2 * LANES : (pair % 2 + 1) * LANES]
        cell = jnp.where(even, weight[:, 2 * pair : 2 * pair + 1], weight[:, 2 * pair + 1 : 2 * pair + 2])
        value = log_ref[rows, :]
        held = mean > 0
        loss = loss + cell * jnp.where(held, mean * (jnp.log(jnp.where(held, mean, 1.0)) - value), 0.0)
        grad = (cell * (jnp.exp(value) - mean) + base_ref[rows, :]) * scale
        turned = pltpu.roll(grad, 64, 1)
        row, col = 2 * pair // edge, 2 * pair % edge
        for down in range(tiles // across):
            start = (down * edge + row) * width + col
            natural[pl.ds(start, across, stride=edge), :] = grad[down * across : (down + 1) * across]
            natural[pl.ds(start + 1, across, stride=edge), :] = turned[down * across : (down + 1) * across]
    cells, channels = two_ref.shape
    logit_grad = natural[...].astype(BF16)
    head_grad_ref[:channels, :] = dot(twot_ref[...], logit_grad)
    head_grad_ref[channels:, :] = loss
    block = 4 * width
    for start in range(0, cells, block):
        rows = slice(start, start + block)
        grad = dot(logit_grad[rows], headt_ref[...])
        grad_ref[rows, :] = jnp.where(two_ref[rows, :].astype(F32) > 0, grad, 0.0).astype(BF16)
    top_ref[...] = grad_ref[: 2 * width, :]
    bottom_ref[...] = grad_ref[cells - 2 * width :, :]


def head_step(got, log, base, label_sum, two, twot, headt, scale, width):
    cells, channels = two.shape
    shape = jax.ShapeDtypeStruct
    return pl.pallas_call(
        functools.partial(head_kernel, scale, width),
        in_specs=whole(7),
        out_specs=whole(4),
        out_shape=[
            shape((cells, channels), BF16),
            shape((2 * width, channels), BF16),
            shape((2 * width, channels), BF16),
            shape((channels + label_sum.shape[0], LANES), F32),
        ],
        scratch_shapes=[pltpu.VMEM((cells, LANES), F32)],
        compiler_params=pltpu.CompilerParams(vmem_limit_bytes=14 << 20),
        cost_estimate=pl.CostEstimate(flops=400_000_000, bytes_accessed=5_000_000, transcendentals=500_000),
        name="head_step",
    )(got, log, base, label_sum, two, twot, headt)


def second_kernel(width, ht_ref, grad_ref, out_ref):
    cells, channels = grad_ref.shape
    for tap in range(3):
        part = dot(ht_ref[:, 2 * width * tap : 2 * width * tap + cells], grad_ref[...])
        out_ref[tap * 3 * channels : (tap + 1) * 3 * channels, :] = part.astype(BF16)


def second_step(ht, grad, width):
    channels = grad.shape[1]
    return pl.pallas_call(
        functools.partial(second_kernel, width),
        in_specs=whole(2),
        out_specs=pl.BlockSpec(memory_space=pltpu.VMEM),
        out_shape=jax.ShapeDtypeStruct((9 * channels, channels), BF16),
        compiler_params=pltpu.CompilerParams(vmem_limit_bytes=14 << 20),
        cost_estimate=pl.CostEstimate(flops=2_500_000_000, bytes_accessed=7_000_000, transcendentals=0),
        name="second_step",
    )(ht, grad)


def first_kernel(
    width, core_ref, before_ref, grad_ref, after_ref, wt_ref, one_ref, xt_ref, head_grad_ref, second_ref,
    keep_ref, give_ref, gcat, padded, whole_ref,
):
    cells, channels = grad_ref.shape
    halo = before_ref.shape[0]
    block = 4 * width
    put_shifted(gcat, 0, before_ref[...].astype(F32), 2, width)
    put_shifted(gcat, halo + cells, after_ref[...].astype(F32), 2, width)
    for start in range(0, cells, block):
        put_shifted(gcat, halo + start, grad_ref[start : start + block, :].astype(F32), 2, width)
    padded[: 2 * width, :] = jnp.zeros((2 * width, channels), BF16)
    padded[2 * width + cells :, :] = jnp.zeros((2 * width, channels), BF16)
    for start in range(0, cells, block):
        value = None
        for tap in range(3):
            low = start + (2 - tap) * 2 * width
            part = dot(gcat[low : low + block, :], wt_ref[tap])
            value = part if value is None else value + part
        held = one_ref[2 * width + start : 2 * width + start + block, :].astype(F32) > 0
        padded[2 * width + start : 2 * width + start + block, :] = jnp.where(held, value, 0.0).astype(BF16)
    span = cells + 2 * width
    for tap in range(3):
        part = dot(xt_ref[...], padded[(2 - tap) * width : (2 - tap) * width + span, :])
        whole_ref[tap * 3 * channels : (tap + 1) * 3 * channels, :] = part.astype(BF16)
    rows = 9 * channels
    lane = iota((channels // 2, LANES), 1)
    loss = jnp.sum(head_grad_ref[channels:, :])
    high = loss.astype(BF16).astype(F32)
    extra = jnp.where(lane == 64, high, jnp.where(lane == 65, loss - high, 0.0))
    for side in range(2):
        value = jnp.where(lane < 64, head_grad_ref[side * channels // 2 : (side + 1) * channels // 2, :], extra)
        whole_ref[rows : rows + channels // 2, side * LANES : (side + 1) * LANES] = value.astype(BF16)
    whole_ref[rows + channels // 2 :, :] = jnp.zeros((channels // 2, channels), BF16)
    half = keep_ref.shape[0]
    core = core_ref[0]
    keep_ref[...] = whole_ref[pl.ds(pl.multiple_of(core * half, 16), half), :]
    give_ref[...] = whole_ref[pl.ds(pl.multiple_of((1 - core) * half, 16), half), :]


def first_step(core, before, grad, after, wt, one, xt, head_grad, second, width):
    cells, channels = grad.shape
    halo = before.shape[0]
    rows = 10 * channels
    half = jax.ShapeDtypeStruct((rows // 2, channels), BF16)
    return pl.pallas_call(
        functools.partial(first_kernel, width),
        in_specs=[pl.BlockSpec(memory_space=pltpu.SMEM), *whole(7), pl.BlockSpec(memory_space=pl.ANY)],
        out_specs=whole(2),
        out_shape=[half, half],
        scratch_shapes=[
            pltpu.VMEM((cells + 2 * halo, 3 * channels), BF16),
            pltpu.VMEM((cells + 4 * width, channels), BF16),
            pltpu.VMEM((rows, channels), BF16),
        ],
        compiler_params=pltpu.CompilerParams(vmem_limit_bytes=24 << 20),
        cost_estimate=pl.CostEstimate(flops=5_000_000_000, bytes_accessed=10_000_000, transcendentals=0),
        name="first_step",
    )(core, before, grad, after, wt, one, xt, head_grad, second)


def exchange(array, axis):
    return lax.all_to_all(array, axis, split_axis=0, concat_axis=0, tiled=True)


def neighbours(first, last, axis):
    count = lax.axis_size(axis)
    up = [(i, i + 1) for i in range(count - 1)]
    down = [(i + 1, i) for i in range(count - 1)]
    return (lax.ppermute(last, axis, up), lax.ppermute(first, axis, down))


def gradient_total(keep, give, groups, chips):
    half, width = keep.shape
    core = lax.axis_index("core")
    got = lax.ppermute(give, "core", [(0, 1), (1, 0)])
    mine = (keep.astype(F32) + got.astype(F32)).astype(BF16)
    mine = exchange(mine.reshape(chips, half // chips, width), "chip")
    mine = jnp.sum(mine.astype(F32), axis=0).astype(BF16)
    mine = exchange(mine.reshape(groups, half // (chips * groups), width), "member")
    mine = jnp.sum(mine.astype(F32), axis=0).astype(BF16)
    mine = exchange(jnp.broadcast_to(mine[None], (groups, *mine.shape)), "member").reshape(half // chips, width)
    mine = exchange(jnp.broadcast_to(mine[None], (chips, *mine.shape)), "chip").reshape(half, width)
    other = lax.ppermute(mine, "core", [(0, 1), (1, 0)])
    zero = jnp.where(core == 0, mine, other)
    one = jnp.where(core == 0, other, mine)
    return jnp.concatenate([zero, one], axis=0).astype(F32)


def body(teacher_logits, coverage, features, labels, first_weight, second_weight, head_weight):
    channels, classes = head_weight.shape
    members, tiles_here, flat_width = teacher_logits.shape
    pixels = flat_width // classes
    edge = math.isqrt(pixels)
    groups = lax.axis_size("member")
    chips = lax.axis_size("chip")
    columns = chips * 2
    tile_axes = ("chip", "core")
    block_tiles = tiles_here // groups
    capacity = max(2, 2 * block_tiles // columns)
    local = features[0]
    lines, width = local.shape[:2]
    cells = lines * width
    cell_total = groups * columns * cells
    column = lax.axis_index(tile_axes)
    core = lax.axis_index("core").astype(jnp.int32).reshape(1)
    member = lax.axis_index("member").astype(jnp.int32).reshape(1)
    edges = jnp.stack([column == 0, column == columns - 1]).astype(jnp.int32)

    flat = local.reshape(cells, channels)
    before, after = neighbours(flat[: 3 * width], flat[cells - 3 * width :], tile_axes)
    payload = teacher_moments(teacher_logits, classes)
    got = exchange(payload.reshape(groups, block_tiles, -1), "member")
    label_rows = (
        labels[0].reshape(lines // edge, edge, width // edge, edge).transpose(0, 2, 1, 3).reshape(block_tiles, pixels)
    )
    second_rows = second_weight.reshape(3, 3 * channels, channels)
    one, two, log, base, label_sum = student_forward(
        edges,
        before,
        flat,
        after,
        first_weight.reshape(3, 3 * channels, channels),
        second_rows,
        jnp.concatenate([head_weight, head_weight], axis=1),
        label_rows,
        payload,
        width,
    )
    cover = coverage.reshape(groups, 1, block_tiles)
    sent = combine(got, cover, member, label_sum, classes, members, columns, capacity)
    received = exchange(sent.reshape(columns, capacity, -1), tile_axes).reshape(columns * capacity, -1)
    xt, ht, twot, wt = turn(before, flat, after, one, two, second_rows, sent, width)
    headt = jnp.pad(head_weight.T, ((0, LANES - classes), (0, 0)))
    grad_two, top, bottom, head_grad = head_step(
        received, log, base, label_sum, two, twot, headt, 1.0 / math.sqrt(cell_total), width
    )
    grad_before, grad_after = neighbours(top, bottom, tile_axes)
    second = second_step(ht, grad_two, width)
    second_total = lax.psum(second, ("member", "chip", "core")).astype(F32)
    keep, give = first_step(core, grad_before, grad_two, grad_after, wt, one, xt, head_grad, second, width)
    first_total = gradient_total(keep, give, groups, chips)
    rows = 9 * channels
    extra = first_total[rows : rows + channels // 2]
    head_total = jnp.concatenate([extra[:, :classes], extra[:, LANES : LANES + classes]], axis=0)
    loss_total = (extra[0, 64] + extra[0, 65]) / cell_total
    kernel_shape = (3, 3, channels, channels)
    return (first_total[:rows].reshape(kernel_shape), second_total.reshape(kernel_shape), head_total, loss_total)


def solution(mesh):
    groups, columns = mesh.shape["member"], mesh.shape["tile"]
    split = jax.sharding.Mesh(mesh.devices.reshape(groups, columns // 2, 2), ("member", "chip", "core"))
    tile = ("chip", "core")
    return jax.shard_map(
        body,
        mesh=split,
        in_specs=(
            P("member", tile, None),
            P(tile),
            P("member", tile, None, None),
            P("member", tile, None),
            P(),
            P(),
            P(),
        ),
        out_specs=(P(), P(), P(), P()),
        check_vma=False,
    )
```

```python
import functools
import math

import jax
import jax.numpy as jnp
from jax import lax
from jax.experimental import pallas as pl
from jax.experimental.pallas import tpu as pltpu
from jax.sharding import PartitionSpec as P

BF16 = jnp.bfloat16
F32 = jnp.float32
LANES = 128
MXU = 256


def whole(count):
    return [pl.BlockSpec(memory_space=pltpu.VMEM)] * count


def iota(shape, axis):
    return lax.broadcasted_iota(jnp.int32, shape, axis)


def dot(left, right):
    return jnp.dot(left, right, preferred_element_type=F32)


def split_lanes(value):
    high = value.astype(BF16).astype(F32)
    return jnp.where(iota(value.shape, 1) < 64, high, value - high).astype(BF16)


def join_lanes(value):
    return value + pltpu.roll(value, 64, 1)


def class_sums(value, classes):
    pick = (iota((MXU, LANES), 0) // classes == iota((MXU, LANES), 1) % (MXU // classes)).astype(BF16)
    high = value.astype(BF16)
    low = (value - high.astype(F32)).astype(BF16)
    return dot(high, pick) + dot(low, pick)


def teacher_kernel(classes, block_ref, x_ref, *refs):
    *out_refs, acc_ref = refs
    turn, step = pl.program_id(0), pl.program_id(1)
    members, tiles, width = x_ref.shape
    parts = width // MXU
    per = MXU // classes
    same = (iota((MXU, MXU), 0) // classes == iota((MXU, MXU), 1) // classes).astype(BF16)

    @pl.when(step == 0)
    def _():
        acc_ref[...] = jnp.zeros_like(acc_ref)

    x = jnp.concatenate(
        [x_ref[:, :, part * MXU : (part + 1) * MXU].reshape(members * tiles, MXU) for part in range(parts)], axis=0
    )
    root = jnp.exp(x.astype(F32) * 0.25)
    root = root * pl.reciprocal(dot(root.astype(BF16), same), approx=True)
    square = root * root
    power = square * square
    total = dot(power.astype(BF16), same)
    inverse = pl.reciprocal(total, approx=True)
    inverse = inverse * (2.0 - total * inverse)
    probs = (power * inverse).reshape(parts, members, tiles, MXU)
    first = jnp.sum(probs, axis=1)
    within = jnp.sum(probs * probs, axis=1) - first * first * (1.0 / members)
    sums = class_sums(within.reshape(parts * tiles, MXU), classes).reshape(parts, tiles, LANES)
    acc = acc_ref[...]
    for part in range(parts):
        hit = iota(acc.shape, 1) % 64 // per == step * parts + part
        acc = jnp.where(hit, sums[part], acc)
    acc_ref[...] = acc
    for index, out_ref in enumerate(out_refs):

        @pl.when(turn == index)
        def _():
            for part in range(parts):
                place = pl.multiple_of((step * parts + part) * MXU, MXU)
                out_ref[:, pl.ds(place, MXU)] = first[part].astype(BF16)

            @pl.when(step == pl.num_programs(1) - 1)
            def _():
                out_ref[:, out_ref.shape[1] - LANES :] = split_lanes(acc)


def teacher_moments(blocks, logits, tiles, classes):
    members, _, width = logits.shape
    count = blocks.shape[0]
    block = width // 4
    return pl.pallas_call(
        functools.partial(teacher_kernel, classes),
        grid_spec=pltpu.PrefetchScalarGridSpec(
            num_scalar_prefetch=1,
            grid=(count, width // block),
            in_specs=[pl.BlockSpec((members, tiles, block), lambda i, j, place: (0, place[i], j))],
            out_specs=[pl.BlockSpec((tiles, width + LANES), lambda i, j, place: (0, 0))] * count,
            scratch_shapes=[pltpu.VMEM((tiles, LANES), F32)],
        ),
        out_shape=[jax.ShapeDtypeStruct((tiles, width + LANES), BF16)] * count,
        compiler_params=pltpu.CompilerParams(vmem_limit_bytes=58 << 20),
        cost_estimate=pl.CostEstimate(flops=1_500_000_000, bytes_accessed=2_600_000, transcendentals=3_000_000),
        name="teacher_moments",
    )(blocks, logits)


def combine_kernel(classes, members, columns, capacity, where_ref, cover_ref, after_ref, *refs):
    *got_refs, out_ref = refs
    groups = len(got_refs)
    tiles, extended = got_refs[0].shape
    width = extended - LANES
    means, gaps = [], []
    for start in range(0, width, MXU):
        sums = [got_ref[:, start : start + MXU].astype(F32) for got_ref in got_refs]
        total = sums[0]
        for one in sums[1:]:
            total = total + one
        mean = total * (1.0 / (members * groups))
        means.append(mean.astype(BF16))
        gap = jnp.zeros_like(mean)
        for one in sums:
            off = one * (1.0 / members) - mean
            gap = gap + off * off
        gaps.append(gap)
    between = class_sums(jnp.concatenate(gaps, axis=0), classes)
    lane = iota((tiles, LANES), 1)
    spread = jnp.zeros((tiles, LANES), F32)
    per = MXU // classes
    for i in range(width // MXU):
        spread = jnp.where(lane % 64 // per == i, between[i * tiles : (i + 1) * tiles], spread)
    inner = got_refs[0][:, width:].astype(F32)
    for got_ref in got_refs[1:]:
        inner = inner + got_ref[:, width:].astype(F32)
    spread = spread * (1.0 / groups) + join_lanes(inner) * (1.0 / (members * groups))
    index = (iota((tiles, LANES), 0) + 1).astype(F32).astype(BF16)
    rows = jnp.concatenate([*means, split_lanes(spread), index], axis=1)
    target = cover_ref[where_ref[0]]
    onehot = (iota((columns, tiles), 0) == target).astype(F32)
    earlier = (iota((tiles, tiles), 0) < iota((tiles, tiles), 1)).astype(BF16)
    before = dot(onehot.astype(BF16), earlier)
    rank = jnp.sum(before * onehot, axis=0, keepdims=True).astype(jnp.int32)
    place = (iota((columns * capacity, tiles), 0) == target * capacity + rank).astype(BF16)
    out_ref[...] = dot(place, rows).astype(BF16)


def combine(got, cover, where, after, classes, members, columns, capacity):
    extended = got[0].shape[1]
    return pl.pallas_call(
        functools.partial(combine_kernel, classes, members, columns, capacity),
        in_specs=[pl.BlockSpec(memory_space=pltpu.SMEM), *whole(1), pl.BlockSpec(memory_space=pl.ANY), *whole(len(got))],
        out_specs=pl.BlockSpec(memory_space=pltpu.VMEM),
        out_shape=jax.ShapeDtypeStruct((columns * capacity, extended + LANES), BF16),
        compiler_params=pltpu.CompilerParams(vmem_limit_bytes=12 << 20),
        cost_estimate=pl.CostEstimate(flops=100_000_000, bytes_accessed=1_700_000, transcendentals=0),
        name="combine",
    )(where, cover, after, *got)


def put_shifted(ref, start, value, shift, width):
    rows, channels = value.shape
    col = iota(value.shape, 0) % width
    left = jnp.where(col >= shift, pltpu.roll(value, shift, 0), 0.0)
    right = jnp.where(col < width - shift, pltpu.roll(value, rows - shift, 0), 0.0)
    ref[pl.ds(start, rows), :channels] = left.astype(BF16)
    ref[pl.ds(start, rows), channels : 2 * channels] = value.astype(BF16)
    ref[pl.ds(start, rows), 2 * channels :] = right.astype(BF16)


def three_dots(ref, start, step, rows, weight_ref):
    total = None
    for tap in range(3):
        part = dot(ref[pl.ds(start + tap * step, rows), :], weight_ref[tap])
        total = part if total is None else total + part
    return total


def student_kernel(
    width, edge_ref, before_ref, x_ref, after_ref, first_ref, second_ref, head_ref, label_ref, payload_ref,
    one_ref, two_ref, log_ref, base_ref, label_sum_ref, xcat, hcat, logit_ref,
):
    cells, channels = x_ref.shape
    halo = before_ref.shape[0]
    block = 4 * width

    @pl.loop(0, halo // width)
    def _(i):
        start = pl.multiple_of(i * width, width)
        put_shifted(xcat, start, before_ref[pl.ds(start, width)].astype(F32), 1, width)
        low = pl.multiple_of(halo + cells + start, width)
        put_shifted(xcat, low, after_ref[pl.ds(start, width)].astype(F32), 1, width)

    @pl.loop(0, cells // block)
    def _(i):
        start = pl.multiple_of(i * block, block)
        low = pl.multiple_of(halo + start, width)
        put_shifted(xcat, low, x_ref[pl.ds(start, block)].astype(F32), 1, width)

    lines = cells // width

    @pl.loop(0, (cells + block) // block)
    def _(i):
        start = pl.multiple_of(i * block, block)
        value = three_dots(xcat, start, width, block, first_ref)
        line = i * 4 + iota(value.shape, 0) // width
        low = jnp.where(edge_ref[0] == 1, 2, 0)
        high = jnp.where(edge_ref[1] == 1, lines + 2, lines + 4)
        value = jnp.where((line >= low) & (line < high) & (value > 0), value, 0.0)
        put_shifted(hcat, start, value, 2, width)
        one_ref[pl.ds(start, block), :] = value.astype(BF16)

    @pl.loop(0, cells // block)
    def _(i):
        start = pl.multiple_of(i * block, block)
        value = three_dots(hcat, start, 2 * width, block, second_ref)
        value = jnp.where(value > 0, value, 0.0)
        two = value.astype(BF16)
        two_ref[pl.ds(start, block), :] = two
        logit_ref[pl.ds(start, block), :] = dot(two, head_ref[...])

    tiles, pixels = label_ref.shape
    edge = math.isqrt(pixels)
    across = width // edge
    lane = iota((tiles, LANES), 1)
    even = lane < 64
    label_sum = jnp.zeros((tiles, LANES), F32)
    for pair in range(pixels // 2):
        row, col = 2 * pair // edge, 2 * pair % edge
        parts = []
        for down in range(tiles // across):
            start = (down * edge + row) * width + col
            left = logit_ref[pl.ds(start, across, stride=edge), :]
            right = logit_ref[pl.ds(start + 1, across, stride=edge), :]
            parts.append(jnp.where(iota(left.shape, 1) < 64, left, right))
        value = jnp.concatenate(parts, axis=0)
        top = jnp.where(
            even,
            jnp.max(jnp.where(even, value, -jnp.inf), axis=1, keepdims=True),
            jnp.max(jnp.where(even, -jnp.inf, value), axis=1, keepdims=True),
        )
        value = value - top
        power = jnp.exp(value)
        total = jnp.where(
            even,
            jnp.sum(jnp.where(even, power, 0.0), axis=1, keepdims=True),
            jnp.sum(jnp.where(even, 0.0, power), axis=1, keepdims=True),
        )
        value = value - jnp.log(total)
        label = jnp.where(even, label_ref[:, 2 * pair : 2 * pair + 1], label_ref[:, 2 * pair + 1 : 2 * pair + 2])
        hit = label == lane % 64
        label_sum = label_sum + jnp.where(hit, value, 0.0)
        log_ref[pair * tiles : (pair + 1) * tiles, :] = value
        base_ref[pair * tiles : (pair + 1) * tiles, :] = jnp.exp(value) - hit.astype(F32)
    label_sum_ref[...] = label_sum


def student_forward(edges, before, x, after, first, second, head, labels, payload, width):
    cells, channels = x.shape
    halo = before.shape[0]
    tiles, pixels = labels.shape
    shape = jax.ShapeDtypeStruct
    return pl.pallas_call(
        functools.partial(student_kernel, width),
        in_specs=[pl.BlockSpec(memory_space=pltpu.SMEM), *whole(7), pl.BlockSpec(memory_space=pl.ANY)],
        out_specs=whole(5),
        out_shape=[
            shape((cells + 4 * width, channels), BF16),
            shape((cells, channels), BF16),
            shape((cells // 2, LANES), F32),
            shape((cells // 2, LANES), F32),
            shape((tiles, LANES), F32),
        ],
        scratch_shapes=[
            pltpu.VMEM((cells + 2 * halo, 3 * channels), BF16),
            pltpu.VMEM((cells + 4 * width, 3 * channels), BF16),
            pltpu.VMEM((cells, LANES), F32),
        ],
        compiler_params=pltpu.CompilerParams(vmem_limit_bytes=28 << 20),
        cost_estimate=pl.CostEstimate(flops=6_000_000_000, bytes_accessed=18_000_000, transcendentals=500_000),
        name="student_forward",
    )(edges, before, x, after, first, second, head, labels, payload)


def put_turned(ref, start, value, shift, width):
    rows, channels = value.shape
    col = iota(value.shape, 0) % width
    left = jnp.where(col >= shift, pltpu.roll(value, shift, 0), 0.0)
    right = jnp.where(col < width - shift, pltpu.roll(value, rows - shift, 0), 0.0)
    for tap, one in enumerate((left, value, right)):
        ref[tap * channels : (tap + 1) * channels, pl.ds(start, rows)] = one.T.astype(BF16)


def turn_kernel(
    width, before_ref, x_ref, after_ref, one_ref, two_ref, second_ref, sent_ref, xt_ref, ht_ref, twot_ref, wt_ref
):
    cells, channels = x_ref.shape
    halo = before_ref.shape[0]
    pair = 2 * width
    first = jnp.concatenate([before_ref[halo - width :], x_ref[:width]], axis=0).astype(F32)
    put_turned(xt_ref, 0, first, 1, width)
    last = jnp.concatenate([x_ref[cells - width :], after_ref[:width]], axis=0).astype(F32)
    put_turned(xt_ref, cells, last, 1, width)

    @pl.loop(1, cells // pair)
    def _(i):
        start = pl.multiple_of(i * pair, pair)
        put_turned(xt_ref, start, x_ref[pl.ds(pl.multiple_of(start - width, width), pair)].astype(F32), 1, width)

    @pl.loop(0, one_ref.shape[0] // pair)
    def _(i):
        start = pl.multiple_of(i * pair, pair)
        put_turned(ht_ref, start, one_ref[pl.ds(start, pair)].astype(F32), 2, width)

    @pl.loop(0, cells // MXU)
    def _(i):
        start = pl.multiple_of(i * MXU, MXU)
        twot_ref[:, pl.ds(start, MXU)] = two_ref[pl.ds(start, MXU)].astype(F32).T.astype(BF16)

    @pl.loop(0, 3)
    def _(i):
        for tap in range(3):
            part = slice(tap * channels, (tap + 1) * channels)
            mirror = slice((2 - tap) * channels, (3 - tap) * channels)
            wt_ref[i, part, :] = second_ref[i, mirror, :].astype(F32).T.astype(BF16)


def turn(before, x, after, one, two, second, sent, width):
    cells, channels = x.shape
    shape = jax.ShapeDtypeStruct
    return pl.pallas_call(
        functools.partial(turn_kernel, width),
        in_specs=[*whole(6), pl.BlockSpec(memory_space=pl.ANY)],
        out_specs=whole(4),
        out_shape=[
            shape((3 * channels, cells + 2 * width), BF16),
            shape((3 * channels, cells + 4 * width), BF16),
            shape((channels, cells), BF16),
            shape((3, 3 * channels, channels), BF16),
        ],
        compiler_params=pltpu.CompilerParams(vmem_limit_bytes=20 << 20),
        cost_estimate=pl.CostEstimate(flops=3_000_000_000, bytes_accessed=14_000_000, transcendentals=0),
        name="turn",
    )(before, x, after, one, two, second, sent)


def head_kernel(
    scale, width, got_ref, log_ref, base_ref, label_sum_ref, two_ref, twot_ref, headt_ref,
    grad_ref, top_ref, bottom_ref, head_grad_ref, natural,
):
    slots, extended = got_ref.shape
    tiles = label_sum_ref.shape[0]
    flat = extended - 2 * LANES
    pixels = flat // 64
    edge = math.isqrt(pixels)
    across = width // edge
    index = got_ref[:, flat + LANES :].astype(F32)
    take = (index == (iota((slots, LANES), 1) + 1).astype(F32)).astype(F32).T[:tiles].astype(BF16)
    spread = join_lanes(dot(take, got_ref[:, flat : flat + LANES]))
    weight = 1.0 / (0.1 + spread)
    even = iota((tiles, LANES), 1) < 64
    loss = -label_sum_ref[...]
    for pair in range(pixels // 2):
        rows = slice(pair * tiles, (pair + 1) * tiles)
        if pair % 2 == 0:
            both = dot(take, got_ref[:, pair * LANES : (pair + 2) * LANES])
        mean = both[:, pair % 2 * LANES : (pair % 2 + 1) * LANES]
        cell = jnp.where(even, weight[:, 2 * pair : 2 * pair + 1], weight[:, 2 * pair + 1 : 2 * pair + 2])
        value = log_ref[rows, :]
        held = mean > 0
        loss = loss + cell * jnp.where(held, mean * (jnp.log(jnp.where(held, mean, 1.0)) - value), 0.0)
        grad = (cell * (jnp.exp(value) - mean) + base_ref[rows, :]) * scale
        turned = pltpu.roll(grad, 64, 1)
        row, col = 2 * pair // edge, 2 * pair % edge
        for down in range(tiles // across):
            start = (down * edge + row) * width + col
            natural[pl.ds(start, across, stride=edge), :] = grad[down * across : (down + 1) * across]
            natural[pl.ds(start + 1, across, stride=edge), :] = turned[down * across : (down + 1) * across]
    cells, channels = two_ref.shape
    logit_grad = natural[...].astype(BF16)
    head_grad_ref[:channels, :] = dot(twot_ref[...], logit_grad)
    head_grad_ref[channels:, :] = loss
    block = 4 * width
    for start in range(0, cells, block):
        rows = slice(start, start + block)
        grad = dot(logit_grad[rows], headt_ref[...])
        grad_ref[rows, :] = jnp.where(two_ref[rows, :].astype(F32) > 0, grad, 0.0).astype(BF16)
    top_ref[...] = grad_ref[: 2 * width, :]
    bottom_ref[...] = grad_ref[cells - 2 * width :, :]


def head_step(got, log, base, label_sum, two, twot, headt, scale, width):
    cells, channels = two.shape
    shape = jax.ShapeDtypeStruct
    return pl.pallas_call(
        functools.partial(head_kernel, scale, width),
        in_specs=whole(7),
        out_specs=whole(4),
        out_shape=[
            shape((cells, channels), BF16),
            shape((2 * width, channels), BF16),
            shape((2 * width, channels), BF16),
            shape((channels + label_sum.shape[0], LANES), F32),
        ],
        scratch_shapes=[pltpu.VMEM((cells, LANES), F32)],
        compiler_params=pltpu.CompilerParams(vmem_limit_bytes=14 << 20),
        cost_estimate=pl.CostEstimate(flops=400_000_000, bytes_accessed=5_000_000, transcendentals=500_000),
        name="head_step",
    )(got, log, base, label_sum, two, twot, headt)


def second_kernel(width, ht_ref, grad_ref, out_ref):
    cells, channels = grad_ref.shape
    for tap in range(3):
        part = dot(ht_ref[:, 2 * width * tap : 2 * width * tap + cells], grad_ref[...])
        out_ref[tap * 3 * channels : (tap + 1) * 3 * channels, :] = part.astype(BF16)


def second_step(ht, grad, width):
    channels = grad.shape[1]
    return pl.pallas_call(
        functools.partial(second_kernel, width),
        in_specs=whole(2),
        out_specs=pl.BlockSpec(memory_space=pltpu.VMEM),
        out_shape=jax.ShapeDtypeStruct((9 * channels, channels), BF16),
        compiler_params=pltpu.CompilerParams(vmem_limit_bytes=14 << 20),
        cost_estimate=pl.CostEstimate(flops=2_500_000_000, bytes_accessed=7_000_000, transcendentals=0),
        name="second_step",
    )(ht, grad)


def first_kernel(
    width, core_ref, before_ref, grad_ref, after_ref, wt_ref, one_ref, xt_ref, head_grad_ref, second_ref,
    keep_ref, give_ref, gcat, padded, whole_ref,
):
    cells, channels = grad_ref.shape
    halo = before_ref.shape[0]
    block = 4 * width
    put_shifted(gcat, 0, before_ref[...].astype(F32), 2, width)
    put_shifted(gcat, halo + cells, after_ref[...].astype(F32), 2, width)
    for start in range(0, cells, block):
        put_shifted(gcat, halo + start, grad_ref[start : start + block, :].astype(F32), 2, width)
    padded[: 2 * width, :] = jnp.zeros((2 * width, channels), BF16)
    padded[2 * width + cells :, :] = jnp.zeros((2 * width, channels), BF16)
    for start in range(0, cells, block):
        value = None
        for tap in range(3):
            low = start + (2 - tap) * 2 * width
            part = dot(gcat[low : low + block, :], wt_ref[tap])
            value = part if value is None else value + part
        held = one_ref[2 * width + start : 2 * width + start + block, :].astype(F32) > 0
        padded[2 * width + start : 2 * width + start + block, :] = jnp.where(held, value, 0.0).astype(BF16)
    span = cells + 2 * width
    for tap in range(3):
        part = dot(xt_ref[...], padded[(2 - tap) * width : (2 - tap) * width + span, :])
        whole_ref[tap * 3 * channels : (tap + 1) * 3 * channels, :] = part.astype(BF16)
    rows = 9 * channels
    lane = iota((channels // 2, LANES), 1)
    loss = jnp.sum(head_grad_ref[channels:, :])
    high = loss.astype(BF16).astype(F32)
    extra = jnp.where(lane == 64, high, jnp.where(lane == 65, loss - high, 0.0))
    extra = jnp.where(iota(lane.shape, 0) == core_ref[1] % (channels // 2), extra, 0.0)
    for side in range(2):
        value = jnp.where(lane < 64, head_grad_ref[side * channels // 2 : (side + 1) * channels // 2, :], extra)
        whole_ref[rows : rows + channels // 2, side * LANES : (side + 1) * LANES] = value.astype(BF16)
    used = rows + channels // 2
    half = keep_ref.shape[0]

    def fill(one_half, two_half):
        one_half[:used, :] = whole_ref[:used, :]
        two_half[:rows, :] = second_ref[...]
        one_half[used:, :] = jnp.zeros((half - used, channels), BF16)
        two_half[rows:, :] = jnp.zeros((half - rows, channels), BF16)

    @pl.when(core_ref[0] == 0)
    def _():
        fill(keep_ref, give_ref)

    @pl.when(core_ref[0] != 0)
    def _():
        fill(give_ref, keep_ref)


def first_step(core, before, grad, after, wt, one, xt, head_grad, second, width, half_rows):
    cells, channels = grad.shape
    halo = before.shape[0]
    rows = 10 * channels
    half = jax.ShapeDtypeStruct((half_rows, channels), BF16)
    return pl.pallas_call(
        functools.partial(first_kernel, width),
        in_specs=[pl.BlockSpec(memory_space=pltpu.SMEM), *whole(8)],
        out_specs=whole(2),
        out_shape=[half, half],
        scratch_shapes=[
            pltpu.VMEM((cells + 2 * halo, 3 * channels), BF16),
            pltpu.VMEM((cells + 4 * width, channels), BF16),
            pltpu.VMEM((rows, channels), BF16),
        ],
        compiler_params=pltpu.CompilerParams(vmem_limit_bytes=24 << 20),
        cost_estimate=pl.CostEstimate(flops=5_000_000_000, bytes_accessed=10_000_000, transcendentals=0),
        name="first_step",
    )(core, before, grad, after, wt, one, xt, head_grad, second)


def exchange(array, axis):
    return lax.all_to_all(array, axis, split_axis=0, concat_axis=0, tiled=True)


def neighbours(first, last, axis):
    count = lax.axis_size(axis)
    up = [(i, i + 1) for i in range(count - 1)]
    down = [(i + 1, i) for i in range(count - 1)]
    return (lax.ppermute(last, axis, up), lax.ppermute(first, axis, down))


def pairwise(array, axis, step):
    count = lax.axis_size(axis)
    return lax.ppermute(array, axis, [(i, i ^ step) for i in range(count)])


def scatter_sum(arrays, axis):
    count, me = lax.axis_size(axis), lax.axis_index(axis)
    rows = arrays[0].shape[0] // count

    def block(step):
        start = (me ^ step) * rows
        parts = [lax.dynamic_slice_in_dim(array, start, rows, axis=0).astype(F32) for array in arrays]
        return functools.reduce(jnp.add, parts).astype(BF16)

    order = sorted(range(1, count), key=lambda step: -bin(step).count("1"))
    got = [pairwise(block(step), axis, step) for step in order]
    return [block(0), *got]


def spread_out(array, axis):
    return [array] + [pairwise(array, axis, step) for step in range(1, lax.axis_size(axis))]


def assemble_kernel(place_ref, groups, mine_refs, other_ref, first_ref, second_ref, extra_ref, value_ref, sems):
    chips = len(mine_refs)
    rows = mine_refs[0].shape[0]
    block = rows // groups
    grad_rows = first_ref.shape[0]
    core, chip, member = place_ref[0], place_ref[1], place_ref[2]

    def fill(half, read):
        for s in range(chips):
            for u in range(groups):
                start = ((chip ^ s) * groups + (member ^ u)) * block
                value_ref[half, pl.ds(pl.multiple_of(start, 16), block), :] = read(s, u * block).astype(F32)

    fill(core, lambda s, low: mine_refs[s][low : low + block, :])

    def copies(half):
        out_ref = (first_ref, second_ref)[half]
        return pltpu.make_async_copy(value_ref.at[half, pl.ds(0, grad_rows)], out_ref, sems.at[half])

    @pl.when(core == 0)
    def _():
        copies(0).start()

    @pl.when(core != 0)
    def _():
        copies(1).start()

    fill(1 - core, lambda s, low: other_ref[s * rows + low : s * rows + low + block, :])

    @pl.when(core == 0)
    def _():
        copies(1).start()

    @pl.when(core != 0)
    def _():
        copies(0).start()

    extra_ref[...] = value_ref[0, grad_rows : grad_rows + extra_ref.shape[0], :]
    copies(0).wait()
    copies(1).wait()


def assemble(place, groups, mine, other, grad_rows, extra_rows):
    half, width = other.shape
    shape = jax.ShapeDtypeStruct

    def kernel(place_ref, *refs):
        assemble_kernel(place_ref, groups, refs[: len(mine)], *refs[len(mine) :])

    return pl.pallas_call(
        kernel,
        in_specs=[pl.BlockSpec(memory_space=pltpu.SMEM), *whole(len(mine) + 1)],
        out_specs=[pl.BlockSpec(memory_space=pl.ANY)] * 2 + whole(1),
        out_shape=[shape((grad_rows, width), F32), shape((grad_rows, width), F32), shape((extra_rows, width), F32)],
        scratch_shapes=[pltpu.VMEM((2, half, width), F32), pltpu.SemaphoreType.DMA((2,))],
        compiler_params=pltpu.CompilerParams(vmem_limit_bytes=52 << 20),
        cost_estimate=pl.CostEstimate(flops=1_000_000, bytes_accessed=7_500_000, transcendentals=0),
        name="assemble",
    )(place, *mine, other)


def gradient_total(keep, give, grad_rows, extra_rows):
    groups = lax.axis_size("member")
    got = pairwise(give, "core", 1)
    chip_sums = scatter_sum([keep, got], "chip")
    member_sums = scatter_sum(chip_sums, "member")
    mine = functools.reduce(jnp.add, [part.astype(F32) for part in member_sums]).astype(BF16)
    mine = jnp.concatenate(spread_out(mine, "member"), axis=0)
    mine = spread_out(mine, "chip")
    other = pairwise(jnp.concatenate(mine, axis=0), "core", 1)
    place = jnp.stack([lax.axis_index(axis) for axis in ("core", "chip", "member")]).astype(jnp.int32)
    return assemble(place, groups, mine, other, grad_rows, extra_rows)


def body(teacher_logits, coverage, features, labels, first_weight, second_weight, head_weight):
    channels, classes = head_weight.shape
    members, tiles_here, flat_width = teacher_logits.shape
    pixels = flat_width // classes
    edge = math.isqrt(pixels)
    groups = lax.axis_size("member")
    chips = lax.axis_size("chip")
    columns = chips * 2
    tile_axes = ("chip", "core")
    block_tiles = tiles_here // groups
    capacity = max(2, 2 * block_tiles // columns)
    local = features[0]
    lines, width = local.shape[:2]
    cells = lines * width
    cell_total = groups * columns * cells
    column = lax.axis_index(tile_axes)
    core = jnp.stack([lax.axis_index("core"), lax.axis_index(("member", "chip", "core"))]).astype(jnp.int32)
    member = lax.axis_index("member").astype(jnp.int32).reshape(1)
    edges = jnp.stack([column == 0, column == columns - 1]).astype(jnp.int32)

    flat = local.reshape(cells, channels)
    before, after = neighbours(flat[: 3 * width], flat[cells - 3 * width :], tile_axes)
    order = sorted(range(groups), key=lambda step: -step)
    got = []
    for steps in (order[: groups // 2], order[groups // 2 :]):
        blocks = jnp.stack([lax.axis_index("member") ^ step for step in steps]).astype(jnp.int32)
        payload = teacher_moments(blocks, teacher_logits, block_tiles, classes)
        got += [one if step == 0 else pairwise(one, "member", step) for step, one in zip(steps, payload)]
    payload = payload[-1]
    label_rows = (
        labels[0].reshape(lines // edge, edge, width // edge, edge).transpose(0, 2, 1, 3).reshape(block_tiles, pixels)
    )
    second_rows = second_weight.reshape(3, 3 * channels, channels)
    one, two, log, base, label_sum = student_forward(
        edges,
        before,
        flat,
        after,
        first_weight.reshape(3, 3 * channels, channels),
        second_rows,
        jnp.concatenate([head_weight, head_weight], axis=1),
        label_rows,
        payload,
        width,
    )
    cover = coverage.reshape(groups, 1, block_tiles)
    sent = combine(got, cover, member, label_sum, classes, members, columns, capacity)
    received = exchange(sent.reshape(columns, capacity, -1), tile_axes).reshape(columns * capacity, -1)
    xt, ht, twot, wt = turn(before, flat, after, one, two, second_rows, sent, width)
    headt = jnp.pad(head_weight.T, ((0, LANES - classes), (0, 0)))
    grad_two, top, bottom, head_grad = head_step(
        received, log, base, label_sum, two, twot, headt, 1.0 / math.sqrt(cell_total), width
    )
    grad_before, grad_after = neighbours(top, bottom, tile_axes)
    second = second_step(ht, grad_two, width)
    rows, extra_rows = 9 * channels, channels // 2
    devices = groups * columns
    half_rows = devices // 2 * -(-(rows + extra_rows) // (devices // 2 * 16)) * 16
    keep, give = first_step(core, grad_before, grad_two, grad_after, wt, one, xt, head_grad, second, width, half_rows)
    first_total, second_total, extra = gradient_total(keep, give, rows, extra_rows)
    head_total = jnp.concatenate([extra[:, :classes], extra[:, LANES : LANES + classes]], axis=0)
    loss_total = jnp.sum(extra[:, 64:66]) / cell_total
    kernel_shape = (3, 3, channels, channels)
    return (first_total.reshape(kernel_shape), second_total.reshape(kernel_shape), head_total, loss_total)


def solution(mesh):
    groups, columns = mesh.shape["member"], mesh.shape["tile"]
    split = jax.sharding.Mesh(mesh.devices.reshape(groups, columns // 2, 2), ("member", "chip", "core"))
    tile = ("chip", "core")
    return jax.shard_map(
        body,
        mesh=split,
        in_specs=(
            P("member", tile, None),
            P(tile),
            P("member", tile, None, None),
            P("member", tile, None),
            P(),
            P(),
            P(),
        ),
        out_specs=(P(), P(), P(), P()),
        check_vma=False,
    )
```

```python
import functools
import math

import jax
import jax.numpy as jnp
from jax import lax
from jax.experimental import pallas as pl
from jax.experimental.pallas import tpu as pltpu
from jax.sharding import PartitionSpec as P

BF16 = jnp.bfloat16
F32 = jnp.float32
LANES = 128
MXU = 256


def whole(count):
    return [pl.BlockSpec(memory_space=pltpu.VMEM)] * count


def iota(shape, axis):
    return lax.broadcasted_iota(jnp.int32, shape, axis)


def dot(left, right):
    return jnp.dot(left, right, preferred_element_type=F32)


def split_lanes(value):
    high = value.astype(BF16).astype(F32)
    return jnp.where(iota(value.shape, 1) < 64, high, value - high).astype(BF16)


def join_lanes(value):
    return value + pltpu.roll(value, 64, 1)


def class_sums(value, classes):
    pick = (iota((MXU, LANES), 0) // classes == iota((MXU, LANES), 1) % (MXU // classes)).astype(BF16)
    high = value.astype(BF16)
    low = (value - high.astype(F32)).astype(BF16)
    return dot(high, pick) + dot(low, pick)


def hbm(count):
    return [pl.BlockSpec(memory_space=pl.ANY)] * count


def scalars():
    return pl.BlockSpec(memory_space=pltpu.SMEM)


CORE, CHIP, MEMBER, DEVICE, FIRST, LAST = range(6)


def teacher_kernel(classes, counts, place_ref, x_ref, *refs):
    blocks, edges = counts
    flat_ref, refs = (refs[0], refs[1:]) if edges else (None, refs)
    out_refs, refs = refs[:blocks], refs[blocks:]
    turn = pl.program_id(0)
    members, tiles, width = x_ref.shape
    per = MXU // classes
    group = 4
    same = (iota((MXU, MXU), 0) // classes == iota((MXU, MXU), 1) // classes).astype(BF16)

    if edges:
        top_ref, bottom_ref, sems = refs
        rows = top_ref.shape[0]
        copies = [
            pltpu.make_async_copy(flat_ref.at[pl.ds(0, rows)], top_ref, sems.at[0]),
            pltpu.make_async_copy(flat_ref.at[pl.ds(flat_ref.shape[0] - rows, rows)], bottom_ref, sems.at[1]),
        ]

        @pl.when(turn == 0)
        def _():
            for copy in copies:
                copy.start()

    def moments(out_ref):
        acc = jnp.zeros((tiles, LANES), F32)
        for start in range(0, width, group * MXU):
            x = jnp.concatenate(
                [
                    x_ref[:, :, low : low + MXU].reshape(members * tiles, MXU)
                    for low in range(start, start + group * MXU, MXU)
                ],
                axis=0,
            )
            root = jnp.exp2(x.astype(F32) * (0.25 * math.log2(math.e)))
            root = root * pl.reciprocal(dot(root.astype(BF16), same), approx=True)
            square = root * root
            power = square * square
            total = dot(power.astype(BF16), same)
            inverse = pl.reciprocal(total, approx=True)
            inverse = inverse * (2.0 - total * inverse)
            probs = (power * inverse).reshape(group, members, tiles, MXU)
            first = jnp.sum(probs, axis=1)
            within = jnp.sum(probs * probs, axis=1) - first * first * (1.0 / members)
            sums = class_sums(within.reshape(group * tiles, MXU), classes)
            for part in range(group):
                low = start + part * MXU
                out_ref[:, low : low + MXU] = first[part].astype(BF16)
                hit = iota(acc.shape, 1) % 64 // per == low // MXU
                acc = jnp.where(hit, sums[part * tiles : (part + 1) * tiles], acc)
        out_ref[:, width:] = split_lanes(acc)

    for index, out_ref in enumerate(out_refs):
        pl.when(turn == index)(functools.partial(moments, out_ref))

    if edges:

        @pl.when(turn == pl.num_programs(0) - 1)
        def _():
            for copy in copies:
                copy.wait()


def teacher_moments(place, logits, tiles, classes, steps, flat=None, edge_rows=0):
    members, _, width = logits.shape
    count = len(steps)
    top = steps[0]
    edges = flat is not None
    shape = jax.ShapeDtypeStruct
    extra = [shape((edge_rows, flat.shape[1]), BF16)] * 2 if edges else []
    return pl.pallas_call(
        functools.partial(teacher_kernel, classes, (count, edges)),
        grid_spec=pltpu.PrefetchScalarGridSpec(
            num_scalar_prefetch=1,
            grid=(count,),
            in_specs=[pl.BlockSpec((members, tiles, width), lambda i, at: (0, at[MEMBER] ^ (top - i), 0))]
            + hbm(1 if edges else 0),
            out_specs=[pl.BlockSpec((tiles, width + LANES), lambda i, at: (0, 0))] * count + hbm(len(extra)),
            scratch_shapes=[pltpu.SemaphoreType.DMA((2,))] if edges else [],
        ),
        out_shape=[shape((tiles, width + LANES), BF16)] * count + extra,
        compiler_params=pltpu.CompilerParams(vmem_limit_bytes=56 << 20),
        cost_estimate=pl.CostEstimate(flops=1_500_000_000, bytes_accessed=2_600_000, transcendentals=3_000_000),
        name="teacher_moments",
    )(place, logits, *([flat] if edges else []))


def combine_kernel(classes, members, columns, capacity, where_ref, cover_ref, after_ref, *refs):
    *got_refs, out_ref = refs
    groups = len(got_refs)
    tiles, extended = got_refs[0].shape
    width = extended - LANES
    means, gaps = [], []
    for start in range(0, width, MXU):
        sums = [got_ref[:, start : start + MXU].astype(F32) for got_ref in got_refs]
        total = sums[0]
        for one in sums[1:]:
            total = total + one
        mean = total * (1.0 / (members * groups))
        means.append(mean.astype(BF16))
        gap = jnp.zeros_like(mean)
        for one in sums:
            off = one * (1.0 / members) - mean
            gap = gap + off * off
        gaps.append(gap)
    between = class_sums(jnp.concatenate(gaps, axis=0), classes)
    lane = iota((tiles, LANES), 1)
    spread = jnp.zeros((tiles, LANES), F32)
    per = MXU // classes
    for i in range(width // MXU):
        spread = jnp.where(lane % 64 // per == i, between[i * tiles : (i + 1) * tiles], spread)
    inner = got_refs[0][:, width:].astype(F32)
    for got_ref in got_refs[1:]:
        inner = inner + got_ref[:, width:].astype(F32)
    spread = spread * (1.0 / groups) + join_lanes(inner) * (1.0 / (members * groups))
    index = (iota((tiles, LANES), 0) + 1).astype(F32).astype(BF16)
    rows = jnp.concatenate([*means, split_lanes(spread), index], axis=1)
    target = cover_ref[where_ref[MEMBER]]
    onehot = (iota((columns, tiles), 0) == target).astype(F32)
    earlier = (iota((tiles, tiles), 0) < iota((tiles, tiles), 1)).astype(BF16)
    before = dot(onehot.astype(BF16), earlier)
    rank = jnp.sum(before * onehot, axis=0, keepdims=True).astype(jnp.int32)
    place = (iota((columns * capacity, tiles), 0) == target * capacity + rank).astype(BF16)
    out_ref[...] = dot(place, rows).astype(BF16)


def combine(got, cover, where, after, classes, members, columns, capacity):
    extended = got[0].shape[1]
    return pl.pallas_call(
        functools.partial(combine_kernel, classes, members, columns, capacity),
        in_specs=[pl.BlockSpec(memory_space=pltpu.SMEM), *whole(1), pl.BlockSpec(memory_space=pl.ANY), *whole(len(got))],
        out_specs=pl.BlockSpec(memory_space=pltpu.VMEM),
        out_shape=jax.ShapeDtypeStruct((columns * capacity, extended + LANES), BF16),
        compiler_params=pltpu.CompilerParams(vmem_limit_bytes=12 << 20),
        cost_estimate=pl.CostEstimate(flops=100_000_000, bytes_accessed=1_700_000, transcendentals=0),
        name="combine",
    )(where, cover, after, *got)


def put_shifted(ref, start, value, shift, width):
    rows, channels = value.shape
    col = iota(value.shape, 0) % width
    left = jnp.where(col >= shift, pltpu.roll(value, shift, 0), 0.0)
    right = jnp.where(col < width - shift, pltpu.roll(value, rows - shift, 0), 0.0)
    ref[pl.ds(start, rows), :channels] = left.astype(BF16)
    ref[pl.ds(start, rows), channels : 2 * channels] = value.astype(BF16)
    ref[pl.ds(start, rows), 2 * channels :] = right.astype(BF16)


def three_dots(ref, start, step, rows, weight_ref):
    total = None
    for tap in range(3):
        part = dot(ref[pl.ds(start + tap * step, rows), :], weight_ref[tap])
        total = part if total is None else total + part
    return total


def turned_dot(left, right):
    return lax.dot_general(left, right, (((1,), (1,)), ((), ())), preferred_element_type=F32)


def student_kernel(
    width, place_ref, before_ref, after_ref, head_ref, payload_ref, x_hbm, first_hbm, second_hbm,
    one_hbm, two_hbm, logit_hbm, edge_hbm, x_ref, first_ref, second_ref, xcat, hcat, two_ref, logit_ref, sems,
):
    cells, channels = x_ref.shape
    halo = before_ref.shape[0]
    block = 4 * width
    ins = [
        pltpu.make_async_copy(source, target, sems.at[i])
        for i, (source, target) in enumerate(((x_hbm, x_ref), (first_hbm, first_ref), (second_hbm, second_ref)))
    ]
    for copy in ins:
        copy.start()

    @pl.loop(0, halo // width)
    def _(i):
        start = pl.multiple_of(i * width, width)
        put_shifted(xcat, start, before_ref[pl.ds(start, width)].astype(F32), 1, width)
        low = pl.multiple_of(halo + cells + start, width)
        put_shifted(xcat, low, after_ref[pl.ds(start, width)].astype(F32), 1, width)

    ins[0].wait()
    edges = [
        pltpu.make_async_copy(source, edge_hbm.at[pl.ds(i * width, width)], sems.at[3 + i])
        for i, source in enumerate(
            (
                before_ref.at[pl.ds(halo - width, width)],
                x_ref.at[pl.ds(0, width)],
                x_ref.at[pl.ds(cells - width, width)],
                after_ref.at[pl.ds(0, width)],
            )
        )
    ]
    for copy in edges:
        copy.start()

    @pl.loop(0, cells // block)
    def _(i):
        start = pl.multiple_of(i * block, block)
        low = pl.multiple_of(halo + start, width)
        put_shifted(xcat, low, x_ref[pl.ds(start, block)].astype(F32), 1, width)

    ins[1].wait()
    lines = cells // width

    @pl.loop(0, (cells + block) // block)
    def _(i):
        start = pl.multiple_of(i * block, block)
        value = three_dots(xcat, start, width, block, first_ref)
        line = i * 4 + iota(value.shape, 0) // width
        low = jnp.where(place_ref[FIRST] == 1, 2, 0)
        high = jnp.where(place_ref[LAST] == 1, lines + 2, lines + 4)
        value = jnp.where((line >= low) & (line < high) & (value > 0), value, 0.0)
        put_shifted(hcat, start, value, 2, width)

    one_copy = pltpu.make_async_copy(hcat.at[:, pl.ds(channels, channels)], one_hbm, sems.at[7])
    one_copy.start()
    ins[2].wait()
    head = jnp.concatenate([head_ref[...], head_ref[...]], axis=0)

    @pl.loop(0, cells // block)
    def _(i):
        start = pl.multiple_of(i * block, block)
        rows = pl.ds(start, block)
        value = three_dots(hcat, start, 2 * width, block, second_ref)
        two = jnp.where(value > 0, value, 0.0).astype(BF16)
        two_ref[rows, :] = two
        logit_ref[rows, :] = turned_dot(two, head)
        pltpu.make_async_copy(two_ref.at[rows], two_hbm.at[rows], sems.at[8]).start()
        pltpu.make_async_copy(logit_ref.at[rows], logit_hbm.at[rows], sems.at[9]).start()

    for copy in edges:
        copy.wait()
    one_copy.wait()
    pltpu.make_async_copy(two_ref, two_hbm, sems.at[8]).wait()
    pltpu.make_async_copy(logit_ref, logit_hbm, sems.at[9]).wait()


def student_forward(place, before, after, head, payload, x, first, second, width):
    cells, channels = x.shape
    halo = before.shape[0]
    shape = jax.ShapeDtypeStruct
    return pl.pallas_call(
        functools.partial(student_kernel, width),
        in_specs=[scalars(), *whole(3), *hbm(4)],
        out_specs=hbm(4),
        out_shape=[
            shape((cells + 4 * width, channels), BF16),
            shape((cells, channels), BF16),
            shape((cells, LANES), F32),
            shape((4 * width, channels), BF16),
        ],
        scratch_shapes=[
            pltpu.VMEM((cells, channels), BF16),
            pltpu.VMEM(first.shape, BF16),
            pltpu.VMEM(second.shape, BF16),
            pltpu.VMEM((cells + 2 * halo, 3 * channels), BF16),
            pltpu.VMEM((cells + 4 * width, 3 * channels), BF16),
            pltpu.VMEM((cells, channels), BF16),
            pltpu.VMEM((cells, LANES), F32),
            pltpu.SemaphoreType.DMA((10,)),
        ],
        compiler_params=pltpu.CompilerParams(vmem_limit_bytes=56 << 20),
        cost_estimate=pl.CostEstimate(flops=6_000_000_000, bytes_accessed=12_000_000, transcendentals=0),
        name="student_forward",
    )(place, before, after, head, payload, x, first, second)


def put_turned(ref, start, value, shift, width):
    rows, channels = value.shape
    col = iota(value.shape, 0) % width
    left = jnp.where(col >= shift, pltpu.roll(value, shift, 0), 0.0)
    right = jnp.where(col < width - shift, pltpu.roll(value, rows - shift, 0), 0.0)
    for tap, one in enumerate((left, value, right)):
        ref[tap * channels : (tap + 1) * channels, pl.ds(start, rows)] = one.T.astype(BF16)


def turn_kernel(
    width, label_ref, sent_ref, *refs
):
    ins_hbm, refs = refs[:6], refs[6:]
    outs_hbm, refs = refs[:7], refs[7:]
    ins, refs = refs[:6], refs[6:]
    outs, (in_sems, out_sems) = refs[:7], refs[7:]
    logit_ref, second_ref, edge_ref, x_ref, one_ref, two_ref = ins
    log_ref, base_ref, label_sum_ref, wt_ref, xt_ref, ht_ref, twot_ref = outs
    arrive = [pltpu.make_async_copy(a, b, in_sems.at[i]) for i, (a, b) in enumerate(zip(ins_hbm, ins))]
    leave = [pltpu.make_async_copy(a, b, out_sems.at[i]) for i, (a, b) in enumerate(zip(outs, outs_hbm))]
    for copy in arrive:
        copy.start()
    cells, channels = x_ref.shape
    pair = 2 * width
    arrive[0].wait()

    tiles, pixels = label_ref.shape
    edge = math.isqrt(pixels)
    across = width // edge
    lane = iota((tiles, LANES), 1)
    even = lane < 64
    label_sum = jnp.zeros((tiles, LANES), F32)
    for item in range(pixels // 2):
        row, col = 2 * item // edge, 2 * item % edge
        parts = []
        for down in range(tiles // across):
            start = (down * edge + row) * width + col
            left = logit_ref[pl.ds(start, across, stride=edge), :]
            right = logit_ref[pl.ds(start + 1, across, stride=edge), :]
            parts.append(jnp.where(iota(left.shape, 1) < 64, left, right))
        value = jnp.concatenate(parts, axis=0)
        top = jnp.where(
            even,
            jnp.max(jnp.where(even, value, -jnp.inf), axis=1, keepdims=True),
            jnp.max(jnp.where(even, -jnp.inf, value), axis=1, keepdims=True),
        )
        value = value - top
        power = jnp.exp(value)
        total = jnp.where(
            even,
            jnp.sum(jnp.where(even, power, 0.0), axis=1, keepdims=True),
            jnp.sum(jnp.where(even, 0.0, power), axis=1, keepdims=True),
        )
        value = value - jnp.log(total)
        label = jnp.where(even, label_ref[:, 2 * item : 2 * item + 1], label_ref[:, 2 * item + 1 : 2 * item + 2])
        hit = label == lane % 64
        label_sum = label_sum + jnp.where(hit, value, 0.0)
        log_ref[item * tiles : (item + 1) * tiles, :] = value
        base_ref[item * tiles : (item + 1) * tiles, :] = jnp.exp(value) - hit.astype(F32)
    label_sum_ref[...] = label_sum
    for copy in leave[:3]:
        copy.start()

    arrive[1].wait()

    @pl.loop(0, 3)
    def _(i):
        for tap in range(3):
            part = slice(tap * channels, (tap + 1) * channels)
            mirror = slice((2 - tap) * channels, (3 - tap) * channels)
            wt_ref[i, part, :] = second_ref[i, mirror, :].astype(F32).T.astype(BF16)

    leave[3].start()
    arrive[2].wait()
    put_turned(xt_ref, 0, edge_ref[:pair].astype(F32), 1, width)
    put_turned(xt_ref, cells, edge_ref[pair:].astype(F32), 1, width)
    arrive[3].wait()

    @pl.loop(1, cells // pair)
    def _(i):
        start = pl.multiple_of(i * pair, pair)
        put_turned(xt_ref, start, x_ref[pl.ds(pl.multiple_of(start - width, width), pair)].astype(F32), 1, width)

    leave[4].start()
    arrive[4].wait()

    @pl.loop(0, one_ref.shape[0] // pair)
    def _(i):
        start = pl.multiple_of(i * pair, pair)
        put_turned(ht_ref, start, one_ref[pl.ds(start, pair)].astype(F32), 2, width)

    leave[5].start()
    arrive[5].wait()

    @pl.loop(0, cells // MXU)
    def _(i):
        start = pl.multiple_of(i * MXU, MXU)
        twot_ref[:, pl.ds(start, MXU)] = two_ref[pl.ds(start, MXU)].astype(F32).T.astype(BF16)

    leave[6].start()
    for copy in leave:
        copy.wait()


def turn(labels, sent, logit, second, edge, x, one, two, width):
    cells, channels = x.shape
    tiles = labels.shape[0]
    shape = jax.ShapeDtypeStruct
    outs = [
        shape((cells // 2, LANES), F32),
        shape((cells // 2, LANES), F32),
        shape((tiles, LANES), F32),
        shape((3, 3 * channels, channels), BF16),
        shape((3 * channels, cells + 2 * width), BF16),
        shape((3 * channels, cells + 4 * width), BF16),
        shape((channels, cells), BF16),
    ]
    ins = (logit, second, edge, x, one, two)
    return pl.pallas_call(
        functools.partial(turn_kernel, width),
        in_specs=[*whole(1), *hbm(7)],
        out_specs=hbm(7),
        out_shape=outs,
        scratch_shapes=[
            *[pltpu.VMEM(one_in.shape, one_in.dtype) for one_in in ins],
            *[pltpu.VMEM(one_out.shape, one_out.dtype) for one_out in outs],
            pltpu.SemaphoreType.DMA((6,)),
            pltpu.SemaphoreType.DMA((7,)),
        ],
        compiler_params=pltpu.CompilerParams(vmem_limit_bytes=56 << 20),
        cost_estimate=pl.CostEstimate(flops=5_000_000_000, bytes_accessed=18_000_000, transcendentals=500_000),
        name="turn",
    )(labels, sent, *ins)


def head_kernel(
    scale, width, got_ref, head_ref, *refs
):
    ins_hbm, refs = refs[:5], refs[5:]
    grad_ref, top_ref, bottom_ref, head_grad_ref, *refs = refs
    ins, (natural, sems) = refs[:5], refs[5:]
    label_sum_ref, log_ref, base_ref, twot_ref, two_ref = ins
    arrive = [pltpu.make_async_copy(a, b, sems.at[i]) for i, (a, b) in enumerate(zip(ins_hbm, ins))]
    for copy in arrive:
        copy.start()
    slots, extended = got_ref.shape
    tiles = label_sum_ref.shape[0]
    flat = extended - 2 * LANES
    pixels = flat // 64
    edge = math.isqrt(pixels)
    across = width // edge
    index = got_ref[:, flat + LANES :].astype(F32)
    take = (index == (iota((slots, LANES), 1) + 1).astype(F32)).astype(F32).T[:tiles].astype(BF16)
    spread = join_lanes(dot(take, got_ref[:, flat : flat + LANES]))
    weight = 1.0 / (0.1 + spread)
    even = iota((tiles, LANES), 1) < 64
    for copy in arrive[:3]:
        copy.wait()
    loss = -label_sum_ref[...]
    for pair in range(pixels // 2):
        rows = slice(pair * tiles, (pair + 1) * tiles)
        if pair % 2 == 0:
            both = dot(take, got_ref[:, pair * LANES : (pair + 2) * LANES])
        mean = both[:, pair % 2 * LANES : (pair % 2 + 1) * LANES]
        cell = jnp.where(even, weight[:, 2 * pair : 2 * pair + 1], weight[:, 2 * pair + 1 : 2 * pair + 2])
        value = log_ref[rows, :]
        held = mean > 0
        loss = loss + cell * jnp.where(held, mean * (jnp.log(jnp.where(held, mean, 1.0)) - value), 0.0)
        grad = (cell * (jnp.exp(value) - mean) + base_ref[rows, :]) * scale
        turned = pltpu.roll(grad, 64, 1)
        row, col = 2 * pair // edge, 2 * pair % edge
        for down in range(tiles // across):
            start = (down * edge + row) * width + col
            natural[pl.ds(start, across, stride=edge), :] = grad[down * across : (down + 1) * across]
            natural[pl.ds(start + 1, across, stride=edge), :] = turned[down * across : (down + 1) * across]
    cells, channels = two_ref.shape
    logit_grad = natural[...].astype(BF16)
    head = jnp.concatenate([head_ref[...], jnp.zeros_like(head_ref)], axis=0)
    for copy in arrive[3:]:
        copy.wait()
    head_grad_ref[:channels, :] = dot(twot_ref[...], logit_grad)
    head_grad_ref[channels:, :] = loss
    block = 4 * width
    for start in range(0, cells, block):
        rows = slice(start, start + block)
        grad = dot(logit_grad[rows], head)
        grad_ref[rows, :] = jnp.where(two_ref[rows, :].astype(F32) > 0, grad, 0.0).astype(BF16)
    top_ref[...] = grad_ref[: 2 * width, :]
    bottom_ref[...] = grad_ref[cells - 2 * width :, :]


def head_step(got, head, label_sum, log, base, twot, two, scale, width):
    cells, channels = two.shape
    shape = jax.ShapeDtypeStruct
    ins = (label_sum, log, base, twot, two)
    return pl.pallas_call(
        functools.partial(head_kernel, scale, width),
        in_specs=[*whole(2), *hbm(5)],
        out_specs=whole(4),
        out_shape=[
            shape((cells, channels), BF16),
            shape((2 * width, channels), BF16),
            shape((2 * width, channels), BF16),
            shape((channels + label_sum.shape[0], LANES), F32),
        ],
        scratch_shapes=[
            *[pltpu.VMEM(one.shape, one.dtype) for one in ins],
            pltpu.VMEM((cells, LANES), F32),
            pltpu.SemaphoreType.DMA((5,)),
        ],
        compiler_params=pltpu.CompilerParams(vmem_limit_bytes=52 << 20),
        cost_estimate=pl.CostEstimate(flops=400_000_000, bytes_accessed=5_000_000, transcendentals=500_000),
        name="head_step",
    )(got, head, *ins)


def second_kernel(width, grad_ref, ht_hbm, out_ref, ht_ref, sems):
    cells, channels = grad_ref.shape
    parts = sems.shape[0]
    span = cells // parts
    sizes = [span + (4 * width if i == parts - 1 else 0) for i in range(parts)]
    arrive = [
        pltpu.make_async_copy(
            ht_hbm.at[:, pl.ds(i * span, size)], ht_ref.at[:, pl.ds(i * span, size)], sems.at[i]
        )
        for i, size in enumerate(sizes)
    ]
    for copy in arrive:
        copy.start()
    for copy in arrive:
        copy.wait()
    for tap in range(3):
        part = dot(ht_ref[:, 2 * width * tap : 2 * width * tap + cells], grad_ref[...])
        out_ref[tap * 3 * channels : (tap + 1) * 3 * channels, :] = part.astype(BF16)


def second_step(grad, ht, width):
    channels = grad.shape[1]
    return pl.pallas_call(
        functools.partial(second_kernel, width),
        in_specs=[*whole(1), *hbm(1)],
        out_specs=pl.BlockSpec(memory_space=pltpu.VMEM),
        out_shape=jax.ShapeDtypeStruct((9 * channels, channels), BF16),
        scratch_shapes=[pltpu.VMEM(ht.shape, BF16), pltpu.SemaphoreType.DMA((4,))],
        compiler_params=pltpu.CompilerParams(vmem_limit_bytes=52 << 20),
        cost_estimate=pl.CostEstimate(flops=2_500_000_000, bytes_accessed=7_000_000, transcendentals=0),
        name="second_step",
    )(grad, ht)


def first_kernel(width, chips, place_ref, before_ref, after_ref, grad_ref, head_grad_ref, second_ref, *refs):
    ins_hbm, refs = refs[:3], refs[3:]
    keep_refs, give_refs, refs = refs[:chips], refs[chips : 2 * chips], refs[2 * chips :]
    wt_ref, one_ref, xt_ref, gcat, padded, halves, sems = refs
    arrive = [
        pltpu.make_async_copy(a, b, sems.at[i]) for i, (a, b) in enumerate(zip(ins_hbm, (wt_ref, one_ref, xt_ref)))
    ]
    cells, channels = grad_ref.shape
    rows = 9 * channels
    used = rows + channels // 2
    half = halves.shape[1]
    arrive.append(pltpu.make_async_copy(second_ref, halves.at[1, pl.ds(0, rows)], sems.at[3]))
    for copy in arrive:
        copy.start()
    halo = before_ref.shape[0]
    block = 4 * width
    put_shifted(gcat, 0, before_ref[...].astype(F32), 2, width)
    put_shifted(gcat, halo + cells, after_ref[...].astype(F32), 2, width)
    for start in range(0, cells, block):
        put_shifted(gcat, halo + start, grad_ref[start : start + block, :].astype(F32), 2, width)
    padded[: 2 * width, :] = jnp.zeros((2 * width, channels), BF16)
    padded[2 * width + cells :, :] = jnp.zeros((2 * width, channels), BF16)
    arrive[0].wait()
    arrive[1].wait()
    for start in range(0, cells, block):
        value = None
        for tap in range(3):
            low = start + (2 - tap) * 2 * width
            part = dot(gcat[low : low + block, :], wt_ref[tap])
            value = part if value is None else value + part
        held = one_ref[2 * width + start : 2 * width + start + block, :].astype(F32) > 0
        padded[2 * width + start : 2 * width + start + block, :] = jnp.where(held, value, 0.0).astype(BF16)
    arrive[2].wait()
    span = cells + 2 * width
    for tap in range(3):
        part = dot(xt_ref[...], padded[(2 - tap) * width : (2 - tap) * width + span, :])
        halves[0, tap * 3 * channels : (tap + 1) * 3 * channels, :] = part.astype(BF16)
    lane = iota((channels // 2, LANES), 1)
    loss = jnp.sum(head_grad_ref[channels:, :])
    high = loss.astype(BF16).astype(F32)
    extra = jnp.where(lane == 64, high, jnp.where(lane == 65, loss - high, 0.0))
    extra = jnp.where(iota(lane.shape, 0) == place_ref[DEVICE] % (channels // 2), extra, 0.0)
    for side in range(2):
        value = jnp.where(lane < 64, head_grad_ref[side * channels // 2 : (side + 1) * channels // 2, :], extra)
        halves[0, rows:used, side * LANES : (side + 1) * LANES] = value.astype(BF16)
    halves[0, used:, :] = jnp.zeros((half - used, channels), BF16)
    halves[1, rows:, :] = jnp.zeros((half - rows, channels), BF16)
    arrive[3].wait()
    core, chip = place_ref[CORE], place_ref[CHIP]
    size = half // chips
    for step in range(chips):
        low = pl.multiple_of((chip ^ step) * size, 16)
        give_refs[step][...] = halves[1 - core, pl.ds(low, size), :]
        keep_refs[step][...] = halves[core, pl.ds(low, size), :]


def first_step(place, before, after, grad, head_grad, second, wt, one, xt, width, half_rows, chips):
    cells, channels = grad.shape
    halo = before.shape[0]
    piece = jax.ShapeDtypeStruct((half_rows // chips, channels), BF16)
    outs = pl.pallas_call(
        functools.partial(first_kernel, width, chips),
        in_specs=[scalars(), *whole(5), *hbm(3)],
        out_specs=whole(2 * chips),
        out_shape=[piece] * (2 * chips),
        scratch_shapes=[
            pltpu.VMEM(wt.shape, BF16),
            pltpu.VMEM(one.shape, BF16),
            pltpu.VMEM(xt.shape, BF16),
            pltpu.VMEM((cells + 2 * halo, 3 * channels), BF16),
            pltpu.VMEM((cells + 4 * width, channels), BF16),
            pltpu.VMEM((2, half_rows, channels), BF16),
            pltpu.SemaphoreType.DMA((4,)),
        ],
        compiler_params=pltpu.CompilerParams(vmem_limit_bytes=48 << 20),
        cost_estimate=pl.CostEstimate(flops=5_000_000_000, bytes_accessed=10_000_000, transcendentals=0),
        name="first_step",
    )(place, before, after, grad, head_grad, second, wt, one, xt)
    return (outs[:chips], outs[chips:])


def exchange(array, axis):
    return lax.all_to_all(array, axis, split_axis=0, concat_axis=0, tiled=True)


def neighbours(first, last, axis):
    count = lax.axis_size(axis)
    up = [(i, i + 1) for i in range(count - 1)]
    down = [(i + 1, i) for i in range(count - 1)]
    return (lax.ppermute(last, axis, up), lax.ppermute(first, axis, down))


def pairwise(array, axis, step):
    count = lax.axis_size(axis)
    return lax.ppermute(array, axis, [(i, i ^ step) for i in range(count)])


def add(arrays):
    return functools.reduce(jnp.add, [array.astype(F32) for array in arrays]).astype(BF16)


def assemble_kernel(
    width, chips, groups, cell_total, place_ref, *refs
):
    parts = len(refs) - 6
    pieces, refs = refs[:parts], refs[parts:]
    first_ref, second_ref, head_ref, loss_ref, value_ref, sems = refs
    mine, other = pieces[: parts // 2], pieces[parts // 2 :]
    batches = len(mine) // chips
    size = groups // batches
    block = mine[0].shape[0] // size
    grad_rows = first_ref.shape[0]
    core, chip, member = place_ref[CORE], place_ref[CHIP], place_ref[MEMBER]

    def fill(half, source):
        for batch in range(batches):
            for s in range(chips):
                for u in range(size):
                    start = ((chip ^ s) * groups + (member ^ (batch * size + u))) * block
                    value = source[batch * chips + s][u * block : (u + 1) * block, :]
                    value_ref[half, pl.ds(pl.multiple_of(start, 16), block), :] = value.astype(F32)

    def send(half):
        out_ref = (first_ref, second_ref)[half]
        return pltpu.make_async_copy(value_ref.at[half, pl.ds(0, grad_rows)], out_ref, sems.at[half])

    def start_copy(half):
        pl.when(half == 0)(lambda: send(0).start())
        pl.when(half != 0)(lambda: send(1).start())

    fill(core, mine)
    start_copy(core)
    fill(1 - core, other)
    start_copy(1 - core)
    rows = width // 2
    extra = value_ref[0, grad_rows : grad_rows + rows, :]
    for side in range(2):
        head_ref[:, side * rows : (side + 1) * rows] = extra[:, side * LANES : (side + 1) * LANES].T[: head_ref.shape[0]]
    lane = iota(extra.shape, 1)
    loss = jnp.sum(jnp.where((lane == 64) | (lane == 65), extra, 0.0), keepdims=True)
    loss_ref[...] = loss / cell_total
    send(0).wait()
    send(1).wait()


def assemble(place, pieces, chips, groups, half_rows, grad_rows, classes, cell_total):
    width = pieces[0].shape[1]
    shape = jax.ShapeDtypeStruct
    return pl.pallas_call(
        functools.partial(assemble_kernel, width, chips, groups, cell_total),
        in_specs=[scalars(), *whole(len(pieces))],
        out_specs=[*hbm(2), *whole(2)],
        out_shape=[
            shape((grad_rows, width), F32),
            shape((grad_rows, width), F32),
            shape((classes, width), F32),
            shape((1, 1), F32),
        ],
        scratch_shapes=[pltpu.VMEM((2, half_rows, width), F32), pltpu.SemaphoreType.DMA((2,))],
        compiler_params=pltpu.CompilerParams(vmem_limit_bytes=48 << 20),
        cost_estimate=pl.CostEstimate(flops=1_000_000, bytes_accessed=7_500_000, transcendentals=0),
        name="assemble",
    )(place, *pieces)


def gradient_pieces(place, keep, give, groups, chips):
    got = [pairwise(one, "core", 1) for one in give]
    sums = [add(pair) for pair in zip(keep, got)]
    sums = [sums[0]] + [pairwise(sums[step], "chip", step) for step in range(1, chips)]
    rows = sums[0].shape[0] // groups

    def block(step):
        start = (place[MEMBER] ^ step) * rows
        return add([lax.dynamic_slice_in_dim(one, start, rows, axis=0) for one in sums])

    mine = add([block(0)] + [pairwise(block(step), "member", step) for step in range(1, groups)])
    gathered = [mine] + [pairwise(mine, "member", step) for step in range(1, groups)]
    batches = 2
    size = groups // batches
    held, other = [], []
    for batch in range(batches):
        one = jnp.concatenate(gathered[batch * size : (batch + 1) * size], axis=0)
        for step in range(chips):
            piece = one if step == 0 else pairwise(one, "chip", step)
            held.append(piece)
            other.append(pairwise(piece, "core", 1))
    return held + other


def body(teacher_logits, coverage, features, labels, first_weight, second_weight, head_weight):
    channels, classes = head_weight.shape
    members, tiles_here, flat_width = teacher_logits.shape
    pixels = flat_width // classes
    edge = math.isqrt(pixels)
    groups = lax.axis_size("member")
    chips = lax.axis_size("chip")
    columns = chips * 2
    tile_axes = ("chip", "core")
    block_tiles = tiles_here // groups
    capacity = max(2, 2 * block_tiles // columns)
    local = features[0]
    lines, width = local.shape[:2]
    cells = lines * width
    cell_total = groups * columns * cells
    column = lax.axis_index(tile_axes)
    place = jnp.stack(
        [
            lax.axis_index("core"),
            lax.axis_index("chip"),
            lax.axis_index("member"),
            lax.axis_index(("member", *tile_axes)),
            column == 0,
            column == columns - 1,
        ]
    ).astype(jnp.int32)
    flat = local.reshape(cells, channels)
    first_rows = first_weight.reshape(3, 3 * channels, channels)
    second_rows = second_weight.reshape(3, 3 * channels, channels)
    head = head_weight.T

    steps = list(range(groups - 1, -1, -1))
    early, late = steps[: groups // 2], steps[groups // 2 :]
    *far, top, bottom = teacher_moments(place, teacher_logits, block_tiles, classes, early, flat, 3 * width)
    got = [pairwise(one, "member", step) for step, one in zip(early, far)]
    before, after = neighbours(top, bottom, tile_axes)
    near = teacher_moments(place, teacher_logits, block_tiles, classes, late)
    got += [one if step == 0 else pairwise(one, "member", step) for step, one in zip(late, near)]
    one, two, logit, edge_rows = student_forward(
        place, before, after, head, near[-1], flat, first_rows, second_rows, width
    )
    cover = coverage.reshape(groups, 1, block_tiles)
    sent = combine(got, cover, place, edge_rows, classes, members, columns, capacity)
    received = exchange(sent.reshape(columns, capacity, -1), tile_axes).reshape(columns * capacity, -1)
    label_rows = (
        labels[0].reshape(lines // edge, edge, width // edge, edge).transpose(0, 2, 1, 3).reshape(block_tiles, pixels)
    )
    log, base, label_sum, wt, xt, ht, twot = turn(
        label_rows, sent, logit, second_rows, edge_rows, flat, one, two, width
    )
    grad_two, top, bottom, head_grad = head_step(
        received, head, label_sum, log, base, twot, two, 1.0 / math.sqrt(cell_total), width
    )
    grad_before, grad_after = neighbours(top, bottom, tile_axes)
    second = second_step(grad_two, ht, width)
    rows, extra_rows = 9 * channels, channels // 2
    devices = groups * columns
    half_rows = devices // 2 * -(-(rows + extra_rows) // (devices // 2 * 16)) * 16
    keep, give = first_step(
        place, grad_before, grad_after, grad_two, head_grad, second, wt, one, xt, width, half_rows, chips
    )
    pieces = gradient_pieces(place, keep, give, groups, chips)
    first_total, second_total, head_total, loss = assemble(
        place, pieces, chips, groups, half_rows, rows, classes, cell_total
    )
    kernel_shape = (3, 3, channels, channels)
    return (first_total.reshape(kernel_shape), second_total.reshape(kernel_shape), head_total.T, loss[0, 0])


def solution(mesh):
    groups, columns = mesh.shape["member"], mesh.shape["tile"]
    split = jax.sharding.Mesh(mesh.devices.reshape(groups, columns // 2, 2), ("member", "chip", "core"))
    tile = ("chip", "core")
    return jax.shard_map(
        body,
        mesh=split,
        in_specs=(
            P("member", tile, None),
            P(tile),
            P("member", tile, None, None),
            P("member", tile, None),
            P(),
            P(),
            P(),
        ),
        out_specs=(P(), P(), P(), P()),
        check_vma=False,
    )
```

```python
import functools
import math

import jax
import jax.numpy as jnp
from jax import lax
from jax.experimental import pallas as pl
from jax.experimental.pallas import tpu as pltpu
from jax.sharding import PartitionSpec as P

BF16 = jnp.bfloat16
F32 = jnp.float32
LANES = 128
MXU = 256


def whole(count):
    return [pl.BlockSpec(memory_space=pltpu.VMEM)] * count


def iota(shape, axis):
    return lax.broadcasted_iota(jnp.int32, shape, axis)


def dot(left, right):
    return jnp.dot(left, right, preferred_element_type=F32)


def split_lanes(value):
    high = value.astype(BF16).astype(F32)
    return jnp.where(iota(value.shape, 1) < 64, high, value - high).astype(BF16)


def join_lanes(value):
    return value + pltpu.roll(value, 64, 1)


def class_sums(value, classes):
    pick = (iota((MXU, LANES), 0) // classes == iota((MXU, LANES), 1) % (MXU // classes)).astype(BF16)
    high = value.astype(BF16)
    low = (value - high.astype(F32)).astype(BF16)
    return dot(high, pick) + dot(low, pick)


def hbm(count):
    return [pl.BlockSpec(memory_space=pl.ANY)] * count


def scalars():
    return pl.BlockSpec(memory_space=pltpu.SMEM)


CORE, CHIP, MEMBER, DEVICE, FIRST, LAST = range(6)


def teacher_kernel(classes, edges, place_ref, x_ref, *refs):
    flat_ref, refs = (refs[0], refs[1:]) if edges else (None, refs)
    out_refs, refs = refs[:2], refs[2:]
    if edges:
        top_ref, bottom_ref, *refs = refs
    sum_ref, acc_ref, *sems = refs
    step = pl.program_id(0)
    last = pl.num_programs(0) - 1
    members, tiles, width = x_ref.shape
    per = MXU // classes
    same = (iota((MXU, MXU), 0) // classes == iota((MXU, MXU), 1) // classes).astype(BF16)
    copies = []
    if edges:
        rows = top_ref.shape[0]
        copies = [
            pltpu.make_async_copy(flat_ref.at[pl.ds(0, rows)], top_ref, sems[0].at[0]),
            pltpu.make_async_copy(flat_ref.at[pl.ds(flat_ref.shape[0] - rows, rows)], bottom_ref, sems[0].at[1]),
        ]

    @pl.when(step == 0)
    def _():
        acc_ref[...] = jnp.zeros_like(acc_ref)
        for copy in copies:
            copy.start()

    for part in range(width // MXU):
        where = step * (width // MXU) + part
        x = x_ref[:, :, part * MXU : (part + 1) * MXU].astype(F32).reshape(members * tiles, MXU)
        root = jnp.exp(x * 0.25)
        root = root * pl.reciprocal(dot(root.astype(BF16), same), approx=True)
        square = root * root
        power = square * square
        total = dot(power.astype(BF16), same)
        inverse = pl.reciprocal(total, approx=True)
        inverse = inverse * (2.0 - total * inverse)
        probs = (power * inverse).reshape(members, tiles, MXU)
        first = probs[0]
        within = probs[0] * probs[0]
        for member in range(1, members):
            first = first + probs[member]
            within = within + probs[member] * probs[member]
        within = within - first * first * (1.0 / members)
        sum_ref[:, pl.ds(pl.multiple_of(where * MXU, MXU), MXU)] = first.astype(BF16)
        sums = class_sums(within, classes)
        hit = iota(sums.shape, 1) % 64 // per == where
        acc_ref[...] = jnp.where(hit, sums, acc_ref[...])

    @pl.when(step == last)
    def _():
        sum_ref[:, sum_ref.shape[1] - LANES :] = split_lanes(acc_ref[...])
        half = tiles // 2
        odd = 1 - place_ref[MEMBER] % 2
        for index, out_ref in enumerate(out_refs):
            low = (odd if index == 0 else 1 - odd) * half
            out_ref[...] = sum_ref[pl.ds(pl.multiple_of(low, 16), half), :]
        for copy in copies:
            copy.wait()


def teacher_moments(place, logits, tiles, classes, flip, flat=None, edge_rows=0):
    members, _, width = logits.shape
    block = width // 4
    edges = flat is not None
    shape = jax.ShapeDtypeStruct
    extra = [shape((edge_rows, flat.shape[1]), BF16)] * 2 if edges else []
    return pl.pallas_call(
        functools.partial(teacher_kernel, classes, edges),
        grid_spec=pltpu.PrefetchScalarGridSpec(
            num_scalar_prefetch=1,
            grid=(width // block,),
            in_specs=[pl.BlockSpec((members, 2 * tiles, block), lambda i, at: (0, (at[MEMBER] // 2) ^ flip, i))]
            + hbm(1 if edges else 0),
            out_specs=[pl.BlockSpec((tiles, width + LANES), lambda i, at: (0, 0))] * 2 + hbm(len(extra)),
            scratch_shapes=[pltpu.VMEM((2 * tiles, width + LANES), BF16), pltpu.VMEM((2 * tiles, LANES), F32)]
            + ([pltpu.SemaphoreType.DMA((2,))] if edges else []),
        ),
        out_shape=[shape((tiles, width + LANES), BF16)] * 2 + extra,
        compiler_params=pltpu.CompilerParams(vmem_limit_bytes=58 << 20),
        cost_estimate=pl.CostEstimate(flops=1_500_000_000, bytes_accessed=2_600_000, transcendentals=3_000_000),
        name="teacher_moments",
    )(place, logits, *([flat] if edges else []))


def combine_kernel(classes, members, columns, capacity, where_ref, cover_ref, after_ref, *refs):
    got_refs, out_refs = refs[:-columns], refs[-columns:]
    groups = len(got_refs)
    tiles, extended = got_refs[0].shape
    width = extended - LANES
    means, gaps = [], []
    for start in range(0, width, MXU):
        sums = [got_ref[:, start : start + MXU].astype(F32) for got_ref in got_refs]
        total = sums[0]
        for one in sums[1:]:
            total = total + one
        mean = total * (1.0 / (members * groups))
        means.append(mean.astype(BF16))
        gap = jnp.zeros_like(mean)
        for one in sums:
            off = one * (1.0 / members) - mean
            gap = gap + off * off
        gaps.append(gap)
    between = class_sums(jnp.concatenate(gaps, axis=0), classes)
    lane = iota((tiles, LANES), 1)
    spread = jnp.zeros((tiles, LANES), F32)
    per = MXU // classes
    for i in range(width // MXU):
        spread = jnp.where(lane % 64 // per == i, between[i * tiles : (i + 1) * tiles], spread)
    inner = got_refs[0][:, width:].astype(F32)
    for got_ref in got_refs[1:]:
        inner = inner + got_ref[:, width:].astype(F32)
    spread = spread * (1.0 / groups) + join_lanes(inner) * (1.0 / (members * groups))
    index = (iota((tiles, LANES), 0) + 1).astype(F32).astype(BF16)
    rows = jnp.concatenate([*means, split_lanes(spread), index], axis=1)
    target = cover_ref[where_ref[MEMBER]] ^ (where_ref[CHIP] * 2 + where_ref[CORE])
    onehot = (iota((columns, tiles), 0) == target).astype(F32)
    earlier = (iota((tiles, tiles), 0) < iota((tiles, tiles), 1)).astype(BF16)
    before = dot(onehot.astype(BF16), earlier)
    rank = jnp.sum(before * onehot, axis=0, keepdims=True).astype(jnp.int32)
    place = (iota((columns * capacity, tiles), 0) == target * capacity + rank).astype(BF16)
    sent = dot(place, rows)
    for index, out_ref in enumerate(out_refs):
        out_ref[...] = sent[index * capacity : (index + 1) * capacity].astype(BF16)


def combine(got, cover, where, after, classes, members, columns, capacity):
    extended = got[0].shape[1]
    return pl.pallas_call(
        functools.partial(combine_kernel, classes, members, columns, capacity),
        in_specs=[pl.BlockSpec(memory_space=pltpu.SMEM), *whole(1), pl.BlockSpec(memory_space=pl.ANY), *whole(len(got))],
        out_specs=whole(columns),
        out_shape=[jax.ShapeDtypeStruct((capacity, extended + LANES), BF16)] * columns,
        compiler_params=pltpu.CompilerParams(vmem_limit_bytes=12 << 20),
        cost_estimate=pl.CostEstimate(flops=100_000_000, bytes_accessed=1_700_000, transcendentals=0),
        name="combine",
    )(where, cover, after, *got)


def put_shifted(ref, start, value, shift, width):
    rows, channels = value.shape
    col = iota(value.shape, 0) % width
    left = jnp.where(col >= shift, pltpu.roll(value, shift, 0), 0.0)
    right = jnp.where(col < width - shift, pltpu.roll(value, rows - shift, 0), 0.0)
    ref[pl.ds(start, rows), :channels] = left.astype(BF16)
    ref[pl.ds(start, rows), channels : 2 * channels] = value.astype(BF16)
    ref[pl.ds(start, rows), 2 * channels :] = right.astype(BF16)


def three_dots(ref, start, step, rows, weight_ref):
    total = None
    for tap in range(3):
        part = dot(ref[pl.ds(start + tap * step, rows), :], weight_ref[tap])
        total = part if total is None else total + part
    return total


def turned_dot(left, right):
    return lax.dot_general(left, right, (((1,), (1,)), ((), ())), preferred_element_type=F32)


def turned_dot(left, right):
    return lax.dot_general(left, right, (((1,), (1,)), ((), ())), preferred_element_type=F32)


def student_kernel(
    width, place_ref, before_ref, after_ref, head_ref, label_ref, payload_ref, x_hbm, first_hbm, second_hbm,
    one_ref, two_ref, log_ref, base_ref, label_sum_ref, x_ref, first_ref, second_ref, xcat, hcat, logit_ref, sems,
):
    cells, channels = x_ref.shape
    halo = before_ref.shape[0]
    block = 4 * width
    arrive = [
        pltpu.make_async_copy(source, target, sems.at[i])
        for i, (source, target) in enumerate(((x_hbm, x_ref), (first_hbm, first_ref), (second_hbm, second_ref)))
    ]
    for copy in arrive:
        copy.start()

    @pl.loop(0, halo // width)
    def _(i):
        start = pl.multiple_of(i * width, width)
        put_shifted(xcat, start, before_ref[pl.ds(start, width)].astype(F32), 1, width)
        low = pl.multiple_of(halo + cells + start, width)
        put_shifted(xcat, low, after_ref[pl.ds(start, width)].astype(F32), 1, width)

    arrive[0].wait()

    @pl.loop(0, cells // block)
    def _(i):
        start = pl.multiple_of(i * block, block)
        low = pl.multiple_of(halo + start, width)
        put_shifted(xcat, low, x_ref[pl.ds(start, block)].astype(F32), 1, width)

    arrive[1].wait()
    lines = cells // width

    @pl.loop(0, (cells + block) // block)
    def _(i):
        start = pl.multiple_of(i * block, block)
        value = three_dots(xcat, start, width, block, first_ref)
        line = i * 4 + iota(value.shape, 0) // width
        low = jnp.where(place_ref[FIRST] == 1, 2, 0)
        high = jnp.where(place_ref[LAST] == 1, lines + 2, lines + 4)
        value = jnp.where((line >= low) & (line < high) & (value > 0), value, 0.0)
        put_shifted(hcat, start, value, 2, width)
        one_ref[pl.ds(start, block), :] = value.astype(BF16)

    arrive[2].wait()
    head = jnp.concatenate([head_ref[...], head_ref[...]], axis=0)

    @pl.loop(0, cells // block)
    def _(i):
        start = pl.multiple_of(i * block, block)
        value = three_dots(hcat, start, 2 * width, block, second_ref)
        value = jnp.where(value > 0, value, 0.0)
        two = value.astype(BF16)
        two_ref[pl.ds(start, block), :] = two
        logit_ref[pl.ds(start, block), :] = turned_dot(two, head)

    tiles, pixels = label_ref.shape
    edge = math.isqrt(pixels)
    across = width // edge
    lane = iota((tiles, LANES), 1)
    even = lane < 64
    label_sum = jnp.zeros((tiles, LANES), F32)
    for pair in range(pixels // 2):
        row, col = 2 * pair // edge, 2 * pair % edge
        parts = []
        for down in range(tiles // across):
            start = (down * edge + row) * width + col
            left = logit_ref[pl.ds(start, across, stride=edge), :]
            right = logit_ref[pl.ds(start + 1, across, stride=edge), :]
            parts.append(jnp.where(iota(left.shape, 1) < 64, left, right))
        value = jnp.concatenate(parts, axis=0)
        top = jnp.where(
            even,
            jnp.max(jnp.where(even, value, -jnp.inf), axis=1, keepdims=True),
            jnp.max(jnp.where(even, -jnp.inf, value), axis=1, keepdims=True),
        )
        value = value - top
        power = jnp.exp(value)
        total = jnp.where(
            even,
            jnp.sum(jnp.where(even, power, 0.0), axis=1, keepdims=True),
            jnp.sum(jnp.where(even, 0.0, power), axis=1, keepdims=True),
        )
        value = value - jnp.log(total)
        label = jnp.where(even, label_ref[:, 2 * pair : 2 * pair + 1], label_ref[:, 2 * pair + 1 : 2 * pair + 2])
        hit = label == lane % 64
        label_sum = label_sum + jnp.where(hit, value, 0.0)
        log_ref[pair * tiles : (pair + 1) * tiles, :] = value
        base_ref[pair * tiles : (pair + 1) * tiles, :] = jnp.exp(value) - hit.astype(F32)
    label_sum_ref[...] = label_sum


def student_forward(place, before, after, head, labels, payload, x, first, second, width):
    cells, channels = x.shape
    halo = before.shape[0]
    tiles, pixels = labels.shape
    shape = jax.ShapeDtypeStruct
    return pl.pallas_call(
        functools.partial(student_kernel, width),
        in_specs=[scalars(), *whole(4), *hbm(4)],
        out_specs=whole(5),
        out_shape=[
            shape((cells + 4 * width, channels), BF16),
            shape((cells, channels), BF16),
            shape((cells // 2, LANES), F32),
            shape((cells // 2, LANES), F32),
            shape((tiles, LANES), F32),
        ],
        scratch_shapes=[
            pltpu.VMEM((cells, channels), BF16),
            pltpu.VMEM(first.shape, BF16),
            pltpu.VMEM(second.shape, BF16),
            pltpu.VMEM((cells + 2 * halo, 3 * channels), BF16),
            pltpu.VMEM((cells + 4 * width, 3 * channels), BF16),
            pltpu.VMEM((cells, LANES), F32),
            pltpu.SemaphoreType.DMA((3,)),
        ],
        compiler_params=pltpu.CompilerParams(vmem_limit_bytes=56 << 20),
        cost_estimate=pl.CostEstimate(flops=6_000_000_000, bytes_accessed=12_000_000, transcendentals=500_000),
        name="student_forward",
    )(place, before, after, head, labels, payload, x, first, second)


def put_turned(ref, start, value, shift, width):
    rows, channels = value.shape
    col = iota(value.shape, 0) % width
    left = jnp.where(col >= shift, pltpu.roll(value, shift, 0), 0.0)
    right = jnp.where(col < width - shift, pltpu.roll(value, rows - shift, 0), 0.0)
    for tap, one in enumerate((left, value, right)):
        ref[tap * channels : (tap + 1) * channels, pl.ds(start, rows)] = one.T.astype(BF16)


def turn_kernel(
    width, before_ref, x_ref, after_ref, one_ref, two_ref, second_ref, sent_ref, xt_ref, ht_ref, twot_ref, wt_ref
):
    cells, channels = x_ref.shape
    halo = before_ref.shape[0]
    pair = 2 * width
    first = jnp.concatenate([before_ref[halo - width :], x_ref[:width]], axis=0).astype(F32)
    put_turned(xt_ref, 0, first, 1, width)
    last = jnp.concatenate([x_ref[cells - width :], after_ref[:width]], axis=0).astype(F32)
    put_turned(xt_ref, cells, last, 1, width)

    @pl.loop(1, cells // pair)
    def _(i):
        start = pl.multiple_of(i * pair, pair)
        put_turned(xt_ref, start, x_ref[pl.ds(pl.multiple_of(start - width, width), pair)].astype(F32), 1, width)

    @pl.loop(0, one_ref.shape[0] // pair)
    def _(i):
        start = pl.multiple_of(i * pair, pair)
        put_turned(ht_ref, start, one_ref[pl.ds(start, pair)].astype(F32), 2, width)

    @pl.loop(0, cells // MXU)
    def _(i):
        start = pl.multiple_of(i * MXU, MXU)
        twot_ref[:, pl.ds(start, MXU)] = two_ref[pl.ds(start, MXU)].astype(F32).T.astype(BF16)

    @pl.loop(0, 3)
    def _(i):
        for tap in range(3):
            part = slice(tap * channels, (tap + 1) * channels)
            mirror = slice((2 - tap) * channels, (3 - tap) * channels)
            wt_ref[i, part, :] = second_ref[i, mirror, :].astype(F32).T.astype(BF16)


def turn(before, x, after, one, two, second, sent, width):
    cells, channels = x.shape
    shape = jax.ShapeDtypeStruct
    return pl.pallas_call(
        functools.partial(turn_kernel, width),
        in_specs=[*whole(6), pl.BlockSpec(memory_space=pl.ANY)],
        out_specs=whole(4),
        out_shape=[
            shape((3 * channels, cells + 2 * width), BF16),
            shape((3 * channels, cells + 4 * width), BF16),
            shape((channels, cells), BF16),
            shape((3, 3 * channels, channels), BF16),
        ],
        compiler_params=pltpu.CompilerParams(vmem_limit_bytes=20 << 20),
        cost_estimate=pl.CostEstimate(flops=3_000_000_000, bytes_accessed=14_000_000, transcendentals=0),
        name="turn",
    )(before, x, after, one, two, second, sent)


def head_kernel(
    scale, width, log_ref, base_ref, label_sum_ref, two_ref, twot_ref, head_ref, *refs
):
    *got_refs, grad_ref, top_ref, bottom_ref, head_grad_ref, got_ref, natural = refs
    slots, extended = got_ref.shape
    got_ref[...] = jnp.concatenate([one[...].astype(F32) for one in got_refs], axis=0).astype(BF16)
    tiles = label_sum_ref.shape[0]
    flat = extended - 2 * LANES
    pixels = flat // 64
    edge = math.isqrt(pixels)
    across = width // edge
    index = got_ref[:, flat + LANES :].astype(F32)
    take = (index == (iota((slots, LANES), 1) + 1).astype(F32)).astype(F32).T[:tiles].astype(BF16)
    spread = join_lanes(dot(take, got_ref[:, flat : flat + LANES]))
    weight = 1.0 / (0.1 + spread)
    even = iota((tiles, LANES), 1) < 64
    loss = -label_sum_ref[...]
    for pair in range(pixels // 2):
        rows = slice(pair * tiles, (pair + 1) * tiles)
        if pair % 2 == 0:
            both = dot(take, got_ref[:, pair * LANES : (pair + 2) * LANES])
        mean = both[:, pair % 2 * LANES : (pair % 2 + 1) * LANES]
        cell = jnp.where(even, weight[:, 2 * pair : 2 * pair + 1], weight[:, 2 * pair + 1 : 2 * pair + 2])
        value = log_ref[rows, :]
        held = mean > 0
        loss = loss + cell * jnp.where(held, mean * (jnp.log(jnp.where(held, mean, 1.0)) - value), 0.0)
        grad = (cell * (jnp.exp(value) - mean) + base_ref[rows, :]) * scale
        turned = pltpu.roll(grad, 64, 1)
        row, col = 2 * pair // edge, 2 * pair % edge
        for down in range(tiles // across):
            start = (down * edge + row) * width + col
            natural[pl.ds(start, across, stride=edge), :] = grad[down * across : (down + 1) * across]
            natural[pl.ds(start + 1, across, stride=edge), :] = turned[down * across : (down + 1) * across]
    cells, channels = two_ref.shape
    logit_grad = natural[...].astype(BF16)
    head = jnp.concatenate([head_ref[...], jnp.zeros_like(head_ref)], axis=0)
    head_grad_ref[:channels, :] = dot(twot_ref[...], logit_grad)
    head_grad_ref[channels:, :] = loss
    block = 4 * width
    for start in range(0, cells, block):
        rows = slice(start, start + block)
        grad = dot(logit_grad[rows], head)
        grad_ref[rows, :] = jnp.where(two_ref[rows, :].astype(F32) > 0, grad, 0.0).astype(BF16)
    top_ref[...] = grad_ref[: 2 * width, :]
    bottom_ref[...] = grad_ref[cells - 2 * width :, :]


def head_step(got, log, base, label_sum, two, twot, head, scale, width):
    cells, channels = two.shape
    shape = jax.ShapeDtypeStruct
    return pl.pallas_call(
        functools.partial(head_kernel, scale, width),
        in_specs=whole(6 + len(got)),
        out_specs=whole(4),
        out_shape=[
            shape((cells, channels), BF16),
            shape((2 * width, channels), BF16),
            shape((2 * width, channels), BF16),
            shape((channels + label_sum.shape[0], LANES), F32),
        ],
        scratch_shapes=[
            pltpu.VMEM((len(got) * got[0].shape[0], got[0].shape[1]), BF16),
            pltpu.VMEM((cells, LANES), F32),
        ],
        compiler_params=pltpu.CompilerParams(vmem_limit_bytes=14 << 20),
        cost_estimate=pl.CostEstimate(flops=400_000_000, bytes_accessed=5_000_000, transcendentals=500_000),
        name="head_step",
    )(log, base, label_sum, two, twot, head, *got)


def second_kernel(width, ht_ref, grad_ref, out_ref):
    cells, channels = grad_ref.shape
    for tap in range(3):
        part = dot(ht_ref[:, 2 * width * tap : 2 * width * tap + cells], grad_ref[...])
        out_ref[tap * 3 * channels : (tap + 1) * 3 * channels, :] = part.astype(BF16)


def second_step(ht, grad, width):
    channels = grad.shape[1]
    return pl.pallas_call(
        functools.partial(second_kernel, width),
        in_specs=whole(2),
        out_specs=pl.BlockSpec(memory_space=pltpu.VMEM),
        out_shape=jax.ShapeDtypeStruct((9 * channels, channels), BF16),
        compiler_params=pltpu.CompilerParams(vmem_limit_bytes=14 << 20),
        cost_estimate=pl.CostEstimate(flops=2_500_000_000, bytes_accessed=7_000_000, transcendentals=0),
        name="second_step",
    )(ht, grad)


def first_kernel(width, chips, place_ref, before_ref, after_ref, grad_ref, head_grad_ref, second_ref, *refs):
    wt_ref, one_ref, xt_ref, *refs = refs
    keep_refs, give_refs, refs = refs[:chips], refs[chips : 2 * chips], refs[2 * chips :]
    gcat, padded, halves, sem = refs
    cells, channels = grad_ref.shape
    rows = 9 * channels
    used = rows + channels // 2
    half = halves.shape[1]
    second_copy = pltpu.make_async_copy(second_ref, halves.at[1, pl.ds(0, rows)], sem)
    second_copy.start()
    halo = before_ref.shape[0]
    block = 4 * width
    put_shifted(gcat, 0, before_ref[...].astype(F32), 2, width)
    put_shifted(gcat, halo + cells, after_ref[...].astype(F32), 2, width)
    for start in range(0, cells, block):
        put_shifted(gcat, halo + start, grad_ref[start : start + block, :].astype(F32), 2, width)
    padded[: 2 * width, :] = jnp.zeros((2 * width, channels), BF16)
    padded[2 * width + cells :, :] = jnp.zeros((2 * width, channels), BF16)
    for start in range(0, cells, block):
        value = None
        for tap in range(3):
            low = start + (2 - tap) * 2 * width
            part = dot(gcat[low : low + block, :], wt_ref[tap])
            value = part if value is None else value + part
        held = one_ref[2 * width + start : 2 * width + start + block, :].astype(F32) > 0
        padded[2 * width + start : 2 * width + start + block, :] = jnp.where(held, value, 0.0).astype(BF16)
    span = cells + 2 * width
    for tap in range(3):
        part = dot(xt_ref[...], padded[(2 - tap) * width : (2 - tap) * width + span, :])
        halves[0, tap * 3 * channels : (tap + 1) * 3 * channels, :] = part.astype(BF16)
    lane = iota((channels // 2, LANES), 1)
    loss = jnp.sum(head_grad_ref[channels:, :])
    high = loss.astype(BF16).astype(F32)
    extra = jnp.where(lane == 64, high, jnp.where(lane == 65, loss - high, 0.0))
    extra = jnp.where(iota(lane.shape, 0) == place_ref[DEVICE] % (channels // 2), extra, 0.0)
    for side in range(2):
        value = jnp.where(lane < 64, head_grad_ref[side * channels // 2 : (side + 1) * channels // 2, :], extra)
        halves[0, rows:used, side * LANES : (side + 1) * LANES] = value.astype(BF16)
    halves[0, used:, :] = jnp.zeros((half - used, channels), BF16)
    halves[1, rows:, :] = jnp.zeros((half - rows, channels), BF16)
    second_copy.wait()
    core, chip = place_ref[CORE], place_ref[CHIP]
    size = half // chips
    for step in range(chips):
        low = pl.multiple_of((chip ^ step) * size, 16)
        give_refs[step][...] = halves[1 - core, pl.ds(low, size), :]
        keep_refs[step][...] = halves[core, pl.ds(low, size), :]


def first_step(place, before, after, grad, head_grad, second, wt, one, xt, width, half_rows, chips):
    cells, channels = grad.shape
    halo = before.shape[0]
    piece = jax.ShapeDtypeStruct((half_rows // chips, channels), BF16)
    outs = pl.pallas_call(
        functools.partial(first_kernel, width, chips),
        in_specs=[scalars(), *whole(8)],
        out_specs=whole(2 * chips),
        out_shape=[piece] * (2 * chips),
        scratch_shapes=[
            pltpu.VMEM((cells + 2 * halo, 3 * channels), BF16),
            pltpu.VMEM((cells + 4 * width, channels), BF16),
            pltpu.VMEM((2, half_rows, channels), BF16),
            pltpu.SemaphoreType.DMA,
        ],
        compiler_params=pltpu.CompilerParams(vmem_limit_bytes=24 << 20),
        cost_estimate=pl.CostEstimate(flops=5_000_000_000, bytes_accessed=10_000_000, transcendentals=0),
        name="first_step",
    )(place, before, after, grad, head_grad, second, wt, one, xt)
    return (outs[:chips], outs[chips:])


def neighbours(first, last, axis):
    count = lax.axis_size(axis)
    up = [(i, i + 1) for i in range(count - 1)]
    down = [(i + 1, i) for i in range(count - 1)]
    return (lax.ppermute(last, axis, up), lax.ppermute(first, axis, down))


def pairwise(array, axis, step):
    count = lax.axis_size(axis)
    return lax.ppermute(array, axis, [(i, i ^ step) for i in range(count)])


def add(arrays):
    return functools.reduce(jnp.add, [array.astype(F32) for array in arrays]).astype(BF16)


def assemble_kernel(
    width, chips, groups, cell_total, place_ref, *refs
):
    parts = len(refs) - 6
    pieces, refs = refs[:parts], refs[parts:]
    first_ref, second_ref, head_ref, loss_ref, value_ref, sems = refs
    mine, other = pieces[: parts // 2], pieces[parts // 2 :]
    batches = len(mine) // chips
    size = groups // batches
    block = mine[0].shape[0] // size
    grad_rows = first_ref.shape[0]
    core, chip, member = place_ref[CORE], place_ref[CHIP], place_ref[MEMBER]

    def fill(half, source):
        for batch in range(batches):
            for s in range(chips):
                for u in range(size):
                    start = ((chip ^ s) * groups + (member ^ (batch * size + u))) * block
                    value = source[batch * chips + s][u * block : (u + 1) * block, :]
                    value_ref[half, pl.ds(pl.multiple_of(start, 16), block), :] = value.astype(F32)

    def send(half):
        out_ref = (first_ref, second_ref)[half]
        return pltpu.make_async_copy(value_ref.at[half, pl.ds(0, grad_rows)], out_ref, sems.at[half])

    def start_copy(half):
        pl.when(half == 0)(lambda: send(0).start())
        pl.when(half != 0)(lambda: send(1).start())

    fill(core, mine)
    start_copy(core)
    fill(1 - core, other)
    start_copy(1 - core)
    rows = width // 2
    extra = value_ref[0, grad_rows : grad_rows + rows, :]
    for side in range(2):
        head_ref[:, side * rows : (side + 1) * rows] = extra[:, side * LANES : (side + 1) * LANES].T[: head_ref.shape[0]]
    lane = iota(extra.shape, 1)
    loss = jnp.sum(jnp.where((lane == 64) | (lane == 65), extra, 0.0), keepdims=True)
    loss_ref[...] = loss / cell_total
    send(0).wait()
    send(1).wait()


def assemble(place, pieces, chips, groups, half_rows, grad_rows, classes, cell_total):
    width = pieces[0].shape[1]
    shape = jax.ShapeDtypeStruct
    return pl.pallas_call(
        functools.partial(assemble_kernel, width, chips, groups, cell_total),
        in_specs=[scalars(), *whole(len(pieces))],
        out_specs=[*hbm(2), *whole(2)],
        out_shape=[
            shape((grad_rows, width), F32),
            shape((grad_rows, width), F32),
            shape((classes, width), F32),
            shape((1, 1), F32),
        ],
        scratch_shapes=[pltpu.VMEM((2, half_rows, width), F32), pltpu.SemaphoreType.DMA((2,))],
        compiler_params=pltpu.CompilerParams(vmem_limit_bytes=48 << 20),
        cost_estimate=pl.CostEstimate(flops=1_000_000, bytes_accessed=7_500_000, transcendentals=0),
        name="assemble",
    )(place, *pieces)


def gradient_pieces(place, keep, give, groups, chips):
    got = [pairwise(one, "core", 1) for one in give]
    sums = [add(pair) for pair in zip(keep, got)]
    sums = [sums[0]] + [pairwise(sums[step], "chip", step) for step in range(1, chips)]
    rows = sums[0].shape[0] // groups

    def block(step):
        start = (place[MEMBER] ^ step) * rows
        return add([lax.dynamic_slice_in_dim(one, start, rows, axis=0) for one in sums])

    mine = add([block(0)] + [pairwise(block(step), "member", step) for step in range(1, groups)])
    gathered = [mine] + [pairwise(mine, "member", step) for step in range(1, groups)]
    one = jnp.concatenate(gathered, axis=0)
    held = [one] + [pairwise(one, "chip", step) for step in range(1, chips)]
    return held + [pairwise(piece, "core", 1) for piece in held]


def body(teacher_logits, coverage, features, labels, first_weight, second_weight, head_weight):
    channels, classes = head_weight.shape
    members, tiles_here, flat_width = teacher_logits.shape
    pixels = flat_width // classes
    edge = math.isqrt(pixels)
    groups = lax.axis_size("member")
    chips = lax.axis_size("chip")
    columns = chips * 2
    tile_axes = ("chip", "core")
    block_tiles = tiles_here // groups
    capacity = max(2, 2 * block_tiles // columns)
    local = features[0]
    lines, width = local.shape[:2]
    cells = lines * width
    cell_total = groups * columns * cells
    column = lax.axis_index(tile_axes)
    place = jnp.stack(
        [
            lax.axis_index("core"),
            lax.axis_index("chip"),
            lax.axis_index("member"),
            lax.axis_index(("member", *tile_axes)),
            column == 0,
            column == columns - 1,
        ]
    ).astype(jnp.int32)
    flat = local.reshape(cells, channels)
    first_rows = first_weight.reshape(3, 3 * channels, channels)
    second_rows = second_weight.reshape(3, 3 * channels, channels)
    head = head_weight.T

    far = teacher_moments(place, teacher_logits, block_tiles, classes, 1)
    got = [pairwise(one, "member", step) for step, one in zip((3, 2), far)]
    near, own, top, bottom = teacher_moments(place, teacher_logits, block_tiles, classes, 0, flat, 3 * width)
    got += [pairwise(near, "member", 1), own]
    before, after = neighbours(top, bottom, tile_axes)
    label_rows = (
        labels[0].reshape(lines // edge, edge, width // edge, edge).transpose(0, 2, 1, 3).reshape(block_tiles, pixels)
    )
    one, two, log, base, label_sum = student_forward(
        place, before, after, head, label_rows, own, flat, first_rows, second_rows, width
    )
    cover = coverage.reshape(groups, 1, block_tiles)
    sent = combine(got, cover, place, label_sum, classes, members, columns, capacity)
    received = [sent[0]] + [pairwise(sent[step], tile_axes, step) for step in range(1, columns)]
    xt, ht, twot, wt = turn(before, flat, after, one, two, second_rows, sent[0], width)
    grad_two, top, bottom, head_grad = head_step(
        received, log, base, label_sum, two, twot, head, 1.0 / math.sqrt(cell_total), width
    )
    grad_before, grad_after = neighbours(top, bottom, tile_axes)
    second = second_step(ht, grad_two, width)
    rows, extra_rows = 9 * channels, channels // 2
    devices = groups * columns
    half_rows = devices // 2 * -(-(rows + extra_rows) // (devices // 2 * 16)) * 16
    keep, give = first_step(
        place, grad_before, grad_after, grad_two, head_grad, second, wt, one, xt, width, half_rows, chips
    )
    pieces = gradient_pieces(place, keep, give, groups, chips)
    first_total, second_total, head_total, loss = assemble(
        place, pieces, chips, groups, half_rows, rows, classes, cell_total
    )
    kernel_shape = (3, 3, channels, channels)
    return (first_total.reshape(kernel_shape), second_total.reshape(kernel_shape), head_total.T, loss[0, 0])


def solution(mesh):
    groups, columns = mesh.shape["member"], mesh.shape["tile"]
    split = jax.sharding.Mesh(mesh.devices.reshape(groups, columns // 2, 2), ("member", "chip", "core"))
    tile = ("chip", "core")
    return jax.shard_map(
        body,
        mesh=split,
        in_specs=(
            P("member", tile, None),
            P(tile),
            P("member", tile, None, None),
            P("member", tile, None),
            P(),
            P(),
            P(),
        ),
        out_specs=(P(), P(), P(), P()),
        check_vma=False,
    )
```

```python
import functools
import math

import jax
import jax.numpy as jnp
from jax import lax
from jax.experimental import pallas as pl
from jax.experimental.pallas import tpu as pltpu
from jax.sharding import PartitionSpec as P

BF16 = jnp.bfloat16
F32 = jnp.float32
LANES = 128
MXU = 256


def whole(count):
    return [pl.BlockSpec(memory_space=pltpu.VMEM)] * count


def iota(shape, axis):
    return lax.broadcasted_iota(jnp.int32, shape, axis)


def dot(left, right):
    return jnp.dot(left, right, preferred_element_type=F32)


def split_lanes(value):
    high = value.astype(BF16).astype(F32)
    return jnp.where(iota(value.shape, 1) < 64, high, value - high).astype(BF16)


def join_lanes(value):
    return value + pltpu.roll(value, 64, 1)


def class_sums(value, classes):
    pick = (iota((MXU, LANES), 0) // classes == iota((MXU, LANES), 1) % (MXU // classes)).astype(BF16)
    high = value.astype(BF16)
    low = (value - high.astype(F32)).astype(BF16)
    return dot(high, pick) + dot(low, pick)


def hbm(count):
    return [pl.BlockSpec(memory_space=pl.ANY)] * count


def scalars():
    return pl.BlockSpec(memory_space=pltpu.SMEM)


CORE, CHIP, MEMBER, DEVICE, FIRST, LAST = range(6)


def teacher_kernel(classes, groups, place_ref, logit_hbm, *refs):
    fetched, refs = refs[:3], refs[3:]
    out_refs, refs = refs[:groups], refs[groups:]
    top_ref, bottom_ref, *refs = refs
    held, (x_ref, sum_ref, acc_ref, sems, held_sems) = refs[:3], refs[3:]
    quarters, members, tiles, width = x_ref.shape
    parts = width // MXU
    per = MXU // classes
    arrive = [
        pltpu.make_async_copy(logit_hbm.at[:, :, pl.ds(i * width, width)], x_ref.at[i], sems.at[i])
        for i in range(quarters)
    ]
    later = [pltpu.make_async_copy(a, b, held_sems.at[i]) for i, (a, b) in enumerate(zip(fetched, held))]
    for copy in arrive + later:
        copy.start()
    same = (iota((MXU, MXU), 0) // classes == iota((MXU, MXU), 1) // classes).astype(BF16)
    acc_ref[...] = jnp.zeros_like(acc_ref)

    @pl.loop(0, quarters)
    def _(i):
        pltpu.make_async_copy(logit_hbm.at[:, :, pl.ds(0, width)], x_ref.at[i], sems.at[i]).wait()
        each = range(parts)
        x = [x_ref[i, :, :, n * MXU : (n + 1) * MXU].astype(F32).reshape(members * tiles, MXU) for n in each]
        root = [jnp.exp(one * 0.25) for one in x]
        total = [dot(one.astype(BF16), same) for one in root]
        root = [one * pl.reciprocal(whole_sum, approx=True) for one, whole_sum in zip(root, total)]
        square = [one * one for one in root]
        power = [one * one for one in square]
        total = [dot(one.astype(BF16), same) for one in power]
        inverse = [pl.reciprocal(one, approx=True) for one in total]
        inverse = [one * (2.0 - whole_sum * one) for one, whole_sum in zip(inverse, total)]
        probs = [(one * other).reshape(members, tiles, MXU) for one, other in zip(power, inverse)]
        first = [functools.reduce(jnp.add, [one[m] for m in range(members)]) for one in probs]
        within = [
            functools.reduce(jnp.add, [one[m] * one[m] for m in range(members)]) - sums * sums * (1.0 / members)
            for one, sums in zip(probs, first)
        ]
        sums = [class_sums(one, classes) for one in within]
        acc = acc_ref[...]
        for n in each:
            acc = jnp.where(iota(acc.shape, 1) % 64 // per == i * parts + n, sums[n], acc)
        acc_ref[...] = acc
        for n in each:
            sum_ref[:, pl.ds(pl.multiple_of(i * width + n * MXU, MXU), MXU)] = first[n].astype(BF16)

    sum_ref[:, quarters * width :] = split_lanes(acc_ref[...])
    block = tiles // groups
    for step in range(groups):
        low = pl.multiple_of((place_ref[MEMBER] ^ step) * block, 16)
        out_refs[step][...] = sum_ref[pl.ds(low, block), :]
    for copy in later:
        copy.wait()
    rows = top_ref.shape[0]
    top_ref[...] = held[0][:rows, :]
    bottom_ref[...] = held[0][held[0].shape[0] - rows :, :]


def teacher_moments(place, logits, fetched, tiles, classes, edge_rows):
    members, tiles_here, width = logits.shape
    groups = tiles_here // tiles
    quarters = 4
    shape = jax.ShapeDtypeStruct
    outs = [shape((tiles, width + LANES), BF16)] * groups
    outs += [shape((edge_rows, fetched[0].shape[1]), BF16)] * 2
    outs += [shape(one.shape, one.dtype) for one in fetched]
    got = pl.pallas_call(
        functools.partial(teacher_kernel, classes, groups),
        in_specs=[scalars(), *hbm(1 + len(fetched))],
        out_specs=whole(len(outs)),
        out_shape=outs,
        scratch_shapes=[
            pltpu.VMEM((quarters, members, tiles_here, width // quarters), BF16),
            pltpu.VMEM((tiles_here, width + LANES), BF16),
            pltpu.VMEM((tiles_here, LANES), F32),
            pltpu.SemaphoreType.DMA((quarters,)),
            pltpu.SemaphoreType.DMA((len(fetched),)),
        ],
        compiler_params=pltpu.CompilerParams(vmem_limit_bytes=56 << 20),
        cost_estimate=pl.CostEstimate(flops=3_000_000_000, bytes_accessed=9_000_000, transcendentals=6_000_000),
        name="teacher_moments",
    )(place, logits, *fetched)
    return got[:groups], got[groups : groups + 2], got[groups + 2 :]


def combine_kernel(classes, members, columns, capacity, where_ref, cover_ref, after_ref, *refs):
    got_refs, out_refs = refs[:-columns], refs[-columns:]
    groups = len(got_refs)
    tiles, extended = got_refs[0].shape
    width = extended - LANES
    means, gaps = [], []
    for start in range(0, width, MXU):
        sums = [got_ref[:, start : start + MXU].astype(F32) for got_ref in got_refs]
        total = sums[0]
        for one in sums[1:]:
            total = total + one
        mean = total * (1.0 / (members * groups))
        means.append(mean.astype(BF16))
        gap = jnp.zeros_like(mean)
        for one in sums:
            off = one * (1.0 / members) - mean
            gap = gap + off * off
        gaps.append(gap)
    between = class_sums(jnp.concatenate(gaps, axis=0), classes)
    lane = iota((tiles, LANES), 1)
    spread = jnp.zeros((tiles, LANES), F32)
    per = MXU // classes
    for i in range(width // MXU):
        spread = jnp.where(lane % 64 // per == i, between[i * tiles : (i + 1) * tiles], spread)
    inner = got_refs[0][:, width:].astype(F32)
    for got_ref in got_refs[1:]:
        inner = inner + got_ref[:, width:].astype(F32)
    spread = spread * (1.0 / groups) + join_lanes(inner) * (1.0 / (members * groups))
    index = (iota((tiles, LANES), 0) + 1).astype(F32).astype(BF16)
    rows = jnp.concatenate([*means, split_lanes(spread), index], axis=1)
    target = cover_ref[where_ref[MEMBER]] ^ (where_ref[CHIP] * 2 + where_ref[CORE])
    onehot = (iota((columns, tiles), 0) == target).astype(F32)
    earlier = (iota((tiles, tiles), 0) < iota((tiles, tiles), 1)).astype(BF16)
    before = dot(onehot.astype(BF16), earlier)
    rank = jnp.sum(before * onehot, axis=0, keepdims=True).astype(jnp.int32)
    place = (iota((columns * capacity, tiles), 0) == target * capacity + rank).astype(BF16)
    sent = dot(place, rows)
    for index, out_ref in enumerate(out_refs):
        out_ref[...] = sent[index * capacity : (index + 1) * capacity].astype(BF16)


def combine(got, cover, where, after, classes, members, columns, capacity):
    extended = got[0].shape[1]
    return pl.pallas_call(
        functools.partial(combine_kernel, classes, members, columns, capacity),
        in_specs=[pl.BlockSpec(memory_space=pltpu.SMEM), *whole(1), pl.BlockSpec(memory_space=pl.ANY), *whole(len(got))],
        out_specs=whole(columns),
        out_shape=[jax.ShapeDtypeStruct((capacity, extended + LANES), BF16)] * columns,
        compiler_params=pltpu.CompilerParams(vmem_limit_bytes=12 << 20),
        cost_estimate=pl.CostEstimate(flops=100_000_000, bytes_accessed=1_700_000, transcendentals=0),
        name="combine",
    )(where, cover, after, *got)


def put_shifted(ref, start, value, shift, width):
    rows, channels = value.shape
    col = iota(value.shape, 0) % width
    left = jnp.where(col >= shift, pltpu.roll(value, shift, 0), 0.0)
    right = jnp.where(col < width - shift, pltpu.roll(value, rows - shift, 0), 0.0)
    ref[pl.ds(start, rows), :channels] = left.astype(BF16)
    ref[pl.ds(start, rows), channels : 2 * channels] = value.astype(BF16)
    ref[pl.ds(start, rows), 2 * channels :] = right.astype(BF16)


def three_dots(ref, start, step, rows, weight_ref):
    total = None
    for tap in range(3):
        part = dot(ref[pl.ds(start + tap * step, rows), :], weight_ref[tap])
        total = part if total is None else total + part
    return total


def turned_dot(left, right):
    return lax.dot_general(left, right, (((1,), (1,)), ((), ())), preferred_element_type=F32)


def turned_dot(left, right):
    return lax.dot_general(left, right, (((1,), (1,)), ((), ())), preferred_element_type=F32)


def student_kernel(
    width, place_ref, before_ref, after_ref, head_ref, label_ref, x_ref, first_ref, second_ref,
    one_ref, two_ref, log_ref, base_ref, label_sum_ref, xcat, hcat, logit_ref,
):
    cells, channels = x_ref.shape
    halo = before_ref.shape[0]
    block = 4 * width
    put_shifted(xcat, 0, before_ref[...].astype(F32), 1, width)
    put_shifted(xcat, halo + cells, after_ref[...].astype(F32), 1, width)
    for start in range(0, cells, block):
        put_shifted(xcat, halo + start, x_ref[start : start + block, :].astype(F32), 1, width)
    lines = cells // width
    low = jnp.where(place_ref[FIRST] == 1, 2, 0)
    high = jnp.where(place_ref[LAST] == 1, lines + 2, lines + 4)
    for start in range(0, cells + block, block):
        value = jnp.maximum(three_dots(xcat, start, width, block, first_ref), 0.0)
        if start == 0 or start == cells:
            line = start // width + iota(value.shape, 0) // width
            value = jnp.where((line >= low) & (line < high), value, 0.0)
        put_shifted(hcat, start, value, 2, width)
        one_ref[start : start + block, :] = value.astype(BF16)
    head = jnp.concatenate([head_ref[...], head_ref[...]], axis=0)
    for start in range(0, cells, block):
        rows = slice(start, start + block)
        two = jnp.maximum(three_dots(hcat, start, 2 * width, block, second_ref), 0.0).astype(BF16)
        two_ref[rows, :] = two
        logit_ref[rows, :] = turned_dot(two, head)

    tiles, pixels = label_ref.shape
    edge = math.isqrt(pixels)
    across = width // edge
    lane = iota((tiles, LANES), 1)
    even = lane < 64
    label_sum = jnp.zeros((tiles, LANES), F32)
    for pair in range(pixels // 2):
        row, col = 2 * pair // edge, 2 * pair % edge
        parts = []
        for down in range(tiles // across):
            start = (down * edge + row) * width + col
            left = logit_ref[pl.ds(start, across, stride=edge), :]
            right = logit_ref[pl.ds(start + 1, across, stride=edge), :]
            parts.append(jnp.where(iota(left.shape, 1) < 64, left, right))
        value = jnp.concatenate(parts, axis=0)
        top = jnp.where(
            even,
            jnp.max(jnp.where(even, value, -jnp.inf), axis=1, keepdims=True),
            jnp.max(jnp.where(even, -jnp.inf, value), axis=1, keepdims=True),
        )
        value = value - top
        power = jnp.exp(value)
        total = jnp.where(
            even,
            jnp.sum(jnp.where(even, power, 0.0), axis=1, keepdims=True),
            jnp.sum(jnp.where(even, 0.0, power), axis=1, keepdims=True),
        )
        value = value - jnp.log(total)
        label = jnp.where(even, label_ref[:, 2 * pair : 2 * pair + 1], label_ref[:, 2 * pair + 1 : 2 * pair + 2])
        hit = label == lane % 64
        label_sum = label_sum + jnp.where(hit, value, 0.0)
        log_ref[pair * tiles : (pair + 1) * tiles, :] = value
        base_ref[pair * tiles : (pair + 1) * tiles, :] = jnp.exp(value) - hit.astype(F32)
    label_sum_ref[...] = label_sum


def student_forward(place, before, after, head, labels, x, first, second, width):
    cells, channels = x.shape
    halo = before.shape[0]
    tiles, pixels = labels.shape
    shape = jax.ShapeDtypeStruct
    return pl.pallas_call(
        functools.partial(student_kernel, width),
        in_specs=[scalars(), *whole(7)],
        out_specs=whole(5),
        out_shape=[
            shape((cells + 4 * width, channels), BF16),
            shape((cells, channels), BF16),
            shape((cells // 2, LANES), F32),
            shape((cells // 2, LANES), F32),
            shape((tiles, LANES), F32),
        ],
        scratch_shapes=[
            pltpu.VMEM((cells + 2 * halo, 3 * channels), BF16),
            pltpu.VMEM((cells + 4 * width, 3 * channels), BF16),
            pltpu.VMEM((cells, LANES), F32),
        ],
        compiler_params=pltpu.CompilerParams(vmem_limit_bytes=24 << 20),
        cost_estimate=pl.CostEstimate(flops=6_000_000_000, bytes_accessed=12_000_000, transcendentals=500_000),
        name="student_forward",
    )(place, before, after, head, labels, x, first, second)


def put_turned(ref, start, value, shift, width):
    rows, channels = value.shape
    col = iota(value.shape, 0) % width
    left = jnp.where(col >= shift, pltpu.roll(value, shift, 0), 0.0)
    right = jnp.where(col < width - shift, pltpu.roll(value, rows - shift, 0), 0.0)
    for tap, one in enumerate((left, value, right)):
        ref[tap * channels : (tap + 1) * channels, pl.ds(start, rows)] = one.T.astype(BF16)


def turn_kernel(
    width, before_ref, x_ref, after_ref, one_ref, two_ref, second_ref, sent_ref, xt_ref, ht_ref, twot_ref, wt_ref
):
    cells, channels = x_ref.shape
    halo = before_ref.shape[0]
    pair = 2 * width
    first = jnp.concatenate([before_ref[halo - width :], x_ref[:width]], axis=0).astype(F32)
    put_turned(xt_ref, 0, first, 1, width)
    last = jnp.concatenate([x_ref[cells - width :], after_ref[:width]], axis=0).astype(F32)
    put_turned(xt_ref, cells, last, 1, width)

    for start in range(pair, cells, pair):
        put_turned(xt_ref, start, x_ref[start - width : start + width, :].astype(F32), 1, width)
    for start in range(0, one_ref.shape[0], pair):
        put_turned(ht_ref, start, one_ref[start : start + pair, :].astype(F32), 2, width)
    for start in range(0, cells, MXU):
        twot_ref[:, start : start + MXU] = two_ref[start : start + MXU, :].astype(F32).T.astype(BF16)
    for i in range(3):
        for tap in range(3):
            part = slice(tap * channels, (tap + 1) * channels)
            mirror = slice((2 - tap) * channels, (3 - tap) * channels)
            wt_ref[i, part, :] = second_ref[i, mirror, :].astype(F32).T.astype(BF16)


def turn(before, x, after, one, two, second, sent, width):
    cells, channels = x.shape
    shape = jax.ShapeDtypeStruct
    return pl.pallas_call(
        functools.partial(turn_kernel, width),
        in_specs=[*whole(6), pl.BlockSpec(memory_space=pl.ANY)],
        out_specs=whole(4),
        out_shape=[
            shape((3 * channels, cells + 2 * width), BF16),
            shape((3 * channels, cells + 4 * width), BF16),
            shape((channels, cells), BF16),
            shape((3, 3 * channels, channels), BF16),
        ],
        compiler_params=pltpu.CompilerParams(vmem_limit_bytes=20 << 20),
        cost_estimate=pl.CostEstimate(flops=3_000_000_000, bytes_accessed=14_000_000, transcendentals=0),
        name="turn",
    )(before, x, after, one, two, second, sent)


def head_kernel(
    scale, width, log_ref, base_ref, label_sum_ref, two_ref, twot_ref, head_ref, *refs
):
    *got_refs, grad_ref, top_ref, bottom_ref, head_grad_ref, got_ref, natural = refs
    slots, extended = got_ref.shape
    got_ref[...] = jnp.concatenate([one[...].astype(F32) for one in got_refs], axis=0).astype(BF16)
    tiles = label_sum_ref.shape[0]
    flat = extended - 2 * LANES
    pixels = flat // 64
    edge = math.isqrt(pixels)
    across = width // edge
    index = got_ref[:, flat + LANES :].astype(F32)
    take = (index == (iota((slots, LANES), 1) + 1).astype(F32)).astype(F32).T[:tiles].astype(BF16)
    spread = join_lanes(dot(take, got_ref[:, flat : flat + LANES]))
    weight = 1.0 / (0.1 + spread)
    even = iota((tiles, LANES), 1) < 64
    loss = -label_sum_ref[...]
    for pair in range(pixels // 2):
        rows = slice(pair * tiles, (pair + 1) * tiles)
        if pair % 2 == 0:
            both = dot(take, got_ref[:, pair * LANES : (pair + 2) * LANES])
        mean = both[:, pair % 2 * LANES : (pair % 2 + 1) * LANES]
        cell = jnp.where(even, weight[:, 2 * pair : 2 * pair + 1], weight[:, 2 * pair + 1 : 2 * pair + 2])
        value = log_ref[rows, :]
        held = mean > 0
        loss = loss + cell * jnp.where(held, mean * (jnp.log(jnp.where(held, mean, 1.0)) - value), 0.0)
        grad = (cell * (jnp.exp(value) - mean) + base_ref[rows, :]) * scale
        turned = pltpu.roll(grad, 64, 1)
        row, col = 2 * pair // edge, 2 * pair % edge
        for down in range(tiles // across):
            start = (down * edge + row) * width + col
            natural[pl.ds(start, across, stride=edge), :] = grad[down * across : (down + 1) * across]
            natural[pl.ds(start + 1, across, stride=edge), :] = turned[down * across : (down + 1) * across]
    cells, channels = two_ref.shape
    logit_grad = natural[...].astype(BF16)
    head = jnp.concatenate([head_ref[...], jnp.zeros_like(head_ref)], axis=0)
    head_grad_ref[:channels, :] = dot(twot_ref[...], logit_grad)
    head_grad_ref[channels:, :] = loss
    block = 4 * width
    for start in range(0, cells, block):
        rows = slice(start, start + block)
        grad = dot(logit_grad[rows], head)
        grad_ref[rows, :] = jnp.where(two_ref[rows, :].astype(F32) > 0, grad, 0.0).astype(BF16)
    top_ref[...] = grad_ref[: 2 * width, :]
    bottom_ref[...] = grad_ref[cells - 2 * width :, :]


def head_step(got, log, base, label_sum, two, twot, head, scale, width):
    cells, channels = two.shape
    shape = jax.ShapeDtypeStruct
    return pl.pallas_call(
        functools.partial(head_kernel, scale, width),
        in_specs=whole(6 + len(got)),
        out_specs=whole(4),
        out_shape=[
            shape((cells, channels), BF16),
            shape((2 * width, channels), BF16),
            shape((2 * width, channels), BF16),
            shape((channels + label_sum.shape[0], LANES), F32),
        ],
        scratch_shapes=[
            pltpu.VMEM((len(got) * got[0].shape[0], got[0].shape[1]), BF16),
            pltpu.VMEM((cells, LANES), F32),
        ],
        compiler_params=pltpu.CompilerParams(vmem_limit_bytes=14 << 20),
        cost_estimate=pl.CostEstimate(flops=400_000_000, bytes_accessed=5_000_000, transcendentals=500_000),
        name="head_step",
    )(log, base, label_sum, two, twot, head, *got)


def second_kernel(width, ht_ref, grad_ref, out_ref):
    cells, channels = grad_ref.shape
    for tap in range(3):
        part = dot(ht_ref[:, 2 * width * tap : 2 * width * tap + cells], grad_ref[...])
        out_ref[tap * 3 * channels : (tap + 1) * 3 * channels, :] = part.astype(BF16)


def second_step(ht, grad, width):
    channels = grad.shape[1]
    return pl.pallas_call(
        functools.partial(second_kernel, width),
        in_specs=whole(2),
        out_specs=pl.BlockSpec(memory_space=pltpu.VMEM),
        out_shape=jax.ShapeDtypeStruct((9 * channels, channels), BF16),
        compiler_params=pltpu.CompilerParams(vmem_limit_bytes=14 << 20),
        cost_estimate=pl.CostEstimate(flops=2_500_000_000, bytes_accessed=7_000_000, transcendentals=0),
        name="second_step",
    )(ht, grad)


def first_kernel(width, chips, place_ref, before_ref, after_ref, grad_ref, head_grad_ref, second_ref, *refs):
    wt_ref, one_ref, xt_ref, *refs = refs
    keep_refs, give_refs, refs = refs[:chips], refs[chips : 2 * chips], refs[2 * chips :]
    gcat, padded, halves, sem = refs
    cells, channels = grad_ref.shape
    rows = 9 * channels
    used = rows + channels // 2
    half = halves.shape[1]
    second_copy = pltpu.make_async_copy(second_ref, halves.at[1, pl.ds(0, rows)], sem)
    second_copy.start()
    halo = before_ref.shape[0]
    block = 4 * width
    put_shifted(gcat, 0, before_ref[...].astype(F32), 2, width)
    put_shifted(gcat, halo + cells, after_ref[...].astype(F32), 2, width)
    for start in range(0, cells, block):
        put_shifted(gcat, halo + start, grad_ref[start : start + block, :].astype(F32), 2, width)
    padded[: 2 * width, :] = jnp.zeros((2 * width, channels), BF16)
    padded[2 * width + cells :, :] = jnp.zeros((2 * width, channels), BF16)
    for start in range(0, cells, block):
        value = None
        for tap in range(3):
            low = start + (2 - tap) * 2 * width
            part = dot(gcat[low : low + block, :], wt_ref[tap])
            value = part if value is None else value + part
        held = one_ref[2 * width + start : 2 * width + start + block, :].astype(F32) > 0
        padded[2 * width + start : 2 * width + start + block, :] = jnp.where(held, value, 0.0).astype(BF16)
    span = cells + 2 * width
    for tap in range(3):
        part = dot(xt_ref[...], padded[(2 - tap) * width : (2 - tap) * width + span, :])
        halves[0, tap * 3 * channels : (tap + 1) * 3 * channels, :] = part.astype(BF16)
    lane = iota((channels // 2, LANES), 1)
    loss = jnp.sum(head_grad_ref[channels:, :])
    high = loss.astype(BF16).astype(F32)
    extra = jnp.where(lane == 64, high, jnp.where(lane == 65, loss - high, 0.0))
    extra = jnp.where(iota(lane.shape, 0) == place_ref[DEVICE] % (channels // 2), extra, 0.0)
    for side in range(2):
        value = jnp.where(lane < 64, head_grad_ref[side * channels // 2 : (side + 1) * channels // 2, :], extra)
        halves[0, rows:used, side * LANES : (side + 1) * LANES] = value.astype(BF16)
    if half > used:
        halves[0, used:, :] = jnp.zeros((half - used, channels), BF16)
    halves[1, rows:, :] = jnp.zeros((half - rows, channels), BF16)
    second_copy.wait()
    core, chip = place_ref[CORE], place_ref[CHIP]
    size = half // chips
    for step in range(chips):
        low = pl.multiple_of((chip ^ step) * size, 16)
        give_refs[step][...] = halves[1 - core, pl.ds(low, size), :]
        keep_refs[step][...] = halves[core, pl.ds(low, size), :]


def first_step(place, before, after, grad, head_grad, second, wt, one, xt, width, half_rows, chips):
    cells, channels = grad.shape
    halo = before.shape[0]
    piece = jax.ShapeDtypeStruct((half_rows // chips, channels), BF16)
    outs = pl.pallas_call(
        functools.partial(first_kernel, width, chips),
        in_specs=[scalars(), *whole(8)],
        out_specs=whole(2 * chips),
        out_shape=[piece] * (2 * chips),
        scratch_shapes=[
            pltpu.VMEM((cells + 2 * halo, 3 * channels), BF16),
            pltpu.VMEM((cells + 4 * width, channels), BF16),
            pltpu.VMEM((2, half_rows, channels), BF16),
            pltpu.SemaphoreType.DMA,
        ],
        compiler_params=pltpu.CompilerParams(vmem_limit_bytes=24 << 20),
        cost_estimate=pl.CostEstimate(flops=5_000_000_000, bytes_accessed=10_000_000, transcendentals=0),
        name="first_step",
    )(place, before, after, grad, head_grad, second, wt, one, xt)
    return (outs[:chips], outs[chips:])


def neighbours(first, last, axis):
    count = lax.axis_size(axis)
    up = [(i, i + 1) for i in range(count - 1)]
    down = [(i + 1, i) for i in range(count - 1)]
    return (lax.ppermute(last, axis, up), lax.ppermute(first, axis, down))


def pairwise(array, axis, step):
    count = lax.axis_size(axis)
    return lax.ppermute(array, axis, [(i, i ^ step) for i in range(count)])


def add(arrays):
    return functools.reduce(jnp.add, [array.astype(F32) for array in arrays]).astype(BF16)


def assemble_kernel(
    width, chips, groups, cell_total, place_ref, *refs
):
    parts = len(refs) - 6
    pieces, refs = refs[:parts], refs[parts:]
    first_ref, second_ref, head_ref, loss_ref, value_ref, sems = refs
    mine, other = pieces[: parts // 2], pieces[parts // 2 :]
    batches = len(mine) // chips
    size = groups // batches
    block = mine[0].shape[0] // size
    grad_rows = first_ref.shape[0]
    core, chip, member = place_ref[CORE], place_ref[CHIP], place_ref[MEMBER]

    def fill(half, source):
        for batch in range(batches):
            for s in range(chips):
                value = source[batch * chips + s][...].astype(F32)
                for u in range(size):
                    start = ((chip ^ s) * groups + (member ^ (batch * size + u))) * block
                    value_ref[half, pl.ds(pl.multiple_of(start, 8), block), :] = value[u * block : (u + 1) * block]

    def send(half):
        out_ref = (first_ref, second_ref)[half]
        return pltpu.make_async_copy(value_ref.at[half, pl.ds(0, grad_rows)], out_ref, sems.at[half])

    def start_copy(half):
        pl.when(half == 0)(lambda: send(0).start())
        pl.when(half != 0)(lambda: send(1).start())

    fill(core, mine)
    start_copy(core)
    fill(1 - core, other)
    start_copy(1 - core)
    rows = width // 2
    extra = value_ref[0, grad_rows : grad_rows + rows, :]
    for side in range(2):
        head_ref[:, side * rows : (side + 1) * rows] = extra[:, side * LANES : (side + 1) * LANES].T[: head_ref.shape[0]]
    lane = iota(extra.shape, 1)
    loss = jnp.sum(jnp.where((lane == 64) | (lane == 65), extra, 0.0), keepdims=True)
    loss_ref[...] = loss / cell_total
    send(0).wait()
    send(1).wait()


def assemble(place, pieces, chips, groups, half_rows, grad_rows, classes, cell_total):
    width = pieces[0].shape[1]
    shape = jax.ShapeDtypeStruct
    return pl.pallas_call(
        functools.partial(assemble_kernel, width, chips, groups, cell_total),
        in_specs=[scalars(), *whole(len(pieces))],
        out_specs=[*hbm(2), *whole(2)],
        out_shape=[
            shape((grad_rows, width), F32),
            shape((grad_rows, width), F32),
            shape((classes, width), F32),
            shape((1, 1), F32),
        ],
        scratch_shapes=[pltpu.VMEM((2, half_rows, width), F32), pltpu.SemaphoreType.DMA((2,))],
        compiler_params=pltpu.CompilerParams(vmem_limit_bytes=48 << 20),
        cost_estimate=pl.CostEstimate(flops=1_000_000, bytes_accessed=7_500_000, transcendentals=0),
        name="assemble",
    )(place, *pieces)


def gradient_pieces(place, keep, give, groups, chips):
    got = [pairwise(one, "core", 1) for one in give]
    sums = [add(pair) for pair in zip(keep, got)]
    sums = [sums[0]] + [pairwise(sums[step], "chip", step) for step in range(1, chips)]
    rows = sums[0].shape[0] // groups

    def block(step):
        start = (place[MEMBER] ^ step) * rows
        return add([lax.dynamic_slice_in_dim(one, start, rows, axis=0) for one in sums])

    mine = add([block(0)] + [pairwise(block(step), "member", step) for step in range(1, groups)])
    gathered = [mine] + [pairwise(mine, "member", step) for step in range(1, groups)]
    one = jnp.concatenate(gathered, axis=0)
    held = [one] + [pairwise(one, "chip", step) for step in range(1, chips)]
    return held + [pairwise(piece, "core", 1) for piece in held]


def body(teacher_logits, coverage, features, labels, first_weight, second_weight, head_weight):
    channels, classes = head_weight.shape
    members, tiles_here, flat_width = teacher_logits.shape
    pixels = flat_width // classes
    edge = math.isqrt(pixels)
    groups = lax.axis_size("member")
    chips = lax.axis_size("chip")
    columns = chips * 2
    tile_axes = ("chip", "core")
    block_tiles = tiles_here // groups
    capacity = max(2, 2 * block_tiles // columns)
    local = features[0]
    lines, width = local.shape[:2]
    cells = lines * width
    cell_total = groups * columns * cells
    column = lax.axis_index(tile_axes)
    place = jnp.stack(
        [
            lax.axis_index("core"),
            lax.axis_index("chip"),
            lax.axis_index("member"),
            lax.axis_index(("member", *tile_axes)),
            column == 0,
            column == columns - 1,
        ]
    ).astype(jnp.int32)
    flat = local.reshape(cells, channels)
    first_rows = first_weight.reshape(3, 3 * channels, channels)
    second_rows = second_weight.reshape(3, 3 * channels, channels)
    head = head_weight.T

    payload, (top, bottom), (flat, first_rows, second_rows) = teacher_moments(
        place, teacher_logits, (flat, first_rows, second_rows), block_tiles, classes, 3 * width
    )
    got = [pairwise(payload[step], "member", step) for step in range(groups - 1, 0, -1)] + [payload[0]]
    before, after = neighbours(top, bottom, tile_axes)
    label_rows = (
        labels[0].reshape(lines // edge, edge, width // edge, edge).transpose(0, 2, 1, 3).reshape(block_tiles, pixels)
    )
    one, two, log, base, label_sum = student_forward(
        place, before, after, head, label_rows, flat, first_rows, second_rows, width
    )
    cover = coverage.reshape(groups, 1, block_tiles)
    sent = combine(got, cover, place, label_sum, classes, members, columns, capacity)
    received = [sent[0]] + [pairwise(sent[step], tile_axes, step) for step in range(1, columns)]
    xt, ht, twot, wt = turn(before, flat, after, one, two, second_rows, sent[0], width)
    grad_two, top, bottom, head_grad = head_step(
        received, log, base, label_sum, two, twot, head, 1.0 / math.sqrt(cell_total), width
    )
    grad_before, grad_after = neighbours(top, bottom, tile_axes)
    second = second_step(ht, grad_two, width)
    rows, extra_rows = 9 * channels, channels // 2
    unit = 8 * groups * chips
    half_rows = -(-(rows + extra_rows) // unit) * unit
    keep, give = first_step(
        place, grad_before, grad_after, grad_two, head_grad, second, wt, one, xt, width, half_rows, chips
    )
    pieces = gradient_pieces(place, keep, give, groups, chips)
    first_total, second_total, head_total, loss = assemble(
        place, pieces, chips, groups, half_rows, rows, classes, cell_total
    )
    kernel_shape = (3, 3, channels, channels)
    return (first_total.reshape(kernel_shape), second_total.reshape(kernel_shape), head_total.T, loss[0, 0])


def solution(mesh):
    groups, columns = mesh.shape["member"], mesh.shape["tile"]
    split = jax.sharding.Mesh(mesh.devices.reshape(groups, columns // 2, 2), ("member", "chip", "core"))
    tile = ("chip", "core")
    return jax.shard_map(
        body,
        mesh=split,
        in_specs=(
            P("member", tile, None),
            P(tile),
            P("member", tile, None, None),
            P("member", tile, None),
            P(),
            P(),
            P(),
        ),
        out_specs=(P(), P(), P(), P()),
        check_vma=False,
    )
```

```python
import functools
import math

import jax
import jax.numpy as jnp
from jax import lax
from jax.experimental import pallas as pl
from jax.experimental.pallas import tpu as pltpu
from jax.sharding import PartitionSpec as P

BF16 = jnp.bfloat16
F32 = jnp.float32
LANES = 128
MXU = 256


def whole(count):
    return [pl.BlockSpec(memory_space=pltpu.VMEM)] * count


def iota(shape, axis):
    return lax.broadcasted_iota(jnp.int32, shape, axis)


def dot(left, right):
    return jnp.dot(left, right, preferred_element_type=F32)


def split_lanes(value):
    high = value.astype(BF16).astype(F32)
    return jnp.where(iota(value.shape, 1) < 64, high, value - high).astype(BF16)


def join_lanes(value):
    return value + pltpu.roll(value, 64, 1)


def class_sums(value, classes):
    pick = (iota((MXU, LANES), 0) // classes == iota((MXU, LANES), 1) % (MXU // classes)).astype(BF16)
    high = value.astype(BF16)
    low = (value - high.astype(F32)).astype(BF16)
    return dot(high, pick) + dot(low, pick)


def hbm(count):
    return [pl.BlockSpec(memory_space=pl.ANY)] * count


def scalars():
    return pl.BlockSpec(memory_space=pltpu.SMEM)


CORE, CHIP, MEMBER, DEVICE, FIRST, LAST = range(6)


def teacher_kernel(classes, flip, place_ref, logit_hbm, *refs):
    edges = flip == 0
    if edges:
        flat_hbm, after_ref, near_ref, own_ref, top_ref, bottom_ref, *refs = refs
    else:
        near_ref, own_ref, *refs = refs
    x_ref, sum_ref, acc_ref, sems, edge_sems = refs
    quarters, members, tiles, width = x_ref.shape
    parts = width // MXU
    per = MXU // classes
    tile_rows = pl.ds(pl.multiple_of(((place_ref[MEMBER] // 2) ^ flip) * tiles, tiles), tiles)
    arrive = [
        pltpu.make_async_copy(logit_hbm.at[:, tile_rows, pl.ds(i * width, width)], x_ref.at[i], sems.at[i])
        for i in range(quarters)
    ]
    later = []
    if edges:
        rows = top_ref.shape[0]
        later = [
            pltpu.make_async_copy(flat_hbm.at[pl.ds(0, rows)], top_ref, edge_sems.at[0]),
            pltpu.make_async_copy(flat_hbm.at[pl.ds(flat_hbm.shape[0] - rows, rows)], bottom_ref, edge_sems.at[1]),
        ]
    for copy in arrive + later:
        copy.start()
    same = (iota((MXU, MXU), 0) // classes == iota((MXU, MXU), 1) // classes).astype(BF16)
    acc_ref[...] = jnp.zeros_like(acc_ref)

    @pl.loop(0, quarters)
    def _(i):
        pltpu.make_async_copy(logit_hbm.at[:, tile_rows, pl.ds(0, width)], x_ref.at[i], sems.at[i]).wait()
        each = range(parts)
        x = [x_ref[i, :, :, n * MXU : (n + 1) * MXU].astype(F32).reshape(members * tiles, MXU) for n in each]
        root = [jnp.exp(one * 0.25) for one in x]
        total = [dot(one.astype(BF16), same) for one in root]
        root = [one * pl.reciprocal(whole_sum, approx=True) for one, whole_sum in zip(root, total)]
        square = [one * one for one in root]
        power = [one * one for one in square]
        total = [dot(one.astype(BF16), same) for one in power]
        inverse = [pl.reciprocal(one, approx=True) for one in total]
        inverse = [one * (2.0 - whole_sum * one) for one, whole_sum in zip(inverse, total)]
        probs = [(one * other).reshape(members, tiles, MXU) for one, other in zip(power, inverse)]
        first = [functools.reduce(jnp.add, [one[m] for m in range(members)]) for one in probs]
        within = [
            functools.reduce(jnp.add, [one[m] * one[m] for m in range(members)]) - sums * sums * (1.0 / members)
            for one, sums in zip(probs, first)
        ]
        sums = [class_sums(one, classes) for one in within]
        acc = acc_ref[...]
        for n in each:
            acc = jnp.where(iota(acc.shape, 1) % 64 // per == i * parts + n, sums[n], acc)
        acc_ref[...] = acc
        for n in each:
            sum_ref[:, pl.ds(pl.multiple_of(i * width + n * MXU, MXU), MXU)] = first[n].astype(BF16)

    sum_ref[:, quarters * width :] = split_lanes(acc_ref[...])
    block = tiles // 2
    odd = 1 - place_ref[MEMBER] % 2
    near_ref[...] = sum_ref[pl.ds(pl.multiple_of(odd * block, 16), block), :]
    own_ref[...] = sum_ref[pl.ds(pl.multiple_of((1 - odd) * block, 16), block), :]
    for copy in later:
        copy.wait()


def teacher_moments(place, logits, tiles, classes, flip, *edges, edge_rows=0):
    members, _, width = logits.shape
    quarters = 4
    shape = jax.ShapeDtypeStruct
    outs = [shape((tiles, width + LANES), BF16)] * 2
    if edges:
        outs += [shape((edge_rows, edges[0].shape[1]), BF16)] * 2
    return pl.pallas_call(
        functools.partial(teacher_kernel, classes, flip),
        in_specs=[scalars(), *hbm(1 + len(edges))],
        out_specs=whole(len(outs)),
        out_shape=outs,
        scratch_shapes=[
            pltpu.VMEM((quarters, members, 2 * tiles, width // quarters), BF16),
            pltpu.VMEM((2 * tiles, width + LANES), BF16),
            pltpu.VMEM((2 * tiles, LANES), F32),
            pltpu.SemaphoreType.DMA((quarters,)),
            pltpu.SemaphoreType.DMA((2,)),
        ],
        compiler_params=pltpu.CompilerParams(vmem_limit_bytes=58 << 20),
        cost_estimate=pl.CostEstimate(flops=1_500_000_000, bytes_accessed=2_600_000, transcendentals=3_000_000),
        name="teacher_moments",
    )(place, logits, *edges)


def combine_kernel(classes, members, columns, capacity, where_ref, cover_ref, after_ref, *refs):
    got_refs, out_refs = refs[:-columns], refs[-columns:]
    groups = len(got_refs)
    tiles, extended = got_refs[0].shape
    width = extended - LANES
    means, gaps = [], []
    for start in range(0, width, MXU):
        sums = [got_ref[:, start : start + MXU].astype(F32) for got_ref in got_refs]
        total = sums[0]
        for one in sums[1:]:
            total = total + one
        mean = total * (1.0 / (members * groups))
        means.append(mean.astype(BF16))
        gap = jnp.zeros_like(mean)
        for one in sums:
            off = one * (1.0 / members) - mean
            gap = gap + off * off
        gaps.append(gap)
    between = class_sums(jnp.concatenate(gaps, axis=0), classes)
    lane = iota((tiles, LANES), 1)
    spread = jnp.zeros((tiles, LANES), F32)
    per = MXU // classes
    for i in range(width // MXU):
        spread = jnp.where(lane % 64 // per == i, between[i * tiles : (i + 1) * tiles], spread)
    inner = got_refs[0][:, width:].astype(F32)
    for got_ref in got_refs[1:]:
        inner = inner + got_ref[:, width:].astype(F32)
    spread = spread * (1.0 / groups) + join_lanes(inner) * (1.0 / (members * groups))
    index = (iota((tiles, LANES), 0) + 1).astype(F32).astype(BF16)
    rows = jnp.concatenate([*means, split_lanes(spread), index], axis=1)
    target = cover_ref[where_ref[MEMBER]] ^ (where_ref[CHIP] * 2 + where_ref[CORE])
    onehot = (iota((columns, tiles), 0) == target).astype(F32)
    earlier = (iota((tiles, tiles), 0) < iota((tiles, tiles), 1)).astype(BF16)
    before = dot(onehot.astype(BF16), earlier)
    rank = jnp.sum(before * onehot, axis=0, keepdims=True).astype(jnp.int32)
    place = (iota((columns * capacity, tiles), 0) == target * capacity + rank).astype(BF16)
    sent = dot(place, rows)
    for index, out_ref in enumerate(out_refs):
        out_ref[...] = sent[index * capacity : (index + 1) * capacity].astype(BF16)


def combine(got, cover, where, after, classes, members, columns, capacity):
    extended = got[0].shape[1]
    return pl.pallas_call(
        functools.partial(combine_kernel, classes, members, columns, capacity),
        in_specs=[pl.BlockSpec(memory_space=pltpu.SMEM), *whole(1), pl.BlockSpec(memory_space=pl.ANY), *whole(len(got))],
        out_specs=whole(columns),
        out_shape=[jax.ShapeDtypeStruct((capacity, extended + LANES), BF16)] * columns,
        compiler_params=pltpu.CompilerParams(vmem_limit_bytes=12 << 20),
        cost_estimate=pl.CostEstimate(flops=100_000_000, bytes_accessed=1_700_000, transcendentals=0),
        name="combine",
    )(where, cover, after, *got)


def put_shifted(ref, start, value, shift, width):
    rows, channels = value.shape
    col = iota(value.shape, 0) % width
    left = jnp.where(col >= shift, pltpu.roll(value, shift, 0), 0.0)
    right = jnp.where(col < width - shift, pltpu.roll(value, rows - shift, 0), 0.0)
    ref[pl.ds(start, rows), :channels] = left.astype(BF16)
    ref[pl.ds(start, rows), channels : 2 * channels] = value.astype(BF16)
    ref[pl.ds(start, rows), 2 * channels :] = right.astype(BF16)


def three_dots(ref, start, step, rows, weight_ref):
    total = None
    for tap in range(3):
        part = dot(ref[pl.ds(start + tap * step, rows), :], weight_ref[tap])
        total = part if total is None else total + part
    return total


def turned_dot(left, right):
    return lax.dot_general(left, right, (((1,), (1,)), ((), ())), preferred_element_type=F32)


def turned_dot(left, right):
    return lax.dot_general(left, right, (((1,), (1,)), ((), ())), preferred_element_type=F32)


def student_kernel(
    width, place_ref, before_ref, after_ref, head_ref, label_ref, x_ref, first_ref, second_ref,
    one_ref, two_ref, log_ref, base_ref, label_sum_ref, xcat, hcat, logit_ref,
):
    cells, channels = x_ref.shape
    halo = before_ref.shape[0]
    block = 4 * width
    put_shifted(xcat, 0, before_ref[...].astype(F32), 1, width)
    put_shifted(xcat, halo + cells, after_ref[...].astype(F32), 1, width)
    for start in range(0, cells, block):
        put_shifted(xcat, halo + start, x_ref[start : start + block, :].astype(F32), 1, width)
    lines = cells // width
    low = jnp.where(place_ref[FIRST] == 1, 2, 0)
    high = jnp.where(place_ref[LAST] == 1, lines + 2, lines + 4)
    for start in range(0, cells + block, block):
        value = jnp.maximum(three_dots(xcat, start, width, block, first_ref), 0.0)
        if start == 0 or start == cells:
            line = start // width + iota(value.shape, 0) // width
            value = jnp.where((line >= low) & (line < high), value, 0.0)
        put_shifted(hcat, start, value, 2, width)
        one_ref[start : start + block, :] = value.astype(BF16)
    head = jnp.concatenate([head_ref[...], head_ref[...]], axis=0)
    for start in range(0, cells, block):
        rows = slice(start, start + block)
        two = jnp.maximum(three_dots(hcat, start, 2 * width, block, second_ref), 0.0).astype(BF16)
        two_ref[rows, :] = two
        logit_ref[rows, :] = turned_dot(two, head)

    tiles, pixels = label_ref.shape
    edge = math.isqrt(pixels)
    across = width // edge
    lane = iota((tiles, LANES), 1)
    even = lane < 64
    label_sum = jnp.zeros((tiles, LANES), F32)
    for pair in range(pixels // 2):
        row, col = 2 * pair // edge, 2 * pair % edge
        parts = []
        for down in range(tiles // across):
            start = (down * edge + row) * width + col
            left = logit_ref[pl.ds(start, across, stride=edge), :]
            right = logit_ref[pl.ds(start + 1, across, stride=edge), :]
            parts.append(jnp.where(iota(left.shape, 1) < 64, left, right))
        value = jnp.concatenate(parts, axis=0)
        top = jnp.where(
            even,
            jnp.max(jnp.where(even, value, -jnp.inf), axis=1, keepdims=True),
            jnp.max(jnp.where(even, -jnp.inf, value), axis=1, keepdims=True),
        )
        value = value - top
        power = jnp.exp(value)
        total = jnp.where(
            even,
            jnp.sum(jnp.where(even, power, 0.0), axis=1, keepdims=True),
            jnp.sum(jnp.where(even, 0.0, power), axis=1, keepdims=True),
        )
        value = value - jnp.log(total)
        label = jnp.where(even, label_ref[:, 2 * pair : 2 * pair + 1], label_ref[:, 2 * pair + 1 : 2 * pair + 2])
        hit = label == lane % 64
        label_sum = label_sum + jnp.where(hit, value, 0.0)
        log_ref[pair * tiles : (pair + 1) * tiles, :] = value
        base_ref[pair * tiles : (pair + 1) * tiles, :] = jnp.exp(value) - hit.astype(F32)
    label_sum_ref[...] = label_sum


def student_forward(place, before, after, head, labels, x, first, second, width):
    cells, channels = x.shape
    halo = before.shape[0]
    tiles, pixels = labels.shape
    shape = jax.ShapeDtypeStruct
    return pl.pallas_call(
        functools.partial(student_kernel, width),
        in_specs=[scalars(), *whole(7)],
        out_specs=whole(5),
        out_shape=[
            shape((cells + 4 * width, channels), BF16),
            shape((cells, channels), BF16),
            shape((cells // 2, LANES), F32),
            shape((cells // 2, LANES), F32),
            shape((tiles, LANES), F32),
        ],
        scratch_shapes=[
            pltpu.VMEM((cells + 2 * halo, 3 * channels), BF16),
            pltpu.VMEM((cells + 4 * width, 3 * channels), BF16),
            pltpu.VMEM((cells, LANES), F32),
        ],
        compiler_params=pltpu.CompilerParams(vmem_limit_bytes=24 << 20),
        cost_estimate=pl.CostEstimate(flops=6_000_000_000, bytes_accessed=12_000_000, transcendentals=500_000),
        name="student_forward",
    )(place, before, after, head, labels, x, first, second)


def put_turned(ref, start, value, shift, width):
    rows, channels = value.shape
    col = iota(value.shape, 0) % width
    left = jnp.where(col >= shift, pltpu.roll(value, shift, 0), 0.0)
    right = jnp.where(col < width - shift, pltpu.roll(value, rows - shift, 0), 0.0)
    for tap, one in enumerate((left, value, right)):
        ref[tap * channels : (tap + 1) * channels, pl.ds(start, rows)] = one.T.astype(BF16)


def turn_kernel(
    width, before_ref, x_ref, after_ref, one_ref, two_ref, second_ref, sent_ref, xt_ref, ht_ref, twot_ref, wt_ref
):
    cells, channels = x_ref.shape
    halo = before_ref.shape[0]
    pair = 2 * width
    first = jnp.concatenate([before_ref[halo - width :], x_ref[:width]], axis=0).astype(F32)
    put_turned(xt_ref, 0, first, 1, width)
    last = jnp.concatenate([x_ref[cells - width :], after_ref[:width]], axis=0).astype(F32)
    put_turned(xt_ref, cells, last, 1, width)

    for start in range(pair, cells, pair):
        put_turned(xt_ref, start, x_ref[start - width : start + width, :].astype(F32), 1, width)
    for start in range(0, one_ref.shape[0], pair):
        put_turned(ht_ref, start, one_ref[start : start + pair, :].astype(F32), 2, width)
    for start in range(0, cells, MXU):
        twot_ref[:, start : start + MXU] = two_ref[start : start + MXU, :].astype(F32).T.astype(BF16)
    for i in range(3):
        for tap in range(3):
            part = slice(tap * channels, (tap + 1) * channels)
            mirror = slice((2 - tap) * channels, (3 - tap) * channels)
            wt_ref[i, part, :] = second_ref[i, mirror, :].astype(F32).T.astype(BF16)


def turn(before, x, after, one, two, second, sent, width):
    cells, channels = x.shape
    shape = jax.ShapeDtypeStruct
    return pl.pallas_call(
        functools.partial(turn_kernel, width),
        in_specs=[*whole(6), pl.BlockSpec(memory_space=pl.ANY)],
        out_specs=whole(4),
        out_shape=[
            shape((3 * channels, cells + 2 * width), BF16),
            shape((3 * channels, cells + 4 * width), BF16),
            shape((channels, cells), BF16),
            shape((3, 3 * channels, channels), BF16),
        ],
        compiler_params=pltpu.CompilerParams(vmem_limit_bytes=20 << 20),
        cost_estimate=pl.CostEstimate(flops=3_000_000_000, bytes_accessed=14_000_000, transcendentals=0),
        name="turn",
    )(before, x, after, one, two, second, sent)


def head_kernel(
    scale, width, log_ref, base_ref, label_sum_ref, two_ref, twot_ref, head_ref, *refs
):
    *got_refs, grad_ref, top_ref, bottom_ref, head_grad_ref, got_ref, natural = refs
    slots, extended = got_ref.shape
    got_ref[...] = jnp.concatenate([one[...].astype(F32) for one in got_refs], axis=0).astype(BF16)
    tiles = label_sum_ref.shape[0]
    flat = extended - 2 * LANES
    pixels = flat // 64
    edge = math.isqrt(pixels)
    across = width // edge
    index = got_ref[:, flat + LANES :].astype(F32)
    take = (index == (iota((slots, LANES), 1) + 1).astype(F32)).astype(F32).T[:tiles].astype(BF16)
    spread = join_lanes(dot(take, got_ref[:, flat : flat + LANES]))
    weight = 1.0 / (0.1 + spread)
    even = iota((tiles, LANES), 1) < 64
    loss = -label_sum_ref[...]
    for pair in range(pixels // 2):
        rows = slice(pair * tiles, (pair + 1) * tiles)
        if pair % 2 == 0:
            both = dot(take, got_ref[:, pair * LANES : (pair + 2) * LANES])
        mean = both[:, pair % 2 * LANES : (pair % 2 + 1) * LANES]
        cell = jnp.where(even, weight[:, 2 * pair : 2 * pair + 1], weight[:, 2 * pair + 1 : 2 * pair + 2])
        value = log_ref[rows, :]
        held = mean > 0
        loss = loss + cell * jnp.where(held, mean * (jnp.log(jnp.where(held, mean, 1.0)) - value), 0.0)
        grad = (cell * (jnp.exp(value) - mean) + base_ref[rows, :]) * scale
        turned = pltpu.roll(grad, 64, 1)
        row, col = 2 * pair // edge, 2 * pair % edge
        for down in range(tiles // across):
            start = (down * edge + row) * width + col
            natural[pl.ds(start, across, stride=edge), :] = grad[down * across : (down + 1) * across]
            natural[pl.ds(start + 1, across, stride=edge), :] = turned[down * across : (down + 1) * across]
    cells, channels = two_ref.shape
    logit_grad = natural[...].astype(BF16)
    head = jnp.concatenate([head_ref[...], jnp.zeros_like(head_ref)], axis=0)
    head_grad_ref[:channels, :] = dot(twot_ref[...], logit_grad)
    head_grad_ref[channels:, :] = loss
    block = 4 * width
    for start in range(0, cells, block):
        rows = slice(start, start + block)
        grad = dot(logit_grad[rows], head)
        grad_ref[rows, :] = jnp.where(two_ref[rows, :].astype(F32) > 0, grad, 0.0).astype(BF16)
    top_ref[...] = grad_ref[: 2 * width, :]
    bottom_ref[...] = grad_ref[cells - 2 * width :, :]


def head_step(got, log, base, label_sum, two, twot, head, scale, width):
    cells, channels = two.shape
    shape = jax.ShapeDtypeStruct
    return pl.pallas_call(
        functools.partial(head_kernel, scale, width),
        in_specs=whole(6 + len(got)),
        out_specs=whole(4),
        out_shape=[
            shape((cells, channels), BF16),
            shape((2 * width, channels), BF16),
            shape((2 * width, channels), BF16),
            shape((channels + label_sum.shape[0], LANES), F32),
        ],
        scratch_shapes=[
            pltpu.VMEM((len(got) * got[0].shape[0], got[0].shape[1]), BF16),
            pltpu.VMEM((cells, LANES), F32),
        ],
        compiler_params=pltpu.CompilerParams(vmem_limit_bytes=14 << 20),
        cost_estimate=pl.CostEstimate(flops=400_000_000, bytes_accessed=5_000_000, transcendentals=500_000),
        name="head_step",
    )(log, base, label_sum, two, twot, head, *got)


def second_kernel(width, ht_ref, grad_ref, out_ref):
    cells, channels = grad_ref.shape
    for tap in range(3):
        part = dot(ht_ref[:, 2 * width * tap : 2 * width * tap + cells], grad_ref[...])
        out_ref[tap * 3 * channels : (tap + 1) * 3 * channels, :] = part.astype(BF16)


def second_step(ht, grad, width):
    channels = grad.shape[1]
    return pl.pallas_call(
        functools.partial(second_kernel, width),
        in_specs=whole(2),
        out_specs=pl.BlockSpec(memory_space=pltpu.VMEM),
        out_shape=jax.ShapeDtypeStruct((9 * channels, channels), BF16),
        compiler_params=pltpu.CompilerParams(vmem_limit_bytes=14 << 20),
        cost_estimate=pl.CostEstimate(flops=2_500_000_000, bytes_accessed=7_000_000, transcendentals=0),
        name="second_step",
    )(ht, grad)


def first_kernel(width, plan, place_ref, before_ref, after_ref, grad_ref, head_grad_ref, second_ref, *refs):
    wt_ref, one_ref, xt_ref, *refs = refs
    chips, groups, near_rows, far_rows = plan
    keep_refs, give_refs, refs = refs[: chips + 1], refs[chips + 1 : 2 * chips + 2], refs[2 * chips + 2 :]
    gcat, padded, halves, sem = refs
    cells, channels = grad_ref.shape
    rows = 9 * channels
    used = rows + channels // 2
    half = halves.shape[1]
    second_copy = pltpu.make_async_copy(second_ref, halves.at[1, pl.ds(0, rows)], sem)
    second_copy.start()
    halo = before_ref.shape[0]
    block = 4 * width
    put_shifted(gcat, 0, before_ref[...].astype(F32), 2, width)
    put_shifted(gcat, halo + cells, after_ref[...].astype(F32), 2, width)
    for start in range(0, cells, block):
        put_shifted(gcat, halo + start, grad_ref[start : start + block, :].astype(F32), 2, width)
    padded[: 2 * width, :] = jnp.zeros((2 * width, channels), BF16)
    padded[2 * width + cells :, :] = jnp.zeros((2 * width, channels), BF16)
    for start in range(0, cells, block):
        value = None
        for tap in range(3):
            low = start + (2 - tap) * 2 * width
            part = dot(gcat[low : low + block, :], wt_ref[tap])
            value = part if value is None else value + part
        held = one_ref[2 * width + start : 2 * width + start + block, :].astype(F32) > 0
        padded[2 * width + start : 2 * width + start + block, :] = jnp.where(held, value, 0.0).astype(BF16)
    span = cells + 2 * width
    for tap in range(3):
        part = dot(xt_ref[...], padded[(2 - tap) * width : (2 - tap) * width + span, :])
        halves[0, tap * 3 * channels : (tap + 1) * 3 * channels, :] = part.astype(BF16)
    lane = iota((channels // 2, LANES), 1)
    loss = jnp.sum(head_grad_ref[channels:, :])
    high = loss.astype(BF16).astype(F32)
    extra = jnp.where(lane == 64, high, jnp.where(lane == 65, loss - high, 0.0))
    extra = jnp.where(iota(lane.shape, 0) == place_ref[DEVICE] % (channels // 2), extra, 0.0)
    for side in range(2):
        value = jnp.where(lane < 64, head_grad_ref[side * channels // 2 : (side + 1) * channels // 2, :], extra)
        halves[0, rows:used, side * LANES : (side + 1) * LANES] = value.astype(BF16)
    if half > used:
        halves[0, used:, :] = jnp.zeros((half - used, channels), BF16)
    halves[1, rows:, :] = jnp.zeros((half - rows, channels), BF16)
    second_copy.wait()
    core, chip = place_ref[CORE], place_ref[CHIP]
    size = groups * near_rows
    for step in range(chips):
        low = pl.multiple_of((chip ^ step) * size, 16)
        give_refs[step][...] = halves[1 - core, pl.ds(low, size), :]
        keep_refs[step][...] = halves[core, pl.ds(low, size), :]
    give_refs[chips][...] = halves[1 - core, chips * size :, :]
    keep_refs[chips][...] = halves[core, chips * size :, :]


def first_step(place, before, after, grad, head_grad, second, wt, one, xt, width, plan):
    cells, channels = grad.shape
    halo = before.shape[0]
    chips, groups, near_rows, far_rows = plan
    half_rows = chips * groups * (near_rows + far_rows)
    piece = [jax.ShapeDtypeStruct((groups * near_rows, channels), BF16)] * chips
    piece += [jax.ShapeDtypeStruct((chips * groups * far_rows, channels), BF16)]
    outs = pl.pallas_call(
        functools.partial(first_kernel, width, plan),
        in_specs=[scalars(), *whole(8)],
        out_specs=whole(2 * chips + 2),
        out_shape=piece * 2,
        scratch_shapes=[
            pltpu.VMEM((cells + 2 * halo, 3 * channels), BF16),
            pltpu.VMEM((cells + 4 * width, channels), BF16),
            pltpu.VMEM((2, half_rows, channels), BF16),
            pltpu.SemaphoreType.DMA,
        ],
        compiler_params=pltpu.CompilerParams(vmem_limit_bytes=24 << 20),
        cost_estimate=pl.CostEstimate(flops=5_000_000_000, bytes_accessed=10_000_000, transcendentals=0),
        name="first_step",
    )(place, before, after, grad, head_grad, second, wt, one, xt)
    return (outs[: chips + 1], outs[chips + 1 :])


def neighbours(first, last, axis):
    count = lax.axis_size(axis)
    up = [(i, i + 1) for i in range(count - 1)]
    down = [(i + 1, i) for i in range(count - 1)]
    return (lax.ppermute(last, axis, up), lax.ppermute(first, axis, down))


def pairwise(array, axis, step):
    count = lax.axis_size(axis)
    return lax.ppermute(array, axis, [(i, i ^ step) for i in range(count)])


def add(arrays):
    return functools.reduce(jnp.add, [array.astype(F32) for array in arrays]).astype(BF16)


def assemble_kernel(width, plan, cell_total, place_ref, *refs):
    chips, groups, near_rows, far_rows = plan
    parts = len(refs) - 6
    pieces, refs = refs[:parts], refs[parts:]
    first_ref, second_ref, head_ref, loss_ref, value_ref, sems = refs
    grad_rows = first_ref.shape[0]
    core, chip, member = place_ref[CORE], place_ref[CHIP], place_ref[MEMBER]

    def fill(half, source):
        for s in range(chips):
            value = source[s][...].astype(F32)
            for u in range(groups):
                start = pl.multiple_of(((chip ^ s) * groups + (member ^ u)) * near_rows, 8)
                value_ref[half, pl.ds(start, near_rows), :] = value[u * near_rows : (u + 1) * near_rows]
        value = source[chips][...].astype(F32)
        for u in range(groups):
            for s in range(chips):
                low = (u * chips + s) * far_rows
                start = chips * groups * near_rows + ((member ^ u) * chips + (chip ^ s)) * far_rows
                value_ref[half, pl.ds(pl.multiple_of(start, 8), far_rows), :] = value[low : low + far_rows]

    mine, other = pieces[: parts // 2], pieces[parts // 2 :]

    def send(half):
        out_ref = (first_ref, second_ref)[half]
        return pltpu.make_async_copy(value_ref.at[half, pl.ds(0, grad_rows)], out_ref, sems.at[half])

    def start_copy(half):
        pl.when(half == 0)(lambda: send(0).start())
        pl.when(half != 0)(lambda: send(1).start())

    fill(core, mine)
    start_copy(core)
    fill(1 - core, other)
    start_copy(1 - core)
    rows = width // 2
    extra = value_ref[0, grad_rows : grad_rows + rows, :]
    for side in range(2):
        head_ref[:, side * rows : (side + 1) * rows] = extra[:, side * LANES : (side + 1) * LANES].T[: head_ref.shape[0]]
    lane = iota(extra.shape, 1)
    loss = jnp.sum(jnp.where((lane == 64) | (lane == 65), extra, 0.0), keepdims=True)
    loss_ref[...] = loss / cell_total
    send(0).wait()
    send(1).wait()


def assemble(place, pieces, plan, grad_rows, classes, cell_total):
    chips, groups, near_rows, far_rows = plan
    half_rows = chips * groups * (near_rows + far_rows)
    width = pieces[0].shape[1]
    shape = jax.ShapeDtypeStruct
    return pl.pallas_call(
        functools.partial(assemble_kernel, width, plan, cell_total),
        in_specs=[scalars(), *whole(len(pieces))],
        out_specs=[*hbm(2), *whole(2)],
        out_shape=[
            shape((grad_rows, width), F32),
            shape((grad_rows, width), F32),
            shape((classes, width), F32),
            shape((1, 1), F32),
        ],
        scratch_shapes=[pltpu.VMEM((2, half_rows, width), F32), pltpu.SemaphoreType.DMA((2,))],
        compiler_params=pltpu.CompilerParams(vmem_limit_bytes=48 << 20),
        cost_estimate=pl.CostEstimate(flops=1_000_000, bytes_accessed=7_500_000, transcendentals=0),
        name="assemble",
    )(place, *pieces)


def gradient_pieces(place, keep, give, plan):
    chips, groups, near_rows, far_rows = plan
    got = [pairwise(one, "core", 1) for one in give]
    near = [add(pair) for pair in zip(keep[:chips], got[:chips])]
    far = [keep[chips], got[chips]]

    def block(arrays, axis, me, step, rows):
        start = (me ^ step) * rows
        return add([lax.dynamic_slice_in_dim(one, start, rows, axis=0) for one in arrays])

    chip, member = place[CHIP], place[MEMBER]
    far = [block(far, "member", member, step, chips * far_rows) for step in range(groups)]
    near = [near[0]] + [pairwise(near[step], "chip", step) for step in range(1, chips)]
    far = [far[0]] + [pairwise(far[step], "member", step) for step in range(1, groups)]
    near = [block(near, "member", member, step, near_rows) for step in range(groups)]
    far = [block(far, "chip", chip, step, far_rows) for step in range(chips)]
    near = add([near[0]] + [pairwise(near[step], "member", step) for step in range(1, groups)])
    far = add([far[0]] + [pairwise(far[step], "chip", step) for step in range(1, chips)])

    near = jnp.concatenate([near] + [pairwise(near, "member", step) for step in range(1, groups)], axis=0)
    far = jnp.concatenate([far] + [pairwise(far, "chip", step) for step in range(1, chips)], axis=0)
    held = [near] + [pairwise(near, "chip", step) for step in range(1, chips)]
    held += [jnp.concatenate([far] + [pairwise(far, "member", step) for step in range(1, groups)], axis=0)]
    return held + [pairwise(piece, "core", 1) for piece in held]


def body(teacher_logits, coverage, features, labels, first_weight, second_weight, head_weight):
    channels, classes = head_weight.shape
    members, tiles_here, flat_width = teacher_logits.shape
    pixels = flat_width // classes
    edge = math.isqrt(pixels)
    groups = lax.axis_size("member")
    chips = lax.axis_size("chip")
    columns = chips * 2
    tile_axes = ("chip", "core")
    block_tiles = tiles_here // groups
    capacity = max(2, 2 * block_tiles // columns)
    local = features[0]
    lines, width = local.shape[:2]
    cells = lines * width
    cell_total = groups * columns * cells
    column = lax.axis_index(tile_axes)
    place = jnp.stack(
        [
            lax.axis_index("core"),
            lax.axis_index("chip"),
            lax.axis_index("member"),
            lax.axis_index(("member", *tile_axes)),
            column == 0,
            column == columns - 1,
        ]
    ).astype(jnp.int32)
    flat = local.reshape(cells, channels)
    first_rows = first_weight.reshape(3, 3 * channels, channels)
    second_rows = second_weight.reshape(3, 3 * channels, channels)
    head = head_weight.T

    far = teacher_moments(place, teacher_logits, block_tiles, classes, 1)
    got = [pairwise(one, "member", step) for step, one in zip((3, 2), far)]
    near, own, top, bottom = teacher_moments(
        place, teacher_logits, block_tiles, classes, 0, flat, far[0], edge_rows=3 * width
    )
    got += [pairwise(near, "member", 1), own]
    before, after = neighbours(top, bottom, tile_axes)
    label_rows = (
        labels[0].reshape(lines // edge, edge, width // edge, edge).transpose(0, 2, 1, 3).reshape(block_tiles, pixels)
    )
    one, two, log, base, label_sum = student_forward(
        place, before, after, head, label_rows, flat, first_rows, second_rows, width
    )
    cover = coverage.reshape(groups, 1, block_tiles)
    sent = combine(got, cover, place, label_sum, classes, members, columns, capacity)
    received = [sent[0]] + [pairwise(sent[step], tile_axes, step) for step in range(1, columns)]
    xt, ht, twot, wt = turn(before, flat, after, one, two, second_rows, sent[0], width)
    grad_two, top, bottom, head_grad = head_step(
        received, log, base, label_sum, two, twot, head, 1.0 / math.sqrt(cell_total), width
    )
    grad_before, grad_after = neighbours(top, bottom, tile_axes)
    second = second_step(ht, grad_two, width)
    rows, extra_rows = 9 * channels, channels // 2
    unit = 8 * groups * chips
    block_rows = -(-(rows + extra_rows) // unit) * 8
    far_rows = block_rows // 24 * 8
    plan = (chips, groups, block_rows - far_rows, far_rows)
    keep, give = first_step(
        place, grad_before, grad_after, grad_two, head_grad, second, wt, one, xt, width, plan
    )
    pieces = gradient_pieces(place, keep, give, plan)
    first_total, second_total, head_total, loss = assemble(
        place, pieces, plan, rows, classes, cell_total
    )
    kernel_shape = (3, 3, channels, channels)
    return (first_total.reshape(kernel_shape), second_total.reshape(kernel_shape), head_total.T, loss[0, 0])


def solution(mesh):
    groups, columns = mesh.shape["member"], mesh.shape["tile"]
    split = jax.sharding.Mesh(mesh.devices.reshape(groups, columns // 2, 2), ("member", "chip", "core"))
    tile = ("chip", "core")
    return jax.shard_map(
        body,
        mesh=split,
        in_specs=(
            P("member", tile, None),
            P(tile),
            P("member", tile, None, None),
            P("member", tile, None),
            P(),
            P(),
            P(),
        ),
        out_specs=(P(), P(), P(), P()),
        check_vma=False,
    )
```

```python
import functools
import math

import jax
import jax.numpy as jnp
from jax import lax
from jax.experimental import pallas as pl
from jax.experimental.pallas import tpu as pltpu
from jax.sharding import PartitionSpec as P

BF16 = jnp.bfloat16
F32 = jnp.float32
LANES = 128
MXU = 256


def whole(count):
    return [pl.BlockSpec(memory_space=pltpu.VMEM)] * count


def iota(shape, axis):
    return lax.broadcasted_iota(jnp.int32, shape, axis)


def dot(left, right):
    return jnp.dot(left, right, preferred_element_type=F32)


def split_lanes(value):
    high = value.astype(BF16).astype(F32)
    return jnp.where(iota(value.shape, 1) < 64, high, value - high).astype(BF16)


def join_lanes(value):
    return value + pltpu.roll(value, 64, 1)


def class_sums(value, classes):
    pick = (iota((MXU, LANES), 0) // classes == iota((MXU, LANES), 1) % (MXU // classes)).astype(BF16)
    high = value.astype(BF16)
    low = (value - high.astype(F32)).astype(BF16)
    return dot(high, pick) + dot(low, pick)


def hbm(count):
    return [pl.BlockSpec(memory_space=pl.ANY)] * count


def scalars():
    return pl.BlockSpec(memory_space=pltpu.SMEM)


CORE, CHIP, MEMBER, DEVICE, FIRST, LAST = range(6)


def teacher_kernel(classes, flip, place_ref, logit_hbm, *refs):
    near_ref, own_ref, x_ref, sum_ref, acc_ref, sems = refs[-6:]
    quarters, members, tiles, width = x_ref.shape
    parts = width // MXU
    per = MXU // classes
    tile_rows = pl.ds(pl.multiple_of(((place_ref[MEMBER] // 2) ^ flip) * tiles, tiles), tiles)
    arrive = [
        pltpu.make_async_copy(logit_hbm.at[:, tile_rows, pl.ds(i * width, width)], x_ref.at[i], sems.at[i])
        for i in range(quarters)
    ]
    for copy in arrive:
        copy.start()
    same = (iota((MXU, MXU), 0) // classes == iota((MXU, MXU), 1) // classes).astype(BF16)
    acc_ref[...] = jnp.zeros_like(acc_ref)

    @pl.loop(0, quarters)
    def _(i):
        pltpu.make_async_copy(logit_hbm.at[:, tile_rows, pl.ds(0, width)], x_ref.at[i], sems.at[i]).wait()
        each = range(parts)
        x = [x_ref[i, :, :, n * MXU : (n + 1) * MXU].astype(F32).reshape(members * tiles, MXU) for n in each]
        root = [jnp.exp(one * 0.25) for one in x]
        total = [dot(one.astype(BF16), same) for one in root]
        root = [one * pl.reciprocal(whole_sum, approx=True) for one, whole_sum in zip(root, total)]
        square = [one * one for one in root]
        power = [one * one for one in square]
        total = [dot(one.astype(BF16), same) for one in power]
        inverse = [pl.reciprocal(one, approx=True) for one in total]
        inverse = [one * (2.0 - whole_sum * one) for one, whole_sum in zip(inverse, total)]
        probs = [(one * other).reshape(members, tiles, MXU) for one, other in zip(power, inverse)]
        first = [functools.reduce(jnp.add, [one[m] for m in range(members)]) for one in probs]
        within = [
            functools.reduce(jnp.add, [one[m] * one[m] for m in range(members)]) - sums * sums * (1.0 / members)
            for one, sums in zip(probs, first)
        ]
        sums = [class_sums(one, classes) for one in within]
        acc = acc_ref[...]
        for n in each:
            acc = jnp.where(iota(acc.shape, 1) % 64 // per == i * parts + n, sums[n], acc)
        acc_ref[...] = acc
        for n in each:
            sum_ref[:, pl.ds(pl.multiple_of(i * width + n * MXU, MXU), MXU)] = first[n].astype(BF16)

    sum_ref[:, quarters * width :] = split_lanes(acc_ref[...])
    block = tiles // 2
    odd = 1 - place_ref[MEMBER] % 2
    near_ref[...] = sum_ref[pl.ds(pl.multiple_of(odd * block, 16), block), :]
    own_ref[...] = sum_ref[pl.ds(pl.multiple_of((1 - odd) * block, 16), block), :]


def teacher_moments(place, logits, tiles, classes, flip, *earlier):
    members, _, width = logits.shape
    quarters = 4
    shape = jax.ShapeDtypeStruct
    outs = [shape((tiles, width + LANES), BF16)] * 2
    return pl.pallas_call(
        functools.partial(teacher_kernel, classes, flip),
        in_specs=[scalars(), *hbm(1 + len(earlier))],
        out_specs=whole(len(outs)),
        out_shape=outs,
        scratch_shapes=[
            pltpu.VMEM((quarters, members, 2 * tiles, width // quarters), BF16),
            pltpu.VMEM((2 * tiles, width + LANES), BF16),
            pltpu.VMEM((2 * tiles, LANES), F32),
            pltpu.SemaphoreType.DMA((quarters,)),
        ],
        compiler_params=pltpu.CompilerParams(vmem_limit_bytes=58 << 20),
        cost_estimate=pl.CostEstimate(flops=1_500_000_000, bytes_accessed=2_600_000, transcendentals=3_000_000),
        name="teacher_moments",
    )(place, logits, *earlier)


def combine_kernel(classes, members, columns, capacity, where_ref, cover_ref, after_ref, *refs):
    got_refs, out_refs = refs[:-columns], refs[-columns:]
    groups = len(got_refs)
    tiles, extended = got_refs[0].shape
    width = extended - LANES
    means, gaps = [], []
    for start in range(0, width, MXU):
        sums = [got_ref[:, start : start + MXU].astype(F32) for got_ref in got_refs]
        total = sums[0]
        for one in sums[1:]:
            total = total + one
        mean = total * (1.0 / (members * groups))
        means.append(mean.astype(BF16))
        gap = jnp.zeros_like(mean)
        for one in sums:
            off = one * (1.0 / members) - mean
            gap = gap + off * off
        gaps.append(gap)
    between = class_sums(jnp.concatenate(gaps, axis=0), classes)
    lane = iota((tiles, LANES), 1)
    spread = jnp.zeros((tiles, LANES), F32)
    per = MXU // classes
    for i in range(width // MXU):
        spread = jnp.where(lane % 64 // per == i, between[i * tiles : (i + 1) * tiles], spread)
    inner = got_refs[0][:, width:].astype(F32)
    for got_ref in got_refs[1:]:
        inner = inner + got_ref[:, width:].astype(F32)
    spread = spread * (1.0 / groups) + join_lanes(inner) * (1.0 / (members * groups))
    index = (iota((tiles, LANES), 0) + 1).astype(F32).astype(BF16)
    rows = jnp.concatenate([*means, split_lanes(spread), index], axis=1)
    target = cover_ref[where_ref[MEMBER]] ^ (where_ref[CHIP] * 2 + where_ref[CORE])
    onehot = (iota((columns, tiles), 0) == target).astype(F32)
    earlier = (iota((tiles, tiles), 0) < iota((tiles, tiles), 1)).astype(BF16)
    before = dot(onehot.astype(BF16), earlier)
    rank = jnp.sum(before * onehot, axis=0, keepdims=True).astype(jnp.int32)
    place = (iota((columns * capacity, tiles), 0) == target * capacity + rank).astype(BF16)
    sent = dot(place, rows)
    for index, out_ref in enumerate(out_refs):
        out_ref[...] = sent[index * capacity : (index + 1) * capacity].astype(BF16)


def combine(got, cover, where, after, classes, members, columns, capacity):
    extended = got[0].shape[1]
    return pl.pallas_call(
        functools.partial(combine_kernel, classes, members, columns, capacity),
        in_specs=[pl.BlockSpec(memory_space=pltpu.SMEM), *whole(1), pl.BlockSpec(memory_space=pl.ANY), *whole(len(got))],
        out_specs=whole(columns),
        out_shape=[jax.ShapeDtypeStruct((capacity, extended + LANES), BF16)] * columns,
        compiler_params=pltpu.CompilerParams(vmem_limit_bytes=12 << 20),
        cost_estimate=pl.CostEstimate(flops=100_000_000, bytes_accessed=1_700_000, transcendentals=0),
        name="combine",
    )(where, cover, after, *got)


def put_shifted(ref, start, value, shift, width):
    rows, channels = value.shape
    col = iota(value.shape, 0) % width
    left = jnp.where(col >= shift, pltpu.roll(value, shift, 0), 0.0)
    right = jnp.where(col < width - shift, pltpu.roll(value, rows - shift, 0), 0.0)
    ref[pl.ds(start, rows), :channels] = left.astype(BF16)
    ref[pl.ds(start, rows), channels : 2 * channels] = value.astype(BF16)
    ref[pl.ds(start, rows), 2 * channels :] = right.astype(BF16)


def three_dots(ref, start, step, rows, weight_ref):
    total = None
    for tap in range(3):
        part = dot(ref[pl.ds(start + tap * step, rows), :], weight_ref[tap])
        total = part if total is None else total + part
    return total


def turned_dot(left, right):
    return lax.dot_general(left, right, (((1,), (1,)), ((), ())), preferred_element_type=F32)


def turned_dot(left, right):
    return lax.dot_general(left, right, (((1,), (1,)), ((), ())), preferred_element_type=F32)


def student_kernel(
    width, place_ref, before_ref, after_ref, head_ref, label_ref, x_ref, first_ref, second_ref, own_ref,
    one_ref, two_ref, log_ref, base_ref, label_sum_ref, xcat, hcat, logit_ref,
):
    cells, channels = x_ref.shape
    halo = before_ref.shape[0]
    block = 4 * width
    put_shifted(xcat, 0, before_ref[...].astype(F32), 1, width)
    put_shifted(xcat, halo + cells, after_ref[...].astype(F32), 1, width)
    for start in range(0, cells, block):
        put_shifted(xcat, halo + start, x_ref[start : start + block, :].astype(F32), 1, width)
    lines = cells // width
    low = jnp.where(place_ref[FIRST] == 1, 2, 0)
    high = jnp.where(place_ref[LAST] == 1, lines + 2, lines + 4)
    for start in range(0, cells + block, block):
        value = jnp.maximum(three_dots(xcat, start, width, block, first_ref), 0.0)
        if start == 0 or start == cells:
            line = start // width + iota(value.shape, 0) // width
            value = jnp.where((line >= low) & (line < high), value, 0.0)
        put_shifted(hcat, start, value, 2, width)
        one_ref[start : start + block, :] = value.astype(BF16)
    head = jnp.concatenate([head_ref[...], head_ref[...]], axis=0)
    for start in range(0, cells, block):
        rows = slice(start, start + block)
        two = jnp.maximum(three_dots(hcat, start, 2 * width, block, second_ref), 0.0).astype(BF16)
        two_ref[rows, :] = two
        logit_ref[rows, :] = turned_dot(two, head)

    tiles, pixels = label_ref.shape
    edge = math.isqrt(pixels)
    across = width // edge
    lane = iota((tiles, LANES), 1)
    even = lane < 64
    label_sum = jnp.zeros((tiles, LANES), F32)
    for pair in range(pixels // 2):
        row, col = 2 * pair // edge, 2 * pair % edge
        parts = []
        for down in range(tiles // across):
            start = (down * edge + row) * width + col
            left = logit_ref[pl.ds(start, across, stride=edge), :]
            right = logit_ref[pl.ds(start + 1, across, stride=edge), :]
            parts.append(jnp.where(iota(left.shape, 1) < 64, left, right))
        value = jnp.concatenate(parts, axis=0)
        top = jnp.where(
            even,
            jnp.max(jnp.where(even, value, -jnp.inf), axis=1, keepdims=True),
            jnp.max(jnp.where(even, -jnp.inf, value), axis=1, keepdims=True),
        )
        value = value - top
        power = jnp.exp(value)
        total = jnp.where(
            even,
            jnp.sum(jnp.where(even, power, 0.0), axis=1, keepdims=True),
            jnp.sum(jnp.where(even, 0.0, power), axis=1, keepdims=True),
        )
        value = value - jnp.log(total)
        label = jnp.where(even, label_ref[:, 2 * pair : 2 * pair + 1], label_ref[:, 2 * pair + 1 : 2 * pair + 2])
        hit = label == lane % 64
        label_sum = label_sum + jnp.where(hit, value, 0.0)
        log_ref[pair * tiles : (pair + 1) * tiles, :] = value
        base_ref[pair * tiles : (pair + 1) * tiles, :] = jnp.exp(value) - hit.astype(F32)
    label_sum_ref[...] = label_sum


def student_forward(place, before, after, head, labels, x, first, second, own, width):
    cells, channels = x.shape
    halo = before.shape[0]
    tiles, pixels = labels.shape
    shape = jax.ShapeDtypeStruct
    return pl.pallas_call(
        functools.partial(student_kernel, width),
        in_specs=[scalars(), *whole(7), *hbm(1)],
        out_specs=whole(5),
        out_shape=[
            shape((cells + 4 * width, channels), BF16),
            shape((cells, channels), BF16),
            shape((cells // 2, LANES), F32),
            shape((cells // 2, LANES), F32),
            shape((tiles, LANES), F32),
        ],
        scratch_shapes=[
            pltpu.VMEM((cells + 2 * halo, 3 * channels), BF16),
            pltpu.VMEM((cells + 4 * width, 3 * channels), BF16),
            pltpu.VMEM((cells, LANES), F32),
        ],
        compiler_params=pltpu.CompilerParams(vmem_limit_bytes=24 << 20),
        cost_estimate=pl.CostEstimate(flops=6_000_000_000, bytes_accessed=12_000_000, transcendentals=500_000),
        name="student_forward",
    )(place, before, after, head, labels, x, first, second, own)


def put_turned(ref, start, value, shift, width):
    rows, channels = value.shape
    col = iota(value.shape, 0) % width
    left = jnp.where(col >= shift, pltpu.roll(value, shift, 0), 0.0)
    right = jnp.where(col < width - shift, pltpu.roll(value, rows - shift, 0), 0.0)
    for tap, one in enumerate((left, value, right)):
        ref[tap * channels : (tap + 1) * channels, pl.ds(start, rows)] = one.T.astype(BF16)


def turn_kernel(
    width, before_ref, x_ref, after_ref, one_ref, two_ref, second_ref, sent_ref, xt_ref, ht_ref, twot_ref, wt_ref
):
    cells, channels = x_ref.shape
    halo = before_ref.shape[0]
    pair = 2 * width
    first = jnp.concatenate([before_ref[halo - width :], x_ref[:width]], axis=0).astype(F32)
    put_turned(xt_ref, 0, first, 1, width)
    last = jnp.concatenate([x_ref[cells - width :], after_ref[:width]], axis=0).astype(F32)
    put_turned(xt_ref, cells, last, 1, width)

    for start in range(pair, cells, pair):
        put_turned(xt_ref, start, x_ref[start - width : start + width, :].astype(F32), 1, width)
    for start in range(0, one_ref.shape[0], pair):
        put_turned(ht_ref, start, one_ref[start : start + pair, :].astype(F32), 2, width)
    for start in range(0, cells, MXU):
        twot_ref[:, start : start + MXU] = two_ref[start : start + MXU, :].astype(F32).T.astype(BF16)
    for i in range(3):
        for tap in range(3):
            part = slice(tap * channels, (tap + 1) * channels)
            mirror = slice((2 - tap) * channels, (3 - tap) * channels)
            wt_ref[i, part, :] = second_ref[i, mirror, :].astype(F32).T.astype(BF16)


def turn(before, x, after, one, two, second, sent, width):
    cells, channels = x.shape
    shape = jax.ShapeDtypeStruct
    return pl.pallas_call(
        functools.partial(turn_kernel, width),
        in_specs=[*whole(6), pl.BlockSpec(memory_space=pl.ANY)],
        out_specs=whole(4),
        out_shape=[
            shape((3 * channels, cells + 2 * width), BF16),
            shape((3 * channels, cells + 4 * width), BF16),
            shape((channels, cells), BF16),
            shape((3, 3 * channels, channels), BF16),
        ],
        compiler_params=pltpu.CompilerParams(vmem_limit_bytes=20 << 20),
        cost_estimate=pl.CostEstimate(flops=3_000_000_000, bytes_accessed=14_000_000, transcendentals=0),
        name="turn",
    )(before, x, after, one, two, second, sent)


def head_kernel(
    scale, width, log_ref, base_ref, label_sum_ref, two_ref, twot_ref, head_ref, *refs
):
    *got_refs, grad_ref, top_ref, bottom_ref, head_grad_ref, got_ref, natural = refs
    slots, extended = got_ref.shape
    got_ref[...] = jnp.concatenate([one[...].astype(F32) for one in got_refs], axis=0).astype(BF16)
    tiles = label_sum_ref.shape[0]
    flat = extended - 2 * LANES
    pixels = flat // 64
    edge = math.isqrt(pixels)
    across = width // edge
    index = got_ref[:, flat + LANES :].astype(F32)
    take = (index == (iota((slots, LANES), 1) + 1).astype(F32)).astype(F32).T[:tiles].astype(BF16)
    spread = join_lanes(dot(take, got_ref[:, flat : flat + LANES]))
    weight = 1.0 / (0.1 + spread)
    even = iota((tiles, LANES), 1) < 64
    loss = -label_sum_ref[...]
    for pair in range(pixels // 2):
        rows = slice(pair * tiles, (pair + 1) * tiles)
        if pair % 2 == 0:
            both = dot(take, got_ref[:, pair * LANES : (pair + 2) * LANES])
        mean = both[:, pair % 2 * LANES : (pair % 2 + 1) * LANES]
        cell = jnp.where(even, weight[:, 2 * pair : 2 * pair + 1], weight[:, 2 * pair + 1 : 2 * pair + 2])
        value = log_ref[rows, :]
        held = mean > 0
        loss = loss + cell * jnp.where(held, mean * (jnp.log(jnp.where(held, mean, 1.0)) - value), 0.0)
        grad = (cell * (jnp.exp(value) - mean) + base_ref[rows, :]) * scale
        turned = pltpu.roll(grad, 64, 1)
        row, col = 2 * pair // edge, 2 * pair % edge
        for down in range(tiles // across):
            start = (down * edge + row) * width + col
            natural[pl.ds(start, across, stride=edge), :] = grad[down * across : (down + 1) * across]
            natural[pl.ds(start + 1, across, stride=edge), :] = turned[down * across : (down + 1) * across]
    cells, channels = two_ref.shape
    logit_grad = natural[...].astype(BF16)
    head = jnp.concatenate([head_ref[...], jnp.zeros_like(head_ref)], axis=0)
    head_grad_ref[:channels, :] = dot(twot_ref[...], logit_grad)
    head_grad_ref[channels:, :] = loss
    block = 4 * width
    for start in range(0, cells, block):
        rows = slice(start, start + block)
        grad = dot(logit_grad[rows], head)
        grad_ref[rows, :] = jnp.where(two_ref[rows, :].astype(F32) > 0, grad, 0.0).astype(BF16)
    top_ref[...] = grad_ref[: 2 * width, :]
    bottom_ref[...] = grad_ref[cells - 2 * width :, :]


def head_step(got, log, base, label_sum, two, twot, head, scale, width):
    cells, channels = two.shape
    shape = jax.ShapeDtypeStruct
    return pl.pallas_call(
        functools.partial(head_kernel, scale, width),
        in_specs=whole(6 + len(got)),
        out_specs=whole(4),
        out_shape=[
            shape((cells, channels), BF16),
            shape((2 * width, channels), BF16),
            shape((2 * width, channels), BF16),
            shape((channels + label_sum.shape[0], LANES), F32),
        ],
        scratch_shapes=[
            pltpu.VMEM((len(got) * got[0].shape[0], got[0].shape[1]), BF16),
            pltpu.VMEM((cells, LANES), F32),
        ],
        compiler_params=pltpu.CompilerParams(vmem_limit_bytes=14 << 20),
        cost_estimate=pl.CostEstimate(flops=400_000_000, bytes_accessed=5_000_000, transcendentals=500_000),
        name="head_step",
    )(log, base, label_sum, two, twot, head, *got)


def inner_dots(ref, start, step, rows, weight_ref):
    total = None
    for tap in range(3):
        part = dot(ref[start + (2 - tap) * step : start + (2 - tap) * step + rows, :], weight_ref[tap])
        total = part if total is None else total + part
    return total


def second_kernel(width, ht_ref, grad_ref, wt_ref, one_ref, out_ref, inner_ref, gcat):
    cells, channels = grad_ref.shape
    block = 4 * width
    halo = 2 * width
    for start in range(0, cells, block):
        put_shifted(gcat, start, grad_ref[start : start + block, :].astype(F32), 2, width)
    for tap in range(3):
        part = dot(ht_ref[:, halo * tap : halo * tap + cells], grad_ref[...])
        out_ref[tap * 3 * channels : (tap + 1) * 3 * channels, :] = part.astype(BF16)
    for start in range(block, cells - block, block):
        value = inner_dots(gcat, start - halo, halo, block, wt_ref)
        held = one_ref[halo + start : halo + start + block, :].astype(F32) > 0
        inner_ref[start - block : start, :] = jnp.where(held, value, 0.0).astype(BF16)


def second_step(ht, grad, wt, one, width):
    cells, channels = grad.shape
    return pl.pallas_call(
        functools.partial(second_kernel, width),
        in_specs=whole(4),
        out_specs=whole(2),
        out_shape=[
            jax.ShapeDtypeStruct((9 * channels, channels), BF16),
            jax.ShapeDtypeStruct((cells - 8 * width, channels), BF16),
        ],
        scratch_shapes=[pltpu.VMEM((cells, 3 * channels), BF16)],
        compiler_params=pltpu.CompilerParams(vmem_limit_bytes=20 << 20),
        cost_estimate=pl.CostEstimate(flops=4_500_000_000, bytes_accessed=9_000_000, transcendentals=0),
        name="second_step",
    )(ht, grad, wt, one)


def first_kernel(width, plan, place_ref, before_ref, after_ref, grad_ref, head_grad_ref, second_ref, inner_ref, *refs):
    wt_ref, one_ref, xt_ref, *refs = refs
    chips, groups, near_rows, far_rows = plan
    keep_refs, give_refs, refs = refs[: chips + 1], refs[chips + 1 : 2 * chips + 2], refs[2 * chips + 2 :]
    gtop, gbottom, padded, halves, sem = refs
    cells, channels = grad_ref.shape
    rows = 9 * channels
    used = rows + channels // 2
    half = halves.shape[1]
    second_copy = pltpu.make_async_copy(second_ref, halves.at[1, pl.ds(0, rows)], sem)
    second_copy.start()
    halo = before_ref.shape[0]
    block = 4 * width
    inside = 3 * halo
    put_shifted(gtop, 0, before_ref[...].astype(F32), 2, width)
    put_shifted(gtop, halo, grad_ref[:inside, :].astype(F32), 2, width)
    put_shifted(gbottom, 0, grad_ref[cells - inside :, :].astype(F32), 2, width)
    put_shifted(gbottom, inside, after_ref[...].astype(F32), 2, width)
    padded[:halo, :] = jnp.zeros((halo, channels), BF16)
    padded[halo + cells :, :] = jnp.zeros((halo, channels), BF16)
    padded[halo + block : halo + cells - block, :] = inner_ref[...]
    for ref, start in ((gtop, 0), (gbottom, cells - block)):
        value = inner_dots(ref, 0, halo, block, wt_ref)
        held = one_ref[halo + start : halo + start + block, :].astype(F32) > 0
        padded[halo + start : halo + start + block, :] = jnp.where(held, value, 0.0).astype(BF16)
    span = cells + 2 * width
    for tap in range(3):
        part = dot(xt_ref[...], padded[(2 - tap) * width : (2 - tap) * width + span, :])
        halves[0, tap * 3 * channels : (tap + 1) * 3 * channels, :] = part.astype(BF16)
    lane = iota((channels // 2, LANES), 1)
    loss = jnp.sum(head_grad_ref[channels:, :])
    high = loss.astype(BF16).astype(F32)
    extra = jnp.where(lane == 64, high, jnp.where(lane == 65, loss - high, 0.0))
    extra = jnp.where(iota(lane.shape, 0) == place_ref[DEVICE] % (channels // 2), extra, 0.0)
    for side in range(2):
        value = jnp.where(lane < 64, head_grad_ref[side * channels // 2 : (side + 1) * channels // 2, :], extra)
        halves[0, rows:used, side * LANES : (side + 1) * LANES] = value.astype(BF16)
    if half > used:
        halves[0, used:, :] = jnp.zeros((half - used, channels), BF16)
    halves[1, rows:, :] = jnp.zeros((half - rows, channels), BF16)
    second_copy.wait()
    core, chip = place_ref[CORE], place_ref[CHIP]
    size = groups * near_rows
    for step in range(chips):
        low = pl.multiple_of((chip ^ step) * size, 16)
        give_refs[step][...] = halves[1 - core, pl.ds(low, size), :]
        keep_refs[step][...] = halves[core, pl.ds(low, size), :]
    give_refs[chips][...] = halves[1 - core, chips * size :, :]
    keep_refs[chips][...] = halves[core, chips * size :, :]


def first_step(place, before, after, grad, head_grad, second, inner, wt, one, xt, width, plan):
    cells, channels = grad.shape
    halo = before.shape[0]
    chips, groups, near_rows, far_rows = plan
    half_rows = chips * groups * (near_rows + far_rows)
    piece = [jax.ShapeDtypeStruct((groups * near_rows, channels), BF16)] * chips
    piece += [jax.ShapeDtypeStruct((chips * groups * far_rows, channels), BF16)]
    outs = pl.pallas_call(
        functools.partial(first_kernel, width, plan),
        in_specs=[scalars(), *whole(9)],
        out_specs=whole(2 * chips + 2),
        out_shape=piece * 2,
        scratch_shapes=[
            pltpu.VMEM((4 * halo, 3 * channels), BF16),
            pltpu.VMEM((4 * halo, 3 * channels), BF16),
            pltpu.VMEM((cells + 4 * width, channels), BF16),
            pltpu.VMEM((2, half_rows, channels), BF16),
            pltpu.SemaphoreType.DMA,
        ],
        compiler_params=pltpu.CompilerParams(vmem_limit_bytes=24 << 20),
        cost_estimate=pl.CostEstimate(flops=5_000_000_000, bytes_accessed=10_000_000, transcendentals=0),
        name="first_step",
    )(place, before, after, grad, head_grad, second, inner, wt, one, xt)
    return (outs[: chips + 1], outs[chips + 1 :])


def neighbours(first, last, axis):
    count = lax.axis_size(axis)
    up = [(i, i + 1) for i in range(count - 1)]
    down = [(i + 1, i) for i in range(count - 1)]
    return (lax.ppermute(last, axis, up), lax.ppermute(first, axis, down))


def pairwise(array, axis, step):
    count = lax.axis_size(axis)
    return lax.ppermute(array, axis, [(i, i ^ step) for i in range(count)])


def add(arrays):
    return functools.reduce(jnp.add, [array.astype(F32) for array in arrays]).astype(BF16)


def assemble_kernel(width, plan, cell_total, place_ref, *refs):
    chips, groups, near_rows, far_rows = plan
    parts = len(refs) - 6
    pieces, refs = refs[:parts], refs[parts:]
    first_ref, second_ref, head_ref, loss_ref, value_ref, sems = refs
    grad_rows = first_ref.shape[0]
    core, chip, member = place_ref[CORE], place_ref[CHIP], place_ref[MEMBER]

    def fill(half, source):
        for s in range(chips):
            value = source[s][...].astype(F32)
            for u in range(groups):
                start = pl.multiple_of(((chip ^ s) * groups + (member ^ u)) * near_rows, 8)
                value_ref[half, pl.ds(start, near_rows), :] = value[u * near_rows : (u + 1) * near_rows]
        value = source[chips][...].astype(F32)
        for u in range(groups):
            for s in range(chips):
                low = (u * chips + s) * far_rows
                start = chips * groups * near_rows + ((member ^ u) * chips + (chip ^ s)) * far_rows
                value_ref[half, pl.ds(pl.multiple_of(start, 8), far_rows), :] = value[low : low + far_rows]

    mine, other = pieces[: parts // 2], pieces[parts // 2 :]

    def send(half):
        out_ref = (first_ref, second_ref)[half]
        return pltpu.make_async_copy(value_ref.at[half, pl.ds(0, grad_rows)], out_ref, sems.at[half])

    def start_copy(half):
        pl.when(half == 0)(lambda: send(0).start())
        pl.when(half != 0)(lambda: send(1).start())

    fill(core, mine)
    start_copy(core)
    fill(1 - core, other)
    start_copy(1 - core)
    rows = width // 2
    extra = value_ref[0, grad_rows : grad_rows + rows, :]
    for side in range(2):
        head_ref[:, side * rows : (side + 1) * rows] = extra[:, side * LANES : (side + 1) * LANES].T[: head_ref.shape[0]]
    lane = iota(extra.shape, 1)
    loss = jnp.sum(jnp.where((lane == 64) | (lane == 65), extra, 0.0), keepdims=True)
    loss_ref[...] = loss / cell_total
    send(0).wait()
    send(1).wait()


def assemble(place, pieces, plan, grad_rows, classes, cell_total):
    chips, groups, near_rows, far_rows = plan
    half_rows = chips * groups * (near_rows + far_rows)
    width = pieces[0].shape[1]
    shape = jax.ShapeDtypeStruct
    return pl.pallas_call(
        functools.partial(assemble_kernel, width, plan, cell_total),
        in_specs=[scalars(), *whole(len(pieces))],
        out_specs=[*hbm(2), *whole(2)],
        out_shape=[
            shape((grad_rows, width), F32),
            shape((grad_rows, width), F32),
            shape((classes, width), F32),
            shape((1, 1), F32),
        ],
        scratch_shapes=[pltpu.VMEM((2, half_rows, width), F32), pltpu.SemaphoreType.DMA((2,))],
        compiler_params=pltpu.CompilerParams(vmem_limit_bytes=48 << 20),
        cost_estimate=pl.CostEstimate(flops=1_000_000, bytes_accessed=7_500_000, transcendentals=0),
        name="assemble",
    )(place, *pieces)


def gradient_pieces(place, keep, give, plan):
    chips, groups, near_rows, far_rows = plan
    got = [pairwise(one, "core", 1) for one in give]
    near = [add(pair) for pair in zip(keep[:chips], got[:chips])]
    far = [keep[chips], got[chips]]

    def block(arrays, axis, me, step, rows):
        start = (me ^ step) * rows
        return add([lax.dynamic_slice_in_dim(one, start, rows, axis=0) for one in arrays])

    chip, member = place[CHIP], place[MEMBER]
    far = [block(far, "member", member, step, chips * far_rows) for step in range(groups)]
    near = [near[0]] + [pairwise(near[step], "chip", step) for step in range(1, chips)]
    far = [far[0]] + [pairwise(far[step], "member", step) for step in range(1, groups)]
    near = [block(near, "member", member, step, near_rows) for step in range(groups)]
    far = [block(far, "chip", chip, step, far_rows) for step in range(chips)]
    near = add([near[0]] + [pairwise(near[step], "member", step) for step in range(1, groups)])
    far = add([far[0]] + [pairwise(far[step], "chip", step) for step in range(1, chips)])

    near = jnp.concatenate([near] + [pairwise(near, "member", step) for step in range(1, groups)], axis=0)
    far = jnp.concatenate([far] + [pairwise(far, "chip", step) for step in range(1, chips)], axis=0)
    held = [near] + [pairwise(near, "chip", step) for step in range(1, chips)]
    far = jnp.concatenate([far] + [pairwise(far, "member", step) for step in range(1, groups)], axis=0)
    other = [pairwise(piece, "core", 1) for piece in held]
    far, *other = lax.optimization_barrier((far, *other))
    return held + [far] + other + [pairwise(far, "core", 1)]


def body(teacher_logits, coverage, features, labels, first_weight, second_weight, head_weight):
    channels, classes = head_weight.shape
    members, tiles_here, flat_width = teacher_logits.shape
    pixels = flat_width // classes
    edge = math.isqrt(pixels)
    groups = lax.axis_size("member")
    chips = lax.axis_size("chip")
    columns = chips * 2
    tile_axes = ("chip", "core")
    block_tiles = tiles_here // groups
    capacity = max(2, 2 * block_tiles // columns)
    local = features[0]
    lines, width = local.shape[:2]
    cells = lines * width
    cell_total = groups * columns * cells
    column = lax.axis_index(tile_axes)
    place = jnp.stack(
        [
            lax.axis_index("core"),
            lax.axis_index("chip"),
            lax.axis_index("member"),
            lax.axis_index(("member", *tile_axes)),
            column == 0,
            column == columns - 1,
        ]
    ).astype(jnp.int32)
    flat = local.reshape(cells, channels)
    first_rows = first_weight.reshape(3, 3 * channels, channels)
    second_rows = second_weight.reshape(3, 3 * channels, channels)
    head = head_weight.T

    before, after = neighbours(flat[: 3 * width], flat[cells - 3 * width :], tile_axes)
    far = teacher_moments(place, teacher_logits, block_tiles, classes, 1)
    got = [pairwise(one, "member", step) for step, one in zip((3, 2), far)]
    near, own = teacher_moments(place, teacher_logits, block_tiles, classes, 0, far[0])
    got += [pairwise(near, "member", 1), own]
    label_rows = (
        labels[0].reshape(lines // edge, edge, width // edge, edge).transpose(0, 2, 1, 3).reshape(block_tiles, pixels)
    )
    one, two, log, base, label_sum = student_forward(
        place, before, after, head, label_rows, flat, first_rows, second_rows, own, width
    )
    cover = coverage.reshape(groups, 1, block_tiles)
    sent = combine(got, cover, place, label_sum, classes, members, columns, capacity)
    received = [sent[0]] + [pairwise(sent[step], tile_axes, step) for step in range(1, columns)]
    xt, ht, twot, wt = turn(before, flat, after, one, two, second_rows, sent[0], width)
    grad_two, top, bottom, head_grad = head_step(
        received, log, base, label_sum, two, twot, head, 1.0 / math.sqrt(cell_total), width
    )
    grad_before, grad_after = neighbours(top, bottom, tile_axes)
    second, inner = second_step(ht, grad_two, wt, one, width)
    rows, extra_rows = 9 * channels, channels // 2
    unit = 8 * groups * chips
    block_rows = -(-(rows + extra_rows) // unit) * 8
    far_rows = block_rows // 24 * 8
    plan = (chips, groups, block_rows - far_rows, far_rows)
    keep, give = first_step(
        place, grad_before, grad_after, grad_two, head_grad, second, inner, wt, one, xt, width, plan
    )
    pieces = gradient_pieces(place, keep, give, plan)
    first_total, second_total, head_total, loss = assemble(
        place, pieces, plan, rows, classes, cell_total
    )
    kernel_shape = (3, 3, channels, channels)
    return (first_total.reshape(kernel_shape), second_total.reshape(kernel_shape), head_total.T, loss[0, 0])


def solution(mesh):
    groups, columns = mesh.shape["member"], mesh.shape["tile"]
    split = jax.sharding.Mesh(mesh.devices.reshape(groups, columns // 2, 2), ("member", "chip", "core"))
    tile = ("chip", "core")
    return jax.shard_map(
        body,
        mesh=split,
        in_specs=(
            P("member", tile, None),
            P(tile),
            P("member", tile, None, None),
            P("member", tile, None),
            P(),
            P(),
            P(),
        ),
        out_specs=(P(), P(), P(), P()),
        check_vma=False,
    )
```

```python
import functools
import math

import jax
import jax.numpy as jnp
from jax import lax
from jax.experimental import pallas as pl
from jax.experimental.pallas import tpu as pltpu
from jax.sharding import PartitionSpec as P

BF16 = jnp.bfloat16
F32 = jnp.float32
LANES = 128
MXU = 256


def whole(count):
    return [pl.BlockSpec(memory_space=pltpu.VMEM)] * count


def iota(shape, axis):
    return lax.broadcasted_iota(jnp.int32, shape, axis)


def dot(left, right):
    return jnp.dot(left, right, preferred_element_type=F32)


def split_lanes(value):
    high = value.astype(BF16).astype(F32)
    return jnp.where(iota(value.shape, 1) < 64, high, value - high).astype(BF16)


def join_lanes(value):
    return value + pltpu.roll(value, 64, 1)


def class_sums(value, classes):
    pick = (iota((MXU, LANES), 0) // classes == iota((MXU, LANES), 1) % (MXU // classes)).astype(BF16)
    high = value.astype(BF16)
    low = (value - high.astype(F32)).astype(BF16)
    return dot(high, pick) + dot(low, pick)


def hbm(count):
    return [pl.BlockSpec(memory_space=pl.ANY)] * count


def scalars():
    return pl.BlockSpec(memory_space=pltpu.SMEM)


CORE, CHIP, MEMBER, DEVICE, FIRST, LAST = range(6)


def teacher_kernel(classes, flip, place_ref, logit_hbm, *refs):
    near_ref, own_ref, x_ref, sum_ref, acc_ref, sems = refs[-6:]
    quarters, members, tiles, width = x_ref.shape
    parts = width // MXU
    per = MXU // classes
    tile_rows = pl.ds(pl.multiple_of(((place_ref[MEMBER] // 2) ^ flip) * tiles, tiles), tiles)
    arrive = [
        pltpu.make_async_copy(logit_hbm.at[:, tile_rows, pl.ds(i * width, width)], x_ref.at[i], sems.at[i])
        for i in range(quarters)
    ]
    for copy in arrive:
        copy.start()
    same = (iota((MXU, MXU), 0) // classes == iota((MXU, MXU), 1) // classes).astype(BF16)
    acc_ref[...] = jnp.zeros_like(acc_ref)

    @pl.loop(0, quarters)
    def _(i):
        pltpu.make_async_copy(logit_hbm.at[:, tile_rows, pl.ds(0, width)], x_ref.at[i], sems.at[i]).wait()
        each = range(parts)
        x = [x_ref[i, :, :, n * MXU : (n + 1) * MXU].astype(F32).reshape(members * tiles, MXU) for n in each]
        root = [jnp.exp(one * 0.25) for one in x]
        total = [dot(one.astype(BF16), same) for one in root]
        root = [one * pl.reciprocal(whole_sum, approx=True) for one, whole_sum in zip(root, total)]
        square = [one * one for one in root]
        power = [one * one for one in square]
        total = [dot(one.astype(BF16), same) for one in power]
        inverse = [pl.reciprocal(one, approx=True) for one in total]
        inverse = [one * (2.0 - whole_sum * one) for one, whole_sum in zip(inverse, total)]
        probs = [(one * other).reshape(members, tiles, MXU) for one, other in zip(power, inverse)]
        first = [functools.reduce(jnp.add, [one[m] for m in range(members)]) for one in probs]
        within = [
            functools.reduce(jnp.add, [one[m] * one[m] for m in range(members)]) - sums * sums * (1.0 / members)
            for one, sums in zip(probs, first)
        ]
        sums = [class_sums(one, classes) for one in within]
        acc = acc_ref[...]
        for n in each:
            acc = jnp.where(iota(acc.shape, 1) % 64 // per == i * parts + n, sums[n], acc)
        acc_ref[...] = acc
        for n in each:
            sum_ref[:, pl.ds(pl.multiple_of(i * width + n * MXU, MXU), MXU)] = first[n].astype(BF16)

    sum_ref[:, quarters * width :] = split_lanes(acc_ref[...])
    block = tiles // 2
    odd = 1 - place_ref[MEMBER] % 2
    near_ref[...] = sum_ref[pl.ds(pl.multiple_of(odd * block, 16), block), :]
    own_ref[...] = sum_ref[pl.ds(pl.multiple_of((1 - odd) * block, 16), block), :]


def teacher_moments(place, logits, tiles, classes, flip, *earlier):
    members, _, width = logits.shape
    quarters = 4
    shape = jax.ShapeDtypeStruct
    outs = [shape((tiles, width + LANES), BF16)] * 2
    return pl.pallas_call(
        functools.partial(teacher_kernel, classes, flip),
        in_specs=[scalars(), *hbm(1 + len(earlier))],
        out_specs=whole(len(outs)),
        out_shape=outs,
        scratch_shapes=[
            pltpu.VMEM((quarters, members, 2 * tiles, width // quarters), BF16),
            pltpu.VMEM((2 * tiles, width + LANES), BF16),
            pltpu.VMEM((2 * tiles, LANES), F32),
            pltpu.SemaphoreType.DMA((quarters,)),
        ],
        compiler_params=pltpu.CompilerParams(vmem_limit_bytes=58 << 20),
        cost_estimate=pl.CostEstimate(flops=1_500_000_000, bytes_accessed=2_600_000, transcendentals=3_000_000),
        name="teacher_moments",
    )(place, logits, *earlier)


def combine_kernel(classes, members, columns, capacity, where_ref, cover_ref, after_ref, *refs):
    got_refs, out_refs = refs[:-columns], refs[-columns:]
    groups = len(got_refs)
    tiles, extended = got_refs[0].shape
    width = extended - LANES
    means, gaps = [], []
    for start in range(0, width, MXU):
        sums = [got_ref[:, start : start + MXU].astype(F32) for got_ref in got_refs]
        total = sums[0]
        for one in sums[1:]:
            total = total + one
        mean = total * (1.0 / (members * groups))
        means.append(mean.astype(BF16))
        gap = jnp.zeros_like(mean)
        for one in sums:
            off = one * (1.0 / members) - mean
            gap = gap + off * off
        gaps.append(gap)
    between = class_sums(jnp.concatenate(gaps, axis=0), classes)
    lane = iota((tiles, LANES), 1)
    spread = jnp.zeros((tiles, LANES), F32)
    per = MXU // classes
    for i in range(width // MXU):
        spread = jnp.where(lane % 64 // per == i, between[i * tiles : (i + 1) * tiles], spread)
    inner = got_refs[0][:, width:].astype(F32)
    for got_ref in got_refs[1:]:
        inner = inner + got_ref[:, width:].astype(F32)
    spread = spread * (1.0 / groups) + join_lanes(inner) * (1.0 / (members * groups))
    index = (iota((tiles, LANES), 0) + 1).astype(F32).astype(BF16)
    rows = jnp.concatenate([*means, split_lanes(spread), index], axis=1)
    target = cover_ref[where_ref[MEMBER]] ^ (where_ref[CHIP] * 2 + where_ref[CORE])
    onehot = (iota((columns, tiles), 0) == target).astype(F32)
    earlier = (iota((tiles, tiles), 0) < iota((tiles, tiles), 1)).astype(BF16)
    before = dot(onehot.astype(BF16), earlier)
    rank = jnp.sum(before * onehot, axis=0, keepdims=True).astype(jnp.int32)
    place = (iota((columns * capacity, tiles), 0) == target * capacity + rank).astype(BF16)
    sent = dot(place, rows)
    for index, out_ref in enumerate(out_refs):
        out_ref[...] = sent[index * capacity : (index + 1) * capacity].astype(BF16)


def combine(got, cover, where, after, classes, members, columns, capacity):
    extended = got[0].shape[1]
    return pl.pallas_call(
        functools.partial(combine_kernel, classes, members, columns, capacity),
        in_specs=[pl.BlockSpec(memory_space=pltpu.SMEM), *whole(1), pl.BlockSpec(memory_space=pl.ANY), *whole(len(got))],
        out_specs=whole(columns),
        out_shape=[jax.ShapeDtypeStruct((capacity, extended + LANES), BF16)] * columns,
        compiler_params=pltpu.CompilerParams(vmem_limit_bytes=12 << 20),
        cost_estimate=pl.CostEstimate(flops=100_000_000, bytes_accessed=1_700_000, transcendentals=0),
        name="combine",
    )(where, cover, after, *got)


def put_shifted(ref, start, value, shift, width):
    rows, channels = value.shape
    col = iota(value.shape, 0) % width
    left = jnp.where(col >= shift, pltpu.roll(value, shift, 0), 0.0)
    right = jnp.where(col < width - shift, pltpu.roll(value, rows - shift, 0), 0.0)
    ref[pl.ds(start, rows), :channels] = left.astype(BF16)
    ref[pl.ds(start, rows), channels : 2 * channels] = value.astype(BF16)
    ref[pl.ds(start, rows), 2 * channels :] = right.astype(BF16)


def three_dots(ref, start, step, rows, weight_ref):
    total = None
    for tap in range(3):
        part = dot(ref[pl.ds(start + tap * step, rows), :], weight_ref[tap])
        total = part if total is None else total + part
    return total


def turned_dot(left, right):
    return lax.dot_general(left, right, (((1,), (1,)), ((), ())), preferred_element_type=F32)


def turned_dot(left, right):
    return lax.dot_general(left, right, (((1,), (1,)), ((), ())), preferred_element_type=F32)


def student_kernel(
    width, place_ref, before_ref, after_ref, head_ref, label_ref, x_ref, first_ref, second_ref, own_ref,
    one_ref, two_ref, log_ref, base_ref, label_sum_ref, xcat, hcat, logit_ref,
):
    cells, channels = x_ref.shape
    halo = before_ref.shape[0]
    block = 4 * width
    put_shifted(xcat, 0, before_ref[...].astype(F32), 1, width)
    put_shifted(xcat, halo + cells, after_ref[...].astype(F32), 1, width)
    for start in range(0, cells, block):
        put_shifted(xcat, halo + start, x_ref[start : start + block, :].astype(F32), 1, width)
    lines = cells // width
    low = jnp.where(place_ref[FIRST] == 1, 2, 0)
    high = jnp.where(place_ref[LAST] == 1, lines + 2, lines + 4)
    for start in range(0, cells + block, block):
        value = jnp.maximum(three_dots(xcat, start, width, block, first_ref), 0.0)
        if start == 0 or start == cells:
            line = start // width + iota(value.shape, 0) // width
            value = jnp.where((line >= low) & (line < high), value, 0.0)
        put_shifted(hcat, start, value, 2, width)
        one_ref[start : start + block, :] = value.astype(BF16)
    head = jnp.concatenate([head_ref[...], head_ref[...]], axis=0)
    for start in range(0, cells, block):
        rows = slice(start, start + block)
        two = jnp.maximum(three_dots(hcat, start, 2 * width, block, second_ref), 0.0).astype(BF16)
        two_ref[rows, :] = two
        logit_ref[rows, :] = turned_dot(two, head)

    tiles, pixels = label_ref.shape
    edge = math.isqrt(pixels)
    across = width // edge
    lane = iota((tiles, LANES), 1)
    even = lane < 64
    label_sum = jnp.zeros((tiles, LANES), F32)
    for pair in range(pixels // 2):
        row, col = 2 * pair // edge, 2 * pair % edge
        parts = []
        for down in range(tiles // across):
            start = (down * edge + row) * width + col
            left = logit_ref[pl.ds(start, across, stride=edge), :]
            right = logit_ref[pl.ds(start + 1, across, stride=edge), :]
            parts.append(jnp.where(iota(left.shape, 1) < 64, left, right))
        value = jnp.concatenate(parts, axis=0)
        top = jnp.where(
            even,
            jnp.max(jnp.where(even, value, -jnp.inf), axis=1, keepdims=True),
            jnp.max(jnp.where(even, -jnp.inf, value), axis=1, keepdims=True),
        )
        value = value - top
        power = jnp.exp(value)
        total = jnp.where(
            even,
            jnp.sum(jnp.where(even, power, 0.0), axis=1, keepdims=True),
            jnp.sum(jnp.where(even, 0.0, power), axis=1, keepdims=True),
        )
        value = value - jnp.log(total)
        label = jnp.where(even, label_ref[:, 2 * pair : 2 * pair + 1], label_ref[:, 2 * pair + 1 : 2 * pair + 2])
        hit = label == lane % 64
        label_sum = label_sum + jnp.where(hit, value, 0.0)
        log_ref[pair * tiles : (pair + 1) * tiles, :] = value
        base_ref[pair * tiles : (pair + 1) * tiles, :] = jnp.exp(value) - hit.astype(F32)
    label_sum_ref[...] = label_sum


def student_forward(place, before, after, head, labels, x, first, second, own, width):
    cells, channels = x.shape
    halo = before.shape[0]
    tiles, pixels = labels.shape
    shape = jax.ShapeDtypeStruct
    return pl.pallas_call(
        functools.partial(student_kernel, width),
        in_specs=[scalars(), *whole(7), *hbm(1)],
        out_specs=whole(5),
        out_shape=[
            shape((cells + 4 * width, channels), BF16),
            shape((cells, channels), BF16),
            shape((cells // 2, LANES), F32),
            shape((cells // 2, LANES), F32),
            shape((tiles, LANES), F32),
        ],
        scratch_shapes=[
            pltpu.VMEM((cells + 2 * halo, 3 * channels), BF16),
            pltpu.VMEM((cells + 4 * width, 3 * channels), BF16),
            pltpu.VMEM((cells, LANES), F32),
        ],
        compiler_params=pltpu.CompilerParams(vmem_limit_bytes=24 << 20),
        cost_estimate=pl.CostEstimate(flops=6_000_000_000, bytes_accessed=12_000_000, transcendentals=500_000),
        name="student_forward",
    )(place, before, after, head, labels, x, first, second, own)


def put_turned(ref, start, value, shift, width):
    rows, channels = value.shape
    col = iota(value.shape, 0) % width
    left = jnp.where(col >= shift, pltpu.roll(value, shift, 0), 0.0)
    right = jnp.where(col < width - shift, pltpu.roll(value, rows - shift, 0), 0.0)
    for tap, one in enumerate((left, value, right)):
        ref[tap * channels : (tap + 1) * channels, pl.ds(start, rows)] = one.T.astype(BF16)


def turn_kernel(
    width, before_ref, x_ref, after_ref, one_ref, two_ref, second_ref, sent_ref, xt_ref, ht_ref, twot_ref, wt_ref
):
    cells, channels = x_ref.shape
    halo = before_ref.shape[0]
    pair = 2 * width
    first = jnp.concatenate([before_ref[halo - width :], x_ref[:width]], axis=0).astype(F32)
    put_turned(xt_ref, 0, first, 1, width)
    last = jnp.concatenate([x_ref[cells - width :], after_ref[:width]], axis=0).astype(F32)
    put_turned(xt_ref, cells, last, 1, width)

    for start in range(pair, cells, pair):
        put_turned(xt_ref, start, x_ref[start - width : start + width, :].astype(F32), 1, width)
    for start in range(0, one_ref.shape[0], pair):
        put_turned(ht_ref, start, one_ref[start : start + pair, :].astype(F32), 2, width)
    for start in range(0, cells, MXU):
        twot_ref[:, start : start + MXU] = two_ref[start : start + MXU, :].astype(F32).T.astype(BF16)
    for i in range(3):
        for tap in range(3):
            part = slice(tap * channels, (tap + 1) * channels)
            mirror = slice((2 - tap) * channels, (3 - tap) * channels)
            wt_ref[i, part, :] = second_ref[i, mirror, :].astype(F32).T.astype(BF16)


def turn(before, x, after, one, two, second, sent, width):
    cells, channels = x.shape
    shape = jax.ShapeDtypeStruct
    return pl.pallas_call(
        functools.partial(turn_kernel, width),
        in_specs=[*whole(6), pl.BlockSpec(memory_space=pl.ANY)],
        out_specs=whole(4),
        out_shape=[
            shape((3 * channels, cells + 2 * width), BF16),
            shape((3 * channels, cells + 4 * width), BF16),
            shape((channels, cells), BF16),
            shape((3, 3 * channels, channels), BF16),
        ],
        compiler_params=pltpu.CompilerParams(vmem_limit_bytes=20 << 20),
        cost_estimate=pl.CostEstimate(flops=3_000_000_000, bytes_accessed=14_000_000, transcendentals=0),
        name="turn",
    )(before, x, after, one, two, second, sent)


def head_kernel(
    scale, width, log_ref, base_ref, label_sum_ref, two_ref, twot_ref, head_ref, *refs
):
    *got_refs, grad_ref, top_ref, bottom_ref, head_grad_ref, got_ref, natural = refs
    slots, extended = got_ref.shape
    got_ref[...] = jnp.concatenate([one[...].astype(F32) for one in got_refs], axis=0).astype(BF16)
    tiles = label_sum_ref.shape[0]
    flat = extended - 2 * LANES
    pixels = flat // 64
    edge = math.isqrt(pixels)
    across = width // edge
    index = got_ref[:, flat + LANES :].astype(F32)
    take = (index == (iota((slots, LANES), 1) + 1).astype(F32)).astype(F32).T[:tiles].astype(BF16)
    spread = join_lanes(dot(take, got_ref[:, flat : flat + LANES]))
    weight = 1.0 / (0.1 + spread)
    even = iota((tiles, LANES), 1) < 64
    loss = -label_sum_ref[...]
    for pair in range(pixels // 2):
        rows = slice(pair * tiles, (pair + 1) * tiles)
        if pair % 2 == 0:
            both = dot(take, got_ref[:, pair * LANES : (pair + 2) * LANES])
        mean = both[:, pair % 2 * LANES : (pair % 2 + 1) * LANES]
        cell = jnp.where(even, weight[:, 2 * pair : 2 * pair + 1], weight[:, 2 * pair + 1 : 2 * pair + 2])
        value = log_ref[rows, :]
        held = mean > 0
        loss = loss + cell * jnp.where(held, mean * (jnp.log(jnp.where(held, mean, 1.0)) - value), 0.0)
        grad = (cell * (jnp.exp(value) - mean) + base_ref[rows, :]) * scale
        turned = pltpu.roll(grad, 64, 1)
        row, col = 2 * pair // edge, 2 * pair % edge
        for down in range(tiles // across):
            start = (down * edge + row) * width + col
            natural[pl.ds(start, across, stride=edge), :] = grad[down * across : (down + 1) * across]
            natural[pl.ds(start + 1, across, stride=edge), :] = turned[down * across : (down + 1) * across]
    cells, channels = two_ref.shape
    logit_grad = natural[...].astype(BF16)
    head = jnp.concatenate([head_ref[...], jnp.zeros_like(head_ref)], axis=0)
    head_grad_ref[:channels, :] = dot(twot_ref[...], logit_grad)
    head_grad_ref[channels:, :] = loss
    block = 4 * width
    for start in range(0, cells, block):
        rows = slice(start, start + block)
        grad = dot(logit_grad[rows], head)
        grad_ref[rows, :] = jnp.where(two_ref[rows, :].astype(F32) > 0, grad, 0.0).astype(BF16)
    top_ref[...] = grad_ref[: 2 * width, :]
    bottom_ref[...] = grad_ref[cells - 2 * width :, :]


def head_step(got, log, base, label_sum, two, twot, head, scale, width):
    cells, channels = two.shape
    shape = jax.ShapeDtypeStruct
    return pl.pallas_call(
        functools.partial(head_kernel, scale, width),
        in_specs=whole(6 + len(got)),
        out_specs=whole(4),
        out_shape=[
            shape((cells, channels), BF16),
            shape((2 * width, channels), BF16),
            shape((2 * width, channels), BF16),
            shape((channels + label_sum.shape[0], LANES), F32),
        ],
        scratch_shapes=[
            pltpu.VMEM((len(got) * got[0].shape[0], got[0].shape[1]), BF16),
            pltpu.VMEM((cells, LANES), F32),
        ],
        compiler_params=pltpu.CompilerParams(vmem_limit_bytes=14 << 20),
        cost_estimate=pl.CostEstimate(flops=400_000_000, bytes_accessed=5_000_000, transcendentals=500_000),
        name="head_step",
    )(log, base, label_sum, two, twot, head, *got)


def inner_dots(ref, start, step, rows, weight_ref):
    total = None
    for tap in range(3):
        part = dot(ref[start + (2 - tap) * step : start + (2 - tap) * step + rows, :], weight_ref[tap])
        total = part if total is None else total + part
    return total


def second_kernel(width, ht_ref, grad_ref, wt_ref, one_ref, out_ref, inner_ref, gcat):
    cells, channels = grad_ref.shape
    block = 4 * width
    halo = 2 * width
    for start in range(0, cells, block):
        put_shifted(gcat, start, grad_ref[start : start + block, :].astype(F32), 2, width)
    for tap in range(3):
        part = dot(ht_ref[:, halo * tap : halo * tap + cells], grad_ref[...])
        out_ref[tap * 3 * channels : (tap + 1) * 3 * channels, :] = part.astype(BF16)
    for start in range(block, cells - block, block):
        value = inner_dots(gcat, start - halo, halo, block, wt_ref)
        held = one_ref[halo + start : halo + start + block, :].astype(F32) > 0
        inner_ref[start - block : start, :] = jnp.where(held, value, 0.0).astype(BF16)


def second_step(ht, grad, wt, one, width):
    cells, channels = grad.shape
    return pl.pallas_call(
        functools.partial(second_kernel, width),
        in_specs=whole(4),
        out_specs=whole(2),
        out_shape=[
            jax.ShapeDtypeStruct((9 * channels, channels), BF16),
            jax.ShapeDtypeStruct((cells - 8 * width, channels), BF16),
        ],
        scratch_shapes=[pltpu.VMEM((cells, 3 * channels), BF16)],
        compiler_params=pltpu.CompilerParams(vmem_limit_bytes=20 << 20),
        cost_estimate=pl.CostEstimate(flops=4_500_000_000, bytes_accessed=9_000_000, transcendentals=0),
        name="second_step",
    )(ht, grad, wt, one)


def first_kernel(width, plan, place_ref, before_ref, after_ref, grad_ref, head_grad_ref, second_ref, inner_ref, *refs):
    wt_ref, one_ref, xt_ref, *refs = refs
    chips, groups, near_rows, far_rows = plan
    keep_refs, give_refs, refs = refs[: chips + 1], refs[chips + 1 : 2 * chips + 2], refs[2 * chips + 2 :]
    gtop, gbottom, padded, halves, sem = refs
    cells, channels = grad_ref.shape
    rows = 9 * channels
    used = rows + channels // 2
    half = halves.shape[1]
    second_copy = pltpu.make_async_copy(second_ref, halves.at[1, pl.ds(0, rows)], sem)
    second_copy.start()
    halo = before_ref.shape[0]
    block = 4 * width
    inside = 3 * halo
    put_shifted(gtop, 0, before_ref[...].astype(F32), 2, width)
    put_shifted(gtop, halo, grad_ref[:inside, :].astype(F32), 2, width)
    put_shifted(gbottom, 0, grad_ref[cells - inside :, :].astype(F32), 2, width)
    put_shifted(gbottom, inside, after_ref[...].astype(F32), 2, width)
    padded[:halo, :] = jnp.zeros((halo, channels), BF16)
    padded[halo + cells :, :] = jnp.zeros((halo, channels), BF16)
    padded[halo + block : halo + cells - block, :] = inner_ref[...]
    for ref, start in ((gtop, 0), (gbottom, cells - block)):
        value = inner_dots(ref, 0, halo, block, wt_ref)
        held = one_ref[halo + start : halo + start + block, :].astype(F32) > 0
        padded[halo + start : halo + start + block, :] = jnp.where(held, value, 0.0).astype(BF16)
    span = cells + 2 * width
    for tap in range(3):
        part = dot(xt_ref[...], padded[(2 - tap) * width : (2 - tap) * width + span, :])
        halves[0, tap * 3 * channels : (tap + 1) * 3 * channels, :] = part.astype(BF16)
    lane = iota((channels // 2, LANES), 1)
    loss = jnp.sum(head_grad_ref[channels:, :])
    high = loss.astype(BF16).astype(F32)
    extra = jnp.where(lane == 64, high, jnp.where(lane == 65, loss - high, 0.0))
    extra = jnp.where(iota(lane.shape, 0) == place_ref[DEVICE] % (channels // 2), extra, 0.0)
    for side in range(2):
        value = jnp.where(lane < 64, head_grad_ref[side * channels // 2 : (side + 1) * channels // 2, :], extra)
        halves[0, rows:used, side * LANES : (side + 1) * LANES] = value.astype(BF16)
    if half > used:
        halves[0, used:, :] = jnp.zeros((half - used, channels), BF16)
    halves[1, rows:, :] = jnp.zeros((half - rows, channels), BF16)
    second_copy.wait()
    core, chip = place_ref[CORE], place_ref[CHIP]
    size = groups * near_rows
    for step in range(chips):
        low = pl.multiple_of((chip ^ step) * size, 16)
        give_refs[step][...] = halves[1 - core, pl.ds(low, size), :]
        keep_refs[step][...] = halves[core, pl.ds(low, size), :]
    give_refs[chips][...] = halves[1 - core, chips * size :, :]
    keep_refs[chips][...] = halves[core, chips * size :, :]


def first_step(place, before, after, grad, head_grad, second, inner, wt, one, xt, width, plan):
    cells, channels = grad.shape
    halo = before.shape[0]
    chips, groups, near_rows, far_rows = plan
    half_rows = chips * groups * (near_rows + far_rows)
    piece = [jax.ShapeDtypeStruct((groups * near_rows, channels), BF16)] * chips
    piece += [jax.ShapeDtypeStruct((chips * groups * far_rows, channels), BF16)]
    outs = pl.pallas_call(
        functools.partial(first_kernel, width, plan),
        in_specs=[scalars(), *whole(9)],
        out_specs=whole(2 * chips + 2),
        out_shape=piece * 2,
        scratch_shapes=[
            pltpu.VMEM((4 * halo, 3 * channels), BF16),
            pltpu.VMEM((4 * halo, 3 * channels), BF16),
            pltpu.VMEM((cells + 4 * width, channels), BF16),
            pltpu.VMEM((2, half_rows, channels), BF16),
            pltpu.SemaphoreType.DMA,
        ],
        compiler_params=pltpu.CompilerParams(vmem_limit_bytes=24 << 20),
        cost_estimate=pl.CostEstimate(flops=5_000_000_000, bytes_accessed=10_000_000, transcendentals=0),
        name="first_step",
    )(place, before, after, grad, head_grad, second, inner, wt, one, xt)
    return (outs[: chips + 1], outs[chips + 1 :])


def neighbours(first, last, axis):
    count = lax.axis_size(axis)
    up = [(i, i + 1) for i in range(count - 1)]
    down = [(i + 1, i) for i in range(count - 1)]
    return (lax.ppermute(last, axis, up), lax.ppermute(first, axis, down))


def pairwise(array, axis, step):
    count = lax.axis_size(axis)
    return lax.ppermute(array, axis, [(i, i ^ step) for i in range(count)])


def add(arrays):
    return functools.reduce(jnp.add, [array.astype(F32) for array in arrays]).astype(BF16)


def assemble_kernel(width, plan, cell_total, place_ref, *refs):
    chips, groups, near_rows, far_rows = plan
    parts = len(refs) - 6
    pieces, refs = refs[:parts], refs[parts:]
    first_ref, second_ref, head_ref, loss_ref, value_ref, sems = refs
    grad_rows = first_ref.shape[0]
    core, chip, member = place_ref[CORE], place_ref[CHIP], place_ref[MEMBER]

    def fill(half, source):
        for s in range(chips):
            value = source[s][...].astype(F32)
            for u in range(groups):
                start = pl.multiple_of(((chip ^ s) * groups + (member ^ u)) * near_rows, 8)
                value_ref[half, pl.ds(start, near_rows), :] = value[u * near_rows : (u + 1) * near_rows]
        value = source[chips][...].astype(F32)
        for u in range(groups):
            for s in range(chips):
                low = (u * chips + s) * far_rows
                start = chips * groups * near_rows + ((member ^ u) * chips + (chip ^ s)) * far_rows
                value_ref[half, pl.ds(pl.multiple_of(start, 8), far_rows), :] = value[low : low + far_rows]

    mine, other = pieces[: parts // 2], pieces[parts // 2 :]

    def send(half):
        out_ref = (first_ref, second_ref)[half]
        return pltpu.make_async_copy(value_ref.at[half, pl.ds(0, grad_rows)], out_ref, sems.at[half])

    def start_copy(half):
        pl.when(half == 0)(lambda: send(0).start())
        pl.when(half != 0)(lambda: send(1).start())

    fill(core, mine)
    start_copy(core)
    fill(1 - core, other)
    start_copy(1 - core)
    rows = width // 2
    extra = value_ref[0, grad_rows : grad_rows + rows, :]
    for side in range(2):
        head_ref[:, side * rows : (side + 1) * rows] = extra[:, side * LANES : (side + 1) * LANES].T[: head_ref.shape[0]]
    lane = iota(extra.shape, 1)
    loss = jnp.sum(jnp.where((lane == 64) | (lane == 65), extra, 0.0), keepdims=True)
    loss_ref[...] = loss / cell_total
    send(0).wait()
    send(1).wait()


def assemble(place, pieces, plan, grad_rows, classes, cell_total):
    chips, groups, near_rows, far_rows = plan
    half_rows = chips * groups * (near_rows + far_rows)
    width = pieces[0].shape[1]
    shape = jax.ShapeDtypeStruct
    return pl.pallas_call(
        functools.partial(assemble_kernel, width, plan, cell_total),
        in_specs=[scalars(), *whole(len(pieces))],
        out_specs=[*hbm(2), *whole(2)],
        out_shape=[
            shape((grad_rows, width), F32),
            shape((grad_rows, width), F32),
            shape((classes, width), F32),
            shape((1, 1), F32),
        ],
        scratch_shapes=[pltpu.VMEM((2, half_rows, width), F32), pltpu.SemaphoreType.DMA((2,))],
        compiler_params=pltpu.CompilerParams(vmem_limit_bytes=48 << 20),
        cost_estimate=pl.CostEstimate(flops=1_000_000, bytes_accessed=7_500_000, transcendentals=0),
        name="assemble",
    )(place, *pieces)


def gradient_pieces(place, keep, give, plan):
    chips, groups, near_rows, far_rows = plan
    got = [pairwise(one, "core", 1) for one in give]
    near = [add(pair) for pair in zip(keep[:chips], got[:chips])]
    far = [keep[chips], got[chips]]

    def block(arrays, axis, me, step, rows):
        start = (me ^ step) * rows
        return add([lax.dynamic_slice_in_dim(one, start, rows, axis=0) for one in arrays])

    chip, member = place[CHIP], place[MEMBER]
    far = [block(far, "member", member, step, chips * far_rows) for step in range(groups)]
    near = [near[0]] + [pairwise(near[step], "chip", step) for step in range(1, chips)]
    far = [far[0]] + [pairwise(far[step], "member", step) for step in range(1, groups)]
    near = [block(near, "member", member, step, near_rows) for step in range(groups)]
    far = [block(far, "chip", chip, step, far_rows) for step in range(chips)]
    near = add([near[0]] + [pairwise(near[step], "member", step) for step in range(1, groups)])
    far = add([far[0]] + [pairwise(far[step], "chip", step) for step in range(1, chips)])

    near = jnp.concatenate([near] + [pairwise(near, "member", step) for step in range(1, groups)], axis=0)
    far = jnp.concatenate([far] + [pairwise(far, "chip", step) for step in range(1, chips)], axis=0)
    held = [near] + [pairwise(near, "chip", step) for step in range(1, chips)]
    far = jnp.concatenate([far] + [pairwise(far, "member", step) for step in range(1, groups)], axis=0)
    held += [far]
    return held + [pairwise(piece, "core", 1) for piece in held]


def body(teacher_logits, coverage, features, labels, first_weight, second_weight, head_weight):
    channels, classes = head_weight.shape
    members, tiles_here, flat_width = teacher_logits.shape
    pixels = flat_width // classes
    edge = math.isqrt(pixels)
    groups = lax.axis_size("member")
    chips = lax.axis_size("chip")
    columns = chips * 2
    tile_axes = ("chip", "core")
    block_tiles = tiles_here // groups
    capacity = max(2, 2 * block_tiles // columns)
    local = features[0]
    lines, width = local.shape[:2]
    cells = lines * width
    cell_total = groups * columns * cells
    column = lax.axis_index(tile_axes)
    place = jnp.stack(
        [
            lax.axis_index("core"),
            lax.axis_index("chip"),
            lax.axis_index("member"),
            lax.axis_index(("member", *tile_axes)),
            column == 0,
            column == columns - 1,
        ]
    ).astype(jnp.int32)
    flat = local.reshape(cells, channels)
    first_rows = first_weight.reshape(3, 3 * channels, channels)
    second_rows = second_weight.reshape(3, 3 * channels, channels)
    head = head_weight.T

    before, after = neighbours(flat[: 3 * width], flat[cells - 3 * width :], tile_axes)
    far = teacher_moments(place, teacher_logits, block_tiles, classes, 1)
    got = [pairwise(one, "member", step) for step, one in zip((3, 2), far)]
    near, own = teacher_moments(place, teacher_logits, block_tiles, classes, 0)
    got += [pairwise(near, "member", 1), own]
    label_rows = (
        labels[0].reshape(lines // edge, edge, width // edge, edge).transpose(0, 2, 1, 3).reshape(block_tiles, pixels)
    )
    one, two, log, base, label_sum = student_forward(
        place, before, after, head, label_rows, flat, first_rows, second_rows, own, width
    )
    cover = coverage.reshape(groups, 1, block_tiles)
    sent = combine(got, cover, place, label_sum, classes, members, columns, capacity)
    received = [sent[0]] + [pairwise(sent[step], tile_axes, step) for step in range(1, columns)]
    xt, ht, twot, wt = turn(before, flat, after, one, two, second_rows, sent[0], width)
    grad_two, top, bottom, head_grad = head_step(
        received, log, base, label_sum, two, twot, head, 1.0 / math.sqrt(cell_total), width
    )
    grad_before, grad_after = neighbours(top, bottom, tile_axes)
    second, inner = second_step(ht, grad_two, wt, one, width)
    rows, extra_rows = 9 * channels, channels // 2
    unit = 8 * groups * chips
    block_rows = -(-(rows + extra_rows) // unit) * 8
    far_rows = block_rows // 24 * 8
    plan = (chips, groups, block_rows - far_rows, far_rows)
    keep, give = first_step(
        place, grad_before, grad_after, grad_two, head_grad, second, inner, wt, one, xt, width, plan
    )
    pieces = gradient_pieces(place, keep, give, plan)
    first_total, second_total, head_total, loss = assemble(
        place, pieces, plan, rows, classes, cell_total
    )
    kernel_shape = (3, 3, channels, channels)
    return (first_total.reshape(kernel_shape), second_total.reshape(kernel_shape), head_total.T, loss[0, 0])


def solution(mesh):
    groups, columns = mesh.shape["member"], mesh.shape["tile"]
    split = jax.sharding.Mesh(mesh.devices.reshape(groups, columns // 2, 2), ("member", "chip", "core"))
    tile = ("chip", "core")
    return jax.shard_map(
        body,
        mesh=split,
        in_specs=(
            P("member", tile, None),
            P(tile),
            P("member", tile, None, None),
            P("member", tile, None),
            P(),
            P(),
            P(),
        ),
        out_specs=(P(), P(), P(), P()),
        check_vma=False,
    )
```

```python
import functools
import math

import jax
import jax.numpy as jnp
from jax import lax
from jax.experimental import pallas as pl
from jax.experimental.pallas import tpu as pltpu
from jax.sharding import PartitionSpec as P

BF16 = jnp.bfloat16
F32 = jnp.float32
LANES = 128
MXU = 256


def whole(count):
    return [pl.BlockSpec(memory_space=pltpu.VMEM)] * count


def iota(shape, axis):
    return lax.broadcasted_iota(jnp.int32, shape, axis)


def dot(left, right):
    return jnp.dot(left, right, preferred_element_type=F32)


def split_lanes(value):
    high = value.astype(BF16).astype(F32)
    return jnp.where(iota(value.shape, 1) < 64, high, value - high).astype(BF16)


def join_lanes(value):
    return value + pltpu.roll(value, 64, 1)


def class_sums(value, classes):
    pick = (iota((MXU, LANES), 0) // classes == iota((MXU, LANES), 1) % (MXU // classes)).astype(BF16)
    high = value.astype(BF16)
    low = (value - high.astype(F32)).astype(BF16)
    return dot(high, pick) + dot(low, pick)


def hbm(count):
    return [pl.BlockSpec(memory_space=pl.ANY)] * count


def scalars():
    return pl.BlockSpec(memory_space=pltpu.SMEM)


CORE, CHIP, MEMBER, DEVICE, FIRST, LAST = range(6)


def teacher_kernel(classes, flip, place_ref, logit_hbm, *refs):
    near_ref, own_ref, x_ref, sum_ref, acc_ref, sems = refs[-6:]
    quarters, members, tiles, width = x_ref.shape
    parts = width // MXU
    per = MXU // classes
    tile_rows = pl.ds(pl.multiple_of(((place_ref[MEMBER] // 2) ^ flip) * tiles, tiles), tiles)
    arrive = [
        pltpu.make_async_copy(logit_hbm.at[:, tile_rows, pl.ds(i * width, width)], x_ref.at[i], sems.at[i])
        for i in range(quarters)
    ]
    for copy in arrive:
        copy.start()
    same = (iota((MXU, MXU), 0) // classes == iota((MXU, MXU), 1) // classes).astype(BF16)
    acc_ref[...] = jnp.zeros_like(acc_ref)

    @pl.loop(0, quarters)
    def _(i):
        pltpu.make_async_copy(logit_hbm.at[:, tile_rows, pl.ds(0, width)], x_ref.at[i], sems.at[i]).wait()
        each = range(parts)
        x = [x_ref[i, :, :, n * MXU : (n + 1) * MXU].astype(F32).reshape(members * tiles, MXU) for n in each]
        root = [jnp.exp(one * 0.25) for one in x]
        total = [dot(one.astype(BF16), same) for one in root]
        root = [one * pl.reciprocal(whole_sum, approx=True) for one, whole_sum in zip(root, total)]
        square = [one * one for one in root]
        power = [one * one for one in square]
        total = [dot(one.astype(BF16), same) for one in power]
        inverse = [pl.reciprocal(one, approx=True) for one in total]
        inverse = [one * (2.0 - whole_sum * one) for one, whole_sum in zip(inverse, total)]
        probs = [(one * other).reshape(members, tiles, MXU) for one, other in zip(power, inverse)]
        first = [functools.reduce(jnp.add, [one[m] for m in range(members)]) for one in probs]
        within = [
            functools.reduce(jnp.add, [one[m] * one[m] for m in range(members)]) - sums * sums * (1.0 / members)
            for one, sums in zip(probs, first)
        ]
        sums = [class_sums(one, classes) for one in within]
        acc = acc_ref[...]
        for n in each:
            acc = jnp.where(iota(acc.shape, 1) % 64 // per == i * parts + n, sums[n], acc)
        acc_ref[...] = acc
        for n in each:
            sum_ref[:, pl.ds(pl.multiple_of(i * width + n * MXU, MXU), MXU)] = first[n].astype(BF16)

    sum_ref[:, quarters * width :] = split_lanes(acc_ref[...])
    block = tiles // 2
    odd = 1 - place_ref[MEMBER] % 2
    near_ref[...] = sum_ref[pl.ds(pl.multiple_of(odd * block, 16), block), :]
    own_ref[...] = sum_ref[pl.ds(pl.multiple_of((1 - odd) * block, 16), block), :]


def teacher_moments(place, logits, tiles, classes, flip, *earlier):
    members, _, width = logits.shape
    quarters = 4
    shape = jax.ShapeDtypeStruct
    outs = [shape((tiles, width + LANES), BF16)] * 2
    return pl.pallas_call(
        functools.partial(teacher_kernel, classes, flip),
        in_specs=[scalars(), *hbm(1 + len(earlier))],
        out_specs=whole(len(outs)),
        out_shape=outs,
        scratch_shapes=[
            pltpu.VMEM((quarters, members, 2 * tiles, width // quarters), BF16),
            pltpu.VMEM((2 * tiles, width + LANES), BF16),
            pltpu.VMEM((2 * tiles, LANES), F32),
            pltpu.SemaphoreType.DMA((quarters,)),
        ],
        compiler_params=pltpu.CompilerParams(vmem_limit_bytes=58 << 20),
        cost_estimate=pl.CostEstimate(flops=1_500_000_000, bytes_accessed=2_600_000, transcendentals=3_000_000),
        name="teacher_moments",
    )(place, logits, *earlier)


def combine_kernel(classes, members, columns, capacity, where_ref, cover_ref, after_ref, *refs):
    chips = columns // 2
    got_refs, out_refs = refs[:-chips], refs[-chips:]
    groups = len(got_refs)
    tiles, extended = got_refs[0].shape
    width = extended - LANES
    means, gaps = [], []
    for start in range(0, width, MXU):
        sums = [got_ref[:, start : start + MXU].astype(F32) for got_ref in got_refs]
        total = sums[0]
        for one in sums[1:]:
            total = total + one
        mean = total * (1.0 / (members * groups))
        means.append(mean.astype(BF16))
        gap = jnp.zeros_like(mean)
        for one in sums:
            off = one * (1.0 / members) - mean
            gap = gap + off * off
        gaps.append(gap)
    between = class_sums(jnp.concatenate(gaps, axis=0), classes)
    lane = iota((tiles, LANES), 1)
    spread = jnp.zeros((tiles, LANES), F32)
    per = MXU // classes
    for i in range(width // MXU):
        spread = jnp.where(lane % 64 // per == i, between[i * tiles : (i + 1) * tiles], spread)
    inner = got_refs[0][:, width:].astype(F32)
    for got_ref in got_refs[1:]:
        inner = inner + got_ref[:, width:].astype(F32)
    spread = spread * (1.0 / groups) + join_lanes(inner) * (1.0 / (members * groups))
    index = (iota((tiles, LANES), 0) + 1).astype(F32).astype(BF16)
    rows = jnp.concatenate([*means, split_lanes(spread), index], axis=1)
    target = cover_ref[where_ref[MEMBER]] ^ (where_ref[CHIP] * 2 + where_ref[CORE])
    onehot = (iota((columns, tiles), 0) == target).astype(F32)
    earlier = (iota((tiles, tiles), 0) < iota((tiles, tiles), 1)).astype(BF16)
    before = dot(onehot.astype(BF16), earlier)
    rank = jnp.sum(before * onehot, axis=0, keepdims=True).astype(jnp.int32)
    place = (iota((columns * capacity, tiles), 0) == target * capacity + rank).astype(BF16)
    sent = dot(place, rows)
    for index, out_ref in enumerate(out_refs):
        out_ref[...] = sent[2 * index * capacity : 2 * (index + 1) * capacity].astype(BF16)


def combine(got, cover, where, after, classes, members, columns, capacity):
    extended = got[0].shape[1]
    return pl.pallas_call(
        functools.partial(combine_kernel, classes, members, columns, capacity),
        in_specs=[pl.BlockSpec(memory_space=pltpu.SMEM), *whole(1), pl.BlockSpec(memory_space=pl.ANY), *whole(len(got))],
        out_specs=whole(columns // 2),
        out_shape=[jax.ShapeDtypeStruct((2 * capacity, extended + LANES), BF16)] * (columns // 2),
        compiler_params=pltpu.CompilerParams(vmem_limit_bytes=12 << 20),
        cost_estimate=pl.CostEstimate(flops=100_000_000, bytes_accessed=1_700_000, transcendentals=0),
        name="combine",
    )(where, cover, after, *got)


def put_shifted(ref, start, value, shift, width):
    rows, channels = value.shape
    col = iota(value.shape, 0) % width
    left = jnp.where(col >= shift, pltpu.roll(value, shift, 0), 0.0)
    right = jnp.where(col < width - shift, pltpu.roll(value, rows - shift, 0), 0.0)
    ref[pl.ds(start, rows), :channels] = left.astype(BF16)
    ref[pl.ds(start, rows), channels : 2 * channels] = value.astype(BF16)
    ref[pl.ds(start, rows), 2 * channels :] = right.astype(BF16)


def three_dots(ref, start, step, rows, weight_ref):
    total = None
    for tap in range(3):
        part = dot(ref[pl.ds(start + tap * step, rows), :], weight_ref[tap])
        total = part if total is None else total + part
    return total


def turned_dot(left, right):
    return lax.dot_general(left, right, (((1,), (1,)), ((), ())), preferred_element_type=F32)


def turned_dot(left, right):
    return lax.dot_general(left, right, (((1,), (1,)), ((), ())), preferred_element_type=F32)


def student_kernel(
    width, place_ref, before_ref, after_ref, head_ref, label_ref, x_ref, first_ref, second_ref, own_ref,
    one_ref, two_ref, log_ref, base_ref, label_sum_ref, xcat, hcat, logit_ref,
):
    cells, channels = x_ref.shape
    halo = before_ref.shape[0]
    block = 4 * width
    put_shifted(xcat, 0, before_ref[...].astype(F32), 1, width)
    put_shifted(xcat, halo + cells, after_ref[...].astype(F32), 1, width)
    for start in range(0, cells, block):
        put_shifted(xcat, halo + start, x_ref[start : start + block, :].astype(F32), 1, width)
    lines = cells // width
    low = jnp.where(place_ref[FIRST] == 1, 2, 0)
    high = jnp.where(place_ref[LAST] == 1, lines + 2, lines + 4)
    for start in range(0, cells + block, block):
        value = jnp.maximum(three_dots(xcat, start, width, block, first_ref), 0.0)
        if start == 0 or start == cells:
            line = start // width + iota(value.shape, 0) // width
            value = jnp.where((line >= low) & (line < high), value, 0.0)
        put_shifted(hcat, start, value, 2, width)
        one_ref[start : start + block, :] = value.astype(BF16)
    head = jnp.concatenate([head_ref[...], head_ref[...]], axis=0)
    for start in range(0, cells, block):
        rows = slice(start, start + block)
        two = jnp.maximum(three_dots(hcat, start, 2 * width, block, second_ref), 0.0).astype(BF16)
        two_ref[rows, :] = two
        logit_ref[rows, :] = turned_dot(two, head)

    tiles, pixels = label_ref.shape
    edge = math.isqrt(pixels)
    across = width // edge
    lane = iota((tiles, LANES), 1)
    even = lane < 64
    label_sum = jnp.zeros((tiles, LANES), F32)
    for pair in range(pixels // 2):
        row, col = 2 * pair // edge, 2 * pair % edge
        parts = []
        for down in range(tiles // across):
            start = (down * edge + row) * width + col
            left = logit_ref[pl.ds(start, across, stride=edge), :]
            right = logit_ref[pl.ds(start + 1, across, stride=edge), :]
            parts.append(jnp.where(iota(left.shape, 1) < 64, left, right))
        value = jnp.concatenate(parts, axis=0)
        top = jnp.where(
            even,
            jnp.max(jnp.where(even, value, -jnp.inf), axis=1, keepdims=True),
            jnp.max(jnp.where(even, -jnp.inf, value), axis=1, keepdims=True),
        )
        value = value - top
        power = jnp.exp(value)
        total = jnp.where(
            even,
            jnp.sum(jnp.where(even, power, 0.0), axis=1, keepdims=True),
            jnp.sum(jnp.where(even, 0.0, power), axis=1, keepdims=True),
        )
        value = value - jnp.log(total)
        label = jnp.where(even, label_ref[:, 2 * pair : 2 * pair + 1], label_ref[:, 2 * pair + 1 : 2 * pair + 2])
        hit = label == lane % 64
        label_sum = label_sum + jnp.where(hit, value, 0.0)
        log_ref[pair * tiles : (pair + 1) * tiles, :] = value
        base_ref[pair * tiles : (pair + 1) * tiles, :] = jnp.exp(value) - hit.astype(F32)
    label_sum_ref[...] = label_sum


def student_forward(place, before, after, head, labels, x, first, second, own, width):
    cells, channels = x.shape
    halo = before.shape[0]
    tiles, pixels = labels.shape
    shape = jax.ShapeDtypeStruct
    return pl.pallas_call(
        functools.partial(student_kernel, width),
        in_specs=[scalars(), *whole(7), *hbm(1)],
        out_specs=whole(5),
        out_shape=[
            shape((cells + 4 * width, channels), BF16),
            shape((cells, channels), BF16),
            shape((cells // 2, LANES), F32),
            shape((cells // 2, LANES), F32),
            shape((tiles, LANES), F32),
        ],
        scratch_shapes=[
            pltpu.VMEM((cells + 2 * halo, 3 * channels), BF16),
            pltpu.VMEM((cells + 4 * width, 3 * channels), BF16),
            pltpu.VMEM((cells, LANES), F32),
        ],
        compiler_params=pltpu.CompilerParams(vmem_limit_bytes=24 << 20),
        cost_estimate=pl.CostEstimate(flops=6_000_000_000, bytes_accessed=12_000_000, transcendentals=500_000),
        name="student_forward",
    )(place, before, after, head, labels, x, first, second, own)


def put_turned(ref, start, value, shift, width):
    rows, channels = value.shape
    col = iota(value.shape, 0) % width
    left = jnp.where(col >= shift, pltpu.roll(value, shift, 0), 0.0)
    right = jnp.where(col < width - shift, pltpu.roll(value, rows - shift, 0), 0.0)
    for tap, one in enumerate((left, value, right)):
        ref[tap * channels : (tap + 1) * channels, pl.ds(start, rows)] = one.T.astype(BF16)


def turn_kernel(
    width, before_ref, x_ref, after_ref, one_ref, two_ref, second_ref, xt_ref, ht_ref, twot_ref, wt_ref
):
    cells, channels = x_ref.shape
    halo = before_ref.shape[0]
    pair = 2 * width
    first = jnp.concatenate([before_ref[halo - width :], x_ref[:width]], axis=0).astype(F32)
    put_turned(xt_ref, 0, first, 1, width)
    last = jnp.concatenate([x_ref[cells - width :], after_ref[:width]], axis=0).astype(F32)
    put_turned(xt_ref, cells, last, 1, width)

    for start in range(pair, cells, pair):
        put_turned(xt_ref, start, x_ref[start - width : start + width, :].astype(F32), 1, width)
    for start in range(0, one_ref.shape[0], pair):
        put_turned(ht_ref, start, one_ref[start : start + pair, :].astype(F32), 2, width)
    for start in range(0, cells, MXU):
        twot_ref[:, start : start + MXU] = two_ref[start : start + MXU, :].astype(F32).T.astype(BF16)
    for i in range(3):
        for tap in range(3):
            part = slice(tap * channels, (tap + 1) * channels)
            mirror = slice((2 - tap) * channels, (3 - tap) * channels)
            wt_ref[i, part, :] = second_ref[i, mirror, :].astype(F32).T.astype(BF16)


def turn(before, x, after, one, two, second, width):
    cells, channels = x.shape
    shape = jax.ShapeDtypeStruct
    return pl.pallas_call(
        functools.partial(turn_kernel, width),
        in_specs=whole(6),
        out_specs=whole(4),
        out_shape=[
            shape((3 * channels, cells + 2 * width), BF16),
            shape((3 * channels, cells + 4 * width), BF16),
            shape((channels, cells), BF16),
            shape((3, 3 * channels, channels), BF16),
        ],
        compiler_params=pltpu.CompilerParams(vmem_limit_bytes=20 << 20),
        cost_estimate=pl.CostEstimate(flops=3_000_000_000, bytes_accessed=14_000_000, transcendentals=0),
        name="turn",
    )(before, x, after, one, two, second)


def head_kernel(
    scale, width, log_ref, base_ref, label_sum_ref, two_ref, twot_ref, head_ref, *refs
):
    *got_refs, grad_ref, top_ref, bottom_ref, head_grad_ref, got_ref, natural = refs
    slots, extended = got_ref.shape
    held = [one[...].astype(F32) for one in got_refs]
    held = [one[: one.shape[0] // 2] for one in held[:-1]] + held[-1:]
    got_ref[...] = jnp.concatenate(held, axis=0).astype(BF16)
    tiles = label_sum_ref.shape[0]
    flat = extended - 2 * LANES
    pixels = flat // 64
    edge = math.isqrt(pixels)
    across = width // edge
    index = got_ref[:, flat + LANES :].astype(F32)
    take = (index == (iota((slots, LANES), 1) + 1).astype(F32)).astype(F32).T[:tiles].astype(BF16)
    spread = join_lanes(dot(take, got_ref[:, flat : flat + LANES]))
    weight = 1.0 / (0.1 + spread)
    even = iota((tiles, LANES), 1) < 64
    loss = -label_sum_ref[...]
    for pair in range(pixels // 2):
        rows = slice(pair * tiles, (pair + 1) * tiles)
        if pair % 2 == 0:
            both = dot(take, got_ref[:, pair * LANES : (pair + 2) * LANES])
        mean = both[:, pair % 2 * LANES : (pair % 2 + 1) * LANES]
        cell = jnp.where(even, weight[:, 2 * pair : 2 * pair + 1], weight[:, 2 * pair + 1 : 2 * pair + 2])
        value = log_ref[rows, :]
        held = mean > 0
        loss = loss + cell * jnp.where(held, mean * (jnp.log(jnp.where(held, mean, 1.0)) - value), 0.0)
        grad = (cell * (jnp.exp(value) - mean) + base_ref[rows, :]) * scale
        turned = pltpu.roll(grad, 64, 1)
        row, col = 2 * pair // edge, 2 * pair % edge
        for down in range(tiles // across):
            start = (down * edge + row) * width + col
            natural[pl.ds(start, across, stride=edge), :] = grad[down * across : (down + 1) * across]
            natural[pl.ds(start + 1, across, stride=edge), :] = turned[down * across : (down + 1) * across]
    cells, channels = two_ref.shape
    logit_grad = natural[...].astype(BF16)
    head = jnp.concatenate([head_ref[...], jnp.zeros_like(head_ref)], axis=0)
    head_grad_ref[:channels, :] = dot(twot_ref[...], logit_grad)
    head_grad_ref[channels:, :] = loss
    block = 4 * width
    for start in range(0, cells, block):
        rows = slice(start, start + block)
        grad = dot(logit_grad[rows], head)
        grad_ref[rows, :] = jnp.where(two_ref[rows, :].astype(F32) > 0, grad, 0.0).astype(BF16)
    top_ref[...] = grad_ref[: 2 * width, :]
    bottom_ref[...] = grad_ref[cells - 2 * width :, :]


def head_step(got, log, base, label_sum, two, twot, head, scale, width):
    cells, channels = two.shape
    shape = jax.ShapeDtypeStruct
    return pl.pallas_call(
        functools.partial(head_kernel, scale, width),
        in_specs=whole(6 + len(got)),
        out_specs=whole(4),
        out_shape=[
            shape((cells, channels), BF16),
            shape((2 * width, channels), BF16),
            shape((2 * width, channels), BF16),
            shape((channels + label_sum.shape[0], LANES), F32),
        ],
        scratch_shapes=[
            pltpu.VMEM((2 * got[-1].shape[0], got[-1].shape[1]), BF16),
            pltpu.VMEM((cells, LANES), F32),
        ],
        compiler_params=pltpu.CompilerParams(vmem_limit_bytes=14 << 20),
        cost_estimate=pl.CostEstimate(flops=400_000_000, bytes_accessed=5_000_000, transcendentals=500_000),
        name="head_step",
    )(log, base, label_sum, two, twot, head, *got)


def inner_dots(ref, start, step, rows, weight_ref):
    total = None
    for tap in range(3):
        part = dot(ref[start + (2 - tap) * step : start + (2 - tap) * step + rows, :], weight_ref[tap])
        total = part if total is None else total + part
    return total


def second_kernel(width, ht_ref, grad_ref, wt_ref, one_ref, out_ref, inner_ref, gcat):
    cells, channels = grad_ref.shape
    block = 4 * width
    halo = 2 * width
    for start in range(0, cells, block):
        put_shifted(gcat, start, grad_ref[start : start + block, :].astype(F32), 2, width)
    for tap in range(3):
        part = dot(ht_ref[:, halo * tap : halo * tap + cells], grad_ref[...])
        out_ref[tap * 3 * channels : (tap + 1) * 3 * channels, :] = part.astype(BF16)
    for start in range(block, cells - block, block):
        value = inner_dots(gcat, start - halo, halo, block, wt_ref)
        held = one_ref[halo + start : halo + start + block, :].astype(F32) > 0
        inner_ref[start - block : start, :] = jnp.where(held, value, 0.0).astype(BF16)


def second_step(ht, grad, wt, one, width):
    cells, channels = grad.shape
    return pl.pallas_call(
        functools.partial(second_kernel, width),
        in_specs=whole(4),
        out_specs=whole(2),
        out_shape=[
            jax.ShapeDtypeStruct((9 * channels, channels), BF16),
            jax.ShapeDtypeStruct((cells - 8 * width, channels), BF16),
        ],
        scratch_shapes=[pltpu.VMEM((cells, 3 * channels), BF16)],
        compiler_params=pltpu.CompilerParams(vmem_limit_bytes=20 << 20),
        cost_estimate=pl.CostEstimate(flops=4_500_000_000, bytes_accessed=9_000_000, transcendentals=0),
        name="second_step",
    )(ht, grad, wt, one)


def first_kernel(width, plan, place_ref, before_ref, after_ref, grad_ref, head_grad_ref, second_ref, inner_ref, *refs):
    wt_ref, one_ref, xt_ref, *refs = refs
    chips, groups, near_rows, far_rows = plan
    keep_refs, give_refs, refs = refs[: chips + 1], refs[chips + 1 : 2 * chips + 2], refs[2 * chips + 2 :]
    gtop, gbottom, padded, halves, sem = refs
    cells, channels = grad_ref.shape
    rows = 9 * channels
    used = rows + channels // 2
    half = halves.shape[1]
    second_copy = pltpu.make_async_copy(second_ref, halves.at[1, pl.ds(0, rows)], sem)
    second_copy.start()
    halo = before_ref.shape[0]
    block = 4 * width
    inside = 3 * halo
    put_shifted(gtop, 0, before_ref[...].astype(F32), 2, width)
    put_shifted(gtop, halo, grad_ref[:inside, :].astype(F32), 2, width)
    put_shifted(gbottom, 0, grad_ref[cells - inside :, :].astype(F32), 2, width)
    put_shifted(gbottom, inside, after_ref[...].astype(F32), 2, width)
    padded[:halo, :] = jnp.zeros((halo, channels), BF16)
    padded[halo + cells :, :] = jnp.zeros((halo, channels), BF16)
    padded[halo + block : halo + cells - block, :] = inner_ref[...]
    for ref, start in ((gtop, 0), (gbottom, cells - block)):
        value = inner_dots(ref, 0, halo, block, wt_ref)
        held = one_ref[halo + start : halo + start + block, :].astype(F32) > 0
        padded[halo + start : halo + start + block, :] = jnp.where(held, value, 0.0).astype(BF16)
    span = cells + 2 * width
    for tap in range(3):
        part = dot(xt_ref[...], padded[(2 - tap) * width : (2 - tap) * width + span, :])
        halves[0, tap * 3 * channels : (tap + 1) * 3 * channels, :] = part.astype(BF16)
    lane = iota((channels // 2, LANES), 1)
    loss = jnp.sum(head_grad_ref[channels:, :])
    high = loss.astype(BF16).astype(F32)
    extra = jnp.where(lane == 64, high, jnp.where(lane == 65, loss - high, 0.0))
    extra = jnp.where(iota(lane.shape, 0) == place_ref[DEVICE] % (channels // 2), extra, 0.0)
    for side in range(2):
        value = jnp.where(lane < 64, head_grad_ref[side * channels // 2 : (side + 1) * channels // 2, :], extra)
        halves[0, rows:used, side * LANES : (side + 1) * LANES] = value.astype(BF16)
    if half > used:
        halves[0, used:, :] = jnp.zeros((half - used, channels), BF16)
    halves[1, rows:, :] = jnp.zeros((half - rows, channels), BF16)
    second_copy.wait()
    core, chip = place_ref[CORE], place_ref[CHIP]
    size = groups * near_rows
    for step in range(chips):
        low = pl.multiple_of((chip ^ step) * size, 16)
        give_refs[step][...] = halves[1 - core, pl.ds(low, size), :]
        keep_refs[step][...] = halves[core, pl.ds(low, size), :]
    give_refs[chips][...] = halves[1 - core, chips * size :, :]
    keep_refs[chips][...] = halves[core, chips * size :, :]


def first_step(place, before, after, grad, head_grad, second, inner, wt, one, xt, width, plan):
    cells, channels = grad.shape
    halo = before.shape[0]
    chips, groups, near_rows, far_rows = plan
    half_rows = chips * groups * (near_rows + far_rows)
    piece = [jax.ShapeDtypeStruct((groups * near_rows, channels), BF16)] * chips
    piece += [jax.ShapeDtypeStruct((chips * groups * far_rows, channels), BF16)]
    outs = pl.pallas_call(
        functools.partial(first_kernel, width, plan),
        in_specs=[scalars(), *whole(9)],
        out_specs=whole(2 * chips + 2),
        out_shape=piece * 2,
        scratch_shapes=[
            pltpu.VMEM((4 * halo, 3 * channels), BF16),
            pltpu.VMEM((4 * halo, 3 * channels), BF16),
            pltpu.VMEM((cells + 4 * width, channels), BF16),
            pltpu.VMEM((2, half_rows, channels), BF16),
            pltpu.SemaphoreType.DMA,
        ],
        compiler_params=pltpu.CompilerParams(vmem_limit_bytes=24 << 20),
        cost_estimate=pl.CostEstimate(flops=5_000_000_000, bytes_accessed=10_000_000, transcendentals=0),
        name="first_step",
    )(place, before, after, grad, head_grad, second, inner, wt, one, xt)
    return (outs[: chips + 1], outs[chips + 1 :])


def neighbours(first, last, axis):
    count = lax.axis_size(axis)
    up = [(i, i + 1) for i in range(count - 1)]
    down = [(i + 1, i) for i in range(count - 1)]
    return (lax.ppermute(last, axis, up), lax.ppermute(first, axis, down))


def pairwise(array, axis, step):
    count = lax.axis_size(axis)
    return lax.ppermute(array, axis, [(i, i ^ step) for i in range(count)])


def add(arrays):
    return functools.reduce(jnp.add, [array.astype(F32) for array in arrays]).astype(BF16)


def assemble_kernel(width, plan, cell_total, place_ref, *refs):
    chips, groups, near_rows, far_rows = plan
    pieces, refs = refs[: chips + 1], refs[chips + 1 :]
    own = len(refs) == 5
    if own:
        first_ref, second_ref, extra_ref, value_ref, sem = refs
    else:
        _, _, held_ref, first_ref, second_ref, head_ref, loss_ref, value_ref, sem = refs
    grad_rows = first_ref.shape[0]
    core, chip, member = place_ref[CORE], place_ref[CHIP], place_ref[MEMBER]
    for s in range(chips):
        value = pieces[s][...].astype(F32)
        for u in range(groups):
            start = pl.multiple_of(((chip ^ s) * groups + (member ^ u)) * near_rows, 8)
            value_ref[pl.ds(start, near_rows), :] = value[u * near_rows : (u + 1) * near_rows]
    value = pieces[chips][...].astype(F32)
    for u in range(groups):
        for s in range(chips):
            low = (u * chips + s) * far_rows
            start = chips * groups * near_rows + ((member ^ u) * chips + (chip ^ s)) * far_rows
            value_ref[pl.ds(pl.multiple_of(start, 8), far_rows), :] = value[low : low + far_rows]
    half = core if own else 1 - core
    filled = value_ref.at[pl.ds(0, grad_rows)]

    @pl.when(half == 0)
    def _():
        pltpu.make_async_copy(filled, first_ref, sem).start()

    @pl.when(half != 0)
    def _():
        pltpu.make_async_copy(filled, second_ref, sem).start()

    rows = width // 2
    extra = value_ref[grad_rows : grad_rows + rows, :]
    if own:
        extra_ref[...] = extra
    else:
        extra = jnp.where(core == 0, held_ref[...], extra)
        for side in range(2):
            part = extra[:, side * LANES : (side + 1) * LANES].T
            head_ref[:, side * rows : (side + 1) * rows] = part[: head_ref.shape[0]]
        lane = iota(extra.shape, 1)
        loss = jnp.sum(jnp.where((lane == 64) | (lane == 65), extra, 0.0), keepdims=True)
        loss_ref[...] = loss / cell_total
    pltpu.make_async_copy(filled, first_ref, sem).wait()


def assemble(place, pieces, plan, grad_rows, classes, cell_total):
    chips, groups, near_rows, far_rows = plan
    half_rows = chips * groups * (near_rows + far_rows)
    width = pieces[0].shape[1]
    shape = jax.ShapeDtypeStruct
    totals = [shape((grad_rows, width), F32)] * 2
    extra = shape((width // 2, width), F32)
    common = dict(
        scratch_shapes=[pltpu.VMEM((half_rows, width), F32), pltpu.SemaphoreType.DMA],
        compiler_params=pltpu.CompilerParams(vmem_limit_bytes=48 << 20),
        cost_estimate=pl.CostEstimate(flops=1_000_000, bytes_accessed=3_700_000, transcendentals=0),
        name="assemble",
    )
    kernel = functools.partial(assemble_kernel, width, plan, cell_total)
    count = chips + 1
    held = pl.pallas_call(
        kernel,
        in_specs=[scalars(), *whole(count)],
        out_specs=[*hbm(2), *whole(1)],
        out_shape=[*totals, extra],
        **common,
    )(place, *pieces[:count])
    return pl.pallas_call(
        kernel,
        in_specs=[scalars(), *whole(count), *hbm(2), *whole(1)],
        out_specs=[*hbm(2), *whole(2)],
        out_shape=[*totals, shape((classes, width), F32), shape((1, 1), F32)],
        input_output_aliases={count + 1: 0, count + 2: 1},
        **common,
    )(place, *pieces[count:], *held)


def gradient_pieces(place, keep, give, plan):
    chips, groups, near_rows, far_rows = plan
    got = [pairwise(one, "core", 1) for one in give]
    near = [add(pair) for pair in zip(keep[:chips], got[:chips])]
    far = [keep[chips], got[chips]]

    def block(arrays, axis, me, step, rows):
        start = (me ^ step) * rows
        return add([lax.dynamic_slice_in_dim(one, start, rows, axis=0) for one in arrays])

    chip, member = place[CHIP], place[MEMBER]
    far = [block(far, "member", member, step, chips * far_rows) for step in range(groups)]
    near = [near[0]] + [pairwise(near[step], "chip", step) for step in range(1, chips)]
    far = [far[0]] + [pairwise(far[step], "member", step) for step in range(1, groups)]
    near = [block(near, "member", member, step, near_rows) for step in range(groups)]
    far = [block(far, "chip", chip, step, far_rows) for step in range(chips)]
    near = add([near[0]] + [pairwise(near[step], "member", step) for step in range(1, groups)])
    far = add([far[0]] + [pairwise(far[step], "chip", step) for step in range(1, chips)])

    near = jnp.concatenate([near] + [pairwise(near, "member", step) for step in range(1, groups)], axis=0)
    far = jnp.concatenate([far] + [pairwise(far, "chip", step) for step in range(1, chips)], axis=0)
    held = [near] + [pairwise(near, "chip", step) for step in range(1, chips)]
    far = jnp.concatenate([far] + [pairwise(far, "member", step) for step in range(1, groups)], axis=0)
    held += [far]
    return held + [pairwise(piece, "core", 1) for piece in held]


def body(teacher_logits, coverage, features, labels, first_weight, second_weight, head_weight):
    channels, classes = head_weight.shape
    members, tiles_here, flat_width = teacher_logits.shape
    pixels = flat_width // classes
    edge = math.isqrt(pixels)
    groups = lax.axis_size("member")
    chips = lax.axis_size("chip")
    columns = chips * 2
    tile_axes = ("chip", "core")
    block_tiles = tiles_here // groups
    capacity = max(2, 2 * block_tiles // columns)
    local = features[0]
    lines, width = local.shape[:2]
    cells = lines * width
    cell_total = groups * columns * cells
    column = lax.axis_index(tile_axes)
    place = jnp.stack(
        [
            lax.axis_index("core"),
            lax.axis_index("chip"),
            lax.axis_index("member"),
            lax.axis_index(("member", *tile_axes)),
            column == 0,
            column == columns - 1,
        ]
    ).astype(jnp.int32)
    flat = local.reshape(cells, channels)
    first_rows = first_weight.reshape(3, 3 * channels, channels)
    second_rows = second_weight.reshape(3, 3 * channels, channels)
    head = head_weight.T

    before, after = neighbours(flat[: 3 * width], flat[cells - 3 * width :], tile_axes)
    far = teacher_moments(place, teacher_logits, block_tiles, classes, 1)
    got = [pairwise(one, "member", step) for step, one in zip((3, 2), far)]
    near, own = teacher_moments(place, teacher_logits, block_tiles, classes, 0)
    got += [pairwise(near, "member", 1), own]
    label_rows = (
        labels[0].reshape(lines // edge, edge, width // edge, edge).transpose(0, 2, 1, 3).reshape(block_tiles, pixels)
    )
    one, two, log, base, label_sum = student_forward(
        place, before, after, head, label_rows, flat, first_rows, second_rows, own, width
    )
    xt, ht, twot, wt = turn(before, flat, after, one, two, second_rows, width)
    cover = coverage.reshape(groups, 1, block_tiles)
    sent = combine(got, cover, place, twot, classes, members, columns, capacity)
    received = [sent[0]] + [pairwise(sent[step], "chip", step) for step in range(1, chips)]
    passed = pairwise(jnp.concatenate([piece[capacity:] for piece in received], axis=0), "core", 1)
    received = [*received, passed]
    grad_two, top, bottom, head_grad = head_step(
        received, log, base, label_sum, two, twot, head, 1.0 / math.sqrt(cell_total), width
    )
    grad_before, grad_after = neighbours(top, bottom, tile_axes)
    second, inner = second_step(ht, grad_two, wt, one, width)
    rows, extra_rows = 9 * channels, channels // 2
    unit = 8 * groups * chips
    block_rows = -(-(rows + extra_rows) // unit) * 8
    far_rows = block_rows // 24 * 8
    plan = (chips, groups, block_rows - far_rows, far_rows)
    keep, give = first_step(
        place, grad_before, grad_after, grad_two, head_grad, second, inner, wt, one, xt, width, plan
    )
    pieces = gradient_pieces(place, keep, give, plan)
    first_total, second_total, head_total, loss = assemble(
        place, pieces, plan, rows, classes, cell_total
    )
    kernel_shape = (3, 3, channels, channels)
    return (first_total.reshape(kernel_shape), second_total.reshape(kernel_shape), head_total.T, loss[0, 0])


def solution(mesh):
    groups, columns = mesh.shape["member"], mesh.shape["tile"]
    split = jax.sharding.Mesh(mesh.devices.reshape(groups, columns // 2, 2), ("member", "chip", "core"))
    tile = ("chip", "core")
    return jax.shard_map(
        body,
        mesh=split,
        in_specs=(
            P("member", tile, None),
            P(tile),
            P("member", tile, None, None),
            P("member", tile, None),
            P(),
            P(),
            P(),
        ),
        out_specs=(P(), P(), P(), P()),
        check_vma=False,
    )
```

```python
import functools
import math

import jax
import jax.numpy as jnp
from jax import lax
from jax.experimental import pallas as pl
from jax.experimental.pallas import tpu as pltpu
from jax.sharding import PartitionSpec as P

BF16 = jnp.bfloat16
F32 = jnp.float32
LANES = 128
MXU = 256


def whole(count):
    return [pl.BlockSpec(memory_space=pltpu.VMEM)] * count


def iota(shape, axis):
    return lax.broadcasted_iota(jnp.int32, shape, axis)


def dot(left, right):
    return jnp.dot(left, right, preferred_element_type=F32)


def split_lanes(value):
    high = value.astype(BF16).astype(F32)
    return jnp.where(iota(value.shape, 1) < 64, high, value - high).astype(BF16)


def join_lanes(value):
    return value + pltpu.roll(value, 64, 1)


def class_sums(value, classes):
    pick = (iota((MXU, LANES), 0) // classes == iota((MXU, LANES), 1) % (MXU // classes)).astype(BF16)
    high = value.astype(BF16)
    low = (value - high.astype(F32)).astype(BF16)
    return dot(high, pick) + dot(low, pick)


def hbm(count):
    return [pl.BlockSpec(memory_space=pl.ANY)] * count


def scalars():
    return pl.BlockSpec(memory_space=pltpu.SMEM)


CORE, CHIP, MEMBER, DEVICE, FIRST, LAST = range(6)


def teacher_kernel(classes, flip, place_ref, logit_hbm, *refs):
    near_ref, own_ref, x_ref, sum_ref, acc_ref, sems = refs[-6:]
    quarters, members, tiles, width = x_ref.shape
    parts = width // MXU
    per = MXU // classes
    tile_rows = pl.ds(pl.multiple_of(((place_ref[MEMBER] // 2) ^ flip) * tiles, tiles), tiles)
    arrive = [
        pltpu.make_async_copy(logit_hbm.at[:, tile_rows, pl.ds(i * width, width)], x_ref.at[i], sems.at[i])
        for i in range(quarters)
    ]
    for copy in arrive:
        copy.start()
    same = (iota((MXU, MXU), 0) // classes == iota((MXU, MXU), 1) // classes).astype(BF16)
    acc_ref[...] = jnp.zeros_like(acc_ref)

    @pl.loop(0, quarters)
    def _(i):
        pltpu.make_async_copy(logit_hbm.at[:, tile_rows, pl.ds(0, width)], x_ref.at[i], sems.at[i]).wait()
        each = range(parts)
        x = [x_ref[i, :, :, n * MXU : (n + 1) * MXU].astype(F32).reshape(members * tiles, MXU) for n in each]
        root = [jnp.exp(one * 0.25) for one in x]
        total = [dot(one.astype(BF16), same) for one in root]
        root = [one * pl.reciprocal(whole_sum, approx=True) for one, whole_sum in zip(root, total)]
        square = [one * one for one in root]
        power = [one * one for one in square]
        total = [dot(one.astype(BF16), same) for one in power]
        inverse = [pl.reciprocal(one, approx=True) for one in total]
        inverse = [one * (2.0 - whole_sum * one) for one, whole_sum in zip(inverse, total)]
        probs = [(one * other).reshape(members, tiles, MXU) for one, other in zip(power, inverse)]
        first = [functools.reduce(jnp.add, [one[m] for m in range(members)]) for one in probs]
        within = [
            functools.reduce(jnp.add, [one[m] * one[m] for m in range(members)]) - sums * sums * (1.0 / members)
            for one, sums in zip(probs, first)
        ]
        sums = [class_sums(one, classes) for one in within]
        acc = acc_ref[...]
        for n in each:
            acc = jnp.where(iota(acc.shape, 1) % 64 // per == i * parts + n, sums[n], acc)
        acc_ref[...] = acc
        for n in each:
            sum_ref[:, pl.ds(pl.multiple_of(i * width + n * MXU, MXU), MXU)] = first[n].astype(BF16)

    sum_ref[:, quarters * width :] = split_lanes(acc_ref[...])
    block = tiles // 2
    odd = 1 - place_ref[MEMBER] % 2
    near_ref[...] = sum_ref[pl.ds(pl.multiple_of(odd * block, 16), block), :]
    own_ref[...] = sum_ref[pl.ds(pl.multiple_of((1 - odd) * block, 16), block), :]


def teacher_moments(place, logits, tiles, classes, flip, *earlier):
    members, _, width = logits.shape
    quarters = 4
    shape = jax.ShapeDtypeStruct
    outs = [shape((tiles, width + LANES), BF16)] * 2
    return pl.pallas_call(
        functools.partial(teacher_kernel, classes, flip),
        in_specs=[scalars(), *hbm(1 + len(earlier))],
        out_specs=whole(len(outs)),
        out_shape=outs,
        scratch_shapes=[
            pltpu.VMEM((quarters, members, 2 * tiles, width // quarters), BF16),
            pltpu.VMEM((2 * tiles, width + LANES), BF16),
            pltpu.VMEM((2 * tiles, LANES), F32),
            pltpu.SemaphoreType.DMA((quarters,)),
        ],
        compiler_params=pltpu.CompilerParams(vmem_limit_bytes=58 << 20),
        cost_estimate=pl.CostEstimate(flops=1_500_000_000, bytes_accessed=2_600_000, transcendentals=3_000_000),
        name="teacher_moments",
    )(place, logits, *earlier)


def combine_kernel(classes, members, columns, capacity, where_ref, cover_ref, after_ref, *refs):
    chips = columns // 2
    got_refs, out_refs = refs[:-chips], refs[-chips:]
    groups = len(got_refs)
    tiles, extended = got_refs[0].shape
    width = extended - LANES
    means, gaps = [], []
    for start in range(0, width, MXU):
        sums = [got_ref[:, start : start + MXU].astype(F32) for got_ref in got_refs]
        total = sums[0]
        for one in sums[1:]:
            total = total + one
        mean = total * (1.0 / (members * groups))
        means.append(mean.astype(BF16))
        gap = jnp.zeros_like(mean)
        for one in sums:
            off = one * (1.0 / members) - mean
            gap = gap + off * off
        gaps.append(gap)
    between = class_sums(jnp.concatenate(gaps, axis=0), classes)
    lane = iota((tiles, LANES), 1)
    spread = jnp.zeros((tiles, LANES), F32)
    per = MXU // classes
    for i in range(width // MXU):
        spread = jnp.where(lane % 64 // per == i, between[i * tiles : (i + 1) * tiles], spread)
    inner = got_refs[0][:, width:].astype(F32)
    for got_ref in got_refs[1:]:
        inner = inner + got_ref[:, width:].astype(F32)
    spread = spread * (1.0 / groups) + join_lanes(inner) * (1.0 / (members * groups))
    index = (iota((tiles, LANES), 0) + 1).astype(F32).astype(BF16)
    rows = jnp.concatenate([*means, split_lanes(spread), index], axis=1)
    target = cover_ref[where_ref[MEMBER]] ^ (where_ref[CHIP] * 2 + where_ref[CORE])
    onehot = (iota((columns, tiles), 0) == target).astype(F32)
    earlier = (iota((tiles, tiles), 0) < iota((tiles, tiles), 1)).astype(BF16)
    before = dot(onehot.astype(BF16), earlier)
    rank = jnp.sum(before * onehot, axis=0, keepdims=True).astype(jnp.int32)
    place = (iota((columns * capacity, tiles), 0) == target * capacity + rank).astype(BF16)
    sent = dot(place, rows)
    for index, out_ref in enumerate(out_refs):
        out_ref[...] = sent[2 * index * capacity : 2 * (index + 1) * capacity].astype(BF16)


def combine(got, cover, where, after, classes, members, columns, capacity):
    extended = got[0].shape[1]
    return pl.pallas_call(
        functools.partial(combine_kernel, classes, members, columns, capacity),
        in_specs=[pl.BlockSpec(memory_space=pltpu.SMEM), *whole(1), pl.BlockSpec(memory_space=pl.ANY), *whole(len(got))],
        out_specs=whole(columns // 2),
        out_shape=[jax.ShapeDtypeStruct((2 * capacity, extended + LANES), BF16)] * (columns // 2),
        compiler_params=pltpu.CompilerParams(vmem_limit_bytes=12 << 20),
        cost_estimate=pl.CostEstimate(flops=100_000_000, bytes_accessed=1_700_000, transcendentals=0),
        name="combine",
    )(where, cover, after, *got)


def put_shifted(ref, start, value, shift, width):
    rows, channels = value.shape
    col = iota(value.shape, 0) % width
    left = jnp.where(col >= shift, pltpu.roll(value, shift, 0), 0.0)
    right = jnp.where(col < width - shift, pltpu.roll(value, rows - shift, 0), 0.0)
    ref[pl.ds(start, rows), :channels] = left.astype(BF16)
    ref[pl.ds(start, rows), channels : 2 * channels] = value.astype(BF16)
    ref[pl.ds(start, rows), 2 * channels :] = right.astype(BF16)


def three_dots(ref, start, step, rows, weight_ref):
    total = None
    for tap in range(3):
        part = dot(ref[pl.ds(start + tap * step, rows), :], weight_ref[tap])
        total = part if total is None else total + part
    return total


def turned_dot(left, right):
    return lax.dot_general(left, right, (((1,), (1,)), ((), ())), preferred_element_type=F32)


def turned_dot(left, right):
    return lax.dot_general(left, right, (((1,), (1,)), ((), ())), preferred_element_type=F32)


def student_kernel(
    width, place_ref, before_ref, after_ref, head_ref, label_ref, x_ref, first_ref, second_ref, own_ref,
    one_ref, two_ref, log_ref, base_ref, label_sum_ref, xcat, hcat, logit_ref,
):
    cells, channels = x_ref.shape
    halo = before_ref.shape[0]
    block = 4 * width
    put_shifted(xcat, 0, before_ref[...].astype(F32), 1, width)
    put_shifted(xcat, halo + cells, after_ref[...].astype(F32), 1, width)
    for start in range(0, cells, block):
        put_shifted(xcat, halo + start, x_ref[start : start + block, :].astype(F32), 1, width)
    lines = cells // width
    low = jnp.where(place_ref[FIRST] == 1, 2, 0)
    high = jnp.where(place_ref[LAST] == 1, lines + 2, lines + 4)
    for start in range(0, cells + block, block):
        value = jnp.maximum(three_dots(xcat, start, width, block, first_ref), 0.0)
        if start == 0 or start == cells:
            line = start // width + iota(value.shape, 0) // width
            value = jnp.where((line >= low) & (line < high), value, 0.0)
        put_shifted(hcat, start, value, 2, width)
        one_ref[start : start + block, :] = value.astype(BF16)
    head = jnp.concatenate([head_ref[...], head_ref[...]], axis=0)
    for start in range(0, cells, block):
        rows = slice(start, start + block)
        two = jnp.maximum(three_dots(hcat, start, 2 * width, block, second_ref), 0.0).astype(BF16)
        two_ref[rows, :] = two
        logit_ref[rows, :] = turned_dot(two, head)

    tiles, pixels = label_ref.shape
    edge = math.isqrt(pixels)
    across = width // edge
    lane = iota((tiles, LANES), 1)
    even = lane < 64
    label_sum = jnp.zeros((tiles, LANES), F32)
    for pair in range(pixels // 2):
        row, col = 2 * pair // edge, 2 * pair % edge
        parts = []
        for down in range(tiles // across):
            start = (down * edge + row) * width + col
            left = logit_ref[pl.ds(start, across, stride=edge), :]
            right = logit_ref[pl.ds(start + 1, across, stride=edge), :]
            parts.append(jnp.where(iota(left.shape, 1) < 64, left, right))
        value = jnp.concatenate(parts, axis=0)
        top = jnp.where(
            even,
            jnp.max(jnp.where(even, value, -jnp.inf), axis=1, keepdims=True),
            jnp.max(jnp.where(even, -jnp.inf, value), axis=1, keepdims=True),
        )
        value = value - top
        power = jnp.exp(value)
        total = jnp.where(
            even,
            jnp.sum(jnp.where(even, power, 0.0), axis=1, keepdims=True),
            jnp.sum(jnp.where(even, 0.0, power), axis=1, keepdims=True),
        )
        value = value - jnp.log(total)
        label = jnp.where(even, label_ref[:, 2 * pair : 2 * pair + 1], label_ref[:, 2 * pair + 1 : 2 * pair + 2])
        hit = label == lane % 64
        label_sum = label_sum + jnp.where(hit, value, 0.0)
        log_ref[pair * tiles : (pair + 1) * tiles, :] = value
        base_ref[pair * tiles : (pair + 1) * tiles, :] = jnp.exp(value) - hit.astype(F32)
    label_sum_ref[...] = label_sum


def student_forward(place, before, after, head, labels, x, first, second, own, width):
    cells, channels = x.shape
    halo = before.shape[0]
    tiles, pixels = labels.shape
    shape = jax.ShapeDtypeStruct
    return pl.pallas_call(
        functools.partial(student_kernel, width),
        in_specs=[scalars(), *whole(7), *hbm(1)],
        out_specs=whole(5),
        out_shape=[
            shape((cells + 4 * width, channels), BF16),
            shape((cells, channels), BF16),
            shape((cells // 2, LANES), F32),
            shape((cells // 2, LANES), F32),
            shape((tiles, LANES), F32),
        ],
        scratch_shapes=[
            pltpu.VMEM((cells + 2 * halo, 3 * channels), BF16),
            pltpu.VMEM((cells + 4 * width, 3 * channels), BF16),
            pltpu.VMEM((cells, LANES), F32),
        ],
        compiler_params=pltpu.CompilerParams(vmem_limit_bytes=24 << 20),
        cost_estimate=pl.CostEstimate(flops=6_000_000_000, bytes_accessed=12_000_000, transcendentals=500_000),
        name="student_forward",
    )(place, before, after, head, labels, x, first, second, own)


def put_turned(ref, start, value, shift, width):
    rows, channels = value.shape
    col = iota(value.shape, 0) % width
    left = jnp.where(col >= shift, pltpu.roll(value, shift, 0), 0.0)
    right = jnp.where(col < width - shift, pltpu.roll(value, rows - shift, 0), 0.0)
    for tap, one in enumerate((left, value, right)):
        ref[tap * channels : (tap + 1) * channels, pl.ds(start, rows)] = one.T.astype(BF16)


def turn_kernel(
    width, before_ref, x_ref, after_ref, one_ref, two_ref, second_ref, xt_ref, ht_ref, twot_ref, wt_ref
):
    cells, channels = x_ref.shape
    halo = before_ref.shape[0]
    pair = 2 * width
    first = jnp.concatenate([before_ref[halo - width :], x_ref[:width]], axis=0).astype(F32)
    put_turned(xt_ref, 0, first, 1, width)
    last = jnp.concatenate([x_ref[cells - width :], after_ref[:width]], axis=0).astype(F32)
    put_turned(xt_ref, cells, last, 1, width)

    for start in range(pair, cells, pair):
        put_turned(xt_ref, start, x_ref[start - width : start + width, :].astype(F32), 1, width)
    for start in range(0, one_ref.shape[0], pair):
        put_turned(ht_ref, start, one_ref[start : start + pair, :].astype(F32), 2, width)
    for start in range(0, cells, MXU):
        twot_ref[:, start : start + MXU] = two_ref[start : start + MXU, :].astype(F32).T.astype(BF16)
    for i in range(3):
        for tap in range(3):
            part = slice(tap * channels, (tap + 1) * channels)
            mirror = slice((2 - tap) * channels, (3 - tap) * channels)
            wt_ref[i, part, :] = second_ref[i, mirror, :].astype(F32).T.astype(BF16)


def turn(before, x, after, one, two, second, width):
    cells, channels = x.shape
    shape = jax.ShapeDtypeStruct
    return pl.pallas_call(
        functools.partial(turn_kernel, width),
        in_specs=whole(6),
        out_specs=whole(4),
        out_shape=[
            shape((3 * channels, cells + 2 * width), BF16),
            shape((3 * channels, cells + 4 * width), BF16),
            shape((channels, cells), BF16),
            shape((3, 3 * channels, channels), BF16),
        ],
        compiler_params=pltpu.CompilerParams(vmem_limit_bytes=20 << 20),
        cost_estimate=pl.CostEstimate(flops=3_000_000_000, bytes_accessed=14_000_000, transcendentals=0),
        name="turn",
    )(before, x, after, one, two, second)


def head_kernel(
    scale, width, log_ref, base_ref, label_sum_ref, two_ref, twot_ref, head_ref, *refs
):
    *got_refs, grad_ref, top_ref, bottom_ref, head_grad_ref, got_ref, natural = refs
    slots, extended = got_ref.shape
    held = [one[...].astype(F32) for one in got_refs]
    held = [one[: one.shape[0] // 2] for one in held[:-1]] + held[-1:]
    got_ref[...] = jnp.concatenate(held, axis=0).astype(BF16)
    tiles = label_sum_ref.shape[0]
    flat = extended - 2 * LANES
    pixels = flat // 64
    edge = math.isqrt(pixels)
    across = width // edge
    index = got_ref[:, flat + LANES :].astype(F32)
    take = (index == (iota((slots, LANES), 1) + 1).astype(F32)).astype(F32).T[:tiles].astype(BF16)
    spread = join_lanes(dot(take, got_ref[:, flat : flat + LANES]))
    weight = 1.0 / (0.1 + spread)
    even = iota((tiles, LANES), 1) < 64
    loss = -label_sum_ref[...]
    for pair in range(pixels // 2):
        rows = slice(pair * tiles, (pair + 1) * tiles)
        if pair % 2 == 0:
            both = dot(take, got_ref[:, pair * LANES : (pair + 2) * LANES])
        mean = both[:, pair % 2 * LANES : (pair % 2 + 1) * LANES]
        cell = jnp.where(even, weight[:, 2 * pair : 2 * pair + 1], weight[:, 2 * pair + 1 : 2 * pair + 2])
        value = log_ref[rows, :]
        held = mean > 0
        loss = loss + cell * jnp.where(held, mean * (jnp.log(jnp.where(held, mean, 1.0)) - value), 0.0)
        grad = (cell * (jnp.exp(value) - mean) + base_ref[rows, :]) * scale
        turned = pltpu.roll(grad, 64, 1)
        row, col = 2 * pair // edge, 2 * pair % edge
        for down in range(tiles // across):
            start = (down * edge + row) * width + col
            natural[pl.ds(start, across, stride=edge), :] = grad[down * across : (down + 1) * across]
            natural[pl.ds(start + 1, across, stride=edge), :] = turned[down * across : (down + 1) * across]
    cells, channels = two_ref.shape
    logit_grad = natural[...].astype(BF16)
    head = jnp.concatenate([head_ref[...], jnp.zeros_like(head_ref)], axis=0)
    head_grad_ref[:channels, :] = dot(twot_ref[...], logit_grad)
    head_grad_ref[channels:, :] = loss
    block = 4 * width
    for start in range(0, cells, block):
        rows = slice(start, start + block)
        grad = dot(logit_grad[rows], head)
        grad_ref[rows, :] = jnp.where(two_ref[rows, :].astype(F32) > 0, grad, 0.0).astype(BF16)
    top_ref[...] = grad_ref[: 2 * width, :]
    bottom_ref[...] = grad_ref[cells - 2 * width :, :]


def head_step(got, log, base, label_sum, two, twot, head, scale, width):
    cells, channels = two.shape
    shape = jax.ShapeDtypeStruct
    return pl.pallas_call(
        functools.partial(head_kernel, scale, width),
        in_specs=whole(6 + len(got)),
        out_specs=whole(4),
        out_shape=[
            shape((cells, channels), BF16),
            shape((2 * width, channels), BF16),
            shape((2 * width, channels), BF16),
            shape((channels + label_sum.shape[0], LANES), F32),
        ],
        scratch_shapes=[
            pltpu.VMEM((2 * got[-1].shape[0], got[-1].shape[1]), BF16),
            pltpu.VMEM((cells, LANES), F32),
        ],
        compiler_params=pltpu.CompilerParams(vmem_limit_bytes=14 << 20),
        cost_estimate=pl.CostEstimate(flops=400_000_000, bytes_accessed=5_000_000, transcendentals=500_000),
        name="head_step",
    )(log, base, label_sum, two, twot, head, *got)


def inner_dots(ref, start, step, rows, weight_ref):
    total = None
    for tap in range(3):
        part = dot(ref[start + (2 - tap) * step : start + (2 - tap) * step + rows, :], weight_ref[tap])
        total = part if total is None else total + part
    return total


def second_kernel(width, ht_ref, grad_ref, wt_ref, one_ref, out_ref, inner_ref, gcat):
    cells, channels = grad_ref.shape
    block = 4 * width
    halo = 2 * width
    for start in range(0, cells, block):
        put_shifted(gcat, start, grad_ref[start : start + block, :].astype(F32), 2, width)
    for tap in range(3):
        part = dot(ht_ref[:, halo * tap : halo * tap + cells], grad_ref[...])
        out_ref[tap * 3 * channels : (tap + 1) * 3 * channels, :] = part.astype(BF16)
    for start in range(block, cells - block, block):
        value = inner_dots(gcat, start - halo, halo, block, wt_ref)
        held = one_ref[halo + start : halo + start + block, :].astype(F32) > 0
        inner_ref[start - block : start, :] = jnp.where(held, value, 0.0).astype(BF16)


def second_step(ht, grad, wt, one, width):
    cells, channels = grad.shape
    return pl.pallas_call(
        functools.partial(second_kernel, width),
        in_specs=whole(4),
        out_specs=whole(2),
        out_shape=[
            jax.ShapeDtypeStruct((9 * channels, channels), BF16),
            jax.ShapeDtypeStruct((cells - 8 * width, channels), BF16),
        ],
        scratch_shapes=[pltpu.VMEM((cells, 3 * channels), BF16)],
        compiler_params=pltpu.CompilerParams(vmem_limit_bytes=20 << 20),
        cost_estimate=pl.CostEstimate(flops=4_500_000_000, bytes_accessed=9_000_000, transcendentals=0),
        name="second_step",
    )(ht, grad, wt, one)


def first_kernel(width, plan, place_ref, before_ref, after_ref, grad_ref, head_grad_ref, second_ref, inner_ref, *refs):
    wt_ref, one_ref, xt_ref, *refs = refs
    chips, groups, near_rows, far_rows = plan
    keep_refs, give_refs, refs = refs[:2], refs[2:4], refs[4:]
    gtop, gbottom, padded, halves, sem = refs
    cells, channels = grad_ref.shape
    rows = 9 * channels
    used = rows + channels // 2
    half = halves.shape[1]
    second_copy = pltpu.make_async_copy(second_ref, halves.at[1, pl.ds(0, rows)], sem)
    second_copy.start()
    halo = before_ref.shape[0]
    block = 4 * width
    inside = 3 * halo
    put_shifted(gtop, 0, before_ref[...].astype(F32), 2, width)
    put_shifted(gtop, halo, grad_ref[:inside, :].astype(F32), 2, width)
    put_shifted(gbottom, 0, grad_ref[cells - inside :, :].astype(F32), 2, width)
    put_shifted(gbottom, inside, after_ref[...].astype(F32), 2, width)
    padded[:halo, :] = jnp.zeros((halo, channels), BF16)
    padded[halo + cells :, :] = jnp.zeros((halo, channels), BF16)
    padded[halo + block : halo + cells - block, :] = inner_ref[...]
    for ref, start in ((gtop, 0), (gbottom, cells - block)):
        value = inner_dots(ref, 0, halo, block, wt_ref)
        held = one_ref[halo + start : halo + start + block, :].astype(F32) > 0
        padded[halo + start : halo + start + block, :] = jnp.where(held, value, 0.0).astype(BF16)
    span = cells + 2 * width
    for tap in range(3):
        part = dot(xt_ref[...], padded[(2 - tap) * width : (2 - tap) * width + span, :])
        halves[0, tap * 3 * channels : (tap + 1) * 3 * channels, :] = part.astype(BF16)
    lane = iota((channels // 2, LANES), 1)
    loss = jnp.sum(head_grad_ref[channels:, :])
    high = loss.astype(BF16).astype(F32)
    extra = jnp.where(lane == 64, high, jnp.where(lane == 65, loss - high, 0.0))
    extra = jnp.where(iota(lane.shape, 0) == place_ref[DEVICE] % (channels // 2), extra, 0.0)
    for side in range(2):
        value = jnp.where(lane < 64, head_grad_ref[side * channels // 2 : (side + 1) * channels // 2, :], extra)
        halves[0, rows:used, side * LANES : (side + 1) * LANES] = value.astype(BF16)
    if half > used:
        halves[0, used:, :] = jnp.zeros((half - used, channels), BF16)
    halves[1, rows:, :] = jnp.zeros((half - rows, channels), BF16)
    second_copy.wait()
    core, chip = place_ref[CORE], place_ref[CHIP]
    size = groups * near_rows
    for step in range(chips):
        low = pl.multiple_of((chip ^ step) * size, 16)
        give_refs[0][step * size : (step + 1) * size, :] = halves[1 - core, pl.ds(low, size), :]
        keep_refs[0][step * size : (step + 1) * size, :] = halves[core, pl.ds(low, size), :]
    give_refs[1][...] = halves[1 - core, chips * size :, :]
    keep_refs[1][...] = halves[core, chips * size :, :]


def first_step(place, before, after, grad, head_grad, second, inner, wt, one, xt, width, plan):
    cells, channels = grad.shape
    halo = before.shape[0]
    chips, groups, near_rows, far_rows = plan
    half_rows = chips * groups * (near_rows + far_rows)
    piece = [jax.ShapeDtypeStruct((chips * groups * near_rows, channels), BF16)]
    piece += [jax.ShapeDtypeStruct((chips * groups * far_rows, channels), BF16)]
    outs = pl.pallas_call(
        functools.partial(first_kernel, width, plan),
        in_specs=[scalars(), *whole(9)],
        out_specs=whole(4),
        out_shape=piece * 2,
        scratch_shapes=[
            pltpu.VMEM((4 * halo, 3 * channels), BF16),
            pltpu.VMEM((4 * halo, 3 * channels), BF16),
            pltpu.VMEM((cells + 4 * width, channels), BF16),
            pltpu.VMEM((2, half_rows, channels), BF16),
            pltpu.SemaphoreType.DMA,
        ],
        compiler_params=pltpu.CompilerParams(vmem_limit_bytes=24 << 20),
        cost_estimate=pl.CostEstimate(flops=5_000_000_000, bytes_accessed=10_000_000, transcendentals=0),
        name="first_step",
    )(place, before, after, grad, head_grad, second, inner, wt, one, xt)
    return (outs[:2], outs[2:])


def neighbours(first, last, axis):
    count = lax.axis_size(axis)
    up = [(i, i + 1) for i in range(count - 1)]
    down = [(i + 1, i) for i in range(count - 1)]
    return (lax.ppermute(last, axis, up), lax.ppermute(first, axis, down))


def pairwise(array, axis, step):
    count = lax.axis_size(axis)
    return lax.ppermute(array, axis, [(i, i ^ step) for i in range(count)])


def add(arrays):
    return functools.reduce(jnp.add, [array.astype(F32) for array in arrays]).astype(BF16)


def assemble_kernel(width, plan, cell_total, place_ref, *refs):
    chips, groups, near_rows, far_rows = plan
    pieces, refs = refs[: chips + 1], refs[chips + 1 :]
    own = len(refs) == 5
    if own:
        first_ref, second_ref, extra_ref, value_ref, sem = refs
    else:
        _, _, held_ref, first_ref, second_ref, head_ref, loss_ref, value_ref, sem = refs
    grad_rows = first_ref.shape[0]
    core, chip, member = place_ref[CORE], place_ref[CHIP], place_ref[MEMBER]
    for s in range(chips):
        value = pieces[s][...].astype(F32)
        for u in range(groups):
            start = pl.multiple_of(((chip ^ s) * groups + (member ^ u)) * near_rows, 8)
            value_ref[pl.ds(start, near_rows), :] = value[u * near_rows : (u + 1) * near_rows]
    value = pieces[chips][...].astype(F32)
    for u in range(groups):
        for s in range(chips):
            low = (u * chips + s) * far_rows
            start = chips * groups * near_rows + ((member ^ u) * chips + (chip ^ s)) * far_rows
            value_ref[pl.ds(pl.multiple_of(start, 8), far_rows), :] = value[low : low + far_rows]
    half = core if own else 1 - core
    filled = value_ref.at[pl.ds(0, grad_rows)]

    @pl.when(half == 0)
    def _():
        pltpu.make_async_copy(filled, first_ref, sem).start()

    @pl.when(half != 0)
    def _():
        pltpu.make_async_copy(filled, second_ref, sem).start()

    rows = width // 2
    extra = value_ref[grad_rows : grad_rows + rows, :]
    if own:
        extra_ref[...] = extra
    else:
        extra = jnp.where(core == 0, held_ref[...], extra)
        for side in range(2):
            part = extra[:, side * LANES : (side + 1) * LANES].T
            head_ref[:, side * rows : (side + 1) * rows] = part[: head_ref.shape[0]]
        lane = iota(extra.shape, 1)
        loss = jnp.sum(jnp.where((lane == 64) | (lane == 65), extra, 0.0), keepdims=True)
        loss_ref[...] = loss / cell_total
    pltpu.make_async_copy(filled, first_ref, sem).wait()


def assemble(place, pieces, plan, grad_rows, classes, cell_total):
    chips, groups, near_rows, far_rows = plan
    half_rows = chips * groups * (near_rows + far_rows)
    width = pieces[0].shape[1]
    shape = jax.ShapeDtypeStruct
    totals = [shape((grad_rows, width), F32)] * 2
    extra = shape((width // 2, width), F32)
    common = dict(
        scratch_shapes=[pltpu.VMEM((half_rows, width), F32), pltpu.SemaphoreType.DMA],
        compiler_params=pltpu.CompilerParams(vmem_limit_bytes=48 << 20),
        cost_estimate=pl.CostEstimate(flops=1_000_000, bytes_accessed=3_700_000, transcendentals=0),
        name="assemble",
    )
    kernel = functools.partial(assemble_kernel, width, plan, cell_total)
    count = chips + 1
    held = pl.pallas_call(
        kernel,
        in_specs=[scalars(), *whole(count)],
        out_specs=[*hbm(2), *whole(1)],
        out_shape=[*totals, extra],
        **common,
    )(place, *pieces[:count])
    return pl.pallas_call(
        kernel,
        in_specs=[scalars(), *whole(count), *hbm(2), *whole(1)],
        out_specs=[*hbm(2), *whole(2)],
        out_shape=[*totals, shape((classes, width), F32), shape((1, 1), F32)],
        input_output_aliases={count + 1: 0, count + 2: 1},
        **common,
    )(place, *pieces[count:], *held)


def gradient_pieces(place, keep, give, plan):
    chips, groups, near_rows, far_rows = plan
    got = [pairwise(one, "core", 1) for one in give]
    size = groups * near_rows
    near = [add([one[step * size : (step + 1) * size] for one in (keep[0], got[0])]) for step in range(chips)]
    far = [keep[1], got[1]]

    def block(arrays, axis, me, step, rows):
        start = (me ^ step) * rows
        return add([lax.dynamic_slice_in_dim(one, start, rows, axis=0) for one in arrays])

    chip, member = place[CHIP], place[MEMBER]
    far = [block(far, "member", member, step, chips * far_rows) for step in range(groups)]
    near = [near[0]] + [pairwise(near[step], "chip", step) for step in range(1, chips)]
    far = [far[0]] + [pairwise(far[step], "member", step) for step in range(1, groups)]
    near = [block(near, "member", member, step, near_rows) for step in range(groups)]
    far = [block(far, "chip", chip, step, far_rows) for step in range(chips)]
    near = add([near[0]] + [pairwise(near[step], "member", step) for step in range(1, groups)])
    far = add([far[0]] + [pairwise(far[step], "chip", step) for step in range(1, chips)])

    near = jnp.concatenate([near] + [pairwise(near, "member", step) for step in range(1, groups)], axis=0)
    far = jnp.concatenate([far] + [pairwise(far, "chip", step) for step in range(1, chips)], axis=0)
    near, far = lax.optimization_barrier((near, far))
    held = [near] + [pairwise(near, "chip", step) for step in range(1, chips)]
    far = jnp.concatenate([far] + [pairwise(far, "member", step) for step in range(1, groups)], axis=0)
    held += [far]
    return held + [pairwise(piece, "core", 1) for piece in held]


def body(teacher_logits, coverage, features, labels, first_weight, second_weight, head_weight):
    channels, classes = head_weight.shape
    members, tiles_here, flat_width = teacher_logits.shape
    pixels = flat_width // classes
    edge = math.isqrt(pixels)
    groups = lax.axis_size("member")
    chips = lax.axis_size("chip")
    columns = chips * 2
    tile_axes = ("chip", "core")
    block_tiles = tiles_here // groups
    capacity = max(2, 2 * block_tiles // columns)
    local = features[0]
    lines, width = local.shape[:2]
    cells = lines * width
    cell_total = groups * columns * cells
    column = lax.axis_index(tile_axes)
    place = jnp.stack(
        [
            lax.axis_index("core"),
            lax.axis_index("chip"),
            lax.axis_index("member"),
            lax.axis_index(("member", *tile_axes)),
            column == 0,
            column == columns - 1,
        ]
    ).astype(jnp.int32)
    flat = local.reshape(cells, channels)
    first_rows = first_weight.reshape(3, 3 * channels, channels)
    second_rows = second_weight.reshape(3, 3 * channels, channels)
    head = head_weight.T

    before, after = neighbours(flat[: 3 * width], flat[cells - 3 * width :], tile_axes)
    far = teacher_moments(place, teacher_logits, block_tiles, classes, 1)
    got = [pairwise(one, "member", step) for step, one in zip((3, 2), far)]
    near, own = teacher_moments(place, teacher_logits, block_tiles, classes, 0)
    got += [pairwise(near, "member", 1), own]
    label_rows = (
        labels[0].reshape(lines // edge, edge, width // edge, edge).transpose(0, 2, 1, 3).reshape(block_tiles, pixels)
    )
    one, two, log, base, label_sum = student_forward(
        place, before, after, head, label_rows, flat, first_rows, second_rows, own, width
    )
    xt, ht, twot, wt = turn(before, flat, after, one, two, second_rows, width)
    cover = coverage.reshape(groups, 1, block_tiles)
    sent = combine(got, cover, place, twot, classes, members, columns, capacity)
    received = [sent[0]] + [pairwise(sent[step], "chip", step) for step in range(1, chips)]
    passed = pairwise(jnp.concatenate([piece[capacity:] for piece in received], axis=0), "core", 1)
    received = [*received, passed]
    grad_two, top, bottom, head_grad = head_step(
        received, log, base, label_sum, two, twot, head, 1.0 / math.sqrt(cell_total), width
    )
    grad_before, grad_after = neighbours(top, bottom, tile_axes)
    second, inner = second_step(ht, grad_two, wt, one, width)
    rows, extra_rows = 9 * channels, channels // 2
    unit = 8 * groups * chips
    block_rows = -(-(rows + extra_rows) // unit) * 8
    far_rows = block_rows // 24 * 8
    plan = (chips, groups, block_rows - far_rows, far_rows)
    keep, give = first_step(
        place, grad_before, grad_after, grad_two, head_grad, second, inner, wt, one, xt, width, plan
    )
    pieces = gradient_pieces(place, keep, give, plan)
    first_total, second_total, head_total, loss = assemble(
        place, pieces, plan, rows, classes, cell_total
    )
    kernel_shape = (3, 3, channels, channels)
    return (first_total.reshape(kernel_shape), second_total.reshape(kernel_shape), head_total.T, loss[0, 0])


def solution(mesh):
    groups, columns = mesh.shape["member"], mesh.shape["tile"]
    split = jax.sharding.Mesh(mesh.devices.reshape(groups, columns // 2, 2), ("member", "chip", "core"))
    tile = ("chip", "core")
    return jax.shard_map(
        body,
        mesh=split,
        in_specs=(
            P("member", tile, None),
            P(tile),
            P("member", tile, None, None),
            P("member", tile, None),
            P(),
            P(),
            P(),
        ),
        out_specs=(P(), P(), P(), P()),
        check_vma=False,
    )
```

```python
import functools
import math

import jax
import jax.numpy as jnp
from jax import lax
from jax.experimental import pallas as pl
from jax.experimental.pallas import tpu as pltpu
from jax.sharding import PartitionSpec as P

BF16 = jnp.bfloat16
F32 = jnp.float32
LANES = 128
MXU = 256


def whole(count):
    return [pl.BlockSpec(memory_space=pltpu.VMEM)] * count


def iota(shape, axis):
    return lax.broadcasted_iota(jnp.int32, shape, axis)


def dot(left, right):
    return jnp.dot(left, right, preferred_element_type=F32)


def split_lanes(value):
    high = value.astype(BF16).astype(F32)
    return jnp.where(iota(value.shape, 1) < 64, high, value - high).astype(BF16)


def join_lanes(value):
    return value + pltpu.roll(value, 64, 1)


def class_sums(value, classes):
    pick = (iota((MXU, LANES), 0) // classes == iota((MXU, LANES), 1) % (MXU // classes)).astype(BF16)
    high = value.astype(BF16)
    low = (value - high.astype(F32)).astype(BF16)
    return dot(high, pick) + dot(low, pick)


def hbm(count):
    return [pl.BlockSpec(memory_space=pl.ANY)] * count


def scalars():
    return pl.BlockSpec(memory_space=pltpu.SMEM)


CORE, CHIP, MEMBER, DEVICE, FIRST, LAST = range(6)


def teacher_kernel(classes, flip, logit_hbm, *refs):
    member = lax.axis_index("member")
    near_ref, own_ref, x_ref, sum_ref, acc_ref, sems = refs[-6:]
    quarters, members, tiles, width = x_ref.shape
    parts = width // MXU
    per = MXU // classes
    tile_rows = pl.ds(pl.multiple_of(((member // 2) ^ flip) * tiles, tiles), tiles)
    arrive = [
        pltpu.make_async_copy(logit_hbm.at[:, tile_rows, pl.ds(i * width, width)], x_ref.at[i], sems.at[i])
        for i in range(quarters)
    ]
    for copy in arrive:
        copy.start()
    same = (iota((MXU, MXU), 0) // classes == iota((MXU, MXU), 1) // classes).astype(BF16)
    acc_ref[...] = jnp.zeros_like(acc_ref)

    @pl.loop(0, quarters)
    def _(i):
        pltpu.make_async_copy(logit_hbm.at[:, tile_rows, pl.ds(0, width)], x_ref.at[i], sems.at[i]).wait()
        each = range(parts)
        x = [x_ref[i, :, :, n * MXU : (n + 1) * MXU].astype(F32).reshape(members * tiles, MXU) for n in each]
        root = [jnp.exp(one * 0.25) for one in x]
        total = [dot(one.astype(BF16), same) for one in root]
        root = [one * pl.reciprocal(whole_sum, approx=True) for one, whole_sum in zip(root, total)]
        square = [one * one for one in root]
        power = [one * one for one in square]
        total = [dot(one.astype(BF16), same) for one in power]
        inverse = [pl.reciprocal(one, approx=True) for one in total]
        inverse = [one * (2.0 - whole_sum * one) for one, whole_sum in zip(inverse, total)]
        probs = [(one * other).reshape(members, tiles, MXU) for one, other in zip(power, inverse)]
        first = [functools.reduce(jnp.add, [one[m] for m in range(members)]) for one in probs]
        within = [
            functools.reduce(jnp.add, [one[m] * one[m] for m in range(members)]) - sums * sums * (1.0 / members)
            for one, sums in zip(probs, first)
        ]
        sums = [class_sums(one, classes) for one in within]
        acc = acc_ref[...]
        for n in each:
            acc = jnp.where(iota(acc.shape, 1) % 64 // per == i * parts + n, sums[n], acc)
        acc_ref[...] = acc
        for n in each:
            sum_ref[:, pl.ds(pl.multiple_of(i * width + n * MXU, MXU), MXU)] = first[n].astype(BF16)

    sum_ref[:, quarters * width :] = split_lanes(acc_ref[...])
    block = tiles // 2
    odd = 1 - member % 2
    near_ref[...] = sum_ref[pl.ds(pl.multiple_of(odd * block, 16), block), :]
    own_ref[...] = sum_ref[pl.ds(pl.multiple_of((1 - odd) * block, 16), block), :]


def teacher_moments(logits, tiles, classes, flip, *earlier):
    members, _, width = logits.shape
    quarters = 4
    shape = jax.ShapeDtypeStruct
    outs = [shape((tiles, width + LANES), BF16)] * 2
    return pl.pallas_call(
        functools.partial(teacher_kernel, classes, flip),
        in_specs=hbm(1 + len(earlier)),
        out_specs=whole(len(outs)),
        out_shape=outs,
        scratch_shapes=[
            pltpu.VMEM((quarters, members, 2 * tiles, width // quarters), BF16),
            pltpu.VMEM((2 * tiles, width + LANES), BF16),
            pltpu.VMEM((2 * tiles, LANES), F32),
            pltpu.SemaphoreType.DMA((quarters,)),
        ],
        compiler_params=pltpu.CompilerParams(vmem_limit_bytes=58 << 20),
        cost_estimate=pl.CostEstimate(flops=1_500_000_000, bytes_accessed=2_600_000, transcendentals=3_000_000),
        name="teacher_moments",
    )(logits, *earlier)


def combine_kernel(classes, members, columns, capacity, where_ref, cover_ref, after_ref, *refs):
    chips = columns // 2
    got_refs, out_refs = refs[:-chips], refs[-chips:]
    groups = len(got_refs)
    tiles, extended = got_refs[0].shape
    width = extended - LANES
    means, gaps = [], []
    for start in range(0, width, MXU):
        sums = [got_ref[:, start : start + MXU].astype(F32) for got_ref in got_refs]
        total = sums[0]
        for one in sums[1:]:
            total = total + one
        mean = total * (1.0 / (members * groups))
        means.append(mean.astype(BF16))
        gap = jnp.zeros_like(mean)
        for one in sums:
            off = one * (1.0 / members) - mean
            gap = gap + off * off
        gaps.append(gap)
    between = class_sums(jnp.concatenate(gaps, axis=0), classes)
    lane = iota((tiles, LANES), 1)
    spread = jnp.zeros((tiles, LANES), F32)
    per = MXU // classes
    for i in range(width // MXU):
        spread = jnp.where(lane % 64 // per == i, between[i * tiles : (i + 1) * tiles], spread)
    inner = got_refs[0][:, width:].astype(F32)
    for got_ref in got_refs[1:]:
        inner = inner + got_ref[:, width:].astype(F32)
    spread = spread * (1.0 / groups) + join_lanes(inner) * (1.0 / (members * groups))
    index = (iota((tiles, LANES), 0) + 1).astype(F32).astype(BF16)
    rows = jnp.concatenate([*means, split_lanes(spread), index], axis=1)
    target = cover_ref[where_ref[MEMBER]] ^ (where_ref[CHIP] * 2 + where_ref[CORE])
    onehot = (iota((columns, tiles), 0) == target).astype(F32)
    earlier = (iota((tiles, tiles), 0) < iota((tiles, tiles), 1)).astype(BF16)
    before = dot(onehot.astype(BF16), earlier)
    rank = jnp.sum(before * onehot, axis=0, keepdims=True).astype(jnp.int32)
    place = (iota((columns * capacity, tiles), 0) == target * capacity + rank).astype(BF16)
    sent = dot(place, rows)
    for index, out_ref in enumerate(out_refs):
        out_ref[...] = sent[2 * index * capacity : 2 * (index + 1) * capacity].astype(BF16)


def combine(got, cover, where, after, classes, members, columns, capacity):
    extended = got[0].shape[1]
    return pl.pallas_call(
        functools.partial(combine_kernel, classes, members, columns, capacity),
        in_specs=[pl.BlockSpec(memory_space=pltpu.SMEM), *whole(1), pl.BlockSpec(memory_space=pl.ANY), *whole(len(got))],
        out_specs=whole(columns // 2),
        out_shape=[jax.ShapeDtypeStruct((2 * capacity, extended + LANES), BF16)] * (columns // 2),
        compiler_params=pltpu.CompilerParams(vmem_limit_bytes=12 << 20),
        cost_estimate=pl.CostEstimate(flops=100_000_000, bytes_accessed=1_700_000, transcendentals=0),
        name="combine",
    )(where, cover, after, *got)


def put_shifted(ref, start, value, shift, width):
    rows, channels = value.shape
    col = iota(value.shape, 0) % width
    left = jnp.where(col >= shift, pltpu.roll(value, shift, 0), 0.0)
    right = jnp.where(col < width - shift, pltpu.roll(value, rows - shift, 0), 0.0)
    ref[pl.ds(start, rows), :channels] = left.astype(BF16)
    ref[pl.ds(start, rows), channels : 2 * channels] = value.astype(BF16)
    ref[pl.ds(start, rows), 2 * channels :] = right.astype(BF16)


def three_dots(ref, start, step, rows, weight_ref):
    total = None
    for tap in range(3):
        part = dot(ref[pl.ds(start + tap * step, rows), :], weight_ref[tap])
        total = part if total is None else total + part
    return total


def turned_dot(left, right):
    return lax.dot_general(left, right, (((1,), (1,)), ((), ())), preferred_element_type=F32)


def turned_dot(left, right):
    return lax.dot_general(left, right, (((1,), (1,)), ((), ())), preferred_element_type=F32)


def student_kernel(
    width, place_ref, before_ref, after_ref, head_ref, label_ref, x_ref, first_ref, second_ref, own_ref,
    one_ref, two_ref, log_ref, base_ref, label_sum_ref, xcat, hcat, logit_ref,
):
    cells, channels = x_ref.shape
    halo = before_ref.shape[0]
    block = 4 * width
    put_shifted(xcat, 0, before_ref[...].astype(F32), 1, width)
    put_shifted(xcat, halo + cells, after_ref[...].astype(F32), 1, width)
    for start in range(0, cells, block):
        put_shifted(xcat, halo + start, x_ref[start : start + block, :].astype(F32), 1, width)
    lines = cells // width
    low = jnp.where(place_ref[FIRST] == 1, 2, 0)
    high = jnp.where(place_ref[LAST] == 1, lines + 2, lines + 4)
    for start in range(0, cells + block, block):
        value = jnp.maximum(three_dots(xcat, start, width, block, first_ref), 0.0)
        if start == 0 or start == cells:
            line = start // width + iota(value.shape, 0) // width
            value = jnp.where((line >= low) & (line < high), value, 0.0)
        put_shifted(hcat, start, value, 2, width)
        one_ref[start : start + block, :] = value.astype(BF16)
    head = jnp.concatenate([head_ref[...], head_ref[...]], axis=0)
    for start in range(0, cells, block):
        rows = slice(start, start + block)
        two = jnp.maximum(three_dots(hcat, start, 2 * width, block, second_ref), 0.0).astype(BF16)
        two_ref[rows, :] = two
        logit_ref[rows, :] = turned_dot(two, head)

    tiles, pixels = label_ref.shape
    edge = math.isqrt(pixels)
    across = width // edge
    lane = iota((tiles, LANES), 1)
    even = lane < 64
    label_sum = jnp.zeros((tiles, LANES), F32)
    for pair in range(pixels // 2):
        row, col = 2 * pair // edge, 2 * pair % edge
        parts = []
        for down in range(tiles // across):
            start = (down * edge + row) * width + col
            left = logit_ref[pl.ds(start, across, stride=edge), :]
            right = logit_ref[pl.ds(start + 1, across, stride=edge), :]
            parts.append(jnp.where(iota(left.shape, 1) < 64, left, right))
        value = jnp.concatenate(parts, axis=0)
        top = jnp.where(
            even,
            jnp.max(jnp.where(even, value, -jnp.inf), axis=1, keepdims=True),
            jnp.max(jnp.where(even, -jnp.inf, value), axis=1, keepdims=True),
        )
        value = value - top
        power = jnp.exp(value)
        total = jnp.where(
            even,
            jnp.sum(jnp.where(even, power, 0.0), axis=1, keepdims=True),
            jnp.sum(jnp.where(even, 0.0, power), axis=1, keepdims=True),
        )
        value = value - jnp.log(total)
        label = jnp.where(even, label_ref[:, 2 * pair : 2 * pair + 1], label_ref[:, 2 * pair + 1 : 2 * pair + 2])
        hit = label == lane % 64
        label_sum = label_sum + jnp.where(hit, value, 0.0)
        log_ref[pair * tiles : (pair + 1) * tiles, :] = value
        base_ref[pair * tiles : (pair + 1) * tiles, :] = jnp.exp(value) - hit.astype(F32)
    label_sum_ref[...] = label_sum


def student_forward(place, before, after, head, labels, x, first, second, own, width):
    cells, channels = x.shape
    halo = before.shape[0]
    tiles, pixels = labels.shape
    shape = jax.ShapeDtypeStruct
    return pl.pallas_call(
        functools.partial(student_kernel, width),
        in_specs=[scalars(), *whole(7), *hbm(1)],
        out_specs=whole(5),
        out_shape=[
            shape((cells + 4 * width, channels), BF16),
            shape((cells, channels), BF16),
            shape((cells // 2, LANES), F32),
            shape((cells // 2, LANES), F32),
            shape((tiles, LANES), F32),
        ],
        scratch_shapes=[
            pltpu.VMEM((cells + 2 * halo, 3 * channels), BF16),
            pltpu.VMEM((cells + 4 * width, 3 * channels), BF16),
            pltpu.VMEM((cells, LANES), F32),
        ],
        compiler_params=pltpu.CompilerParams(vmem_limit_bytes=24 << 20),
        cost_estimate=pl.CostEstimate(flops=6_000_000_000, bytes_accessed=12_000_000, transcendentals=500_000),
        name="student_forward",
    )(place, before, after, head, labels, x, first, second, own)


def put_turned(ref, start, value, shift, width):
    rows, channels = value.shape
    col = iota(value.shape, 0) % width
    left = jnp.where(col >= shift, pltpu.roll(value, shift, 0), 0.0)
    right = jnp.where(col < width - shift, pltpu.roll(value, rows - shift, 0), 0.0)
    for tap, one in enumerate((left, value, right)):
        ref[tap * channels : (tap + 1) * channels, pl.ds(start, rows)] = one.T.astype(BF16)


def turn_kernel(
    width, before_ref, x_ref, after_ref, one_ref, two_ref, second_ref, xt_ref, ht_ref, twot_ref, wt_ref
):
    cells, channels = x_ref.shape
    halo = before_ref.shape[0]
    pair = 2 * width
    first = jnp.concatenate([before_ref[halo - width :], x_ref[:width]], axis=0).astype(F32)
    put_turned(xt_ref, 0, first, 1, width)
    last = jnp.concatenate([x_ref[cells - width :], after_ref[:width]], axis=0).astype(F32)
    put_turned(xt_ref, cells, last, 1, width)

    for start in range(pair, cells, pair):
        put_turned(xt_ref, start, x_ref[start - width : start + width, :].astype(F32), 1, width)
    for start in range(0, one_ref.shape[0], pair):
        put_turned(ht_ref, start, one_ref[start : start + pair, :].astype(F32), 2, width)
    for start in range(0, cells, MXU):
        twot_ref[:, start : start + MXU] = two_ref[start : start + MXU, :].astype(F32).T.astype(BF16)
    for i in range(3):
        for tap in range(3):
            part = slice(tap * channels, (tap + 1) * channels)
            mirror = slice((2 - tap) * channels, (3 - tap) * channels)
            wt_ref[i, part, :] = second_ref[i, mirror, :].astype(F32).T.astype(BF16)


def turn(before, x, after, one, two, second, width):
    cells, channels = x.shape
    shape = jax.ShapeDtypeStruct
    return pl.pallas_call(
        functools.partial(turn_kernel, width),
        in_specs=whole(6),
        out_specs=whole(4),
        out_shape=[
            shape((3 * channels, cells + 2 * width), BF16),
            shape((3 * channels, cells + 4 * width), BF16),
            shape((channels, cells), BF16),
            shape((3, 3 * channels, channels), BF16),
        ],
        compiler_params=pltpu.CompilerParams(vmem_limit_bytes=20 << 20),
        cost_estimate=pl.CostEstimate(flops=3_000_000_000, bytes_accessed=14_000_000, transcendentals=0),
        name="turn",
    )(before, x, after, one, two, second)


def head_kernel(
    scale, width, log_ref, base_ref, label_sum_ref, two_ref, twot_ref, head_ref, *refs
):
    *got_refs, grad_ref, top_ref, bottom_ref, head_grad_ref, got_ref, natural = refs
    slots, extended = got_ref.shape
    held = [one[...].astype(F32) for one in got_refs]
    held = [one[: one.shape[0] // 2] for one in held[:-1]] + held[-1:]
    got_ref[...] = jnp.concatenate(held, axis=0).astype(BF16)
    tiles = label_sum_ref.shape[0]
    flat = extended - 2 * LANES
    pixels = flat // 64
    edge = math.isqrt(pixels)
    across = width // edge
    index = got_ref[:, flat + LANES :].astype(F32)
    take = (index == (iota((slots, LANES), 1) + 1).astype(F32)).astype(F32).T[:tiles].astype(BF16)
    spread = join_lanes(dot(take, got_ref[:, flat : flat + LANES]))
    weight = 1.0 / (0.1 + spread)
    even = iota((tiles, LANES), 1) < 64
    loss = -label_sum_ref[...]
    for pair in range(pixels // 2):
        rows = slice(pair * tiles, (pair + 1) * tiles)
        if pair % 2 == 0:
            both = dot(take, got_ref[:, pair * LANES : (pair + 2) * LANES])
        mean = both[:, pair % 2 * LANES : (pair % 2 + 1) * LANES]
        cell = jnp.where(even, weight[:, 2 * pair : 2 * pair + 1], weight[:, 2 * pair + 1 : 2 * pair + 2])
        value = log_ref[rows, :]
        held = mean > 0
        loss = loss + cell * jnp.where(held, mean * (jnp.log(jnp.where(held, mean, 1.0)) - value), 0.0)
        grad = (cell * (jnp.exp(value) - mean) + base_ref[rows, :]) * scale
        turned = pltpu.roll(grad, 64, 1)
        row, col = 2 * pair // edge, 2 * pair % edge
        for down in range(tiles // across):
            start = (down * edge + row) * width + col
            natural[pl.ds(start, across, stride=edge), :] = grad[down * across : (down + 1) * across]
            natural[pl.ds(start + 1, across, stride=edge), :] = turned[down * across : (down + 1) * across]
    cells, channels = two_ref.shape
    logit_grad = natural[...].astype(BF16)
    head = jnp.concatenate([head_ref[...], jnp.zeros_like(head_ref)], axis=0)
    head_grad_ref[:channels, :] = dot(twot_ref[...], logit_grad)
    head_grad_ref[channels:, :] = loss
    block = 4 * width
    for start in range(0, cells, block):
        rows = slice(start, start + block)
        grad = dot(logit_grad[rows], head)
        grad_ref[rows, :] = jnp.where(two_ref[rows, :].astype(F32) > 0, grad, 0.0).astype(BF16)
    top_ref[...] = grad_ref[: 2 * width, :]
    bottom_ref[...] = grad_ref[cells - 2 * width :, :]


def head_step(got, log, base, label_sum, two, twot, head, scale, width):
    cells, channels = two.shape
    shape = jax.ShapeDtypeStruct
    return pl.pallas_call(
        functools.partial(head_kernel, scale, width),
        in_specs=whole(6 + len(got)),
        out_specs=whole(4),
        out_shape=[
            shape((cells, channels), BF16),
            shape((2 * width, channels), BF16),
            shape((2 * width, channels), BF16),
            shape((channels + label_sum.shape[0], LANES), F32),
        ],
        scratch_shapes=[
            pltpu.VMEM((2 * got[-1].shape[0], got[-1].shape[1]), BF16),
            pltpu.VMEM((cells, LANES), F32),
        ],
        compiler_params=pltpu.CompilerParams(vmem_limit_bytes=14 << 20),
        cost_estimate=pl.CostEstimate(flops=400_000_000, bytes_accessed=5_000_000, transcendentals=500_000),
        name="head_step",
    )(log, base, label_sum, two, twot, head, *got)


def inner_dots(ref, start, step, rows, weight_ref):
    total = None
    for tap in range(3):
        part = dot(ref[start + (2 - tap) * step : start + (2 - tap) * step + rows, :], weight_ref[tap])
        total = part if total is None else total + part
    return total


def second_kernel(width, ht_ref, grad_ref, wt_ref, one_ref, out_ref, inner_ref, gcat):
    cells, channels = grad_ref.shape
    block = 4 * width
    halo = 2 * width
    for start in range(0, cells, block):
        put_shifted(gcat, start, grad_ref[start : start + block, :].astype(F32), 2, width)
    for tap in range(3):
        part = dot(ht_ref[:, halo * tap : halo * tap + cells], grad_ref[...])
        out_ref[tap * 3 * channels : (tap + 1) * 3 * channels, :] = part.astype(BF16)
    for start in range(block, cells - block, block):
        value = inner_dots(gcat, start - halo, halo, block, wt_ref)
        held = one_ref[halo + start : halo + start + block, :].astype(F32) > 0
        inner_ref[start - block : start, :] = jnp.where(held, value, 0.0).astype(BF16)


def second_step(ht, grad, wt, one, width):
    cells, channels = grad.shape
    return pl.pallas_call(
        functools.partial(second_kernel, width),
        in_specs=whole(4),
        out_specs=whole(2),
        out_shape=[
            jax.ShapeDtypeStruct((9 * channels, channels), BF16),
            jax.ShapeDtypeStruct((cells - 8 * width, channels), BF16),
        ],
        scratch_shapes=[pltpu.VMEM((cells, 3 * channels), BF16)],
        compiler_params=pltpu.CompilerParams(vmem_limit_bytes=20 << 20),
        cost_estimate=pl.CostEstimate(flops=4_500_000_000, bytes_accessed=9_000_000, transcendentals=0),
        name="second_step",
    )(ht, grad, wt, one)


def first_kernel(width, plan, place_ref, before_ref, after_ref, grad_ref, head_grad_ref, second_ref, inner_ref, *refs):
    wt_ref, one_ref, xt_ref, *refs = refs
    chips, groups, near_rows, far_rows = plan
    keep_refs, give_refs, refs = refs[: chips + 1], refs[chips + 1 : 2 * chips + 2], refs[2 * chips + 2 :]
    gtop, gbottom, padded, halves, sem = refs
    cells, channels = grad_ref.shape
    rows = 9 * channels
    used = rows + channels // 2
    half = halves.shape[1]
    second_copy = pltpu.make_async_copy(second_ref, halves.at[1, pl.ds(0, rows)], sem)
    second_copy.start()
    halo = before_ref.shape[0]
    block = 4 * width
    inside = 3 * halo
    put_shifted(gtop, 0, before_ref[...].astype(F32), 2, width)
    put_shifted(gtop, halo, grad_ref[:inside, :].astype(F32), 2, width)
    put_shifted(gbottom, 0, grad_ref[cells - inside :, :].astype(F32), 2, width)
    put_shifted(gbottom, inside, after_ref[...].astype(F32), 2, width)
    padded[:halo, :] = jnp.zeros((halo, channels), BF16)
    padded[halo + cells :, :] = jnp.zeros((halo, channels), BF16)
    padded[halo + block : halo + cells - block, :] = inner_ref[...]
    for ref, start in ((gtop, 0), (gbottom, cells - block)):
        value = inner_dots(ref, 0, halo, block, wt_ref)
        held = one_ref[halo + start : halo + start + block, :].astype(F32) > 0
        padded[halo + start : halo + start + block, :] = jnp.where(held, value, 0.0).astype(BF16)
    span = cells + 2 * width
    for tap in range(3):
        part = dot(xt_ref[...], padded[(2 - tap) * width : (2 - tap) * width + span, :])
        halves[0, tap * 3 * channels : (tap + 1) * 3 * channels, :] = part.astype(BF16)
    lane = iota((channels // 2, LANES), 1)
    loss = jnp.sum(head_grad_ref[channels:, :])
    high = loss.astype(BF16).astype(F32)
    extra = jnp.where(lane == 64, high, jnp.where(lane == 65, loss - high, 0.0))
    extra = jnp.where(iota(lane.shape, 0) == place_ref[DEVICE] % (channels // 2), extra, 0.0)
    for side in range(2):
        value = jnp.where(lane < 64, head_grad_ref[side * channels // 2 : (side + 1) * channels // 2, :], extra)
        halves[0, rows:used, side * LANES : (side + 1) * LANES] = value.astype(BF16)
    if half > used:
        halves[0, used:, :] = jnp.zeros((half - used, channels), BF16)
    halves[1, rows:, :] = jnp.zeros((half - rows, channels), BF16)
    second_copy.wait()
    core, chip = place_ref[CORE], place_ref[CHIP]
    size = groups * near_rows
    for step in range(chips):
        low = pl.multiple_of((chip ^ step) * size, 16)
        give_refs[step][...] = halves[1 - core, pl.ds(low, size), :]
        keep_refs[step][...] = halves[core, pl.ds(low, size), :]
    give_refs[chips][...] = halves[1 - core, chips * size :, :]
    keep_refs[chips][...] = halves[core, chips * size :, :]


def first_step(place, before, after, grad, head_grad, second, inner, wt, one, xt, width, plan):
    cells, channels = grad.shape
    halo = before.shape[0]
    chips, groups, near_rows, far_rows = plan
    half_rows = chips * groups * (near_rows + far_rows)
    piece = [jax.ShapeDtypeStruct((groups * near_rows, channels), BF16)] * chips
    piece += [jax.ShapeDtypeStruct((chips * groups * far_rows, channels), BF16)]
    outs = pl.pallas_call(
        functools.partial(first_kernel, width, plan),
        in_specs=[scalars(), *whole(9)],
        out_specs=whole(2 * chips + 2),
        out_shape=piece * 2,
        scratch_shapes=[
            pltpu.VMEM((4 * halo, 3 * channels), BF16),
            pltpu.VMEM((4 * halo, 3 * channels), BF16),
            pltpu.VMEM((cells + 4 * width, channels), BF16),
            pltpu.VMEM((2, half_rows, channels), BF16),
            pltpu.SemaphoreType.DMA,
        ],
        compiler_params=pltpu.CompilerParams(vmem_limit_bytes=24 << 20),
        cost_estimate=pl.CostEstimate(flops=5_000_000_000, bytes_accessed=10_000_000, transcendentals=0),
        name="first_step",
    )(place, before, after, grad, head_grad, second, inner, wt, one, xt)
    return (outs[: chips + 1], outs[chips + 1 :])


def neighbours(first, last, axis):
    count = lax.axis_size(axis)
    up = [(i, i + 1) for i in range(count - 1)]
    down = [(i + 1, i) for i in range(count - 1)]
    return (lax.ppermute(last, axis, up), lax.ppermute(first, axis, down))


def pairwise(array, axis, step):
    count = lax.axis_size(axis)
    return lax.ppermute(array, axis, [(i, i ^ step) for i in range(count)])


def add(arrays):
    return functools.reduce(jnp.add, [array.astype(F32) for array in arrays]).astype(BF16)


def assemble_kernel(width, plan, cell_total, place_ref, *refs):
    chips, groups, near_rows, far_rows = plan
    pieces, refs = refs[: chips + 1], refs[chips + 1 :]
    own = len(refs) == 5
    if own:
        first_ref, second_ref, extra_ref, value_ref, sem = refs
    else:
        _, _, held_ref, first_ref, second_ref, head_ref, loss_ref, value_ref, sem = refs
    grad_rows = first_ref.shape[0]
    core, chip, member = place_ref[CORE], place_ref[CHIP], place_ref[MEMBER]
    for s in range(chips):
        value = pieces[s][...].astype(F32)
        for u in range(groups):
            start = pl.multiple_of(((chip ^ s) * groups + (member ^ u)) * near_rows, 8)
            value_ref[pl.ds(start, near_rows), :] = value[u * near_rows : (u + 1) * near_rows]
    value = pieces[chips][...].astype(F32)
    for u in range(groups):
        for s in range(chips):
            low = (u * chips + s) * far_rows
            start = chips * groups * near_rows + ((member ^ u) * chips + (chip ^ s)) * far_rows
            value_ref[pl.ds(pl.multiple_of(start, 8), far_rows), :] = value[low : low + far_rows]
    half = core if own else 1 - core
    filled = value_ref.at[pl.ds(0, grad_rows)]

    @pl.when(half == 0)
    def _():
        pltpu.make_async_copy(filled, first_ref, sem).start()

    @pl.when(half != 0)
    def _():
        pltpu.make_async_copy(filled, second_ref, sem).start()

    rows = width // 2
    extra = value_ref[grad_rows : grad_rows + rows, :]
    if own:
        extra_ref[...] = extra
    else:
        extra = jnp.where(core == 0, held_ref[...], extra)
        for side in range(2):
            part = extra[:, side * LANES : (side + 1) * LANES].T
            head_ref[:, side * rows : (side + 1) * rows] = part[: head_ref.shape[0]]
        lane = iota(extra.shape, 1)
        loss = jnp.sum(jnp.where((lane == 64) | (lane == 65), extra, 0.0), keepdims=True)
        loss_ref[...] = loss / cell_total
    pltpu.make_async_copy(filled, first_ref, sem).wait()


def assemble(place, pieces, plan, grad_rows, classes, cell_total):
    chips, groups, near_rows, far_rows = plan
    half_rows = chips * groups * (near_rows + far_rows)
    width = pieces[0].shape[1]
    shape = jax.ShapeDtypeStruct
    totals = [shape((grad_rows, width), F32)] * 2
    extra = shape((width // 2, width), F32)
    common = dict(
        scratch_shapes=[pltpu.VMEM((half_rows, width), F32), pltpu.SemaphoreType.DMA],
        compiler_params=pltpu.CompilerParams(vmem_limit_bytes=48 << 20),
        cost_estimate=pl.CostEstimate(flops=1_000_000, bytes_accessed=3_700_000, transcendentals=0),
        name="assemble",
    )
    kernel = functools.partial(assemble_kernel, width, plan, cell_total)
    count = chips + 1
    held = pl.pallas_call(
        kernel,
        in_specs=[scalars(), *whole(count)],
        out_specs=[*hbm(2), *whole(1)],
        out_shape=[*totals, extra],
        **common,
    )(place, *pieces[:count])
    return pl.pallas_call(
        kernel,
        in_specs=[scalars(), *whole(count), *hbm(2), *whole(1)],
        out_specs=[*hbm(2), *whole(2)],
        out_shape=[*totals, shape((classes, width), F32), shape((1, 1), F32)],
        input_output_aliases={count + 1: 0, count + 2: 1},
        **common,
    )(place, *pieces[count:], *held)


def gradient_pieces(place, keep, give, plan):
    chips, groups, near_rows, far_rows = plan
    got = [pairwise(one, "core", 1) for one in give]
    near = [add(pair) for pair in zip(keep[:chips], got[:chips])]
    far = [keep[chips], got[chips]]

    def block(arrays, axis, me, step, rows):
        start = (me ^ step) * rows
        return add([lax.dynamic_slice_in_dim(one, start, rows, axis=0) for one in arrays])

    chip, member = place[CHIP], place[MEMBER]
    far = [block(far, "member", member, step, chips * far_rows) for step in range(groups)]
    near = [near[0]] + [pairwise(near[step], "chip", step) for step in range(1, chips)]
    far = [far[0]] + [pairwise(far[step], "member", step) for step in range(1, groups)]
    near = [block(near, "member", member, step, near_rows) for step in range(groups)]
    far = [block(far, "chip", chip, step, far_rows) for step in range(chips)]
    near = add([near[0]] + [pairwise(near[step], "member", step) for step in range(1, groups)])
    far = add([far[0]] + [pairwise(far[step], "chip", step) for step in range(1, chips)])

    near = jnp.concatenate([near] + [pairwise(near, "member", step) for step in range(1, groups)], axis=0)
    far = jnp.concatenate([far] + [pairwise(far, "chip", step) for step in range(1, chips)], axis=0)
    near, far = lax.optimization_barrier((near, far))
    held = [near] + [pairwise(near, "chip", step) for step in range(1, chips)]
    far = jnp.concatenate([far] + [pairwise(far, "member", step) for step in range(1, groups)], axis=0)
    held += [far]
    return held + [pairwise(piece, "core", 1) for piece in held]


def body(teacher_logits, coverage, features, labels, first_weight, second_weight, head_weight):
    channels, classes = head_weight.shape
    members, tiles_here, flat_width = teacher_logits.shape
    pixels = flat_width // classes
    edge = math.isqrt(pixels)
    groups = lax.axis_size("member")
    chips = lax.axis_size("chip")
    columns = chips * 2
    tile_axes = ("chip", "core")
    block_tiles = tiles_here // groups
    capacity = max(2, 2 * block_tiles // columns)
    local = features[0]
    lines, width = local.shape[:2]
    cells = lines * width
    cell_total = groups * columns * cells
    column = lax.axis_index(tile_axes)
    place = jnp.stack(
        [
            lax.axis_index("core"),
            lax.axis_index("chip"),
            lax.axis_index("member"),
            lax.axis_index(("member", *tile_axes)),
            column == 0,
            column == columns - 1,
        ]
    ).astype(jnp.int32)
    flat = local.reshape(cells, channels)
    first_rows = first_weight.reshape(3, 3 * channels, channels)
    second_rows = second_weight.reshape(3, 3 * channels, channels)
    head = head_weight.T

    before, after = neighbours(flat[: 3 * width], flat[cells - 3 * width :], tile_axes)
    far = teacher_moments(teacher_logits, block_tiles, classes, 1)
    got = [pairwise(one, "member", step) for step, one in zip((3, 2), far)]
    near, own = teacher_moments(teacher_logits, block_tiles, classes, 0)
    got += [pairwise(near, "member", 1), own]
    label_rows = (
        labels[0].reshape(lines // edge, edge, width // edge, edge).transpose(0, 2, 1, 3).reshape(block_tiles, pixels)
    )
    one, two, log, base, label_sum = student_forward(
        place, before, after, head, label_rows, flat, first_rows, second_rows, own, width
    )
    xt, ht, twot, wt = turn(before, flat, after, one, two, second_rows, width)
    cover = coverage.reshape(groups, 1, block_tiles)
    sent = combine(got, cover, place, twot, classes, members, columns, capacity)
    received = [sent[0]] + [pairwise(sent[step], "chip", step) for step in range(1, chips)]
    passed = pairwise(jnp.concatenate([piece[capacity:] for piece in received], axis=0), "core", 1)
    received = [*received, passed]
    grad_two, top, bottom, head_grad = head_step(
        received, log, base, label_sum, two, twot, head, 1.0 / math.sqrt(cell_total), width
    )
    grad_before, grad_after = neighbours(top, bottom, tile_axes)
    second, inner = second_step(ht, grad_two, wt, one, width)
    rows, extra_rows = 9 * channels, channels // 2
    unit = 8 * groups * chips
    block_rows = -(-(rows + extra_rows) // unit) * 8
    far_rows = block_rows // 24 * 8
    plan = (chips, groups, block_rows - far_rows, far_rows)
    keep, give = first_step(
        place, grad_before, grad_after, grad_two, head_grad, second, inner, wt, one, xt, width, plan
    )
    pieces = gradient_pieces(place, keep, give, plan)
    first_total, second_total, head_total, loss = assemble(
        place, pieces, plan, rows, classes, cell_total
    )
    kernel_shape = (3, 3, channels, channels)
    return (first_total.reshape(kernel_shape), second_total.reshape(kernel_shape), head_total.T, loss[0, 0])


def solution(mesh):
    groups, columns = mesh.shape["member"], mesh.shape["tile"]
    split = jax.sharding.Mesh(mesh.devices.reshape(groups, columns // 2, 2), ("member", "chip", "core"))
    tile = ("chip", "core")
    return jax.shard_map(
        body,
        mesh=split,
        in_specs=(
            P("member", tile, None),
            P(tile),
            P("member", tile, None, None),
            P("member", tile, None),
            P(),
            P(),
            P(),
        ),
        out_specs=(P(), P(), P(), P()),
        check_vma=False,
    )
```

```python
import functools
import math

import jax
import jax.numpy as jnp
from jax import lax
from jax.experimental import pallas as pl
from jax.experimental.pallas import tpu as pltpu
from jax.sharding import PartitionSpec as P

BF16 = jnp.bfloat16
F32 = jnp.float32
LANES = 128
MXU = 256


def whole(count):
    return [pl.BlockSpec(memory_space=pltpu.VMEM)] * count


def iota(shape, axis):
    return lax.broadcasted_iota(jnp.int32, shape, axis)


def dot(left, right):
    return jnp.dot(left, right, preferred_element_type=F32)


def split_lanes(value):
    high = value.astype(BF16).astype(F32)
    return jnp.where(iota(value.shape, 1) < 64, high, value - high).astype(BF16)


def join_lanes(value):
    return value + pltpu.roll(value, 64, 1)


def class_sums(value, classes):
    pick = (iota((MXU, LANES), 0) // classes == iota((MXU, LANES), 1) % (MXU // classes)).astype(BF16)
    high = value.astype(BF16)
    low = (value - high.astype(F32)).astype(BF16)
    return dot(high, pick) + dot(low, pick)


def hbm(count):
    return [pl.BlockSpec(memory_space=pl.ANY)] * count


def scalars():
    return pl.BlockSpec(memory_space=pltpu.SMEM)


CORE, CHIP, MEMBER, DEVICE, FIRST, LAST = range(6)


def teacher_kernel(classes, flip, logit_hbm, *refs):
    member = lax.axis_index("member")
    near_ref, own_ref, x_ref, sum_ref, acc_ref, sems = refs[-6:]
    quarters, members, tiles, width = x_ref.shape
    parts = width // MXU
    per = MXU // classes
    tile_rows = pl.ds(pl.multiple_of(((member // 2) ^ flip) * tiles, tiles), tiles)
    arrive = [
        pltpu.make_async_copy(logit_hbm.at[:, tile_rows, pl.ds(i * width, width)], x_ref.at[i], sems.at[i])
        for i in range(quarters)
    ]
    for copy in arrive:
        copy.start()
    same = (iota((MXU, MXU), 0) // classes == iota((MXU, MXU), 1) // classes).astype(BF16)
    acc_ref[...] = jnp.zeros_like(acc_ref)

    def group_sums(values):
        rows = values[0].shape[0]
        stacked = dot(jnp.concatenate([one.astype(BF16) for one in values], axis=0), same)
        return [stacked[n * rows : (n + 1) * rows] for n in range(len(values))]

    @pl.loop(0, quarters)
    def _(i):
        pltpu.make_async_copy(logit_hbm.at[:, tile_rows, pl.ds(0, width)], x_ref.at[i], sems.at[i]).wait()
        each = range(parts)
        x = [x_ref[i, :, :, n * MXU : (n + 1) * MXU].astype(F32).reshape(members * tiles, MXU) for n in each]
        root = [jnp.exp(one * 0.25) for one in x]
        total = group_sums(root)
        root = [one * pl.reciprocal(whole_sum, approx=True) for one, whole_sum in zip(root, total)]
        square = [one * one for one in root]
        power = [one * one for one in square]
        total = group_sums(power)
        inverse = [pl.reciprocal(one, approx=True) for one in total]
        inverse = [one * (2.0 - whole_sum * one) for one, whole_sum in zip(inverse, total)]
        probs = [(one * other).reshape(members, tiles, MXU) for one, other in zip(power, inverse)]
        first = [functools.reduce(jnp.add, [one[m] for m in range(members)]) for one in probs]
        within = [
            functools.reduce(jnp.add, [one[m] * one[m] for m in range(members)]) - sums * sums * (1.0 / members)
            for one, sums in zip(probs, first)
        ]
        sums = class_sums(jnp.concatenate(within, axis=0), classes)
        sums = [sums[n * tiles : (n + 1) * tiles] for n in each]
        acc = acc_ref[...]
        for n in each:
            acc = jnp.where(iota(acc.shape, 1) % 64 // per == i * parts + n, sums[n], acc)
        acc_ref[...] = acc
        for n in each:
            sum_ref[:, pl.ds(pl.multiple_of(i * width + n * MXU, MXU), MXU)] = first[n].astype(BF16)

    sum_ref[:, quarters * width :] = split_lanes(acc_ref[...])
    block = tiles // 2
    odd = 1 - member % 2
    near_ref[...] = sum_ref[pl.ds(pl.multiple_of(odd * block, 16), block), :]
    own_ref[...] = sum_ref[pl.ds(pl.multiple_of((1 - odd) * block, 16), block), :]


def teacher_moments(logits, tiles, classes, flip, *earlier):
    members, _, width = logits.shape
    quarters = 4
    shape = jax.ShapeDtypeStruct
    outs = [shape((tiles, width + LANES), BF16)] * 2
    return pl.pallas_call(
        functools.partial(teacher_kernel, classes, flip),
        in_specs=hbm(1 + len(earlier)),
        out_specs=whole(len(outs)),
        out_shape=outs,
        scratch_shapes=[
            pltpu.VMEM((quarters, members, 2 * tiles, width // quarters), BF16),
            pltpu.VMEM((2 * tiles, width + LANES), BF16),
            pltpu.VMEM((2 * tiles, LANES), F32),
            pltpu.SemaphoreType.DMA((quarters,)),
        ],
        compiler_params=pltpu.CompilerParams(vmem_limit_bytes=58 << 20),
        cost_estimate=pl.CostEstimate(flops=1_500_000_000, bytes_accessed=2_600_000, transcendentals=3_000_000),
        name="teacher_moments",
    )(logits, *earlier)


def combine_kernel(classes, members, columns, capacity, where_ref, cover_ref, after_ref, *refs):
    chips = columns // 2
    got_refs, out_refs = refs[:-chips], refs[-chips:]
    groups = len(got_refs)
    tiles, extended = got_refs[0].shape
    width = extended - LANES
    means, gaps = [], []
    for start in range(0, width, MXU):
        sums = [got_ref[:, start : start + MXU].astype(F32) for got_ref in got_refs]
        total = sums[0]
        for one in sums[1:]:
            total = total + one
        mean = total * (1.0 / (members * groups))
        means.append(mean.astype(BF16))
        gap = jnp.zeros_like(mean)
        for one in sums:
            off = one * (1.0 / members) - mean
            gap = gap + off * off
        gaps.append(gap)
    between = class_sums(jnp.concatenate(gaps, axis=0), classes)
    lane = iota((tiles, LANES), 1)
    spread = jnp.zeros((tiles, LANES), F32)
    per = MXU // classes
    for i in range(width // MXU):
        spread = jnp.where(lane % 64 // per == i, between[i * tiles : (i + 1) * tiles], spread)
    inner = got_refs[0][:, width:].astype(F32)
    for got_ref in got_refs[1:]:
        inner = inner + got_ref[:, width:].astype(F32)
    spread = spread * (1.0 / groups) + join_lanes(inner) * (1.0 / (members * groups))
    index = (iota((tiles, LANES), 0) + 1).astype(F32).astype(BF16)
    rows = jnp.concatenate([*means, split_lanes(spread), index], axis=1)
    target = cover_ref[where_ref[MEMBER]] ^ (where_ref[CHIP] * 2 + where_ref[CORE])
    onehot = (iota((columns, tiles), 0) == target).astype(F32)
    earlier = (iota((tiles, tiles), 0) < iota((tiles, tiles), 1)).astype(BF16)
    before = dot(onehot.astype(BF16), earlier)
    rank = jnp.sum(before * onehot, axis=0, keepdims=True).astype(jnp.int32)
    place = (iota((columns * capacity, tiles), 0) == target * capacity + rank).astype(BF16)
    sent = dot(place, rows)
    for index, out_ref in enumerate(out_refs):
        out_ref[...] = sent[2 * index * capacity : 2 * (index + 1) * capacity].astype(BF16)


def combine(got, cover, where, after, classes, members, columns, capacity):
    extended = got[0].shape[1]
    return pl.pallas_call(
        functools.partial(combine_kernel, classes, members, columns, capacity),
        in_specs=[pl.BlockSpec(memory_space=pltpu.SMEM), *whole(1), pl.BlockSpec(memory_space=pl.ANY), *whole(len(got))],
        out_specs=whole(columns // 2),
        out_shape=[jax.ShapeDtypeStruct((2 * capacity, extended + LANES), BF16)] * (columns // 2),
        compiler_params=pltpu.CompilerParams(vmem_limit_bytes=12 << 20),
        cost_estimate=pl.CostEstimate(flops=100_000_000, bytes_accessed=1_700_000, transcendentals=0),
        name="combine",
    )(where, cover, after, *got)


def put_shifted(ref, start, value, shift, width):
    rows, channels = value.shape
    col = iota(value.shape, 0) % width
    left = jnp.where(col >= shift, pltpu.roll(value, shift, 0), 0.0)
    right = jnp.where(col < width - shift, pltpu.roll(value, rows - shift, 0), 0.0)
    ref[pl.ds(start, rows), :channels] = left.astype(BF16)
    ref[pl.ds(start, rows), channels : 2 * channels] = value.astype(BF16)
    ref[pl.ds(start, rows), 2 * channels :] = right.astype(BF16)


def three_dots(ref, start, step, rows, weight_ref):
    total = None
    for tap in range(3):
        part = dot(ref[pl.ds(start + tap * step, rows), :], weight_ref[tap])
        total = part if total is None else total + part
    return total


def turned_dot(left, right):
    return lax.dot_general(left, right, (((1,), (1,)), ((), ())), preferred_element_type=F32)


def turned_dot(left, right):
    return lax.dot_general(left, right, (((1,), (1,)), ((), ())), preferred_element_type=F32)


def student_kernel(
    width, place_ref, before_ref, after_ref, head_ref, label_ref, x_ref, first_ref, second_ref, own_ref,
    one_ref, two_ref, log_ref, base_ref, label_sum_ref, xcat, hcat, logit_ref,
):
    cells, channels = x_ref.shape
    halo = before_ref.shape[0]
    block = 4 * width
    put_shifted(xcat, 0, before_ref[...].astype(F32), 1, width)
    put_shifted(xcat, halo + cells, after_ref[...].astype(F32), 1, width)
    for start in range(0, cells, block):
        put_shifted(xcat, halo + start, x_ref[start : start + block, :].astype(F32), 1, width)
    lines = cells // width
    low = jnp.where(place_ref[FIRST] == 1, 2, 0)
    high = jnp.where(place_ref[LAST] == 1, lines + 2, lines + 4)
    for start in range(0, cells + block, block):
        value = jnp.maximum(three_dots(xcat, start, width, block, first_ref), 0.0)
        if start == 0 or start == cells:
            line = start // width + iota(value.shape, 0) // width
            value = jnp.where((line >= low) & (line < high), value, 0.0)
        put_shifted(hcat, start, value, 2, width)
        one_ref[start : start + block, :] = value.astype(BF16)
    head = jnp.concatenate([head_ref[...], head_ref[...]], axis=0)
    for start in range(0, cells, block):
        rows = slice(start, start + block)
        two = jnp.maximum(three_dots(hcat, start, 2 * width, block, second_ref), 0.0).astype(BF16)
        two_ref[rows, :] = two
        logit_ref[rows, :] = turned_dot(two, head)

    tiles, pixels = label_ref.shape
    edge = math.isqrt(pixels)
    across = width // edge
    lane = iota((tiles, LANES), 1)
    even = lane < 64
    label_sum = jnp.zeros((tiles, LANES), F32)
    for pair in range(pixels // 2):
        row, col = 2 * pair // edge, 2 * pair % edge
        parts = []
        for down in range(tiles // across):
            start = (down * edge + row) * width + col
            left = logit_ref[pl.ds(start, across, stride=edge), :]
            right = logit_ref[pl.ds(start + 1, across, stride=edge), :]
            parts.append(jnp.where(iota(left.shape, 1) < 64, left, right))
        value = jnp.concatenate(parts, axis=0)
        top = jnp.where(
            even,
            jnp.max(jnp.where(even, value, -jnp.inf), axis=1, keepdims=True),
            jnp.max(jnp.where(even, -jnp.inf, value), axis=1, keepdims=True),
        )
        value = value - top
        power = jnp.exp(value)
        total = jnp.where(
            even,
            jnp.sum(jnp.where(even, power, 0.0), axis=1, keepdims=True),
            jnp.sum(jnp.where(even, 0.0, power), axis=1, keepdims=True),
        )
        value = value - jnp.log(total)
        label = jnp.where(even, label_ref[:, 2 * pair : 2 * pair + 1], label_ref[:, 2 * pair + 1 : 2 * pair + 2])
        hit = label == lane % 64
        label_sum = label_sum + jnp.where(hit, value, 0.0)
        log_ref[pair * tiles : (pair + 1) * tiles, :] = value
        base_ref[pair * tiles : (pair + 1) * tiles, :] = jnp.exp(value) - hit.astype(F32)
    label_sum_ref[...] = label_sum


def student_forward(place, before, after, head, labels, x, first, second, own, width):
    cells, channels = x.shape
    halo = before.shape[0]
    tiles, pixels = labels.shape
    shape = jax.ShapeDtypeStruct
    return pl.pallas_call(
        functools.partial(student_kernel, width),
        in_specs=[scalars(), *whole(7), *hbm(1)],
        out_specs=whole(5),
        out_shape=[
            shape((cells + 4 * width, channels), BF16),
            shape((cells, channels), BF16),
            shape((cells // 2, LANES), F32),
            shape((cells // 2, LANES), F32),
            shape((tiles, LANES), F32),
        ],
        scratch_shapes=[
            pltpu.VMEM((cells + 2 * halo, 3 * channels), BF16),
            pltpu.VMEM((cells + 4 * width, 3 * channels), BF16),
            pltpu.VMEM((cells, LANES), F32),
        ],
        compiler_params=pltpu.CompilerParams(vmem_limit_bytes=24 << 20),
        cost_estimate=pl.CostEstimate(flops=6_000_000_000, bytes_accessed=12_000_000, transcendentals=500_000),
        name="student_forward",
    )(place, before, after, head, labels, x, first, second, own)


def put_turned(ref, start, value, shift, width):
    rows, channels = value.shape
    col = iota(value.shape, 0) % width
    left = jnp.where(col >= shift, pltpu.roll(value, shift, 0), 0.0)
    right = jnp.where(col < width - shift, pltpu.roll(value, rows - shift, 0), 0.0)
    for tap, one in enumerate((left, value, right)):
        ref[tap * channels : (tap + 1) * channels, pl.ds(start, rows)] = one.T.astype(BF16)


def turn_kernel(
    width, before_ref, x_ref, after_ref, one_ref, two_ref, second_ref, xt_ref, ht_ref, twot_ref, wt_ref
):
    cells, channels = x_ref.shape
    halo = before_ref.shape[0]
    pair = 2 * width
    first = jnp.concatenate([before_ref[halo - width :], x_ref[:width]], axis=0).astype(F32)
    put_turned(xt_ref, 0, first, 1, width)
    last = jnp.concatenate([x_ref[cells - width :], after_ref[:width]], axis=0).astype(F32)
    put_turned(xt_ref, cells, last, 1, width)

    for start in range(pair, cells, pair):
        put_turned(xt_ref, start, x_ref[start - width : start + width, :].astype(F32), 1, width)
    for start in range(0, one_ref.shape[0], pair):
        put_turned(ht_ref, start, one_ref[start : start + pair, :].astype(F32), 2, width)
    for start in range(0, cells, MXU):
        twot_ref[:, start : start + MXU] = two_ref[start : start + MXU, :].astype(F32).T.astype(BF16)
    for i in range(3):
        for tap in range(3):
            part = slice(tap * channels, (tap + 1) * channels)
            mirror = slice((2 - tap) * channels, (3 - tap) * channels)
            wt_ref[i, part, :] = second_ref[i, mirror, :].astype(F32).T.astype(BF16)


def turn(before, x, after, one, two, second, width):
    cells, channels = x.shape
    shape = jax.ShapeDtypeStruct
    return pl.pallas_call(
        functools.partial(turn_kernel, width),
        in_specs=whole(6),
        out_specs=whole(4),
        out_shape=[
            shape((3 * channels, cells + 2 * width), BF16),
            shape((3 * channels, cells + 4 * width), BF16),
            shape((channels, cells), BF16),
            shape((3, 3 * channels, channels), BF16),
        ],
        compiler_params=pltpu.CompilerParams(vmem_limit_bytes=20 << 20),
        cost_estimate=pl.CostEstimate(flops=3_000_000_000, bytes_accessed=14_000_000, transcendentals=0),
        name="turn",
    )(before, x, after, one, two, second)


def head_kernel(
    scale, width, log_ref, base_ref, label_sum_ref, two_ref, twot_ref, head_ref, *refs
):
    *got_refs, grad_ref, top_ref, bottom_ref, head_grad_ref, got_ref, natural = refs
    slots, extended = got_ref.shape
    held = [one[...].astype(F32) for one in got_refs]
    held = [one[: one.shape[0] // 2] for one in held[:-1]] + held[-1:]
    got_ref[...] = jnp.concatenate(held, axis=0).astype(BF16)
    tiles = label_sum_ref.shape[0]
    flat = extended - 2 * LANES
    pixels = flat // 64
    edge = math.isqrt(pixels)
    across = width // edge
    index = got_ref[:, flat + LANES :].astype(F32)
    take = (index == (iota((slots, LANES), 1) + 1).astype(F32)).astype(F32).T[:tiles].astype(BF16)
    spread = join_lanes(dot(take, got_ref[:, flat : flat + LANES]))
    weight = 1.0 / (0.1 + spread)
    even = iota((tiles, LANES), 1) < 64
    loss = -label_sum_ref[...]
    for pair in range(pixels // 2):
        rows = slice(pair * tiles, (pair + 1) * tiles)
        if pair % 2 == 0:
            both = dot(take, got_ref[:, pair * LANES : (pair + 2) * LANES])
        mean = both[:, pair % 2 * LANES : (pair % 2 + 1) * LANES]
        cell = jnp.where(even, weight[:, 2 * pair : 2 * pair + 1], weight[:, 2 * pair + 1 : 2 * pair + 2])
        value = log_ref[rows, :]
        held = mean > 0
        loss = loss + cell * jnp.where(held, mean * (jnp.log(jnp.where(held, mean, 1.0)) - value), 0.0)
        grad = (cell * (jnp.exp(value) - mean) + base_ref[rows, :]) * scale
        turned = pltpu.roll(grad, 64, 1)
        row, col = 2 * pair // edge, 2 * pair % edge
        for down in range(tiles // across):
            start = (down * edge + row) * width + col
            natural[pl.ds(start, across, stride=edge), :] = grad[down * across : (down + 1) * across]
            natural[pl.ds(start + 1, across, stride=edge), :] = turned[down * across : (down + 1) * across]
    cells, channels = two_ref.shape
    logit_grad = natural[...].astype(BF16)
    head = jnp.concatenate([head_ref[...], jnp.zeros_like(head_ref)], axis=0)
    head_grad_ref[:channels, :] = dot(twot_ref[...], logit_grad)
    head_grad_ref[channels:, :] = loss
    block = 4 * width
    for start in range(0, cells, block):
        rows = slice(start, start + block)
        grad = dot(logit_grad[rows], head)
        grad_ref[rows, :] = jnp.where(two_ref[rows, :].astype(F32) > 0, grad, 0.0).astype(BF16)
    top_ref[...] = grad_ref[: 2 * width, :]
    bottom_ref[...] = grad_ref[cells - 2 * width :, :]


def head_step(got, log, base, label_sum, two, twot, head, scale, width):
    cells, channels = two.shape
    shape = jax.ShapeDtypeStruct
    return pl.pallas_call(
        functools.partial(head_kernel, scale, width),
        in_specs=whole(6 + len(got)),
        out_specs=whole(4),
        out_shape=[
            shape((cells, channels), BF16),
            shape((2 * width, channels), BF16),
            shape((2 * width, channels), BF16),
            shape((channels + label_sum.shape[0], LANES), F32),
        ],
        scratch_shapes=[
            pltpu.VMEM((2 * got[-1].shape[0], got[-1].shape[1]), BF16),
            pltpu.VMEM((cells, LANES), F32),
        ],
        compiler_params=pltpu.CompilerParams(vmem_limit_bytes=14 << 20),
        cost_estimate=pl.CostEstimate(flops=400_000_000, bytes_accessed=5_000_000, transcendentals=500_000),
        name="head_step",
    )(log, base, label_sum, two, twot, head, *got)


def inner_dots(ref, start, step, rows, weight_ref):
    total = None
    for tap in range(3):
        part = dot(ref[start + (2 - tap) * step : start + (2 - tap) * step + rows, :], weight_ref[tap])
        total = part if total is None else total + part
    return total


def second_kernel(width, ht_ref, grad_ref, wt_ref, one_ref, out_ref, inner_ref, gcat):
    cells, channels = grad_ref.shape
    block = 4 * width
    halo = 2 * width
    for start in range(0, cells, block):
        put_shifted(gcat, start, grad_ref[start : start + block, :].astype(F32), 2, width)
    for tap in range(3):
        part = dot(ht_ref[:, halo * tap : halo * tap + cells], grad_ref[...])
        out_ref[tap * 3 * channels : (tap + 1) * 3 * channels, :] = part.astype(BF16)
    for start in range(block, cells - block, block):
        value = inner_dots(gcat, start - halo, halo, block, wt_ref)
        held = one_ref[halo + start : halo + start + block, :].astype(F32) > 0
        inner_ref[start - block : start, :] = jnp.where(held, value, 0.0).astype(BF16)


def second_step(ht, grad, wt, one, width):
    cells, channels = grad.shape
    return pl.pallas_call(
        functools.partial(second_kernel, width),
        in_specs=whole(4),
        out_specs=whole(2),
        out_shape=[
            jax.ShapeDtypeStruct((9 * channels, channels), BF16),
            jax.ShapeDtypeStruct((cells - 8 * width, channels), BF16),
        ],
        scratch_shapes=[pltpu.VMEM((cells, 3 * channels), BF16)],
        compiler_params=pltpu.CompilerParams(vmem_limit_bytes=20 << 20),
        cost_estimate=pl.CostEstimate(flops=4_500_000_000, bytes_accessed=9_000_000, transcendentals=0),
        name="second_step",
    )(ht, grad, wt, one)


def first_kernel(width, plan, place_ref, before_ref, after_ref, grad_ref, head_grad_ref, second_ref, inner_ref, *refs):
    wt_ref, one_ref, xt_ref, *refs = refs
    chips, groups, near_rows, far_rows = plan
    keep_refs, give_refs, refs = refs[: chips + 1], refs[chips + 1 : 2 * chips + 2], refs[2 * chips + 2 :]
    gtop, gbottom, padded, halves, sem = refs
    cells, channels = grad_ref.shape
    rows = 9 * channels
    used = rows + channels // 2
    half = halves.shape[1]
    second_copy = pltpu.make_async_copy(second_ref, halves.at[1, pl.ds(0, rows)], sem)
    second_copy.start()
    halo = before_ref.shape[0]
    block = 4 * width
    inside = 3 * halo
    put_shifted(gtop, 0, before_ref[...].astype(F32), 2, width)
    put_shifted(gtop, halo, grad_ref[:inside, :].astype(F32), 2, width)
    put_shifted(gbottom, 0, grad_ref[cells - inside :, :].astype(F32), 2, width)
    put_shifted(gbottom, inside, after_ref[...].astype(F32), 2, width)
    padded[:halo, :] = jnp.zeros((halo, channels), BF16)
    padded[halo + cells :, :] = jnp.zeros((halo, channels), BF16)
    padded[halo + block : halo + cells - block, :] = inner_ref[...]
    for ref, start in ((gtop, 0), (gbottom, cells - block)):
        value = inner_dots(ref, 0, halo, block, wt_ref)
        held = one_ref[halo + start : halo + start + block, :].astype(F32) > 0
        padded[halo + start : halo + start + block, :] = jnp.where(held, value, 0.0).astype(BF16)
    span = cells + 2 * width
    for tap in range(3):
        part = dot(xt_ref[...], padded[(2 - tap) * width : (2 - tap) * width + span, :])
        halves[0, tap * 3 * channels : (tap + 1) * 3 * channels, :] = part.astype(BF16)
    lane = iota((channels // 2, LANES), 1)
    loss = jnp.sum(head_grad_ref[channels:, :])
    high = loss.astype(BF16).astype(F32)
    extra = jnp.where(lane == 64, high, jnp.where(lane == 65, loss - high, 0.0))
    extra = jnp.where(iota(lane.shape, 0) == place_ref[DEVICE] % (channels // 2), extra, 0.0)
    for side in range(2):
        value = jnp.where(lane < 64, head_grad_ref[side * channels // 2 : (side + 1) * channels // 2, :], extra)
        halves[0, rows:used, side * LANES : (side + 1) * LANES] = value.astype(BF16)
    if half > used:
        halves[0, used:, :] = jnp.zeros((half - used, channels), BF16)
    halves[1, rows:, :] = jnp.zeros((half - rows, channels), BF16)
    second_copy.wait()
    core, chip = place_ref[CORE], place_ref[CHIP]
    size = groups * near_rows
    for step in range(chips):
        low = pl.multiple_of((chip ^ step) * size, 16)
        give_refs[step][...] = halves[1 - core, pl.ds(low, size), :]
        keep_refs[step][...] = halves[core, pl.ds(low, size), :]
    give_refs[chips][...] = halves[1 - core, chips * size :, :]
    keep_refs[chips][...] = halves[core, chips * size :, :]


def first_step(place, before, after, grad, head_grad, second, inner, wt, one, xt, width, plan):
    cells, channels = grad.shape
    halo = before.shape[0]
    chips, groups, near_rows, far_rows = plan
    half_rows = chips * groups * (near_rows + far_rows)
    piece = [jax.ShapeDtypeStruct((groups * near_rows, channels), BF16)] * chips
    piece += [jax.ShapeDtypeStruct((chips * groups * far_rows, channels), BF16)]
    outs = pl.pallas_call(
        functools.partial(first_kernel, width, plan),
        in_specs=[scalars(), *whole(9)],
        out_specs=whole(2 * chips + 2),
        out_shape=piece * 2,
        scratch_shapes=[
            pltpu.VMEM((4 * halo, 3 * channels), BF16),
            pltpu.VMEM((4 * halo, 3 * channels), BF16),
            pltpu.VMEM((cells + 4 * width, channels), BF16),
            pltpu.VMEM((2, half_rows, channels), BF16),
            pltpu.SemaphoreType.DMA,
        ],
        compiler_params=pltpu.CompilerParams(vmem_limit_bytes=24 << 20),
        cost_estimate=pl.CostEstimate(flops=5_000_000_000, bytes_accessed=10_000_000, transcendentals=0),
        name="first_step",
    )(place, before, after, grad, head_grad, second, inner, wt, one, xt)
    return (outs[: chips + 1], outs[chips + 1 :])


def neighbours(first, last, axis):
    count = lax.axis_size(axis)
    up = [(i, i + 1) for i in range(count - 1)]
    down = [(i + 1, i) for i in range(count - 1)]
    return (lax.ppermute(last, axis, up), lax.ppermute(first, axis, down))


def pairwise(array, axis, step):
    count = lax.axis_size(axis)
    return lax.ppermute(array, axis, [(i, i ^ step) for i in range(count)])


def add(arrays):
    return functools.reduce(jnp.add, [array.astype(F32) for array in arrays]).astype(BF16)


def assemble_kernel(width, plan, cell_total, place_ref, *refs):
    chips, groups, near_rows, far_rows = plan
    pieces, refs = refs[: chips + 1], refs[chips + 1 :]
    own = len(refs) == 5
    if own:
        first_ref, second_ref, extra_ref, value_ref, sem = refs
    else:
        _, _, held_ref, first_ref, second_ref, head_ref, loss_ref, value_ref, sem = refs
    grad_rows = first_ref.shape[0]
    core, chip, member = place_ref[CORE], place_ref[CHIP], place_ref[MEMBER]
    for s in range(chips):
        value = pieces[s][...].astype(F32)
        for u in range(groups):
            start = pl.multiple_of(((chip ^ s) * groups + (member ^ u)) * near_rows, 8)
            value_ref[pl.ds(start, near_rows), :] = value[u * near_rows : (u + 1) * near_rows]
    value = pieces[chips][...].astype(F32)
    for u in range(groups):
        for s in range(chips):
            low = (u * chips + s) * far_rows
            start = chips * groups * near_rows + ((member ^ u) * chips + (chip ^ s)) * far_rows
            value_ref[pl.ds(pl.multiple_of(start, 8), far_rows), :] = value[low : low + far_rows]
    half = core if own else 1 - core
    filled = value_ref.at[pl.ds(0, grad_rows)]

    @pl.when(half == 0)
    def _():
        pltpu.make_async_copy(filled, first_ref, sem).start()

    @pl.when(half != 0)
    def _():
        pltpu.make_async_copy(filled, second_ref, sem).start()

    rows = width // 2
    extra = value_ref[grad_rows : grad_rows + rows, :]
    if own:
        extra_ref[...] = extra
    else:
        extra = jnp.where(core == 0, held_ref[...], extra)
        for side in range(2):
            part = extra[:, side * LANES : (side + 1) * LANES].T
            head_ref[:, side * rows : (side + 1) * rows] = part[: head_ref.shape[0]]
        lane = iota(extra.shape, 1)
        loss = jnp.sum(jnp.where((lane == 64) | (lane == 65), extra, 0.0), keepdims=True)
        loss_ref[...] = loss / cell_total
    pltpu.make_async_copy(filled, first_ref, sem).wait()


def assemble(place, pieces, plan, grad_rows, classes, cell_total):
    chips, groups, near_rows, far_rows = plan
    half_rows = chips * groups * (near_rows + far_rows)
    width = pieces[0].shape[1]
    shape = jax.ShapeDtypeStruct
    totals = [shape((grad_rows, width), F32)] * 2
    extra = shape((width // 2, width), F32)
    common = dict(
        scratch_shapes=[pltpu.VMEM((half_rows, width), F32), pltpu.SemaphoreType.DMA],
        compiler_params=pltpu.CompilerParams(vmem_limit_bytes=48 << 20),
        cost_estimate=pl.CostEstimate(flops=1_000_000, bytes_accessed=3_700_000, transcendentals=0),
        name="assemble",
    )
    kernel = functools.partial(assemble_kernel, width, plan, cell_total)
    count = chips + 1
    held = pl.pallas_call(
        kernel,
        in_specs=[scalars(), *whole(count)],
        out_specs=[*hbm(2), *whole(1)],
        out_shape=[*totals, extra],
        **common,
    )(place, *pieces[:count])
    return pl.pallas_call(
        kernel,
        in_specs=[scalars(), *whole(count), *hbm(2), *whole(1)],
        out_specs=[*hbm(2), *whole(2)],
        out_shape=[*totals, shape((classes, width), F32), shape((1, 1), F32)],
        input_output_aliases={count + 1: 0, count + 2: 1},
        **common,
    )(place, *pieces[count:], *held)


def gradient_pieces(place, keep, give, plan):
    chips, groups, near_rows, far_rows = plan
    got = [pairwise(one, "core", 1) for one in give]
    near = [add(pair) for pair in zip(keep[:chips], got[:chips])]
    far = [keep[chips], got[chips]]

    def block(arrays, axis, me, step, rows):
        start = (me ^ step) * rows
        return add([lax.dynamic_slice_in_dim(one, start, rows, axis=0) for one in arrays])

    chip, member = place[CHIP], place[MEMBER]
    far = [block(far, "member", member, step, chips * far_rows) for step in range(groups)]
    near = [near[0]] + [pairwise(near[step], "chip", step) for step in range(1, chips)]
    far = [far[0]] + [pairwise(far[step], "member", step) for step in range(1, groups)]
    near = [block(near, "member", member, step, near_rows) for step in range(groups)]
    far = [block(far, "chip", chip, step, far_rows) for step in range(chips)]
    near = add([near[0]] + [pairwise(near[step], "member", step) for step in range(1, groups)])
    far = add([far[0]] + [pairwise(far[step], "chip", step) for step in range(1, chips)])

    near = jnp.concatenate([near] + [pairwise(near, "member", step) for step in range(1, groups)], axis=0)
    far = jnp.concatenate([far] + [pairwise(far, "chip", step) for step in range(1, chips)], axis=0)
    near, far = lax.optimization_barrier((near, far))
    held = [near] + [pairwise(near, "chip", step) for step in range(1, chips)]
    far = jnp.concatenate([far] + [pairwise(far, "member", step) for step in range(1, groups)], axis=0)
    held += [far]
    return held + [pairwise(piece, "core", 1) for piece in held]


def body(teacher_logits, coverage, features, labels, first_weight, second_weight, head_weight):
    channels, classes = head_weight.shape
    members, tiles_here, flat_width = teacher_logits.shape
    pixels = flat_width // classes
    edge = math.isqrt(pixels)
    groups = lax.axis_size("member")
    chips = lax.axis_size("chip")
    columns = chips * 2
    tile_axes = ("chip", "core")
    block_tiles = tiles_here // groups
    capacity = max(2, 2 * block_tiles // columns)
    local = features[0]
    lines, width = local.shape[:2]
    cells = lines * width
    cell_total = groups * columns * cells
    column = lax.axis_index(tile_axes)
    place = jnp.stack(
        [
            lax.axis_index("core"),
            lax.axis_index("chip"),
            lax.axis_index("member"),
            lax.axis_index(("member", *tile_axes)),
            column == 0,
            column == columns - 1,
        ]
    ).astype(jnp.int32)
    flat = local.reshape(cells, channels)
    first_rows = first_weight.reshape(3, 3 * channels, channels)
    second_rows = second_weight.reshape(3, 3 * channels, channels)
    head = head_weight.T

    before, after = neighbours(flat[: 3 * width], flat[cells - 3 * width :], tile_axes)
    far = teacher_moments(teacher_logits, block_tiles, classes, 1)
    got = [pairwise(one, "member", step) for step, one in zip((3, 2), far)]
    near, own = teacher_moments(teacher_logits, block_tiles, classes, 0)
    got += [pairwise(near, "member", 1), own]
    label_rows = (
        labels[0].reshape(lines // edge, edge, width // edge, edge).transpose(0, 2, 1, 3).reshape(block_tiles, pixels)
    )
    one, two, log, base, label_sum = student_forward(
        place, before, after, head, label_rows, flat, first_rows, second_rows, own, width
    )
    xt, ht, twot, wt = turn(before, flat, after, one, two, second_rows, width)
    cover = coverage.reshape(groups, 1, block_tiles)
    sent = combine(got, cover, place, twot, classes, members, columns, capacity)
    received = [sent[0]] + [pairwise(sent[step], "chip", step) for step in range(1, chips)]
    passed = pairwise(jnp.concatenate([piece[capacity:] for piece in received], axis=0), "core", 1)
    received = [*received, passed]
    grad_two, top, bottom, head_grad = head_step(
        received, log, base, label_sum, two, twot, head, 1.0 / math.sqrt(cell_total), width
    )
    grad_before, grad_after = neighbours(top, bottom, tile_axes)
    second, inner = second_step(ht, grad_two, wt, one, width)
    rows, extra_rows = 9 * channels, channels // 2
    unit = 8 * groups * chips
    block_rows = -(-(rows + extra_rows) // unit) * 8
    far_rows = block_rows // 24 * 8
    plan = (chips, groups, block_rows - far_rows, far_rows)
    keep, give = first_step(
        place, grad_before, grad_after, grad_two, head_grad, second, inner, wt, one, xt, width, plan
    )
    pieces = gradient_pieces(place, keep, give, plan)
    first_total, second_total, head_total, loss = assemble(
        place, pieces, plan, rows, classes, cell_total
    )
    kernel_shape = (3, 3, channels, channels)
    return (first_total.reshape(kernel_shape), second_total.reshape(kernel_shape), head_total.T, loss[0, 0])


def solution(mesh):
    groups, columns = mesh.shape["member"], mesh.shape["tile"]
    split = jax.sharding.Mesh(mesh.devices.reshape(groups, columns // 2, 2), ("member", "chip", "core"))
    tile = ("chip", "core")
    return jax.shard_map(
        body,
        mesh=split,
        in_specs=(
            P("member", tile, None),
            P(tile),
            P("member", tile, None, None),
            P("member", tile, None),
            P(),
            P(),
            P(),
        ),
        out_specs=(P(), P(), P(), P()),
        check_vma=False,
    )
```

```python
import functools
import math

import jax
import jax.numpy as jnp
from jax import lax
from jax.experimental import pallas as pl
from jax.experimental.pallas import tpu as pltpu
from jax.sharding import PartitionSpec as P

BF16 = jnp.bfloat16
F32 = jnp.float32
LANES = 128
MXU = 256


def whole(count):
    return [pl.BlockSpec(memory_space=pltpu.VMEM)] * count


def iota(shape, axis):
    return lax.broadcasted_iota(jnp.int32, shape, axis)


def dot(left, right):
    return jnp.dot(left, right, preferred_element_type=F32)


def split_lanes(value):
    high = value.astype(BF16).astype(F32)
    return jnp.where(iota(value.shape, 1) < 64, high, value - high).astype(BF16)


def join_lanes(value):
    return value + pltpu.roll(value, 64, 1)


def class_sums(value, classes):
    pick = (iota((MXU, LANES), 0) // classes == iota((MXU, LANES), 1) % (MXU // classes)).astype(BF16)
    high = value.astype(BF16)
    low = (value - high.astype(F32)).astype(BF16)
    return dot(high, pick) + dot(low, pick)


def hbm(count):
    return [pl.BlockSpec(memory_space=pl.ANY)] * count


def scalars():
    return pl.BlockSpec(memory_space=pltpu.SMEM)


CORE, CHIP, MEMBER, DEVICE, FIRST, LAST = range(6)


def teacher_kernel(classes, flip, logit_hbm, *refs):
    member = lax.axis_index("member")
    near_ref, own_ref, x_ref, sum_ref, acc_ref, sems = refs[-6:]
    quarters, members, tiles, width = x_ref.shape
    parts = width // MXU
    per = MXU // classes
    tile_rows = pl.ds(pl.multiple_of(((member // 2) ^ flip) * tiles, tiles), tiles)
    arrive = [
        pltpu.make_async_copy(logit_hbm.at[:, tile_rows, pl.ds(i * width, width)], x_ref.at[i], sems.at[i])
        for i in range(quarters)
    ]
    for copy in arrive:
        copy.start()
    same = (iota((MXU, MXU), 0) // classes == iota((MXU, MXU), 1) // classes).astype(BF16)
    acc_ref[...] = jnp.zeros_like(acc_ref)

    @pl.loop(0, quarters)
    def _(i):
        pltpu.make_async_copy(logit_hbm.at[:, tile_rows, pl.ds(0, width)], x_ref.at[i], sems.at[i]).wait()
        each = range(parts)
        x = [x_ref[i, :, :, n * MXU : (n + 1) * MXU].astype(F32).reshape(members * tiles, MXU) for n in each]
        root = [jnp.exp2(one * (0.25 * math.log2(math.e))) for one in x]
        total = [dot(one.astype(BF16), same) for one in root]
        root = [one * pl.reciprocal(whole_sum, approx=True) for one, whole_sum in zip(root, total)]
        square = [one * one for one in root]
        power = [one * one for one in square]
        total = [dot(one.astype(BF16), same) for one in power]
        inverse = [pl.reciprocal(one, approx=True) for one in total]
        inverse = [one * (2.0 - whole_sum * one) for one, whole_sum in zip(inverse, total)]
        probs = [(one * other).reshape(members, tiles, MXU) for one, other in zip(power, inverse)]
        first = [functools.reduce(jnp.add, [one[m] for m in range(members)]) for one in probs]
        within = [
            functools.reduce(jnp.add, [one[m] * one[m] for m in range(members)]) - sums * sums * (1.0 / members)
            for one, sums in zip(probs, first)
        ]
        sums = [class_sums(one, classes) for one in within]
        acc = acc_ref[...]
        for n in each:
            acc = jnp.where(iota(acc.shape, 1) % 64 // per == i * parts + n, sums[n], acc)
        acc_ref[...] = acc
        for n in each:
            sum_ref[:, pl.ds(pl.multiple_of(i * width + n * MXU, MXU), MXU)] = first[n].astype(BF16)

    sum_ref[:, quarters * width :] = split_lanes(acc_ref[...])
    block = tiles // 2
    odd = 1 - member % 2
    near_ref[...] = sum_ref[pl.ds(pl.multiple_of(odd * block, 16), block), :]
    own_ref[...] = sum_ref[pl.ds(pl.multiple_of((1 - odd) * block, 16), block), :]


def teacher_moments(logits, tiles, classes, flip, *earlier):
    members, _, width = logits.shape
    quarters = 4
    shape = jax.ShapeDtypeStruct
    outs = [shape((tiles, width + LANES), BF16)] * 2
    return pl.pallas_call(
        functools.partial(teacher_kernel, classes, flip),
        in_specs=hbm(1 + len(earlier)),
        out_specs=whole(len(outs)),
        out_shape=outs,
        scratch_shapes=[
            pltpu.VMEM((quarters, members, 2 * tiles, width // quarters), BF16),
            pltpu.VMEM((2 * tiles, width + LANES), BF16),
            pltpu.VMEM((2 * tiles, LANES), F32),
            pltpu.SemaphoreType.DMA((quarters,)),
        ],
        compiler_params=pltpu.CompilerParams(vmem_limit_bytes=58 << 20),
        cost_estimate=pl.CostEstimate(flops=1_500_000_000, bytes_accessed=2_600_000, transcendentals=3_000_000),
        name="teacher_moments",
    )(logits, *earlier)


def combine_kernel(classes, members, columns, capacity, where_ref, cover_ref, after_ref, *refs):
    chips = columns // 2
    got_refs, out_refs = refs[:-chips], refs[-chips:]
    groups = len(got_refs)
    tiles, extended = got_refs[0].shape
    width = extended - LANES
    means, gaps = [], []
    for start in range(0, width, MXU):
        sums = [got_ref[:, start : start + MXU].astype(F32) for got_ref in got_refs]
        total = sums[0]
        for one in sums[1:]:
            total = total + one
        mean = total * (1.0 / (members * groups))
        means.append(mean.astype(BF16))
        gap = jnp.zeros_like(mean)
        for one in sums:
            off = one * (1.0 / members) - mean
            gap = gap + off * off
        gaps.append(gap)
    between = class_sums(jnp.concatenate(gaps, axis=0), classes)
    lane = iota((tiles, LANES), 1)
    spread = jnp.zeros((tiles, LANES), F32)
    per = MXU // classes
    for i in range(width // MXU):
        spread = jnp.where(lane % 64 // per == i, between[i * tiles : (i + 1) * tiles], spread)
    inner = got_refs[0][:, width:].astype(F32)
    for got_ref in got_refs[1:]:
        inner = inner + got_ref[:, width:].astype(F32)
    spread = spread * (1.0 / groups) + join_lanes(inner) * (1.0 / (members * groups))
    index = (iota((tiles, LANES), 0) + 1).astype(F32).astype(BF16)
    rows = jnp.concatenate([*means, split_lanes(spread), index], axis=1)
    target = cover_ref[where_ref[MEMBER]] ^ (where_ref[CHIP] * 2 + where_ref[CORE])
    onehot = (iota((columns, tiles), 0) == target).astype(F32)
    earlier = (iota((tiles, tiles), 0) < iota((tiles, tiles), 1)).astype(BF16)
    before = dot(onehot.astype(BF16), earlier)
    rank = jnp.sum(before * onehot, axis=0, keepdims=True).astype(jnp.int32)
    place = (iota((columns * capacity, tiles), 0) == target * capacity + rank).astype(BF16)
    sent = dot(place, rows)
    for index, out_ref in enumerate(out_refs):
        out_ref[...] = sent[2 * index * capacity : 2 * (index + 1) * capacity].astype(BF16)


def combine(got, cover, where, after, classes, members, columns, capacity):
    extended = got[0].shape[1]
    return pl.pallas_call(
        functools.partial(combine_kernel, classes, members, columns, capacity),
        in_specs=[pl.BlockSpec(memory_space=pltpu.SMEM), *whole(1), pl.BlockSpec(memory_space=pl.ANY), *whole(len(got))],
        out_specs=whole(columns // 2),
        out_shape=[jax.ShapeDtypeStruct((2 * capacity, extended + LANES), BF16)] * (columns // 2),
        compiler_params=pltpu.CompilerParams(vmem_limit_bytes=12 << 20),
        cost_estimate=pl.CostEstimate(flops=100_000_000, bytes_accessed=1_700_000, transcendentals=0),
        name="combine",
    )(where, cover, after, *got)


def put_shifted(ref, start, value, shift, width):
    rows, channels = value.shape
    col = iota(value.shape, 0) % width
    left = jnp.where(col >= shift, pltpu.roll(value, shift, 0), 0.0)
    right = jnp.where(col < width - shift, pltpu.roll(value, rows - shift, 0), 0.0)
    ref[pl.ds(start, rows), :channels] = left.astype(BF16)
    ref[pl.ds(start, rows), channels : 2 * channels] = value.astype(BF16)
    ref[pl.ds(start, rows), 2 * channels :] = right.astype(BF16)


def three_dots(ref, start, step, rows, weight_ref):
    total = None
    for tap in range(3):
        part = dot(ref[pl.ds(start + tap * step, rows), :], weight_ref[tap])
        total = part if total is None else total + part
    return total


def turned_dot(left, right):
    return lax.dot_general(left, right, (((1,), (1,)), ((), ())), preferred_element_type=F32)


def turned_dot(left, right):
    return lax.dot_general(left, right, (((1,), (1,)), ((), ())), preferred_element_type=F32)


def student_kernel(
    width, place_ref, before_ref, after_ref, head_ref, label_ref, x_ref, first_ref, second_ref, own_ref,
    one_ref, two_ref, log_ref, base_ref, label_sum_ref, xcat, hcat, logit_ref,
):
    cells, channels = x_ref.shape
    halo = before_ref.shape[0]
    block = 4 * width
    put_shifted(xcat, 0, before_ref[...].astype(F32), 1, width)
    put_shifted(xcat, halo + cells, after_ref[...].astype(F32), 1, width)
    for start in range(0, cells, block):
        put_shifted(xcat, halo + start, x_ref[start : start + block, :].astype(F32), 1, width)
    lines = cells // width
    low = jnp.where(place_ref[FIRST] == 1, 2, 0)
    high = jnp.where(place_ref[LAST] == 1, lines + 2, lines + 4)
    for start in range(0, cells + block, block):
        value = jnp.maximum(three_dots(xcat, start, width, block, first_ref), 0.0)
        if start == 0 or start == cells:
            line = start // width + iota(value.shape, 0) // width
            value = jnp.where((line >= low) & (line < high), value, 0.0)
        put_shifted(hcat, start, value, 2, width)
        one_ref[start : start + block, :] = value.astype(BF16)
    head = jnp.concatenate([head_ref[...], head_ref[...]], axis=0)
    for start in range(0, cells, block):
        rows = slice(start, start + block)
        two = jnp.maximum(three_dots(hcat, start, 2 * width, block, second_ref), 0.0).astype(BF16)
        two_ref[rows, :] = two
        logit_ref[rows, :] = turned_dot(two, head)

    tiles, pixels = label_ref.shape
    edge = math.isqrt(pixels)
    across = width // edge
    lane = iota((tiles, LANES), 1)
    even = lane < 64
    label_sum = jnp.zeros((tiles, LANES), F32)
    for pair in range(pixels // 2):
        row, col = 2 * pair // edge, 2 * pair % edge
        parts = []
        for down in range(tiles // across):
            start = (down * edge + row) * width + col
            left = logit_ref[pl.ds(start, across, stride=edge), :]
            right = logit_ref[pl.ds(start + 1, across, stride=edge), :]
            parts.append(jnp.where(iota(left.shape, 1) < 64, left, right))
        value = jnp.concatenate(parts, axis=0)
        top = jnp.where(
            even,
            jnp.max(jnp.where(even, value, -jnp.inf), axis=1, keepdims=True),
            jnp.max(jnp.where(even, -jnp.inf, value), axis=1, keepdims=True),
        )
        value = value - top
        power = jnp.exp(value)
        total = jnp.where(
            even,
            jnp.sum(jnp.where(even, power, 0.0), axis=1, keepdims=True),
            jnp.sum(jnp.where(even, 0.0, power), axis=1, keepdims=True),
        )
        value = value - jnp.log(total)
        label = jnp.where(even, label_ref[:, 2 * pair : 2 * pair + 1], label_ref[:, 2 * pair + 1 : 2 * pair + 2])
        hit = label == lane % 64
        label_sum = label_sum + jnp.where(hit, value, 0.0)
        log_ref[pair * tiles : (pair + 1) * tiles, :] = value
        base_ref[pair * tiles : (pair + 1) * tiles, :] = jnp.exp(value) - hit.astype(F32)
    label_sum_ref[...] = label_sum


def student_forward(place, before, after, head, labels, x, first, second, own, width):
    cells, channels = x.shape
    halo = before.shape[0]
    tiles, pixels = labels.shape
    shape = jax.ShapeDtypeStruct
    return pl.pallas_call(
        functools.partial(student_kernel, width),
        in_specs=[scalars(), *whole(7), *hbm(1)],
        out_specs=whole(5),
        out_shape=[
            shape((cells + 4 * width, channels), BF16),
            shape((cells, channels), BF16),
            shape((cells // 2, LANES), F32),
            shape((cells // 2, LANES), F32),
            shape((tiles, LANES), F32),
        ],
        scratch_shapes=[
            pltpu.VMEM((cells + 2 * halo, 3 * channels), BF16),
            pltpu.VMEM((cells + 4 * width, 3 * channels), BF16),
            pltpu.VMEM((cells, LANES), F32),
        ],
        compiler_params=pltpu.CompilerParams(vmem_limit_bytes=24 << 20),
        cost_estimate=pl.CostEstimate(flops=6_000_000_000, bytes_accessed=12_000_000, transcendentals=500_000),
        name="student_forward",
    )(place, before, after, head, labels, x, first, second, own)


def put_turned(ref, start, value, shift, width):
    rows, channels = value.shape
    col = iota(value.shape, 0) % width
    left = jnp.where(col >= shift, pltpu.roll(value, shift, 0), 0.0)
    right = jnp.where(col < width - shift, pltpu.roll(value, rows - shift, 0), 0.0)
    for tap, one in enumerate((left, value, right)):
        ref[tap * channels : (tap + 1) * channels, pl.ds(start, rows)] = one.T.astype(BF16)


def turn_kernel(
    width, before_ref, x_ref, after_ref, one_ref, two_ref, second_ref, xt_ref, ht_ref, twot_ref, wt_ref
):
    cells, channels = x_ref.shape
    halo = before_ref.shape[0]
    pair = 2 * width
    first = jnp.concatenate([before_ref[halo - width :], x_ref[:width]], axis=0).astype(F32)
    put_turned(xt_ref, 0, first, 1, width)
    last = jnp.concatenate([x_ref[cells - width :], after_ref[:width]], axis=0).astype(F32)
    put_turned(xt_ref, cells, last, 1, width)

    for start in range(pair, cells, pair):
        put_turned(xt_ref, start, x_ref[start - width : start + width, :].astype(F32), 1, width)
    for start in range(0, one_ref.shape[0], pair):
        put_turned(ht_ref, start, one_ref[start : start + pair, :].astype(F32), 2, width)
    for start in range(0, cells, MXU):
        twot_ref[:, start : start + MXU] = two_ref[start : start + MXU, :].astype(F32).T.astype(BF16)
    for i in range(3):
        for tap in range(3):
            part = slice(tap * channels, (tap + 1) * channels)
            mirror = slice((2 - tap) * channels, (3 - tap) * channels)
            wt_ref[i, part, :] = second_ref[i, mirror, :].astype(F32).T.astype(BF16)


def turn(before, x, after, one, two, second, width):
    cells, channels = x.shape
    shape = jax.ShapeDtypeStruct
    return pl.pallas_call(
        functools.partial(turn_kernel, width),
        in_specs=whole(6),
        out_specs=whole(4),
        out_shape=[
            shape((3 * channels, cells + 2 * width), BF16),
            shape((3 * channels, cells + 4 * width), BF16),
            shape((channels, cells), BF16),
            shape((3, 3 * channels, channels), BF16),
        ],
        compiler_params=pltpu.CompilerParams(vmem_limit_bytes=20 << 20),
        cost_estimate=pl.CostEstimate(flops=3_000_000_000, bytes_accessed=14_000_000, transcendentals=0),
        name="turn",
    )(before, x, after, one, two, second)


def head_kernel(
    scale, width, log_ref, base_ref, label_sum_ref, two_ref, twot_ref, head_ref, *refs
):
    *got_refs, grad_ref, top_ref, bottom_ref, head_grad_ref, got_ref, natural = refs
    slots, extended = got_ref.shape
    held = [one[...].astype(F32) for one in got_refs]
    held = [one[: one.shape[0] // 2] for one in held[:-1]] + held[-1:]
    got_ref[...] = jnp.concatenate(held, axis=0).astype(BF16)
    tiles = label_sum_ref.shape[0]
    flat = extended - 2 * LANES
    pixels = flat // 64
    edge = math.isqrt(pixels)
    across = width // edge
    index = got_ref[:, flat + LANES :].astype(F32)
    take = (index == (iota((slots, LANES), 1) + 1).astype(F32)).astype(F32).T[:tiles].astype(BF16)
    spread = join_lanes(dot(take, got_ref[:, flat : flat + LANES]))
    weight = 1.0 / (0.1 + spread)
    even = iota((tiles, LANES), 1) < 64
    loss = -label_sum_ref[...]
    for pair in range(pixels // 2):
        rows = slice(pair * tiles, (pair + 1) * tiles)
        if pair % 2 == 0:
            both = dot(take, got_ref[:, pair * LANES : (pair + 2) * LANES])
        mean = both[:, pair % 2 * LANES : (pair % 2 + 1) * LANES]
        cell = jnp.where(even, weight[:, 2 * pair : 2 * pair + 1], weight[:, 2 * pair + 1 : 2 * pair + 2])
        value = log_ref[rows, :]
        held = mean > 0
        loss = loss + cell * jnp.where(held, mean * (jnp.log(jnp.where(held, mean, 1.0)) - value), 0.0)
        grad = (cell * (jnp.exp(value) - mean) + base_ref[rows, :]) * scale
        turned = pltpu.roll(grad, 64, 1)
        row, col = 2 * pair // edge, 2 * pair % edge
        for down in range(tiles // across):
            start = (down * edge + row) * width + col
            natural[pl.ds(start, across, stride=edge), :] = grad[down * across : (down + 1) * across]
            natural[pl.ds(start + 1, across, stride=edge), :] = turned[down * across : (down + 1) * across]
    cells, channels = two_ref.shape
    logit_grad = natural[...].astype(BF16)
    head = jnp.concatenate([head_ref[...], jnp.zeros_like(head_ref)], axis=0)
    head_grad_ref[:channels, :] = dot(twot_ref[...], logit_grad)
    head_grad_ref[channels:, :] = loss
    block = 4 * width
    for start in range(0, cells, block):
        rows = slice(start, start + block)
        grad = dot(logit_grad[rows], head)
        grad_ref[rows, :] = jnp.where(two_ref[rows, :].astype(F32) > 0, grad, 0.0).astype(BF16)
    top_ref[...] = grad_ref[: 2 * width, :]
    bottom_ref[...] = grad_ref[cells - 2 * width :, :]


def head_step(got, log, base, label_sum, two, twot, head, scale, width):
    cells, channels = two.shape
    shape = jax.ShapeDtypeStruct
    return pl.pallas_call(
        functools.partial(head_kernel, scale, width),
        in_specs=whole(6 + len(got)),
        out_specs=whole(4),
        out_shape=[
            shape((cells, channels), BF16),
            shape((2 * width, channels), BF16),
            shape((2 * width, channels), BF16),
            shape((channels + label_sum.shape[0], LANES), F32),
        ],
        scratch_shapes=[
            pltpu.VMEM((2 * got[-1].shape[0], got[-1].shape[1]), BF16),
            pltpu.VMEM((cells, LANES), F32),
        ],
        compiler_params=pltpu.CompilerParams(vmem_limit_bytes=14 << 20),
        cost_estimate=pl.CostEstimate(flops=400_000_000, bytes_accessed=5_000_000, transcendentals=500_000),
        name="head_step",
    )(log, base, label_sum, two, twot, head, *got)


def inner_dots(ref, start, step, rows, weight_ref):
    total = None
    for tap in range(3):
        part = dot(ref[start + (2 - tap) * step : start + (2 - tap) * step + rows, :], weight_ref[tap])
        total = part if total is None else total + part
    return total


def second_kernel(width, ht_ref, grad_ref, wt_ref, one_ref, out_ref, inner_ref, gcat):
    cells, channels = grad_ref.shape
    block = 4 * width
    halo = 2 * width
    for start in range(0, cells, block):
        put_shifted(gcat, start, grad_ref[start : start + block, :].astype(F32), 2, width)
    for tap in range(3):
        part = dot(ht_ref[:, halo * tap : halo * tap + cells], grad_ref[...])
        out_ref[tap * 3 * channels : (tap + 1) * 3 * channels, :] = part.astype(BF16)
    for start in range(block, cells - block, block):
        value = inner_dots(gcat, start - halo, halo, block, wt_ref)
        held = one_ref[halo + start : halo + start + block, :].astype(F32) > 0
        inner_ref[start - block : start, :] = jnp.where(held, value, 0.0).astype(BF16)


def second_step(ht, grad, wt, one, width):
    cells, channels = grad.shape
    return pl.pallas_call(
        functools.partial(second_kernel, width),
        in_specs=whole(4),
        out_specs=whole(2),
        out_shape=[
            jax.ShapeDtypeStruct((9 * channels, channels), BF16),
            jax.ShapeDtypeStruct((cells - 8 * width, channels), BF16),
        ],
        scratch_shapes=[pltpu.VMEM((cells, 3 * channels), BF16)],
        compiler_params=pltpu.CompilerParams(vmem_limit_bytes=20 << 20),
        cost_estimate=pl.CostEstimate(flops=4_500_000_000, bytes_accessed=9_000_000, transcendentals=0),
        name="second_step",
    )(ht, grad, wt, one)


def first_kernel(width, plan, place_ref, before_ref, after_ref, grad_ref, head_grad_ref, second_ref, inner_ref, *refs):
    wt_ref, one_ref, xt_ref, *refs = refs
    chips, groups, near_rows, far_rows = plan
    keep_refs, give_refs, refs = refs[: chips + 1], refs[chips + 1 : 2 * chips + 2], refs[2 * chips + 2 :]
    gtop, gbottom, padded, halves, sem = refs
    cells, channels = grad_ref.shape
    rows = 9 * channels
    used = rows + channels // 2
    half = halves.shape[1]
    second_copy = pltpu.make_async_copy(second_ref, halves.at[1, pl.ds(0, rows)], sem)
    second_copy.start()
    halo = before_ref.shape[0]
    block = 4 * width
    inside = 3 * halo
    put_shifted(gtop, 0, before_ref[...].astype(F32), 2, width)
    put_shifted(gtop, halo, grad_ref[:inside, :].astype(F32), 2, width)
    put_shifted(gbottom, 0, grad_ref[cells - inside :, :].astype(F32), 2, width)
    put_shifted(gbottom, inside, after_ref[...].astype(F32), 2, width)
    padded[:halo, :] = jnp.zeros((halo, channels), BF16)
    padded[halo + cells :, :] = jnp.zeros((halo, channels), BF16)
    padded[halo + block : halo + cells - block, :] = inner_ref[...]
    for ref, start in ((gtop, 0), (gbottom, cells - block)):
        value = inner_dots(ref, 0, halo, block, wt_ref)
        held = one_ref[halo + start : halo + start + block, :].astype(F32) > 0
        padded[halo + start : halo + start + block, :] = jnp.where(held, value, 0.0).astype(BF16)
    span = cells + 2 * width
    for tap in range(3):
        part = dot(xt_ref[...], padded[(2 - tap) * width : (2 - tap) * width + span, :])
        halves[0, tap * 3 * channels : (tap + 1) * 3 * channels, :] = part.astype(BF16)
    lane = iota((channels // 2, LANES), 1)
    loss = jnp.sum(head_grad_ref[channels:, :])
    high = loss.astype(BF16).astype(F32)
    extra = jnp.where(lane == 64, high, jnp.where(lane == 65, loss - high, 0.0))
    extra = jnp.where(iota(lane.shape, 0) == place_ref[DEVICE] % (channels // 2), extra, 0.0)
    for side in range(2):
        value = jnp.where(lane < 64, head_grad_ref[side * channels // 2 : (side + 1) * channels // 2, :], extra)
        halves[0, rows:used, side * LANES : (side + 1) * LANES] = value.astype(BF16)
    if half > used:
        halves[0, used:, :] = jnp.zeros((half - used, channels), BF16)
    halves[1, rows:, :] = jnp.zeros((half - rows, channels), BF16)
    second_copy.wait()
    core, chip = place_ref[CORE], place_ref[CHIP]
    size = groups * near_rows
    for step in range(chips):
        low = pl.multiple_of((chip ^ step) * size, 16)
        give_refs[step][...] = halves[1 - core, pl.ds(low, size), :]
        keep_refs[step][...] = halves[core, pl.ds(low, size), :]
    give_refs[chips][...] = halves[1 - core, chips * size :, :]
    keep_refs[chips][...] = halves[core, chips * size :, :]


def first_step(place, before, after, grad, head_grad, second, inner, wt, one, xt, width, plan):
    cells, channels = grad.shape
    halo = before.shape[0]
    chips, groups, near_rows, far_rows = plan
    half_rows = chips * groups * (near_rows + far_rows)
    piece = [jax.ShapeDtypeStruct((groups * near_rows, channels), BF16)] * chips
    piece += [jax.ShapeDtypeStruct((chips * groups * far_rows, channels), BF16)]
    outs = pl.pallas_call(
        functools.partial(first_kernel, width, plan),
        in_specs=[scalars(), *whole(9)],
        out_specs=whole(2 * chips + 2),
        out_shape=piece * 2,
        scratch_shapes=[
            pltpu.VMEM((4 * halo, 3 * channels), BF16),
            pltpu.VMEM((4 * halo, 3 * channels), BF16),
            pltpu.VMEM((cells + 4 * width, channels), BF16),
            pltpu.VMEM((2, half_rows, channels), BF16),
            pltpu.SemaphoreType.DMA,
        ],
        compiler_params=pltpu.CompilerParams(vmem_limit_bytes=24 << 20),
        cost_estimate=pl.CostEstimate(flops=5_000_000_000, bytes_accessed=10_000_000, transcendentals=0),
        name="first_step",
    )(place, before, after, grad, head_grad, second, inner, wt, one, xt)
    return (outs[: chips + 1], outs[chips + 1 :])


def neighbours(first, last, axis):
    count = lax.axis_size(axis)
    up = [(i, i + 1) for i in range(count - 1)]
    down = [(i + 1, i) for i in range(count - 1)]
    return (lax.ppermute(last, axis, up), lax.ppermute(first, axis, down))


def pairwise(array, axis, step):
    count = lax.axis_size(axis)
    return lax.ppermute(array, axis, [(i, i ^ step) for i in range(count)])


def add(arrays):
    return functools.reduce(jnp.add, [array.astype(F32) for array in arrays]).astype(BF16)


def assemble_kernel(width, plan, cell_total, place_ref, *refs):
    chips, groups, near_rows, far_rows = plan
    pieces, refs = refs[: chips + 1], refs[chips + 1 :]
    own = len(refs) == 5
    if own:
        first_ref, second_ref, extra_ref, value_ref, sem = refs
    else:
        _, _, held_ref, first_ref, second_ref, head_ref, loss_ref, value_ref, sem = refs
    grad_rows = first_ref.shape[0]
    core, chip, member = place_ref[CORE], place_ref[CHIP], place_ref[MEMBER]
    for s in range(chips):
        value = pieces[s][...].astype(F32)
        for u in range(groups):
            start = pl.multiple_of(((chip ^ s) * groups + (member ^ u)) * near_rows, 8)
            value_ref[pl.ds(start, near_rows), :] = value[u * near_rows : (u + 1) * near_rows]
    value = pieces[chips][...].astype(F32)
    for u in range(groups):
        for s in range(chips):
            low = (u * chips + s) * far_rows
            start = chips * groups * near_rows + ((member ^ u) * chips + (chip ^ s)) * far_rows
            value_ref[pl.ds(pl.multiple_of(start, 8), far_rows), :] = value[low : low + far_rows]
    half = core if own else 1 - core
    filled = value_ref.at[pl.ds(0, grad_rows)]

    @pl.when(half == 0)
    def _():
        pltpu.make_async_copy(filled, first_ref, sem).start()

    @pl.when(half != 0)
    def _():
        pltpu.make_async_copy(filled, second_ref, sem).start()

    rows = width // 2
    extra = value_ref[grad_rows : grad_rows + rows, :]
    if own:
        extra_ref[...] = extra
    else:
        extra = jnp.where(core == 0, held_ref[...], extra)
        for side in range(2):
            part = extra[:, side * LANES : (side + 1) * LANES].T
            head_ref[:, side * rows : (side + 1) * rows] = part[: head_ref.shape[0]]
        lane = iota(extra.shape, 1)
        loss = jnp.sum(jnp.where((lane == 64) | (lane == 65), extra, 0.0), keepdims=True)
        loss_ref[...] = loss / cell_total
    pltpu.make_async_copy(filled, first_ref, sem).wait()


def assemble(place, pieces, plan, grad_rows, classes, cell_total):
    chips, groups, near_rows, far_rows = plan
    half_rows = chips * groups * (near_rows + far_rows)
    width = pieces[0].shape[1]
    shape = jax.ShapeDtypeStruct
    totals = [shape((grad_rows, width), F32)] * 2
    extra = shape((width // 2, width), F32)
    common = dict(
        scratch_shapes=[pltpu.VMEM((half_rows, width), F32), pltpu.SemaphoreType.DMA],
        compiler_params=pltpu.CompilerParams(vmem_limit_bytes=48 << 20),
        cost_estimate=pl.CostEstimate(flops=1_000_000, bytes_accessed=3_700_000, transcendentals=0),
        name="assemble",
    )
    kernel = functools.partial(assemble_kernel, width, plan, cell_total)
    count = chips + 1
    held = pl.pallas_call(
        kernel,
        in_specs=[scalars(), *whole(count)],
        out_specs=[*hbm(2), *whole(1)],
        out_shape=[*totals, extra],
        **common,
    )(place, *pieces[:count])
    return pl.pallas_call(
        kernel,
        in_specs=[scalars(), *whole(count), *hbm(2), *whole(1)],
        out_specs=[*hbm(2), *whole(2)],
        out_shape=[*totals, shape((classes, width), F32), shape((1, 1), F32)],
        input_output_aliases={count + 1: 0, count + 2: 1},
        **common,
    )(place, *pieces[count:], *held)


def gradient_pieces(place, keep, give, plan):
    chips, groups, near_rows, far_rows = plan
    got = [pairwise(one, "core", 1) for one in give]
    near = [add(pair) for pair in zip(keep[:chips], got[:chips])]
    far = [keep[chips], got[chips]]

    def block(arrays, axis, me, step, rows):
        start = (me ^ step) * rows
        return add([lax.dynamic_slice_in_dim(one, start, rows, axis=0) for one in arrays])

    chip, member = place[CHIP], place[MEMBER]
    far = [block(far, "member", member, step, chips * far_rows) for step in range(groups)]
    near = [near[0]] + [pairwise(near[step], "chip", step) for step in range(1, chips)]
    far = [far[0]] + [pairwise(far[step], "member", step) for step in range(1, groups)]
    near = [block(near, "member", member, step, near_rows) for step in range(groups)]
    far = [block(far, "chip", chip, step, far_rows) for step in range(chips)]
    near = add([near[0]] + [pairwise(near[step], "member", step) for step in range(1, groups)])
    far = add([far[0]] + [pairwise(far[step], "chip", step) for step in range(1, chips)])

    near = jnp.concatenate([near] + [pairwise(near, "member", step) for step in range(1, groups)], axis=0)
    far = jnp.concatenate([far] + [pairwise(far, "chip", step) for step in range(1, chips)], axis=0)
    near, far = lax.optimization_barrier((near, far))
    held = [near] + [pairwise(near, "chip", step) for step in range(1, chips)]
    far = jnp.concatenate([far] + [pairwise(far, "member", step) for step in range(1, groups)], axis=0)
    held += [far]
    return held + [pairwise(piece, "core", 1) for piece in held]


def body(teacher_logits, coverage, features, labels, first_weight, second_weight, head_weight):
    channels, classes = head_weight.shape
    members, tiles_here, flat_width = teacher_logits.shape
    pixels = flat_width // classes
    edge = math.isqrt(pixels)
    groups = lax.axis_size("member")
    chips = lax.axis_size("chip")
    columns = chips * 2
    tile_axes = ("chip", "core")
    block_tiles = tiles_here // groups
    capacity = max(2, 2 * block_tiles // columns)
    local = features[0]
    lines, width = local.shape[:2]
    cells = lines * width
    cell_total = groups * columns * cells
    column = lax.axis_index(tile_axes)
    place = jnp.stack(
        [
            lax.axis_index("core"),
            lax.axis_index("chip"),
            lax.axis_index("member"),
            lax.axis_index(("member", *tile_axes)),
            column == 0,
            column == columns - 1,
        ]
    ).astype(jnp.int32)
    flat = local.reshape(cells, channels)
    first_rows = first_weight.reshape(3, 3 * channels, channels)
    second_rows = second_weight.reshape(3, 3 * channels, channels)
    head = head_weight.T

    before, after = neighbours(flat[: 3 * width], flat[cells - 3 * width :], tile_axes)
    far = teacher_moments(teacher_logits, block_tiles, classes, 1)
    got = [pairwise(one, "member", step) for step, one in zip((3, 2), far)]
    near, own = teacher_moments(teacher_logits, block_tiles, classes, 0)
    got += [pairwise(near, "member", 1), own]
    label_rows = (
        labels[0].reshape(lines // edge, edge, width // edge, edge).transpose(0, 2, 1, 3).reshape(block_tiles, pixels)
    )
    one, two, log, base, label_sum = student_forward(
        place, before, after, head, label_rows, flat, first_rows, second_rows, own, width
    )
    xt, ht, twot, wt = turn(before, flat, after, one, two, second_rows, width)
    cover = coverage.reshape(groups, 1, block_tiles)
    sent = combine(got, cover, place, twot, classes, members, columns, capacity)
    received = [sent[0]] + [pairwise(sent[step], "chip", step) for step in range(1, chips)]
    passed = pairwise(jnp.concatenate([piece[capacity:] for piece in received], axis=0), "core", 1)
    received = [*received, passed]
    grad_two, top, bottom, head_grad = head_step(
        received, log, base, label_sum, two, twot, head, 1.0 / math.sqrt(cell_total), width
    )
    grad_before, grad_after = neighbours(top, bottom, tile_axes)
    second, inner = second_step(ht, grad_two, wt, one, width)
    rows, extra_rows = 9 * channels, channels // 2
    unit = 8 * groups * chips
    block_rows = -(-(rows + extra_rows) // unit) * 8
    far_rows = block_rows // 24 * 8
    plan = (chips, groups, block_rows - far_rows, far_rows)
    keep, give = first_step(
        place, grad_before, grad_after, grad_two, head_grad, second, inner, wt, one, xt, width, plan
    )
    pieces = gradient_pieces(place, keep, give, plan)
    first_total, second_total, head_total, loss = assemble(
        place, pieces, plan, rows, classes, cell_total
    )
    kernel_shape = (3, 3, channels, channels)
    return (first_total.reshape(kernel_shape), second_total.reshape(kernel_shape), head_total.T, loss[0, 0])


def solution(mesh):
    groups, columns = mesh.shape["member"], mesh.shape["tile"]
    split = jax.sharding.Mesh(mesh.devices.reshape(groups, columns // 2, 2), ("member", "chip", "core"))
    tile = ("chip", "core")
    return jax.shard_map(
        body,
        mesh=split,
        in_specs=(
            P("member", tile, None),
            P(tile),
            P("member", tile, None, None),
            P("member", tile, None),
            P(),
            P(),
            P(),
        ),
        out_specs=(P(), P(), P(), P()),
        check_vma=False,
    )
```
